32 devices in a mesh: pts: 8 (over z, y), mdl: 4 (over x, core).
Axes of the slice: x: 2, y: 2, z: 4, core: 2. Of those that a mesh axis runs over, the one named last changes fastest.
Arguments:
- points: bfloat16 [8192, 512], P('pts', 'mdl'), may hold values from -6 to 6
- cotangent: bfloat16 [8192, 512], P('pts', 'mdl'), may hold values from -6 to 6
- neighbours: int32 [8192, 27], P('pts'), may hold values from -1 to 8191, as said below
- scan_lengths: int32 [2], replicated, may hold values from 3584 to 4608, as said below
- to_patch: int32 [8192], P('pts'), may hold values from 0 to 16383, as said below
- from_patch: int32 [16384], P('pts'), may hold values from -1 to 8191, as said below
- owner_slot: int32 [40], replicated, may hold values from 0 to 39, as said below
- weights: float32 [40, 512, 512], P('mdl', 'pts')
- row_eigen_basis: float32 [40, 512, 512], P('mdl', 'pts'), may hold values from -1 to 1
- right_basis: float32 [40, 512, 512], P('mdl', 'pts'), may hold values from -1 to 1
- first_moment: float32 [40, 512, 512], P('mdl', 'pts'), may hold values from -64 to 64
- second_moment: float32 [40, 512, 512], P('mdl', 'pts'), may hold values from 4.096 to 65.536
- vectors: float32 [16, 512], P(None, 'mdl')
- vector_first: float32 [16, 512], P(None, 'mdl'), may hold values from -64 to 64
- vector_second: float32 [16, 512], P(None, 'mdl'), may hold values from 4.096 to 65.536
Outputs:
- out_points: bfloat16 [8192, 512], P('pts', 'mdl')
- point_grad: float32 [8192, 512], P('pts', 'mdl')
- weight_grad: float32 [40, 512, 512], P('mdl', 'pts')
- new_first: float32 [40, 512, 512], P('mdl', 'pts')
- new_second: float32 [40, 512, 512], P('mdl', 'pts')
- new_weights: float32 [40, 512, 512], P('mdl', 'pts')
- weights_bf16: bfloat16 [40, 512, 512], P('mdl', 'pts')
- vector_grad: float32 [16, 512], P(None, 'mdl')
- new_vector_first: float32 [16, 512], P(None, 'mdl')
- new_vector_second: float32 [16, 512], P(None, 'mdl')
- new_vectors: float32 [16, 512], P(None, 'mdl')
The draws below stay inside these ranges and needn't reach their ends.
Inputs may be any that keep to these rules, and one draw needn't show every extreme that they name: neighbours[p, t] = q >= 0 exactly when neighbours[q, 26 - t] = p; column (26) / 2 is p itself; |q - p| <= 256. `scan_lengths`: the lengths sum to 8192. `to_patch`: one to one; slots d * 2048 to (d + 1) * 2048 - 1 belong to index d of pts, which receives 1024 rows; of the rows of one index of pts at most 256 go to one index, exactly that many to some; in every patch the used slots come first and at least one is used. `from_patch`: the inverse of to_patch, -1 at unused slots. `owner_slot`: a permutation.
All inputs are finite; a program needn't handle non-finite values.
Results may differ from the reference program's by a relative error of at most 0.034.
Values may be sent and summed in bfloat16 or wider, within the bound.
A program may use at most 256 MiB of HBM per device.

```python
import math
import jax
import jax.numpy as jnp
from jax import lax

C = 512
HEADS = 32
HD = 16
FF = 2048
TAPS = 27
HALO = 256
PATCH = 1024
STEP = 5
TOK_DEV = 1024
TOKENS = 8192
SLOTS_DEV = 2048
NBLK = 40
NVEC = 16
N_PTS = 8


RESIDUES = 8


def owner_order(key):
    return jax.random.permutation(jax.random.fold_in(key, 501), NBLK).astype(jnp.int32)


def route_table(key):
    base_key = jax.random.fold_in(key, 502)
    key_sigma, key_rows, key_fill, key_place = jax.random.split(base_key, 4)
    share = TOK_DEV // N_PTS
    sigma = jax.random.permutation(key_sigma, N_PTS).astype(jnp.int32)
    device_ids = jnp.arange(N_PTS, dtype=jnp.int32)
    doubled = (device_ids[None, :] == sigma[:, None]).astype(jnp.int32)
    emptied = (device_ids[None, :] == jnp.roll(sigma, -1)[:, None]).astype(jnp.int32)
    counts = share + share * doubled - share * emptied
    ends = jnp.cumsum(counts, 1).astype(jnp.int32)
    starts = ends - counts
    arrive_base = (jnp.cumsum(counts, 0) - counts).astype(jnp.int32)
    position = jax.vmap(lambda row_key: jax.random.permutation(row_key, TOK_DEV))(jax.random.split(key_rows, N_PTS)).astype(jnp.int32)
    target = jnp.sum((ends[:, None, :] <= position[:, :, None]).astype(jnp.int32), -1)
    start_at = jnp.take_along_axis(starts, target, 1)
    arrival = jnp.take_along_axis(arrive_base, target, 1) + position - start_at
    placing = jax.vmap(lambda row_key: jax.random.permutation(row_key, TOK_DEV))(jax.random.split(key_place, N_PTS)).astype(jnp.int32)
    listed = placing[target, arrival]
    patch_count = TOK_DEV // PATCH + 1
    base_gap = PATCH // patch_count
    jitter = jax.random.randint(key_fill, (N_PTS, patch_count), 0, max(base_gap // 2, 1))
    gaps_head = base_gap + jitter[:, :-1] - jitter[:, 1:]
    gaps = jnp.concatenate([gaps_head, PATCH - jnp.sum(gaps_head, 1, keepdims=True)], 1)
    fills = PATCH - gaps
    fill_ends = jnp.cumsum(fills, 1).astype(jnp.int32)
    row_ends = fill_ends[target]
    patch_index = jnp.sum((row_ends <= listed[..., None]).astype(jnp.int32), -1)
    before = jnp.take_along_axis(row_ends - fills[target], patch_index[..., None], -1)[..., 0]
    slot_ids = target * (patch_count * PATCH) + patch_index * PATCH + listed - before
    return slot_ids.reshape(TOKENS).astype(jnp.int32)


def signed_cosines(key):
    key_freq, key_place, key_row, key_col = jax.random.split(key, 4)
    freq = jax.vmap(lambda row_key: jax.random.permutation(row_key, C))(jax.random.split(key_freq, NBLK)).astype(jnp.int32)
    place = jax.vmap(lambda row_key: jax.random.permutation(row_key, C))(jax.random.split(key_place, NBLK)).astype(jnp.int32)
    row_sign = (2 * jax.random.randint(key_row, (NBLK, C), 0, 2) - 1).astype(jnp.float32)
    col_sign = (2 * jax.random.randint(key_col, (NBLK, C), 0, 2) - 1).astype(jnp.float32)
    phase = (2 * place[:, None, :] + 1) * freq[:, :, None] % (4 * C)
    row_weight = jnp.where(freq == 0, (1.0 / C) ** 0.5, (2.0 / C) ** 0.5).astype(jnp.float32)
    table = jnp.cos(phase.astype(jnp.float32) * (math.pi / (2 * C)))
    return table * (row_weight * row_sign)[:, :, None] * col_sign[:, None, :]


def draw_neighbours(key, part):
    key = jax.random.fold_in(key, 3)
    key_base, key_mult, key_hit = jax.random.split(key, 3)
    half_taps = TAPS // 2
    base = jax.random.randint(key_base, (half_taps,), 1, RESIDUES + 1).astype(jnp.int32)
    base = base.at[0].set(RESIDUES)
    top = (HALO - base) // RESIDUES + 1
    mult = jax.random.randint(key_mult, (half_taps, RESIDUES), 0, top[:, None]).astype(jnp.int32)
    mult = mult.at[0, 0].set(HALO // RESIDUES - 1)
    offsets = base[:, None] + RESIDUES * mult
    hits = jax.random.randint(key_hit, (TOKENS, half_taps), 0, 2)
    row_ids = jnp.arange(TOKENS, dtype=jnp.int32)
    lower_off = offsets.T[row_ids % RESIDUES]
    lower_ids = row_ids[:, None] - lower_off
    lower = jnp.where((hits == 1) & (lower_ids >= 0), lower_ids, -1)
    upper_res = (row_ids[:, None] + base[None, :]) % RESIDUES
    upper_off = jnp.take_along_axis(offsets.T[upper_res], jnp.arange(half_taps)[None, :, None], 2)[..., 0]
    upper_ids = row_ids[:, None] + upper_off
    upper_hits = jnp.take_along_axis(hits, jnp.minimum(upper_ids, TOKENS - 1), 0)
    upper = jnp.where((upper_hits == 1) & (upper_ids < TOKENS), upper_ids, -1)
    return jnp.concatenate([lower, row_ids[:, None], upper[:, ::-1]], 1).astype(jnp.int32)


def draw_scan_lengths(key, part):
    key = jax.random.fold_in(key, 4)
    sign_bit = jax.random.randint(key, (), 0, 2)
    offset = (2 * sign_bit - 1) * (TOKENS // 8 - TOK_DEV // 2)
    leading = TOKENS // 2 + offset
    return jnp.stack([leading, TOKENS - leading]).astype(jnp.int32)


def draw_to_patch(key, part):
    return route_table(key)


def draw_from_patch(key, part):
    slot_ids = route_table(key)
    empty = jnp.full((N_PTS * SLOTS_DEV,), -1, jnp.int32)
    return empty.at[slot_ids].set(jnp.arange(TOKENS, dtype=jnp.int32))


def draw_owner_slot(key, part):
    return owner_order(key)


def draw_weights(key, part):
    block_of_slot = jnp.argsort(owner_order(key))
    key = jax.random.fold_in(key, 5)
    block_ids = jnp.arange(NBLK)
    scales = jnp.where(block_ids < TAPS, (14.0 * C) ** (-0.5), C ** (-0.5))
    scales = jnp.where(block_ids == TAPS + 4, 16.0 * C ** (-0.5), scales)
    scales = jnp.where(block_ids >= TAPS + 5 + FF // C, 1.5 * FF ** (-0.5), scales)
    values = jax.random.normal(key, (NBLK, C, C), jnp.float32)
    return values * scales[block_of_slot][:, None, None].astype(jnp.float32)


def draw_row_eigen_basis(key, part):
    key = jax.random.fold_in(key, 6)
    return signed_cosines(key)


def draw_right_basis(key, part):
    key = jax.random.fold_in(key, 7)
    return signed_cosines(key)


def draw_vectors(key, part):
    key = jax.random.fold_in(key, 8)
    key_gain, key_shift = jax.random.split(key)
    gains = jax.random.uniform(key_gain, (NVEC, C), jnp.float32, 0.6, 1.4)
    shifts = 0.3 * jax.random.normal(key_shift, (NVEC, C), jnp.float32)
    row_ids = jnp.arange(NVEC)[:, None]
    is_gain = (row_ids == 2) | (row_ids == 4) | (row_ids == 9)
    return jnp.where(is_gain, gains, shifts)


def block_scale(rng, shape, shards, low, largest):
    loudness = 1.0
    for dim, parts in shards:
        steps = jax.random.uniform(jax.random.fold_in(jax.random.fold_in(rng, 6), dim), (parts,), jnp.float32, low / len(shards), largest / len(shards))
        loudness = loudness * jnp.repeat(jnp.exp(steps), shape[dim] // parts).reshape((-1,) + (1,) * (len(shape) - 1 - dim))
    return loudness


def noise(stream_key, extent, scale, limit, pieces=(), kind=jnp.bfloat16):
    values = scale * jax.random.normal(stream_key, extent, jnp.float32)
    if pieces:
        values = values * block_scale(stream_key, extent, pieces, -0.22, 0.18)
    return jnp.clip(values, -limit, limit).astype(kind)


def setup_inputs(seed: int = 0) -> dict:
    splits = jax.random.split(jax.random.key(seed), 16)
    return {
        "points": noise(splits[0], (TOKENS, C), 1.0, 6.0, ((0, 8), (1, 4))),
        "cotangent": noise(splits[1], (TOKENS, C), 1.0, 6.0, ((0, 8), (1, 4))),
        "neighbours": draw_neighbours(jax.random.fold_in(splits[15], 71), 0),
        "scan_lengths": draw_scan_lengths(jax.random.fold_in(splits[15], 71), 0),
        "to_patch": draw_to_patch(jax.random.fold_in(splits[15], 71), 0),
        "from_patch": draw_from_patch(jax.random.fold_in(splits[15], 71), 0),
        "owner_slot": draw_owner_slot(jax.random.fold_in(splits[15], 71), 0),
        "weights": draw_weights(jax.random.fold_in(splits[15], 71), 0),
        "row_eigen_basis": draw_row_eigen_basis(jax.random.fold_in(splits[15], 71), 0),
        "right_basis": draw_right_basis(jax.random.fold_in(splits[15], 71), 0),
        "first_moment": noise(splits[10], (NBLK, C, C), (0.11 * TOKENS ** 0.5), 64.0, ((0, 4), (1, 8)), jnp.float32),
        "second_moment": jnp.clip(jnp.exp(math.log(65.536) - 2.7725887 * jax.random.uniform(splits[11], (NBLK, C, C), jnp.float32) ** block_scale(splits[11], (NBLK, C, C), ((0, 4), (1, 8)), -0.2, 0.2)), 4.096, 65.536),
        "vectors": draw_vectors(jax.random.fold_in(splits[15], 71), 0),
        "vector_first": noise(splits[13], (NVEC, C), (0.11 * TOKENS ** 0.5), 64.0, ((1, 4),), jnp.float32),
        "vector_second": jnp.clip(jnp.exp(math.log(65.536) - 2.7725887 * jax.random.uniform(splits[14], (NVEC, C), jnp.float32) ** block_scale(splits[14], (NVEC, C), ((1, 4),), -0.2, 0.2)), 4.096, 65.536),
    }


EXACT_PRECISION = lax.Precision.HIGHEST
NORM_EPS = 1e-05
BETA_ONE = 0.9
BETA_TWO = 0.999
ADAM_EPS = 1e-08
VECTOR_RATE = 0.5
MATRIX_DECAY = 0.05
MASKED = -1e+30

@jax.custom_vjp
def low(v):
    return lax.optimization_barrier(v.astype(jnp.bfloat16)).astype(jnp.float32)

@jax.custom_vjp
def low_back(v):
    return v

def low_keep(v):
    return (low(v), None)

def low_pass(kept, grad):
    return (grad,)

def back_keep(v):
    return (v, None)

def back_low(kept, grad):
    return (low(grad),)
low.defvjp(low_keep, low_pass)
low_back.defvjp(back_keep, back_low)

def product(left_side, right_product):
    return jnp.dot(left_side, right_product, precision=EXACT_PRECISION, preferred_element_type=jnp.float32)

def layer_norm(values, gain_row, shift_row):
    row_mean = lax.optimization_barrier(jnp.mean(values, -1, keepdims=True))
    centred = values - row_mean
    spread = lax.optimization_barrier(jnp.mean(centred * centred, -1, keepdims=True))
    return centred * lax.rsqrt(spread + NORM_EPS) * gain_row + shift_row

def scan_index(row_ids, scan_lengths):
    bounds = jnp.cumsum(scan_lengths).astype(jnp.int32)
    return lax.optimization_barrier(jnp.sum((row_ids[..., None] >= bounds[:-1]).astype(jnp.int32), -1))

def layer(points32, weight_stack, vector_rows, neighbours, scan_lengths, to_patch, from_patch, owner_slot):
    blocks = weight_stack[owner_slot]
    ff_blocks = FF // C
    tap_maps = blocks[:TAPS]
    linear_map = blocks[TAPS]
    query_map = blocks[TAPS + 1]
    key_map = blocks[TAPS + 2]
    value_map = blocks[TAPS + 3]
    projection = blocks[TAPS + 4]
    first_mlp = jnp.concatenate([blocks[TAPS + 5 + block_id] for block_id in range(ff_blocks)], 1)
    second_mlp = jnp.concatenate([blocks[TAPS + 5 + ff_blocks + block_id].T for block_id in range(ff_blocks)], 0)
    first_bias = vector_rows[11:11 + ff_blocks].reshape(FF)
    row_ids = jnp.arange(TOKENS, dtype=jnp.int32)
    own_scan = scan_index(row_ids, scan_lengths)
    safe_ids = jnp.where(neighbours >= 0, neighbours, 0).astype(jnp.int32)
    usable = (neighbours >= 0) & (scan_index(safe_ids, scan_lengths) == own_scan[:, None])
    tap_rows = jnp.where(usable, neighbours, TOKENS).astype(jnp.int32)
    padded = jnp.concatenate([points32, jnp.zeros((1, C), jnp.float32)], 0)

    def conv_block(block_id):
        start = block_id * TOK_DEV
        block_taps = lax.dynamic_slice_in_dim(tap_rows, start, TOK_DEV, 0)
        own_rows = lax.dynamic_slice_in_dim(points32, start, TOK_DEV, 0)
        running = jnp.zeros((TOK_DEV, C), jnp.float32)
        for tap_id in range(TAPS):
            running = running + product(padded[block_taps[:, tap_id]], tap_maps[tap_id].T)
        hidden = low(low_back(running + vector_rows[0]))
        mixed_rows = low_back(product(hidden, linear_map) + vector_rows[1])
        stream_one = own_rows + layer_norm(mixed_rows, vector_rows[2], vector_rows[3])
        normed = low(layer_norm(stream_one, vector_rows[4], vector_rows[5]))
        return (stream_one, normed)
    stream_one, normed = lax.map(jax.checkpoint(conv_block), jnp.arange(N_PTS, dtype=jnp.int32))
    stream_one = stream_one.reshape(TOKENS, C)
    normed = normed.reshape(TOKENS, C)
    slot_total = from_patch.shape[0]
    filled = from_patch >= 0
    safe_slots = jnp.where(filled, from_patch, 0).astype(jnp.int32)
    slot_scan = jnp.where(filled, scan_index(safe_slots, scan_lengths), -1)
    normed_pad = jnp.concatenate([normed, jnp.zeros((1, C), jnp.float32)], 0)
    slot_in = low_back(normed_pad[jnp.where(filled, from_patch, TOKENS).astype(jnp.int32)])
    score_scale = HD ** (-0.5)

    def patch_block(patch_id):
        start = patch_id * PATCH
        rows_in = lax.dynamic_slice_in_dim(slot_in, start, PATCH, 0)
        key_valid = lax.dynamic_slice_in_dim(filled, start, PATCH, 0)
        scan_group = lax.dynamic_slice_in_dim(slot_scan, start, PATCH, 0)
        queries = low(low_back(product(rows_in, query_map) + vector_rows[6])).reshape(PATCH, HEADS, HD)
        keys_in = low(low_back(product(rows_in, key_map))).reshape(PATCH, HEADS, HD)
        values_in = low(low_back(product(rows_in, value_map) + vector_rows[7])).reshape(PATCH, HEADS, HD)
        scores = low_back(jnp.einsum('qhd,khd->hqk', queries, keys_in, precision=EXACT_PRECISION) * score_scale)
        allowed = key_valid[None, :] & ((scan_group[:, None] == scan_group[None, :]) | ~key_valid[:, None])
        scores = jnp.where(allowed[None], scores, MASKED)
        soft_weights = low(jax.nn.softmax(scores, -1))
        attended = jnp.einsum('hqk,khd->qhd', soft_weights, values_in, precision=EXACT_PRECISION).reshape(PATCH, C)
        attended = low(low_back(attended))
        return low(low_back(product(attended, projection.T) + vector_rows[8]))
    branch = lax.map(jax.checkpoint(patch_block), jnp.arange(slot_total // PATCH, dtype=jnp.int32))
    branch = branch.reshape(slot_total, C)
    stream_two = stream_one + branch[to_patch]

    def mlp_block(block_id):
        start = block_id * TOK_DEV
        own_rows = lax.dynamic_slice_in_dim(stream_two, start, TOK_DEV, 0)
        normed_two = low(layer_norm(own_rows, vector_rows[9], vector_rows[10]))
        pre_act = low_back(product(normed_two, first_mlp) + first_bias)
        activ = low(jax.nn.gelu(pre_act, approximate=False))
        return own_rows + low_back(product(activ, second_mlp) + vector_rows[11 + ff_blocks])
    result = lax.map(jax.checkpoint(mlp_block), jnp.arange(N_PTS, dtype=jnp.int32))
    return result.reshape(TOKENS, C)

def reference(points, cotangent, neighbours, scan_lengths, to_patch, from_patch, owner_slot, weights, row_eigen_basis, right_basis, first_moment, second_moment, vectors, vector_first, vector_second):
    matrix_rate = 1.6 * C ** (-0.5)

    def forward(points32, weight_stack, vector_rows):
        return layer(points32, weight_stack, vector_rows, neighbours, scan_lengths, to_patch, from_patch, owner_slot)
    result, pullback = jax.vjp(forward, points.astype(jnp.float32), weights, vectors)
    point_grad, weight_grad, vector_grad = pullback(cotangent.astype(jnp.float32))
    right_product = jnp.einsum('brc,bcd->brd', weight_grad, right_basis, precision=EXACT_PRECISION)
    rotated_gradient = jnp.einsum('gfo,gfu->gou', row_eigen_basis, right_product, precision=EXACT_PRECISION)
    new_first = BETA_ONE * first_moment + (1.0 - BETA_ONE) * rotated_gradient
    new_second = BETA_TWO * second_moment + (1.0 - BETA_TWO) * rotated_gradient * rotated_gradient
    direction = new_first / (1.0 - BETA_ONE ** STEP) / (jnp.sqrt(new_second / (1.0 - BETA_TWO ** STEP)) + ADAM_EPS)
    turned_matrix = jnp.einsum('bic,bdc->bid', direction, right_basis, precision=EXACT_PRECISION)
    update_direction = jnp.einsum('zua,zaf->zuf', row_eigen_basis, turned_matrix, precision=EXACT_PRECISION)
    new_weights = weights - matrix_rate * (update_direction + MATRIX_DECAY * weights)
    new_vector_first = BETA_ONE * vector_first + (1.0 - BETA_ONE) * vector_grad
    new_vector_second = BETA_TWO * vector_second + (1.0 - BETA_TWO) * vector_grad * vector_grad
    vector_step = new_vector_first / (1.0 - BETA_ONE ** STEP) / (jnp.sqrt(new_vector_second / (1.0 - BETA_TWO ** STEP)) + ADAM_EPS)
    new_vectors = vectors - VECTOR_RATE * vector_step
    return (result.astype(jnp.bfloat16), point_grad, weight_grad, new_first, new_second, new_weights, new_weights.astype(jnp.bfloat16), vector_grad, new_vector_first, new_vector_second, new_vectors)
```

```python
import functools

import jax
import jax.numpy as jnp
from jax import lax
from jax.experimental import pallas as pl
from jax.experimental.pallas import tpu as pltpu
from jax.sharding import PartitionSpec as P

C = 512
HD = 16
FF = 2048
TAPS = 27
HALO = 256
PATCH = 1024
STEP = 5

NORM_EPS = 1e-05
BETA_ONE = 0.9
BETA_TWO = 0.999
ADAM_EPS = 1e-08
VECTOR_RATE = 0.5
MATRIX_DECAY = 0.05
TILE = 256
WINDOW = TILE + 2 * HALO
BF = jnp.bfloat16
F32 = jnp.float32
VMEM_LIMIT = 48 * 1024 * 1024

NN = (((1,), (0,)), ((), ()))
NT = (((1,), (1,)), ((), ()))
TN = (((0,), (0,)), ((), ()))


def dot(a, b, dims=NN):
    return lax.dot_general(a, b, dims, preferred_element_type=F32)


def params(**kw):
    return pltpu.CompilerParams(vmem_limit_bytes=VMEM_LIMIT, **kw)


def one_hot_window(ids_ref, tap, tile):
    row = ids_ref[pl.ds(tap, 1), pl.ds(tile * TILE, TILE)]
    places = lax.broadcasted_iota(jnp.int32, (WINDOW, TILE), 0) + tile * TILE
    return jnp.where(places == row, 1.0, 0.0).astype(BF)


def gather_kernel(ids_ref, ext_ref, out_ref):
    tap = pl.program_id(0)
    for tile in range(out_ref.shape[2] // TILE):
        hot = one_hot_window(ids_ref, tap, tile)
        taken = dot(ext_ref[:, tile * TILE : tile * TILE + WINDOW], hot)
        out_ref[0, :, tile * TILE : (tile + 1) * TILE] = taken.astype(BF)


def gather_taps(ids, ext):
    taps, rows = ids.shape
    cols = ext.shape[0]
    return pl.pallas_call(
        gather_kernel,
        grid=(taps,),
        in_specs=[
            pl.BlockSpec(ids.shape, lambda t: (0, 0)),
            pl.BlockSpec(ext.shape, lambda t: (0, 0)),
        ],
        out_specs=pl.BlockSpec((1, cols, rows), lambda t: (t, 0, 0)),
        out_shape=jax.ShapeDtypeStruct((taps, cols, rows), BF),
        compiler_params=params(),
        cost_estimate=pl.CostEstimate(
            flops=2 * taps * rows * WINDOW * cols * 2,
            bytes_accessed=taps * rows * cols * 2,
            transcendentals=0,
        ),
        name="gather_taps",
    )(ids, ext)


GROUP = 3


def conv_kernel(slot_ref, *refs):
    w_refs, x_ref, out_ref, acc_ref = refs[:GROUP], refs[GROUP], refs[GROUP + 1], refs[GROUP + 2]
    step = pl.program_id(0)

    @pl.when(step == 0)
    def _():
        acc_ref[...] = jnp.zeros_like(acc_ref)

    total = acc_ref[...]
    for j in range(GROUP):
        w = w_refs[j][...].reshape(C, x_ref.shape[1])
        total = total + dot(w, x_ref[j])
    acc_ref[...] = total

    @pl.when(step == pl.num_programs(0) - 1)
    def _():
        out_ref[...] = acc_ref[...].T.astype(BF)


def weight_spec(shape, pick):
    return pl.BlockSpec(
        (shape[0], 1, shape[2], shape[3]), lambda t, slots: (0, slots[pick(t)], 0, 0)
    )


def conv_forward(owner_slot, blocks, taken):
    taps, cols, rows = taken.shape
    specs = [weight_spec(blocks.shape, lambda t, j=j: t * GROUP + j) for j in range(GROUP)]
    return pl.pallas_call(
        conv_kernel,
        grid_spec=pltpu.PrefetchScalarGridSpec(
            num_scalar_prefetch=1,
            grid=(taps // GROUP,),
            in_specs=specs + [pl.BlockSpec((GROUP, cols, rows), lambda t, s: (t, 0, 0))],
            out_specs=pl.BlockSpec((rows, C), lambda t, s: (0, 0)),
            scratch_shapes=[pltpu.VMEM((C, rows), F32)],
        ),
        out_shape=jax.ShapeDtypeStruct((rows, C), BF),
        compiler_params=params(),
        cost_estimate=pl.CostEstimate(
            flops=2 * taps * rows * C * cols,
            bytes_accessed=taps * (rows + C) * cols * 2,
            transcendentals=0,
        ),
        name="conv_forward",
    )(owner_slot, *([blocks] * GROUP), taken)


def tap_grad_kernel(back_ref, x_ref, out_ref):
    grad = dot(back_ref[...], x_ref[0], NT)
    out_ref[...] = grad.astype(BF).reshape(out_ref.shape)


def tap_grads(back, taken, parts):
    taps, cols, rows = taken.shape
    share = C // parts
    return pl.pallas_call(
        tap_grad_kernel,
        grid=(taps,),
        in_specs=[
            pl.BlockSpec((C, rows), lambda t: (0, 0)),
            pl.BlockSpec((1, cols, rows), lambda t: (t, 0, 0)),
        ],
        out_specs=pl.BlockSpec((parts, 1, share, cols), lambda t: (0, t, 0, 0)),
        out_shape=jax.ShapeDtypeStruct((parts, taps, share, cols), BF),
        compiler_params=params(),
        cost_estimate=pl.CostEstimate(
            flops=2 * taps * rows * C * cols,
            bytes_accessed=taps * (rows + C) * cols * 2,
            transcendentals=0,
        ),
        name="tap_grads",
    )(back, taken)


def conv_back_kernel(slot_ref, w_ref, ids_ref, back_ref, out_ref, acc_ref):
    tap = pl.program_id(0)
    cols, rows = acc_ref.shape

    @pl.when(tap == 0)
    def _():
        acc_ref[...] = jnp.zeros_like(acc_ref)

    turned = dot(w_ref[...].reshape(C, cols), back_ref[...], TN).astype(BF)
    for tile in range(rows // TILE):
        hot = one_hot_window(ids_ref, tap, tile)
        acc_ref[:, tile * TILE : (tile + 1) * TILE] += dot(
            turned[:, tile * TILE : tile * TILE + WINDOW], hot
        )

    @pl.when(tap == pl.num_programs(0) - 1)
    def _():
        out_ref[...] = acc_ref[...].T


def conv_back(owner_slot, blocks, ids, back_ext):
    taps, rows = ids.shape
    cols = blocks.shape[3]
    return pl.pallas_call(
        conv_back_kernel,
        grid_spec=pltpu.PrefetchScalarGridSpec(
            num_scalar_prefetch=1,
            grid=(taps,),
            in_specs=[
                weight_spec(blocks.shape, lambda t: taps - 1 - t),
                pl.BlockSpec(ids.shape, lambda t, s: (0, 0)),
                pl.BlockSpec(back_ext.shape, lambda t, s: (0, 0)),
            ],
            out_specs=pl.BlockSpec((rows, cols), lambda t, s: (0, 0)),
            scratch_shapes=[pltpu.VMEM((cols, rows), F32)],
        ),
        out_shape=jax.ShapeDtypeStruct((rows, cols), F32),
        compiler_params=params(),
        cost_estimate=pl.CostEstimate(
            flops=taps * rows * (WINDOW * 4 + 3 * C) * cols,
            bytes_accessed=taps * C * cols * 2,
            transcendentals=0,
        ),
        name="conv_back",
    )(owner_slot, blocks, ids, back_ext)


def head_lanes(ext, cols, head):
    lane = lax.broadcasted_iota(jnp.int32, ext.shape, 1)
    return jnp.where((lane >= cols) | (lane // HD == head), ext, jnp.zeros_like(ext))


def attend_kernel(q_ref, k_ref, v_ref, out_ref, lse_ref):
    head = pl.program_id(0)
    rows, width = q_ref.shape
    keys = k_ref[...]
    values = v_ref[0]
    for tile in range(rows // TILE):
        span = slice(tile * TILE, (tile + 1) * TILE)
        queries = head_lanes(q_ref[span, :], width // 2, head)
        scores = dot(keys, queries, NT)
        top = jnp.max(scores, 0, keepdims=True)
        soft = jnp.exp(scores - top).astype(BF)
        summed = dot(values, soft)
        total = summed[HD : HD + 1]
        out_ref[:, span] = (summed[:HD] / total).astype(BF)
        lse_ref[0, :, span] = top + jnp.log(total)


def attend(q_ext, k_ext, v_aug):
    rows, width = q_ext.shape
    heads = v_aug.shape[0]
    return pl.pallas_call(
        attend_kernel,
        grid=(heads,),
        in_specs=[
            pl.BlockSpec((rows, width), lambda h: (0, 0)),
            pl.BlockSpec((rows, width), lambda h: (0, 0)),
            pl.BlockSpec((1, 2 * HD, rows), lambda h: (h, 0, 0)),
        ],
        out_specs=[
            pl.BlockSpec((HD, rows), lambda h: (h, 0)),
            pl.BlockSpec((1, 1, rows), lambda h: (h, 0, 0)),
        ],
        out_shape=[
            jax.ShapeDtypeStruct((heads * HD, rows), BF),
            jax.ShapeDtypeStruct((heads, 1, rows), F32),
        ],
        compiler_params=params(),
        cost_estimate=pl.CostEstimate(
            flops=2 * heads * rows * rows * width, bytes_accessed=rows * width * 6, transcendentals=heads * rows * rows
        ),
        name="attend",
    )(q_ext, k_ext, v_aug)


def attend_back_kernel(
    q_ref, k_ref, kt_ref, v_ref, do_ref, lse_ref, inner_ref, dq_ref, dk_ref, dv_ref, dk_acc, dv_acc
):
    head = pl.program_id(0)
    rows, width = q_ref.shape
    cols = width // 2

    @pl.when(head == 0)
    def _():
        dk_acc[...] = jnp.zeros_like(dk_acc)
        dv_acc[...] = jnp.zeros_like(dv_acc)

    queries = head_lanes(q_ref[...], cols, head)
    pure = queries[:, :cols]
    grad = head_lanes(do_ref[...], cols, head)
    lse = lse_ref[0]
    inner = inner_ref[0]
    dq = jnp.zeros((HD, rows), F32)
    for tile in range(rows // TILE):
        span = slice(tile * TILE, (tile + 1) * TILE)
        scores = dot(k_ref[span, :], queries, NT)
        soft = jnp.exp(scores - lse)
        grad_soft = dot(v_ref[span, :], grad, NT)
        grad_scores = (soft * (grad_soft - inner)).astype(BF)
        dv_acc[span, :] += dot(soft.astype(BF), grad)
        dk_acc[span, :] += dot(grad_scores, pure)
        dq = dq + dot(kt_ref[:, span], grad_scores)
    dq_ref[...] = (dq * HD ** (-0.5)).astype(BF)

    @pl.when(head == pl.num_programs(0) - 1)
    def _():
        dk_ref[...] = dk_acc[...].astype(BF)
        dv_ref[...] = dv_acc[...].astype(BF)


def attend_back(q_ext, k_ext, keys_t, values, grad, lse, inner):
    rows, width = q_ext.shape
    cols = width // 2
    heads = cols // HD
    whole = lambda h: (0, 0)
    return pl.pallas_call(
        attend_back_kernel,
        grid=(heads,),
        in_specs=[
            pl.BlockSpec((rows, width), whole),
            pl.BlockSpec((rows, width), whole),
            pl.BlockSpec((HD, rows), lambda h: (h, 0)),
            pl.BlockSpec((rows, cols), whole),
            pl.BlockSpec((rows, cols), whole),
            pl.BlockSpec((1, 1, rows), lambda h: (h, 0, 0)),
            pl.BlockSpec((1, 1, rows), lambda h: (h, 0, 0)),
        ],
        out_specs=[
            pl.BlockSpec((HD, rows), lambda h: (h, 0)),
            pl.BlockSpec((rows, cols), whole),
            pl.BlockSpec((rows, cols), whole),
        ],
        out_shape=[
            jax.ShapeDtypeStruct((cols, rows), BF),
            jax.ShapeDtypeStruct((rows, cols), BF),
            jax.ShapeDtypeStruct((rows, cols), BF),
        ],
        scratch_shapes=[pltpu.VMEM((rows, cols), F32), pltpu.VMEM((rows, cols), F32)],
        compiler_params=params(),
        cost_estimate=pl.CostEstimate(
            flops=5 * heads * rows * rows * width, bytes_accessed=rows * width * 20, transcendentals=heads * rows * rows
        ),
        name="attend_back",
    )(q_ext, k_ext, keys_t, values, grad, lse, inner)


def widen(shard_rows):
    return lax.all_gather(shard_rows, "mdl", axis=1, tiled=True)


def add_parts(partial_value):
    return lax.psum_scatter(
        partial_value.astype(BF), "mdl", scatter_dimension=1, tiled=True
    ).astype(F32)


def trade(buffer):
    return lax.all_to_all(buffer, "pts", split_axis=0, concat_axis=0, tiled=True)


def scan_index(row_ids, scan_lengths):
    bounds = jnp.cumsum(scan_lengths)
    return jnp.sum((row_ids[..., None] >= bounds[:-1]).astype(jnp.int32), -1)


def count(mask):
    return jnp.sum(mask.astype(jnp.int32), 1)


def unit_rows(values):
    mean = jnp.mean(values, -1, keepdims=True)
    centred = values - mean
    inv_std = lax.rsqrt(jnp.mean(centred * centred, -1, keepdims=True) + NORM_EPS)
    return centred * inv_std, inv_std


def unit_back(grad_unit, unit, inv_std):
    mean = jnp.mean(grad_unit, -1, keepdims=True)
    cross = jnp.mean(grad_unit * unit, -1, keepdims=True)
    return inv_std * (grad_unit - mean - unit * cross)


def gelu_slope(pre_act):
    return (
        0.5 * (1.0 + lax.erf(pre_act * 0.7071067811865476))
        + pre_act * jnp.exp(-0.5 * pre_act * pre_act) * 0.3989422804014327
    )


def adam(first, second, grad):
    new_first = BETA_ONE * first + (1.0 - BETA_ONE) * grad
    new_second = BETA_TWO * second + (1.0 - BETA_TWO) * grad * grad
    direction = (
        new_first
        / (1.0 - BETA_ONE**STEP)
        / (jnp.sqrt(new_second / (1.0 - BETA_TWO**STEP)) + ADAM_EPS)
    )
    return new_first, new_second, direction


def local(
    points,
    cotangent,
    neighbours,
    scan_lengths,
    to_patch,
    from_patch,
    owner_slot,
    weights,
    row_eigen_basis,
    right_basis,
    first_moment,
    second_moment,
    vectors,
    vector_first,
    vector_second,
):
    rows, cols = points.shape
    slot_count = from_patch.shape[0]
    pts = lax.axis_size("pts")
    mdl = lax.axis_size("mdl")
    pts_index = lax.axis_index("pts")
    mdl_index = lax.axis_index("mdl")
    heads = cols // HD
    ff_blocks = FF // C
    patch_count = slot_count // PATCH
    capacity = 2 * rows // pts
    matrix_rate = 1.6 * C ** (-0.5)

    def own(full):
        return lax.dynamic_slice_in_dim(full, mdl_index * cols, cols, full.ndim - 1)

    spread = lax.all_to_all(
        weights.astype(BF), "mdl", split_axis=2, concat_axis=0, tiled=True
    )
    blocks = lax.all_gather(spread, "pts", axis=0)
    vec = lax.all_gather(vectors, "mdl", axis=1, tiled=True)
    points_full = widen(points)
    cot_full = widen(cotangent)

    def block(b):
        return blocks[:, owner_slot[b]].reshape(C, cols)

    up = [(i, i + 1) for i in range(pts - 1)]
    down = [(i + 1, i) for i in range(pts - 1)]
    low_halo = lax.ppermute(points[rows - HALO :], "pts", up)
    high_halo = lax.ppermute(points[:HALO], "pts", down)
    ext = jnp.concatenate([low_halo, points, high_halo], 0).T
    row_ids = pts_index * rows + jnp.arange(rows, dtype=jnp.int32)
    own_scan = scan_index(row_ids, scan_lengths)
    near = neighbours.T
    usable = (near >= 0) & (scan_index(jnp.maximum(near, 0), scan_lengths) == own_scan[None, :])
    ids = jnp.where(usable, near - (pts_index * rows - HALO), -1)
    taken = gather_taps(ids, ext)
    conv_part = conv_forward(owner_slot, blocks, taken)

    target = to_patch // slot_count
    place = jnp.arange(rows, dtype=jnp.int32)
    rank = count((target[None, :] == target[:, None]) & (place[None, :] < place[:, None]))
    send_pos = target * capacity + rank
    buffer_ids = jnp.arange(pts * capacity, dtype=jnp.int32)
    pack = (buffer_ids[:, None] == send_pos[None, :]).astype(BF)
    held = jnp.zeros((rows + PATCH,), jnp.int32)
    held_patch = jnp.zeros((rows + PATCH,), jnp.int32)
    offset = jnp.int32(0)
    for patch in range(patch_count):
        part = from_patch[patch * PATCH : (patch + 1) * PATCH]
        held = lax.dynamic_update_slice(held, part, (offset,))
        held_patch = lax.dynamic_update_slice(
            held_patch, jnp.full((PATCH,), patch, jnp.int32), (offset,)
        )
        offset = offset + jnp.sum((part >= 0).astype(jnp.int32))
    held = held[:rows]
    held_patch = held_patch[:rows]
    source = held // rows
    arrival = source * capacity + count(
        (source[None, :] == source[:, None]) & (held[None, :] < held[:, None])
    )
    order_key = held_patch * (pts * rows) + held
    order = count(order_key[None, :] < order_key[:, None])
    scan_count = scan_lengths.shape[0]
    held_group = held_patch * scan_count + scan_index(held, scan_lengths)
    sorting = order[None, :] == place[:, None]
    arrival = jnp.sum(jnp.where(sorting, arrival[None, :], 0), 1)
    group = jnp.sum(jnp.where(sorting, held_group[None, :], 0), 1)
    unpack = (buffer_ids[None, :] == arrival[:, None]).astype(BF)
    group_ids = jnp.arange(cols, dtype=jnp.int32)
    same = group[:, None] == group_ids[None, :]
    group_q = same.astype(BF)
    group_k = jnp.where(same | (group_ids[None, :] >= patch_count * scan_count), 0.0, -1e30).astype(BF)

    def to_slots(values):
        return dot(unpack, trade(dot(pack, values).astype(BF))).astype(BF)

    def from_slots(values):
        return dot(pack, trade(dot(unpack, values, TN).astype(BF)), TN).astype(BF)

    pair = jnp.stack([block(TAPS), block(TAPS + 4)])
    pair = lax.all_gather(pair, "mdl", axis=2, tiled=True)
    linear_full, projection_full = pair[0], pair[1]
    hidden = (lax.psum(conv_part, "mdl").astype(F32) + vec[0]).astype(BF)
    mixed = dot(hidden, linear_full) + vec[1]
    mixed_unit, mixed_std = unit_rows(mixed)
    stream_one = points_full.astype(F32) + mixed_unit * vec[2] + vec[3]
    one_unit, one_std = unit_rows(stream_one)
    normed = (one_unit * vec[4] + vec[5]).astype(BF)

    slot_in = widen(to_slots(own(normed)))
    query_map, key_map, value_map = block(TAPS + 1), block(TAPS + 2), block(TAPS + 3)
    projection = block(TAPS + 4)
    queries = (dot(slot_in, query_map) + vectors[6]).astype(BF)
    keys_all = dot(slot_in, key_map).astype(BF)
    values_all = (dot(slot_in, value_map) + vectors[7]).astype(BF)
    q_ext = jnp.concatenate([queries * BF(HD ** (-0.5)), group_q], 1)
    k_ext = jnp.concatenate([keys_all, group_k], 1)
    v_aug = jnp.concatenate(
        [values_all.T.reshape(heads, HD, rows), jnp.ones((heads, HD, rows), BF)], 1
    )
    attended_t, lse = attend(q_ext, k_ext, v_aug)
    attended = attended_t.T
    attended_rows = widen(from_slots(attended))
    branch = (dot(attended_rows, projection_full, NT) + vec[8]).astype(BF)

    stream_two = stream_one + branch.astype(F32)
    two_unit, two_std = unit_rows(stream_two)
    normed_two = (two_unit * vec[9] + vec[10]).astype(BF)
    first_mlp = jnp.concatenate([block(TAPS + 5 + k) for k in range(ff_blocks)], 1)
    second_mlp = jnp.concatenate([block(TAPS + 5 + ff_blocks + k) for k in range(ff_blocks)], 1)
    first_bias = vectors[11 : 11 + ff_blocks].reshape(ff_blocks * cols)
    pre_act = dot(normed_two, first_mlp) + first_bias
    activ = jax.nn.gelu(pre_act, approximate=False).astype(BF)
    out_part = dot(activ, second_mlp, NT)
    result = (own(stream_two) + add_parts(out_part) + vectors[11 + ff_blocks]).astype(BF)
    cot = cotangent.astype(F32)
    grad_pre = (dot(cot_full, second_mlp) * gelu_slope(pre_act)).astype(BF)
    grad_two_part = dot(grad_pre, first_mlp, NT)
    scaled_part = grad_two_part * vec[9]
    row_sums = lax.psum(
        jnp.stack([jnp.sum(scaled_part, 1), jnp.sum(scaled_part * two_unit, 1)]), "mdl"
    )
    grad_normed_two = add_parts(grad_two_part)
    own_two_unit = own(two_unit)
    grad_two = cot + two_std * (
        grad_normed_two * vectors[9]
        - row_sums[0][:, None] / C
        - own_two_unit * row_sums[1][:, None] / C
    )

    grad_branch = grad_two.astype(BF)
    grad_slot = widen(to_slots(grad_branch))
    grad_branch_full = widen(grad_branch)
    grad_attended = dot(grad_slot, projection).astype(BF)
    inner = jnp.sum(
        (grad_attended.astype(F32) * attended.astype(F32)).reshape(rows, heads, HD), -1
    ).T.reshape(heads, 1, rows)
    grad_queries_t, grad_keys, grad_values = attend_back(
        q_ext, k_ext, keys_all.T, values_all, grad_attended, lse, inner
    )
    grad_queries = grad_queries_t.T
    slot_back = (
        dot(grad_queries, query_map, NT)
        + dot(grad_keys, key_map, NT)
        + dot(grad_values, value_map, NT)
    )
    grad_normed = widen(from_slots(add_parts(slot_back).astype(BF))).astype(F32)
    grad_one = grad_branch_full.astype(F32) + unit_back(grad_normed * vec[4], one_unit, one_std)
    own_grad_one = grad_two + own(grad_one - grad_branch_full.astype(F32))
    grad_mixed = unit_back(grad_one * vec[2], mixed_unit, mixed_std).astype(BF)

    back = dot(linear_full, grad_mixed, NT).astype(BF)
    early = [
        dot(hidden, own(grad_mixed), TN),
        dot(slot_in, grad_queries, TN),
        dot(slot_in, grad_keys, TN),
        dot(slot_in, grad_values, TN),
        dot(grad_slot, attended, TN),
    ]
    early += [
        dot(normed_two, grad_pre[:, k * cols : (k + 1) * cols], TN) for k in range(ff_blocks)
    ]
    early += [dot(cot_full, activ[:, k * cols : (k + 1) * cols], TN) for k in range(ff_blocks)]
    early = jnp.stack([e.astype(BF).reshape(pts, C // pts, cols) for e in early], 1)
    early = lax.psum_scatter(early, "pts", scatter_dimension=0)
    late = lax.psum_scatter(tap_grads(back, taken, pts), "pts", scatter_dimension=0)
    summed = jnp.concatenate([late, early], 0)
    block_of_slot = jnp.zeros_like(owner_slot).at[owner_slot].set(
        jnp.arange(owner_slot.shape[0], dtype=jnp.int32)
    )
    reduced = lax.all_to_all(
        summed[block_of_slot], "mdl", split_axis=0, concat_axis=2, tiled=True
    )

    low_back = lax.ppermute(back[:, rows - HALO :], "pts", up)
    high_back = lax.ppermute(back[:, :HALO], "pts", down)
    back_ext = jnp.concatenate([low_back, back, high_back], 1)
    point_grad = own_grad_one + conv_back(owner_slot, blocks, ids, back_ext)

    def total(values):
        return jnp.sum(values.astype(F32), 0)

    vector_local = jnp.stack(
        [
            lax.dynamic_slice_in_dim(jnp.sum(back.astype(F32), 1), mdl_index * cols, cols, 0),
            total(own(grad_mixed)),
            total(own_grad_one * own(mixed_unit)),
            total(own_grad_one),
            total(own(grad_normed) * own(one_unit)),
            total(own(grad_normed)),
            total(grad_queries),
            total(grad_values),
            total(grad_branch),
            total(grad_normed_two * own_two_unit),
            total(grad_normed_two),
        ]
    )
    vector_local = jnp.concatenate(
        [vector_local, total(grad_pre).reshape(ff_blocks, cols), total(cot)[None]], 0
    )
    vector_grad = lax.psum(vector_local, "pts")

    right = lax.all_gather(right_basis.astype(BF), "pts", axis=0)
    right = right.transpose(1, 0, 2, 3).reshape(right_basis.shape[0], C, C)
    left = row_eigen_basis.astype(BF)
    turned = jnp.einsum("brc,bcd->brd", reduced.astype(BF), right, preferred_element_type=F32)
    spread_grad = jnp.einsum(
        "bru,brd->bud", left, turned.astype(BF), preferred_element_type=F32
    ).astype(BF)
    spread_grad = spread_grad.reshape(left.shape[0], pts, C // pts, C).transpose(1, 0, 2, 3)
    rotated = lax.psum_scatter(spread_grad, "pts", scatter_dimension=0).astype(F32)
    new_first, new_second, direction = adam(first_moment, second_moment, rotated)
    turned_back = jnp.einsum(
        "bic,bdc->bid", direction.astype(BF), right, preferred_element_type=F32
    ).astype(BF)
    turned_all = lax.all_gather(turned_back, "pts", axis=0)
    turned_all = turned_all.transpose(1, 0, 2, 3).reshape(left.shape[0], C, C)
    update = jnp.einsum("bua,baf->buf", left, turned_all, preferred_element_type=F32)
    new_weights = weights - matrix_rate * (update + MATRIX_DECAY * weights)
    new_vector_first, new_vector_second, vector_step = adam(
        vector_first, vector_second, vector_grad
    )
    new_vectors = vectors - VECTOR_RATE * vector_step
    return (
        result,
        point_grad,
        reduced.astype(F32),
        new_first,
        new_second,
        new_weights,
        new_weights.astype(BF),
        vector_grad,
        new_vector_first,
        new_vector_second,
        new_vectors,
    )


def solution(mesh):
    by_rows = P("pts", "mdl")
    owned = P("mdl", "pts", None)
    vector = P(None, "mdl")
    return jax.shard_map(
        local,
        mesh=mesh,
        in_specs=(
            by_rows,
            by_rows,
            P("pts", None),
            P(),
            P("pts"),
            P("pts"),
            P(),
            owned,
            owned,
            owned,
            owned,
            owned,
            vector,
            vector,
            vector,
        ),
        out_specs=(
            by_rows,
            by_rows,
            owned,
            owned,
            owned,
            owned,
            owned,
            vector,
            vector,
            vector,
            vector,
        ),
        check_vma=False,
    )
```

```python
import functools

import jax
import jax.numpy as jnp
from jax import lax
from jax.experimental import pallas as pl
from jax.experimental.pallas import tpu as pltpu
from jax.sharding import PartitionSpec as P

C = 512
HD = 16
FF = 2048
TAPS = 27
HALO = 256
PATCH = 1024
STEP = 5

NORM_EPS = 1e-05
BETA_ONE = 0.9
BETA_TWO = 0.999
ADAM_EPS = 1e-08
VECTOR_RATE = 0.5
MATRIX_DECAY = 0.05
TILE = 256
WINDOW = TILE + 2 * HALO
BF = jnp.bfloat16
F32 = jnp.float32
VMEM_LIMIT = 48 * 1024 * 1024

NN = (((1,), (0,)), ((), ()))
NT = (((1,), (1,)), ((), ()))
TN = (((0,), (0,)), ((), ()))


def dot(a, b, dims=NN):
    return lax.dot_general(a, b, dims, preferred_element_type=F32)


def params(**kw):
    return pltpu.CompilerParams(vmem_limit_bytes=VMEM_LIMIT, **kw)


MESH = pl.DeviceIdType.MESH


def push(src, dst, send_sem, recv_sem, **target):
    return pltpu.make_async_remote_copy(
        src_ref=src,
        dst_ref=dst,
        send_sem=send_sem,
        recv_sem=recv_sem,
        device_id=target,
        device_id_type=MESH,
    )


def greet(peers):
    barrier = pltpu.get_barrier_semaphore()
    for peer in peers:
        pl.semaphore_signal(barrier, inc=1, device_id=peer, device_id_type=MESH)
    pl.semaphore_wait(barrier, len(peers))


def others(index, size):
    return [lax.rem(index + step, size) for step in range(1, size)]


class Layout:
    def __init__(self, pts, mdl, blocks):
        self.pts, self.mdl = pts, mdl
        self.slots = blocks // mdl
        self.each = min(k for k in range(1, self.slots + 1) if self.slots % k == 0 and self.slots // k <= pts)
        self.active = self.slots // self.each
        self.first = (pts - self.active) // 2
        self.width = mdl // 2 if pts % (mdl // 2) == 0 else 1
        self.depth = pts // self.width


def fetch_copies(plan, src, dst, sems, act):
    send, recv, here = sems
    me = lax.axis_index("pts")
    for i in range(plan.active):
        target = plan.first + i
        piece = src.at[pl.ds(i * plan.each, plan.each)]

        @pl.when(me != target)
        def _():
            copy = push(piece, dst.at[:, me], send.at[i], recv.at[me], pts=target)
            if act == "start":
                copy.start()
            else:
                copy.wait_send()

        @pl.when(me == target)
        def _():
            copy = pltpu.make_async_copy(piece, dst.at[:, me], here)
            if act == "start":
                copy.start()
            else:
                copy.wait()
                for source in others(me, plan.pts):
                    push(piece, dst.at[:, source], send.at[i], recv.at[source], pts=source).wait_recv()


def fetch_sems(plan):
    dma = pltpu.SemaphoreType.DMA
    return [dma((plan.active,)), dma((plan.pts,)), dma(())]


def fetch_shape(plan, src):
    return jax.ShapeDtypeStruct((plan.each, plan.pts) + src.shape[1:], src.dtype)


def one_hot_window(ids_ref, tap, tile):
    row = ids_ref[pl.ds(tap, 1), pl.ds(tile * TILE, TILE)]
    places = lax.broadcasted_iota(jnp.int32, (WINDOW, TILE), 0) + tile * TILE
    return jnp.where(places == row, 1.0, 0.0).astype(BF)


def gather_kernel(ids_ref, ext_ref, out_ref):
    tap = pl.program_id(0)
    for tile in range(out_ref.shape[2] // TILE):
        hot = one_hot_window(ids_ref, tap, tile)
        taken = dot(ext_ref[:, tile * TILE : tile * TILE + WINDOW], hot)
        out_ref[0, :, tile * TILE : (tile + 1) * TILE] = taken.astype(BF)


def gather_taps(ids, ext):
    taps, rows = ids.shape
    cols = ext.shape[0]
    return pl.pallas_call(
        gather_kernel,
        grid=(taps,),
        in_specs=[
            pl.BlockSpec(ids.shape, lambda t: (0, 0)),
            pl.BlockSpec(ext.shape, lambda t: (0, 0)),
        ],
        out_specs=pl.BlockSpec((1, cols, rows), lambda t: (t, 0, 0)),
        out_shape=jax.ShapeDtypeStruct((taps, cols, rows), BF),
        compiler_params=params(),
        cost_estimate=pl.CostEstimate(
            flops=2 * taps * rows * WINDOW * cols * 2,
            bytes_accessed=taps * rows * cols * 2,
            transcendentals=0,
        ),
        name="gather_taps",
    )(ids, ext)


GROUP = 3


def conv_kernel(w_ref, x_ref, out_ref, acc_ref):
    step = pl.program_id(0)

    @pl.when(step == 0)
    def _():
        acc_ref[...] = jnp.zeros_like(acc_ref)

    total = acc_ref[...]
    for j in range(GROUP):
        total = total + dot(w_ref[:, j].reshape(C, x_ref.shape[1]), x_ref[j])
    acc_ref[...] = total

    @pl.when(step == pl.num_programs(0) - 1)
    def _():
        out_ref[...] = acc_ref[...].T.astype(BF)


def conv_forward(blocks, taken):
    taps, cols, rows = taken.shape
    parts, _, share, _ = blocks.shape
    return pl.pallas_call(
        conv_kernel,
        grid=(taps // GROUP,),
        in_specs=[
            pl.BlockSpec((parts, GROUP, share, cols), lambda t: (0, t, 0, 0)),
            pl.BlockSpec((GROUP, cols, rows), lambda t: (t, 0, 0)),
        ],
        out_specs=pl.BlockSpec((rows, C), lambda t: (0, 0)),
        scratch_shapes=[pltpu.VMEM((C, rows), F32)],
        out_shape=jax.ShapeDtypeStruct((rows, C), BF),
        compiler_params=params(),
        cost_estimate=pl.CostEstimate(
            flops=2 * taps * rows * C * cols,
            bytes_accessed=taps * (rows + C) * cols * 2,
            transcendentals=0,
        ),
        name="conv_forward",
    )(blocks, taken)


PACK = 5


def back_kernel(
    plan, back_ref, x_ref, w_ref, ids_ref, early_ref, out_ref, turn_ref,
    own, side, acc, far, turn_acc, side_send, side_recv, far_send, far_recv,
):
    width, depth = plan.width, plan.depth
    cols, rows = turn_acc.shape
    share = C // plan.pts
    taps = x_ref.shape[0]
    extra = early_ref.shape[0]
    groups = own.shape[1]
    me = lax.axis_index("pts")
    y, z = lax.rem(me, width), me // width
    side_peers = [z * width + v for v in others(y, width)]
    far_peers = [v * width + y for v in others(z, depth)]
    greet([{"pts": v} for v in side_peers + far_peers])

    def store(block, group, place):
        grid = block.astype(BF).reshape(depth, width, share, cols)
        for v in range(width):
            own[v, group, :, pl.ds(place, 1)] = grid[:, v][:, None]

    def grads(group):
        low = max(group * PACK, extra)
        for b in range(group * PACK, min(extra, (group + 1) * PACK)):
            store(early_ref[b], group, b - group * PACK)

        def one(place, carry):
            tap = group * PACK + place - extra
            store(
                dot(back_ref[:, HALO : HALO + rows], x_ref[pl.ds(tap, 1)][0], NT), group, place
            )
            return carry

        if low < (group + 1) * PACK:
            lax.fori_loop(low - group * PACK, PACK, one, 0)

    def side_copy(group, v):
        return push(
            own.at[v, group], side.at[group, y], side_send.at[group, v], side_recv.at[group, y],
            pts=z * width + v,
        )

    def side_wait(group, v):
        return push(
            own.at[v, group], side.at[group, v], side_send.at[group, v], side_recv.at[group, v],
            pts=z * width + v,
        )

    def far_copy(group, v):
        return push(
            acc.at[group, v], far.at[group, z], far_send.at[group, v], far_recv.at[group, z],
            pts=v * width + y,
        )

    def far_wait(group, v):
        return push(
            acc.at[group, v], far.at[group, v], far_send.at[group, v], far_recv.at[group, v],
            pts=v * width + y,
        )

    def start_side(group):
        grads(group)
        for v in others(y, width):
            side_copy(group, v).start()

    def start_far(group):
        total = own[pl.ds(y, 1), group][0].astype(F32)
        for v in others(y, width):
            side_wait(group, v).wait_recv()
            total = total + side[group, pl.ds(v, 1)][0].astype(F32)
        acc[group] = total.astype(BF)
        for v in others(z, depth):
            far_copy(group, v).start()

    def finish(group):
        total = acc[group, pl.ds(z, 1)][0].astype(F32)
        for v in others(z, depth):
            far_wait(group, v).wait_recv()
            total = total + far[group, pl.ds(v, 1)][0].astype(F32)
        out_ref[group * PACK : (group + 1) * PACK] = total.astype(BF)

    def turn(tap, carry):
        weight = w_ref[:, pl.ds(taps - 1 - tap, 1)].reshape(C, cols)
        turned = dot(weight, back_ref[...], TN).astype(BF)
        for tile in range(rows // TILE):
            hot = one_hot_window(ids_ref, tap, tile)
            turn_acc[:, tile * TILE : (tile + 1) * TILE] += dot(
                turned[:, tile * TILE : tile * TILE + WINDOW], hot
            )
        return carry

    turn_acc[...] = jnp.zeros_like(turn_acc)
    lag = 2
    for group in range(groups):
        start_side(group)
        if group >= lag:
            start_far(group - lag)
    left = list(range(groups - lag, groups))
    cuts = [taps * i // (len(left) + 1) for i in range(len(left) + 2)]
    for i, group in enumerate(left):
        lax.fori_loop(cuts[i], cuts[i + 1], turn, 0)
        start_far(group)
    lax.fori_loop(cuts[-2], cuts[-1], turn, 0)
    turn_ref[...] = turn_acc[...].T
    for group in range(groups):
        finish(group)
    for group in range(groups):
        for v in others(y, width):
            side_copy(group, v).wait_send()
        for v in others(z, depth):
            far_copy(group, v).wait_send()


def back_pass(plan, back_ext, taken, blocks, ids, early):
    taps, cols, rows = taken.shape
    total = taps + early.shape[0]
    groups = total // PACK
    share = C // plan.pts
    width, depth = plan.width, plan.depth
    dma = pltpu.SemaphoreType.DMA
    vmem = pl.BlockSpec(memory_space=pltpu.VMEM)
    return pl.pallas_call(
        functools.partial(back_kernel, plan),
        in_specs=[vmem] * 5,
        out_specs=[vmem] * 2,
        out_shape=[
            jax.ShapeDtypeStruct((total, share, cols), BF),
            jax.ShapeDtypeStruct((rows, cols), F32),
        ],
        scratch_shapes=[
            pltpu.VMEM((width, groups, depth, PACK, share, cols), BF),
            pltpu.VMEM((groups, width, depth, PACK, share, cols), BF),
            pltpu.VMEM((groups, depth, PACK, share, cols), BF),
            pltpu.VMEM((groups, depth, PACK, share, cols), BF),
            pltpu.VMEM((cols, rows), F32),
            dma((groups, width)),
            dma((groups, width)),
            dma((groups, depth)),
            dma((groups, depth)),
        ],
        compiler_params=params(collective_id=1, has_side_effects=True),
        cost_estimate=pl.CostEstimate(
            flops=taps * rows * (WINDOW * 4 + 5 * C) * cols,
            bytes_accessed=30000000,
            transcendentals=0,
        ),
        name="back_pass",
    )(back_ext, taken, blocks, ids, early)


def head_lanes(ext, cols, head):
    lane = lax.broadcasted_iota(jnp.int32, ext.shape, 1)
    return jnp.where((lane >= cols) | (lane // HD == head), ext, jnp.zeros_like(ext))


def fetch_step(plan, srcs, dsts, sems):
    me = lax.axis_index("pts")

    @pl.when(pl.program_id(0) == 0)
    def _():
        greet([{"pts": v} for v in others(me, plan.pts)])
        for src, dst, group in zip(srcs, dsts, sems):
            fetch_copies(plan, src, dst, group, "start")


def fetch_end(plan, srcs, dsts, sems):
    @pl.when(pl.program_id(0) == pl.num_programs(0) - 1)
    def _():
        for src, dst, group in zip(srcs, dsts, sems):
            fetch_copies(plan, src, dst, group, "wait")


def attend_kernel(
    plan, q_ref, k_ref, v_ref, one, two, out_ref, lse_ref, one_to, two_to, *sems
):
    head = pl.program_id(0)
    moves = (plan, (one, two), (one_to, two_to), (sems[:3], sems[3:]))
    fetch_step(*moves)
    rows, width = q_ref.shape
    keys = k_ref[...]
    values = v_ref[0]
    for tile in range(rows // TILE):
        span = slice(tile * TILE, (tile + 1) * TILE)
        queries = head_lanes(q_ref[span, :], width // 2, head)
        scores = dot(keys, queries, NT)
        top = jnp.max(scores, 0, keepdims=True)
        soft = jnp.exp(scores - top).astype(BF)
        summed = dot(values, soft)
        total = summed[HD : HD + 1]
        out_ref[:, span] = (summed[:HD] / total).astype(BF)
        lse_ref[0, :, span] = top + jnp.log(total)
    fetch_end(*moves)


def attend(plan, q_ext, k_ext, v_aug, one, two):
    rows, width = q_ext.shape
    heads = v_aug.shape[0]
    return pl.pallas_call(
        functools.partial(attend_kernel, plan),
        grid=(heads,),
        in_specs=[
            pl.BlockSpec((rows, width), lambda h: (0, 0)),
            pl.BlockSpec((rows, width), lambda h: (0, 0)),
            pl.BlockSpec((1, 2 * HD, rows), lambda h: (h, 0, 0)),
            pl.BlockSpec(memory_space=pl.ANY),
            pl.BlockSpec(memory_space=pl.ANY),
        ],
        out_specs=[
            pl.BlockSpec((HD, rows), lambda h: (h, 0)),
            pl.BlockSpec((1, 1, rows), lambda h: (h, 0, 0)),
            pl.BlockSpec(memory_space=pl.ANY),
            pl.BlockSpec(memory_space=pl.ANY),
        ],
        out_shape=[
            jax.ShapeDtypeStruct((heads * HD, rows), BF),
            jax.ShapeDtypeStruct((heads, 1, rows), F32),
            fetch_shape(plan, one),
            fetch_shape(plan, two),
        ],
        scratch_shapes=fetch_sems(plan) + fetch_sems(plan),
        compiler_params=params(collective_id=2, has_side_effects=True),
        cost_estimate=pl.CostEstimate(
            flops=2 * heads * rows * rows * width, bytes_accessed=rows * width * 6, transcendentals=heads * rows * rows
        ),
        name="attend",
    )(q_ext, k_ext, v_aug, one, two)


def attend_back_kernel(
    plan, q_ref, k_ref, kt_ref, v_ref, do_ref, lse_ref, inner_ref, one, two,
    dq_ref, dk_ref, dv_ref, one_to, two_to, dk_acc, dv_acc, *sems,
):
    head = pl.program_id(0)
    moves = (plan, (one, two), (one_to, two_to), (sems[:3], sems[3:]))
    fetch_step(*moves)
    rows, width = q_ref.shape
    cols = width // 2

    @pl.when(head == 0)
    def _():
        dk_acc[...] = jnp.zeros_like(dk_acc)
        dv_acc[...] = jnp.zeros_like(dv_acc)

    queries = head_lanes(q_ref[...], cols, head)
    pure = queries[:, :cols]
    grad = head_lanes(do_ref[...], cols, head)
    lse = lse_ref[0]
    inner = inner_ref[0]
    dq = jnp.zeros((HD, rows), F32)
    for tile in range(rows // TILE):
        span = slice(tile * TILE, (tile + 1) * TILE)
        scores = dot(k_ref[span, :], queries, NT)
        soft = jnp.exp(scores - lse)
        grad_soft = dot(v_ref[span, :], grad, NT)
        grad_scores = (soft * (grad_soft - inner)).astype(BF)
        dv_acc[span, :] += dot(soft.astype(BF), grad)
        dk_acc[span, :] += dot(grad_scores, pure)
        dq = dq + dot(kt_ref[:, span], grad_scores)
    dq_ref[...] = (dq * HD ** (-0.5)).astype(BF)

    @pl.when(head == pl.num_programs(0) - 1)
    def _():
        dk_ref[...] = dk_acc[...].astype(BF)
        dv_ref[...] = dv_acc[...].astype(BF)

    fetch_end(*moves)


def attend_back(plan, q_ext, k_ext, keys_t, values, grad, lse, inner, one, two):
    rows, width = q_ext.shape
    cols = width // 2
    heads = cols // HD
    whole = lambda h: (0, 0)
    return pl.pallas_call(
        functools.partial(attend_back_kernel, plan),
        grid=(heads,),
        in_specs=[
            pl.BlockSpec((rows, width), whole),
            pl.BlockSpec((rows, width), whole),
            pl.BlockSpec((HD, rows), lambda h: (h, 0)),
            pl.BlockSpec((rows, cols), whole),
            pl.BlockSpec((rows, cols), whole),
            pl.BlockSpec((1, 1, rows), lambda h: (h, 0, 0)),
            pl.BlockSpec((1, 1, rows), lambda h: (h, 0, 0)),
            pl.BlockSpec(memory_space=pl.ANY),
            pl.BlockSpec(memory_space=pl.ANY),
        ],
        out_specs=[
            pl.BlockSpec((HD, rows), lambda h: (h, 0)),
            pl.BlockSpec((rows, cols), whole),
            pl.BlockSpec((rows, cols), whole),
            pl.BlockSpec(memory_space=pl.ANY),
            pl.BlockSpec(memory_space=pl.ANY),
        ],
        out_shape=[
            jax.ShapeDtypeStruct((cols, rows), BF),
            jax.ShapeDtypeStruct((rows, cols), BF),
            jax.ShapeDtypeStruct((rows, cols), BF),
            fetch_shape(plan, one),
            fetch_shape(plan, two),
        ],
        scratch_shapes=[pltpu.VMEM((rows, cols), F32), pltpu.VMEM((rows, cols), F32)]
        + fetch_sems(plan)
        + fetch_sems(plan),
        compiler_params=params(collective_id=3, has_side_effects=True),
        cost_estimate=pl.CostEstimate(
            flops=5 * heads * rows * rows * width, bytes_accessed=rows * width * 20, transcendentals=heads * rows * rows
        ),
        name="attend_back",
    )(q_ext, k_ext, keys_t, values, grad, lse, inner, one, two)


def adam(first, second, grad):
    new_first = BETA_ONE * first + (1.0 - BETA_ONE) * grad
    new_second = BETA_TWO * second + (1.0 - BETA_TWO) * grad * grad
    direction = (
        new_first
        / (1.0 - BETA_ONE**STEP)
        / (jnp.sqrt(new_second / (1.0 - BETA_TWO**STEP)) + ADAM_EPS)
    )
    return new_first, new_second, direction


def owner_kernel(
    plan, grad_ref, left_ref, right_ref, first_ref, second_ref, rows_ref, result_ref,
    whole, results, whole_send, whole_recv, whole_here,
    rows_send, rows_recv, rows_here, back_send, back_recv, back_here,
):
    pts, mdl, each = plan.pts, plan.mdl, plan.each
    slots = plan.slots
    share, cols = grad_ref.shape[1:]
    me, plane = lax.axis_index("pts"), lax.axis_index("mdl")
    is_active = (me >= plan.first) & (me < plan.first + plan.active)
    greet(
        [
            {"pts": p, "mdl": m}
            for i, p in enumerate([me] + others(me, pts))
            for j, m in enumerate([plane] + others(plane, mdl))
            if i + j > 0
        ]
    )

    def to_whole(act):
        for step in range(mdl):
            m = lax.rem(plane + step, mdl)
            for i in range(plan.active):
                target = plan.first + i
                piece = grad_ref.at[pl.ds(m * slots + i * each, each)]
                if step == 0:

                    @pl.when(me == target)
                    def _():
                        copy = pltpu.make_async_copy(piece, whole.at[me, plane], whole_here)
                        copy.start() if act == "start" else copy.wait()

                    remote = me != target
                else:
                    remote = me >= 0

                @pl.when(remote)
                def _():
                    copy = push(
                        piece, whole.at[me, plane], whole_send.at[step, i],
                        whole_recv.at[me, plane], pts=target, mdl=m,
                    )
                    copy.start() if act == "start" else copy.wait_send()

    def to_rows(act):
        for m in others(plane, mdl):
            copy = push(
                grad_ref.at[pl.ds(m * slots, slots)], rows_ref.at[plane], rows_send.at[m],
                rows_recv.at[plane], mdl=m,
            )
            if act == "start":
                copy.start()
            else:
                copy.wait_send()
                push(
                    grad_ref.at[pl.ds(m * slots, slots)], rows_ref.at[m], rows_send.at[m],
                    rows_recv.at[m], mdl=m,
                ).wait_recv()
        copy = pltpu.make_async_copy(
            grad_ref.at[pl.ds(plane * slots, slots)], rows_ref.at[plane], rows_here
        )
        copy.start() if act == "start" else copy.wait()

    to_whole("start")
    to_rows("start")

    base = (me - plan.first) * each

    def result_copy(k, p):
        return push(
            results.at[k, :, p], result_ref.at[base + k], back_send.at[k, p],
            back_recv.at[base + k], pts=p,
        )

    def result_here(k):
        return pltpu.make_async_copy(
            results.at[k, :, me], result_ref.at[base + k], back_here.at[k]
        )

    @pl.when(is_active)
    def _():
        pltpu.make_async_copy(
            grad_ref.at[pl.ds(plane * slots + base, each)], whole.at[me, plane], whole_here
        ).wait()
        for p_step in range(pts):
            for m_step in range(mdl):
                if p_step + m_step > 0:
                    p, m = lax.rem(me + p_step, pts), lax.rem(plane + m_step, mdl)
                    push(
                        grad_ref.at[pl.ds(0, each)], whole.at[p, m], whole_send.at[0, 0],
                        whole_recv.at[p, m], pts=p, mdl=m,
                    ).wait_recv()
        for k in range(each):
            left = left_ref[k].reshape(C, C)
            right = right_ref[k].reshape(C, C)
            turned = jnp.zeros((C, C), F32)
            for m in range(mdl):
                columns = whole[:, m, k].reshape(C, cols)
                half = dot(left, columns, TN).astype(BF)
                turned = turned + dot(half, right[m * cols : (m + 1) * cols])
            rotated = turned.astype(BF)
            _, _, direction = adam(
                first_ref[k].reshape(C, C).astype(F32),
                second_ref[k].reshape(C, C).astype(F32),
                rotated.astype(F32),
            )
            update = dot(left, dot(direction.astype(BF), right, NT).astype(BF))
            results[k, 0] = rotated.reshape(pts, share, C)
            results[k, 1] = update.astype(BF).reshape(pts, share, C)
            for p in others(me, pts):
                result_copy(k, p).start()
            result_here(k).start()

    to_rows("wait")
    for i in range(plan.active):
        source = plan.first + i
        for k in range(each):

            @pl.when(me != source)
            def _():
                push(
                    results.at[k, :, me], result_ref.at[i * each + k], back_send.at[k, source],
                    back_recv.at[i * each + k], pts=source,
                ).wait_recv()

    @pl.when(is_active)
    def _():
        for k in range(each):
            result_here(k).wait()
            for p in others(me, pts):
                result_copy(k, p).wait_send()

    for step in range(mdl):
        m = lax.rem(plane + step, mdl)
        for i in range(plan.active):
            target = plan.first + i

            @pl.when((me != target) if step == 0 else (me >= 0))
            def _():
                push(
                    grad_ref.at[pl.ds(m * slots + i * each, each)], whole.at[me, plane],
                    whole_send.at[step, i], whole_recv.at[me, plane], pts=target, mdl=m,
                ).wait_send()


def owner_update(plan, grads, left, right, first, second):
    share, cols = grads.shape[1:]
    pts, mdl, each = plan.pts, plan.mdl, plan.each
    dma = pltpu.SemaphoreType.DMA
    vmem = pl.BlockSpec(memory_space=pltpu.VMEM)
    return pl.pallas_call(
        functools.partial(owner_kernel, plan),
        in_specs=[vmem] * 5,
        out_specs=[vmem] * 2,
        out_shape=[
            jax.ShapeDtypeStruct((mdl, plan.slots, share, cols), BF),
            jax.ShapeDtypeStruct((plan.slots, 2, share, C), BF),
        ],
        scratch_shapes=[
            pltpu.VMEM((pts, mdl, each, share, cols), BF),
            pltpu.VMEM((each, 2, pts, share, C), BF),
            dma((mdl, plan.active)),
            dma((pts, mdl)),
            dma(()),
            dma((mdl,)),
            dma((mdl,)),
            dma(()),
            dma((each, pts)),
            dma((plan.slots,)),
            dma((each,)),
        ],
        compiler_params=params(collective_id=4, has_side_effects=True),
        cost_estimate=pl.CostEstimate(
            flops=8 * each * C * C * C, bytes_accessed=10000000, transcendentals=each * C * C
        ),
        name="owner_update",
    )(grads, left, right, first, second)


def widen(shard_rows):
    return lax.all_gather(shard_rows, "mdl", axis=1, tiled=True)


def add_parts(partial_value):
    return lax.psum_scatter(
        partial_value.astype(BF), "mdl", scatter_dimension=1, tiled=True
    ).astype(F32)


def trade(buffer):
    return lax.all_to_all(buffer, "pts", split_axis=0, concat_axis=0, tiled=True)


def scan_index(row_ids, scan_lengths):
    bounds = jnp.cumsum(scan_lengths)
    return jnp.sum((row_ids[..., None] >= bounds[:-1]).astype(jnp.int32), -1)


def count(mask):
    return jnp.sum(mask.astype(jnp.int32), 1)


def unit_rows(values):
    mean = jnp.mean(values, -1, keepdims=True)
    centred = values - mean
    inv_std = lax.rsqrt(jnp.mean(centred * centred, -1, keepdims=True) + NORM_EPS)
    return centred * inv_std, inv_std


def unit_back(grad_unit, unit, inv_std):
    mean = jnp.mean(grad_unit, -1, keepdims=True)
    cross = jnp.mean(grad_unit * unit, -1, keepdims=True)
    return inv_std * (grad_unit - mean - unit * cross)


def gelu_slope(pre_act):
    return (
        0.5 * (1.0 + lax.erf(pre_act * 0.7071067811865476))
        + pre_act * jnp.exp(-0.5 * pre_act * pre_act) * 0.3989422804014327
    )


def local(
    points,
    cotangent,
    neighbours,
    scan_lengths,
    to_patch,
    from_patch,
    owner_slot,
    weights,
    row_eigen_basis,
    right_basis,
    first_moment,
    second_moment,
    vectors,
    vector_first,
    vector_second,
):
    rows, cols = points.shape
    slot_count = from_patch.shape[0]
    pts = lax.axis_size("pts")
    mdl = lax.axis_size("mdl")
    pts_index = lax.axis_index("pts")
    mdl_index = lax.axis_index("mdl")
    heads = cols // HD
    ff_blocks = FF // C
    patch_count = slot_count // PATCH
    capacity = 2 * rows // pts
    matrix_rate = 1.6 * C ** (-0.5)
    plan = Layout(pts, mdl, owner_slot.shape[0])

    def own(full):
        return lax.dynamic_slice_in_dim(full, mdl_index * cols, cols, full.ndim - 1)

    spread = lax.all_to_all(
        weights.astype(BF), "mdl", split_axis=2, concat_axis=0, tiled=True
    )
    blocks = lax.all_gather(spread[owner_slot], "pts", axis=0)
    vec = lax.all_gather(vectors, "mdl", axis=1, tiled=True)
    points_full = widen(points)
    cot_full = widen(cotangent)

    def block(b):
        return blocks[:, b].reshape(C, cols)

    up = [(i, i + 1) for i in range(pts - 1)]
    down = [(i + 1, i) for i in range(pts - 1)]
    low_halo = lax.ppermute(points[rows - HALO :], "pts", up)
    high_halo = lax.ppermute(points[:HALO], "pts", down)
    ext = jnp.concatenate([low_halo, points, high_halo], 0).T
    row_ids = pts_index * rows + jnp.arange(rows, dtype=jnp.int32)
    own_scan = scan_index(row_ids, scan_lengths)
    near = neighbours.T
    usable = (near >= 0) & (scan_index(jnp.maximum(near, 0), scan_lengths) == own_scan[None, :])
    ids = jnp.where(usable, near - (pts_index * rows - HALO), -1)
    taken = gather_taps(ids, ext)
    conv_part = conv_forward(blocks, taken)

    target = to_patch // slot_count
    place = jnp.arange(rows, dtype=jnp.int32)
    rank = count((target[None, :] == target[:, None]) & (place[None, :] < place[:, None]))
    send_pos = target * capacity + rank
    buffer_ids = jnp.arange(pts * capacity, dtype=jnp.int32)
    pack = (buffer_ids[:, None] == send_pos[None, :]).astype(BF)
    held = jnp.zeros((rows + PATCH,), jnp.int32)
    held_patch = jnp.zeros((rows + PATCH,), jnp.int32)
    offset = jnp.int32(0)
    for patch in range(patch_count):
        part = from_patch[patch * PATCH : (patch + 1) * PATCH]
        held = lax.dynamic_update_slice(held, part, (offset,))
        held_patch = lax.dynamic_update_slice(
            held_patch, jnp.full((PATCH,), patch, jnp.int32), (offset,)
        )
        offset = offset + jnp.sum((part >= 0).astype(jnp.int32))
    held = held[:rows]
    held_patch = held_patch[:rows]
    source = held // rows
    arrival = source * capacity + count(
        (source[None, :] == source[:, None]) & (held[None, :] < held[:, None])
    )
    order_key = held_patch * (pts * rows) + held
    order = count(order_key[None, :] < order_key[:, None])
    scan_count = scan_lengths.shape[0]
    held_group = held_patch * scan_count + scan_index(held, scan_lengths)
    sorting = order[None, :] == place[:, None]
    arrival = jnp.sum(jnp.where(sorting, arrival[None, :], 0), 1)
    group = jnp.sum(jnp.where(sorting, held_group[None, :], 0), 1)
    unpack = (buffer_ids[None, :] == arrival[:, None]).astype(BF)
    group_ids = jnp.arange(cols, dtype=jnp.int32)
    same = group[:, None] == group_ids[None, :]
    group_q = same.astype(BF)
    group_k = jnp.where(same | (group_ids[None, :] >= patch_count * scan_count), 0.0, -1e30).astype(BF)

    def to_slots(values):
        return dot(unpack, trade(dot(pack, values).astype(BF))).astype(BF)

    def from_slots(values):
        return dot(pack, trade(dot(unpack, values, TN).astype(BF)), TN).astype(BF)

    pair = jnp.stack([block(TAPS), block(TAPS + 4)])
    pair = lax.all_gather(pair, "mdl", axis=2, tiled=True)
    linear_full, projection_full = pair[0], pair[1]
    hidden = (lax.psum(conv_part, "mdl").astype(F32) + vec[0]).astype(BF)
    mixed = dot(hidden, linear_full) + vec[1]
    mixed_unit, mixed_std = unit_rows(mixed)
    stream_one = points_full.astype(F32) + mixed_unit * vec[2] + vec[3]
    one_unit, one_std = unit_rows(stream_one)
    normed = (one_unit * vec[4] + vec[5]).astype(BF)

    slot_in = widen(to_slots(own(normed)))
    query_map, key_map, value_map = block(TAPS + 1), block(TAPS + 2), block(TAPS + 3)
    projection = block(TAPS + 4)
    queries = (dot(slot_in, query_map) + vectors[6]).astype(BF)
    keys_all = dot(slot_in, key_map).astype(BF)
    values_all = (dot(slot_in, value_map) + vectors[7]).astype(BF)
    q_ext = jnp.concatenate([queries * BF(HD ** (-0.5)), group_q], 1)
    k_ext = jnp.concatenate([keys_all, group_k], 1)
    v_aug = jnp.concatenate(
        [values_all.T.reshape(heads, HD, rows), jnp.ones((heads, HD, rows), BF)], 1
    )
    attended_t, lse, left_whole, right_whole = attend(
        plan, q_ext, k_ext, v_aug, row_eigen_basis.astype(BF), right_basis.astype(BF)
    )
    attended = attended_t.T
    attended_rows = widen(from_slots(attended))
    branch = (dot(attended_rows, projection_full, NT) + vec[8]).astype(BF)

    stream_two = stream_one + branch.astype(F32)
    two_unit, two_std = unit_rows(stream_two)
    normed_two = (two_unit * vec[9] + vec[10]).astype(BF)
    first_mlp = jnp.concatenate([block(TAPS + 5 + k) for k in range(ff_blocks)], 1)
    second_mlp = jnp.concatenate([block(TAPS + 5 + ff_blocks + k) for k in range(ff_blocks)], 1)
    first_bias = vectors[11 : 11 + ff_blocks].reshape(ff_blocks * cols)
    pre_act = dot(normed_two, first_mlp) + first_bias
    activ = jax.nn.gelu(pre_act, approximate=False).astype(BF)
    out_part = dot(activ, second_mlp, NT)
    result = (own(stream_two) + add_parts(out_part) + vectors[11 + ff_blocks]).astype(BF)
    cot = cotangent.astype(F32)
    grad_pre = (dot(cot_full, second_mlp) * gelu_slope(pre_act)).astype(BF)
    grad_two_part = dot(grad_pre, first_mlp, NT)
    scaled_part = grad_two_part * vec[9]
    row_sums = lax.psum(
        jnp.stack([jnp.sum(scaled_part, 1), jnp.sum(scaled_part * two_unit, 1)]), "mdl"
    )
    grad_normed_two = add_parts(grad_two_part)
    own_two_unit = own(two_unit)
    grad_two = cot + two_std * (
        grad_normed_two * vectors[9]
        - row_sums[0][:, None] / C
        - own_two_unit * row_sums[1][:, None] / C
    )

    grad_branch = grad_two.astype(BF)
    grad_slot = widen(to_slots(grad_branch))
    grad_branch_full = widen(grad_branch)
    grad_attended = dot(grad_slot, projection).astype(BF)
    inner = jnp.sum(
        (grad_attended.astype(F32) * attended.astype(F32)).reshape(rows, heads, HD), -1
    ).T.reshape(heads, 1, rows)
    grad_queries_t, grad_keys, grad_values, first_whole, second_whole = attend_back(
        plan,
        q_ext,
        k_ext,
        keys_all.T,
        values_all,
        grad_attended,
        lse,
        inner,
        first_moment.astype(BF),
        second_moment.astype(BF),
    )
    grad_queries = grad_queries_t.T
    slot_back = (
        dot(grad_queries, query_map, NT)
        + dot(grad_keys, key_map, NT)
        + dot(grad_values, value_map, NT)
    )
    grad_normed = widen(from_slots(add_parts(slot_back).astype(BF))).astype(F32)
    grad_one = grad_branch_full.astype(F32) + unit_back(grad_normed * vec[4], one_unit, one_std)
    own_grad_one = grad_two + own(grad_one - grad_branch_full.astype(F32))
    grad_mixed = unit_back(grad_one * vec[2], mixed_unit, mixed_std).astype(BF)

    back = dot(linear_full, grad_mixed, NT).astype(BF)
    early = [
        dot(hidden, own(grad_mixed), TN),
        dot(slot_in, grad_queries, TN),
        dot(slot_in, grad_keys, TN),
        dot(slot_in, grad_values, TN),
        dot(grad_slot, attended, TN),
    ]
    early += [
        dot(normed_two, grad_pre[:, k * cols : (k + 1) * cols], TN) for k in range(ff_blocks)
    ]
    early += [dot(cot_full, activ[:, k * cols : (k + 1) * cols], TN) for k in range(ff_blocks)]
    early = jnp.stack([e.astype(BF) for e in early])
    low_back = lax.ppermute(back[:, rows - HALO :], "pts", up)
    high_back = lax.ppermute(back[:, :HALO], "pts", down)
    back_ext = jnp.concatenate([low_back, back, high_back], 1)
    summed, conv_grad = back_pass(plan, back_ext, taken, blocks[:, :TAPS], ids, early)
    point_grad = own_grad_one + conv_grad
    block_of_slot = jnp.zeros_like(owner_slot).at[owner_slot].set(
        jnp.arange(owner_slot.shape[0], dtype=jnp.int32)
    )
    summed = summed[(block_of_slot + early.shape[0]) % owner_slot.shape[0]]
    grad_rows, results = owner_update(
        plan, summed, left_whole, right_whole, first_whole, second_whole
    )
    reduced = grad_rows.transpose(1, 2, 0, 3).reshape(plan.slots, C // pts, C)

    def total(values):
        return jnp.sum(values.astype(F32), 0)

    vector_local = jnp.stack(
        [
            lax.dynamic_slice_in_dim(jnp.sum(back.astype(F32), 1), mdl_index * cols, cols, 0),
            total(own(grad_mixed)),
            total(own_grad_one * own(mixed_unit)),
            total(own_grad_one),
            total(own(grad_normed) * own(one_unit)),
            total(own(grad_normed)),
            total(grad_queries),
            total(grad_values),
            total(grad_branch),
            total(grad_normed_two * own_two_unit),
            total(grad_normed_two),
        ]
    )
    vector_local = jnp.concatenate(
        [vector_local, total(grad_pre).reshape(ff_blocks, cols), total(cot)[None]], 0
    )
    vector_grad = lax.psum(vector_local, "pts")

    rotated, update = results[:, 0].astype(F32), results[:, 1].astype(F32)
    new_first, new_second, _ = adam(first_moment, second_moment, rotated)
    new_weights = weights - matrix_rate * (update + MATRIX_DECAY * weights)
    new_vector_first, new_vector_second, vector_step = adam(
        vector_first, vector_second, vector_grad
    )
    new_vectors = vectors - VECTOR_RATE * vector_step
    return (
        result,
        point_grad,
        reduced.astype(F32),
        new_first,
        new_second,
        new_weights,
        new_weights.astype(BF),
        vector_grad,
        new_vector_first,
        new_vector_second,
        new_vectors,
    )


def solution(mesh):
    by_rows = P("pts", "mdl")
    owned = P("mdl", "pts", None)
    vector = P(None, "mdl")
    return jax.shard_map(
        local,
        mesh=mesh,
        in_specs=(
            by_rows,
            by_rows,
            P("pts", None),
            P(),
            P("pts"),
            P("pts"),
            P(),
            owned,
            owned,
            owned,
            owned,
            owned,
            vector,
            vector,
            vector,
        ),
        out_specs=(
            by_rows,
            by_rows,
            owned,
            owned,
            owned,
            owned,
            owned,
            vector,
            vector,
            vector,
            vector,
        ),
        check_vma=False,
    )
```

```python
import functools
import types

import jax
import jax.numpy as jnp
from jax import lax
from jax.experimental import pallas as pl
from jax.experimental.pallas import tpu as pltpu
from jax.sharding import PartitionSpec as P

C = 512
HD = 16
FF = 2048
TAPS = 27
HALO = 256
PATCH = 1024
STEP = 5

NORM_EPS = 1e-05
BETA_ONE = 0.9
BETA_TWO = 0.999
ADAM_EPS = 1e-08
VECTOR_RATE = 0.5
MATRIX_DECAY = 0.05
TILE = 256
WINDOW = TILE + 2 * HALO
BF = jnp.bfloat16
F32 = jnp.float32
VMEM_LIMIT = 48 * 1024 * 1024

NN = (((1,), (0,)), ((), ()))
NT = (((1,), (1,)), ((), ()))
TN = (((0,), (0,)), ((), ()))


def dot(a, b, dims=NN):
    return lax.dot_general(a, b, dims, preferred_element_type=F32)


def params(**kw):
    return pltpu.CompilerParams(vmem_limit_bytes=VMEM_LIMIT, **kw)


MESH = pl.DeviceIdType.MESH


def push(src, dst, send_sem, recv_sem, **target):
    return pltpu.make_async_remote_copy(
        src_ref=src,
        dst_ref=dst,
        send_sem=send_sem,
        recv_sem=recv_sem,
        device_id=target,
        device_id_type=MESH,
    )


def greet(peers):
    barrier = pltpu.get_barrier_semaphore()
    for peer in peers:
        pl.semaphore_signal(barrier, inc=1, device_id=peer, device_id_type=MESH)
    pl.semaphore_wait(barrier, len(peers))


def others(index, size):
    return [lax.rem(index + step, size) for step in range(1, size)]


class Layout:
    def __init__(self, pts, mdl, blocks):
        self.pts, self.mdl = pts, mdl
        self.slots = blocks // mdl
        self.each = min(k for k in range(1, self.slots + 1) if self.slots % k == 0 and self.slots // k <= pts)
        self.active = self.slots // self.each
        self.first = (pts - self.active) // 2
        self.width = mdl // 2 if pts % (mdl // 2) == 0 else 1
        self.depth = pts // self.width


def fetch_copies(plan, src, dst, sems, act):
    send, recv, here = sems
    me = lax.axis_index("pts")
    for i in range(plan.active):
        target = plan.first + i
        piece = src.at[pl.ds(i * plan.each, plan.each)]

        @pl.when(me != target)
        def _():
            copy = push(piece, dst.at[:, me], send.at[i], recv.at[me], pts=target)
            if act == "start":
                copy.start()
            else:
                copy.wait_send()

        @pl.when(me == target)
        def _():
            copy = pltpu.make_async_copy(piece, dst.at[:, me], here)
            if act == "start":
                copy.start()
            else:
                copy.wait()
                for source in others(me, plan.pts):
                    push(piece, dst.at[:, source], send.at[i], recv.at[source], pts=source).wait_recv()


def fetch_sems(plan):
    dma = pltpu.SemaphoreType.DMA
    return [dma((plan.active,)), dma((plan.pts,)), dma(())]


def fetch_shape(plan, src):
    return jax.ShapeDtypeStruct((plan.each, plan.pts) + src.shape[1:], src.dtype)


def call(kernel, name, collective, inputs, outputs, scratch, flops, smem=()):
    vmem = pltpu.VMEM
    names = list(inputs) + list(outputs) + list(scratch)

    def body(*refs):
        kernel(types.SimpleNamespace(**dict(zip(names, refs))))

    results = pl.pallas_call(
        body,
        in_specs=[
            pl.BlockSpec(memory_space=pltpu.SMEM if key in smem else vmem) for key in inputs
        ],
        out_specs=[pl.BlockSpec(memory_space=vmem) for _ in outputs],
        out_shape=[jax.ShapeDtypeStruct(*shape) for shape in outputs.values()],
        scratch_shapes=list(scratch.values()),
        compiler_params=params(collective_id=collective, has_side_effects=True),
        cost_estimate=pl.CostEstimate(
            flops=flops, bytes_accessed=20000000, transcendentals=1000000
        ),
        name=name,
    )(*inputs.values())
    return dict(zip(outputs, results))


def dma(*shape):
    return pltpu.SemaphoreType.DMA(shape)


class Gather:
    def __init__(self, plan, part, sems):
        self.part, self.sems = part, sems
        self.plane = lax.axis_index("mdl")
        self.size = plan.mdl // 2
        self.x, self.core = self.plane // 2, lax.rem(self.plane, 2)

    @staticmethod
    def semaphores(plan):
        return dict(x_send=dma(plan.mdl // 2), recv=dma(plan.mdl), core_send=dma(plan.mdl // 2))

    def along(self, m, target, send):
        return push(self.part(m), self.part(m), send, self.sems["recv"].at[m], mdl=target)

    def x_copy(self, x):
        return self.along(self.plane, x * 2 + self.core, self.sems["x_send"].at[x])

    def core_copy(self, x):
        return self.along(
            x * 2 + self.core, self.x * 2 + 1 - self.core, self.sems["core_send"].at[x]
        )

    def arrived(self, m):
        self.along(m, m, self.sems["x_send"].at[0]).wait_recv()

    def start(self):
        for x in others(self.x, self.size):
            self.x_copy(x).start()
        self.core_copy(self.x).start()

    def forward(self):
        for x in others(self.x, self.size):
            self.arrived(x * 2 + self.core)
            self.core_copy(x).start()

    def finish(self):
        for x in [self.x] + others(self.x, self.size):
            self.arrived(x * 2 + 1 - self.core)
        for x in others(self.x, self.size):
            self.x_copy(x).wait_send()
            self.core_copy(x).wait_send()
        self.core_copy(self.x).wait_send()

    def run(self):
        self.start()
        self.forward()
        self.finish()


class Sum:
    def __init__(self, plan, parts, bufs):
        self.parts, self.bufs = parts, bufs
        self.plane = lax.axis_index("mdl")
        self.size = plan.mdl // 2
        self.x, self.core = self.plane // 2, lax.rem(self.plane, 2)

    @staticmethod
    def buffers(plan, shape):
        x = plan.mdl // 2
        vmem = pltpu.VMEM((x,) + shape, BF)
        return dict(
            near=vmem, middle=vmem, far=vmem,
            near_send=dma(x), near_recv=dma(x), far_send=dma(x), far_recv=dma(x),
        )

    def near_copy(self, x):
        b = self.bufs
        return push(
            self.parts.at[x * 2 + 1 - self.core], b["near"].at[x], b["near_send"].at[x],
            b["near_recv"].at[x], mdl=self.x * 2 + 1 - self.core,
        )

    def far_copy(self, x, slot):
        b = self.bufs
        return push(
            b["middle"].at[x], b["far"].at[slot], b["far_send"].at[x], b["far_recv"].at[slot],
            mdl=x * 2 + self.core,
        )

    def both(self, x):
        self.near_copy(x).wait_recv()
        own = self.parts[pl.ds(x * 2 + self.core, 1)][0].astype(F32)
        return own + self.bufs["near"][pl.ds(x, 1)][0].astype(F32)

    def start(self):
        for x in others(self.x, self.size) + [self.x]:
            self.near_copy(x).start()

    def middle(self):
        for x in others(self.x, self.size):
            self.bufs["middle"][pl.ds(x, 1)] = self.both(x).astype(BF)[None]
            self.far_copy(x, self.x).start()

    def finish(self):
        total = self.both(self.x)
        for x in others(self.x, self.size):
            self.far_copy(x, x).wait_recv()
            total = total + self.bufs["far"][pl.ds(x, 1)][0].astype(F32)
        for x in others(self.x, self.size):
            self.near_copy(x).wait_send()
            self.far_copy(x, self.x).wait_send()
        self.near_copy(self.x).wait_send()
        return total

    def run(self):
        self.start()
        self.middle()
        return self.finish()


class Trade:
    def __init__(self, plan, out_index, in_index, bufs):
        self.out_index, self.in_index, self.bufs = out_index, in_index, bufs
        self.size = plan.pts
        self.me = lax.axis_index("pts")

    @staticmethod
    def buffers(plan, cols, rows):
        capacity = 2 * rows // plan.pts
        vmem = pltpu.VMEM((plan.pts, cols, capacity), BF)
        return dict(leave=vmem, land=vmem, send=dma(plan.pts), recv=dma(plan.pts))

    def hot(self, index, part):
        capacity = self.bufs["leave"].shape[2]
        row = index[...]
        places = lax.broadcasted_iota(jnp.int32, (capacity, row.shape[1]), 0) + part * capacity
        return jnp.where(places == row, 1.0, 0.0).astype(BF)

    def copy(self, part, slot):
        b = self.bufs
        return push(
            b["leave"].at[part], b["land"].at[slot], b["send"].at[part], b["recv"].at[slot],
            pts=part,
        )

    def run(self, values):
        b = self.bufs
        for part in others(self.me, self.size):
            b["leave"][pl.ds(part, 1)] = dot(values, self.hot(self.out_index, part), NT).astype(BF)[None]
            self.copy(part, self.me).start()
        own = dot(values, self.hot(self.out_index, self.me), NT).astype(BF)
        total = dot(own, self.hot(self.in_index, self.me))
        for step in range(1, self.size):
            part = lax.rem(self.me + self.size - step, self.size)
            hot = self.hot(self.in_index, part)
            self.copy(part, part).wait_recv()
            total = total + dot(b["land"][pl.ds(part, 1)][0], hot)
        for part in others(self.me, self.size):
            self.copy(part, self.me).wait_send()
        return total.astype(BF)


def named(prefix, buffers):
    return {prefix + key: value for key, value in buffers.items()}


def taken_from(refs, prefix, buffers):
    return {key: getattr(refs, prefix + key) for key in buffers}


def everyone(plan):
    me, plane = lax.axis_index("pts"), lax.axis_index("mdl")
    return [{"pts": p} for p in others(me, plan.pts)] + [{"mdl": m} for m in others(plane, plan.mdl)]


def unit_columns(values):
    mean = jnp.sum(values, 0, keepdims=True) / C
    centred = values - mean
    inv_std = lax.rsqrt(jnp.sum(centred * centred, 0, keepdims=True) / C + NORM_EPS)
    return centred * inv_std, inv_std


def one_hot_window(ids_ref, tap, tile):
    row = ids_ref[pl.ds(tap, 1), pl.ds(tile * TILE, TILE)]
    places = lax.broadcasted_iota(jnp.int32, (WINDOW, TILE), 0) + tile * TILE
    return jnp.where(places == row, 1.0, 0.0).astype(BF)


PACK = 5
ORDER = [TAPS, TAPS + 4] + list(range(TAPS)) + [TAPS + 1, TAPS + 2, TAPS + 3]
ORDER = ORDER + list(range(TAPS + 5, TAPS + 5 + 2 * FF // C))
PLACE = {block: place for place, block in enumerate(ORDER)}


def front_kernel(plan, r):
    pts, mdl, slots = plan.pts, plan.mdl, plan.slots
    width, depth = plan.width, plan.depth
    me, plane = lax.axis_index("pts"), lax.axis_index("mdl")
    y, z = lax.rem(me, width), me // width
    cols, rows = r.points.shape
    total = r.blocks.shape[1]
    groups = total // PACK
    conv_groups = -(-(2 + TAPS) // PACK)
    greet(everyone(plan))

    def spread_copy(m, slot):
        return push(
            r.owned.at[m], r.spread.at[pl.ds(slot * slots, slots)], r.spread_send.at[m],
            r.spread_recv.at[slot], mdl=m,
        )

    for m in others(plane, mdl):
        spread_copy(m, plane).start()

    def vec_copy(m, slot):
        return push(
            r.vectors, r.vec_all.at[slot], r.vec_send.at[m], r.vec_recv.at[slot], mdl=m
        )

    for m in others(plane, mdl):
        vec_copy(m, plane).start()

    def up_copy():
        return push(
            r.points.at[:, rows - HALO : rows], r.ext.at[:, 0:HALO], r.halo_send.at[0],
            r.halo_recv.at[0], pts=me + 1,
        )

    def down_copy():
        return push(
            r.points.at[:, 0:HALO], r.ext.at[:, HALO + rows : 2 * HALO + rows], r.halo_send.at[1],
            r.halo_recv.at[1], pts=me - 1,
        )

    @pl.when(me < pts - 1)
    def _():
        up_copy().start()

    @pl.when(me == pts - 1)
    def _():
        r.ext[:, HALO + rows :] = jnp.zeros((cols, HALO), BF)

    @pl.when(me > 0)
    def _():
        down_copy().start()

    @pl.when(me == 0)
    def _():
        r.ext[:, :HALO] = jnp.zeros((cols, HALO), BF)

    r.ext[:, HALO : HALO + rows] = r.points[...]
    r.spread[pl.ds(plane * slots, slots)] = r.owned[pl.ds(plane, 1)][0]
    r.vec_all[pl.ds(plane, 1)] = r.vectors[...][None]
    r.points_full[pl.ds(plane * cols, cols), :] = r.points[...]
    r.cot_full[pl.ds(plane * cols, cols), :] = r.cot[...]
    for m in others(plane, mdl):
        spread_copy(m, m).wait_recv()

    def order(place, carry):
        r.blocks[pl.ds(me, 1), pl.ds(place, 1)] = r.spread[pl.ds(r.slots[place], 1)][None]
        return carry

    lax.fori_loop(0, total, order, 0)

    def group_of(source, group):
        return r.blocks.at[source, group * PACK : (group + 1) * PACK]

    def far_copy(group, v, source):
        return push(
            group_of(source, group), group_of(source, group), r.far_send.at[group, v],
            r.far_recv.at[group, source // width], pts=v * width + y,
        )

    def side_copy(group, v, source):
        return push(
            group_of(source, group), group_of(source, group),
            r.side_send.at[group, v, source // width], r.side_recv.at[group, source],
            pts=z * width + v,
        )

    for group in range(groups):
        for v in others(z, depth):
            far_copy(group, v, me).start()
        for v in others(y, width):
            side_copy(group, v, me).start()

    points_gather = Gather(
        plan, lambda m: r.points_full.at[pl.ds(m * cols, cols)],
        taken_from(r, "points_", Gather.semaphores(plan)),
    )
    cot_gather = Gather(
        plan, lambda m: r.cot_full.at[pl.ds(m * cols, cols)],
        taken_from(r, "cot_", Gather.semaphores(plan)),
    )
    points_gather.start()
    cot_gather.start()

    @pl.when(me > 0)
    def _():
        push(
            r.points.at[:, 0:HALO], r.ext.at[:, 0:HALO], r.halo_send.at[0], r.halo_recv.at[0],
            pts=me - 1,
        ).wait_recv()

    @pl.when(me < pts - 1)
    def _():
        push(
            r.points.at[:, 0:HALO], r.ext.at[:, HALO + rows : 2 * HALO + rows], r.halo_send.at[1],
            r.halo_recv.at[1], pts=me + 1,
        ).wait_recv()

    def take(tap, carry):
        for tile in range(rows // TILE):
            hot = one_hot_window(r.ids, tap, tile)
            picked = dot(r.ext[:, tile * TILE : tile * TILE + WINDOW], hot).astype(BF)
            r.taken[pl.ds(tap, 1), :, tile * TILE : (tile + 1) * TILE] = picked[None]
        return carry

    cuts = [TAPS * i // groups for i in range(groups + 1)]
    for group in range(groups):
        lax.fori_loop(cuts[group], cuts[group + 1], take, 0)
        for v in others(z, depth):
            source = v * width + y
            far_copy(group, v, source).wait_recv()
            for u in others(y, width):
                side_copy(group, u, source).start()

    def complete(group):
        for u in others(y, width):
            for v in range(depth):
                side_copy(group, u, v * width + u).wait_recv()

    pair_gather = Gather(
        plan, lambda m: r.pair.at[m], taken_from(r, "pair_", Gather.semaphores(plan))
    )
    for group in range(conv_groups):
        complete(group)
        if group == 0:
            for i in range(2):
                r.pair[pl.ds(plane, 1), i] = r.blocks[:, i].reshape(1, C, cols)
            pair_gather.start()
        low = max(group * PACK - 2, 0)
        high = min(group * PACK - 2 + PACK, TAPS)
        if cols % 128 == 0:
            weight = jnp.concatenate(
                [r.blocks[:, t + 2].reshape(C, cols) for t in range(low, high)], 1
            )
            part = dot(weight, r.taken[low:high].reshape((high - low) * cols, rows))
        else:
            part = sum(dot(r.blocks[:, t + 2].reshape(C, cols), r.taken[t]) for t in range(low, high))
        if group == 0:
            r.acc[...] = part
            pair_gather.forward()
        else:
            r.acc[...] += part

    points_gather.forward()
    cot_gather.forward()
    r.parts[...] = r.acc[...].astype(BF).reshape(mdl, cols, rows)
    hidden_sum = Sum(plan, r.parts, taken_from(r, "sum_", Sum.buffers(plan, (cols, rows))))
    hidden_sum.start()
    for m in others(plane, mdl):
        vec_copy(m, m).wait_recv()
    for m in range(mdl):
        r.vec[m * cols : (m + 1) * cols, :] = r.vec_all[m].T
    pair_gather.finish()
    points_gather.finish()
    hidden_sum.middle()
    bias = r.vec[pl.ds(plane * cols, cols), 0:1]
    r.hidden[pl.ds(plane * cols, cols), :] = (hidden_sum.finish() + bias).astype(BF)
    Gather(
        plan, lambda m: r.hidden.at[pl.ds(m * cols, cols)],
        taken_from(r, "hidden_", Gather.semaphores(plan)),
    ).run()
    hidden = r.hidden[...]
    for m in range(mdl):
        r.acc[m * cols : (m + 1) * cols, :] = dot(r.pair[m, 0], hidden, TN)
    span_size = 128

    def norms(step, carry):
        span = pl.ds(pl.multiple_of(step * span_size, span_size), span_size)
        unit, inv_std = unit_columns(r.acc[:, span] + r.vec[:, 1:2])
        r.mixed_unit[:, span] = unit
        r.mixed_std[:, span] = inv_std
        stream = r.points_full[:, span].astype(F32) + unit * r.vec[:, 2:3] + r.vec[:, 3:4]
        r.stream[:, span] = stream
        unit, inv_std = unit_columns(stream)
        r.one_unit[:, span] = unit
        r.one_std[:, span] = inv_std
        r.normed[:, span] = (unit * r.vec[:, 4:5] + r.vec[:, 5:6]).astype(BF)
        return carry

    lax.fori_loop(0, rows // span_size, norms, 0)
    trade = Trade(
        plan, r.send_pos, r.arrival, taken_from(r, "trade_", Trade.buffers(plan, cols, rows))
    )
    r.slot_in[pl.ds(plane * cols, cols), :] = trade.run(r.normed[pl.ds(plane * cols, cols), :])
    Gather(
        plan, lambda m: r.slot_in.at[pl.ds(m * cols, cols)],
        taken_from(r, "slot_", Gather.semaphores(plan)),
    ).run()
    for group in range(conv_groups, groups):
        complete(group)
    cot_gather.finish()

    @pl.when(me < pts - 1)
    def _():
        up_copy().wait_send()

    @pl.when(me > 0)
    def _():
        down_copy().wait_send()

    for m in others(plane, mdl):
        spread_copy(m, plane).wait_send()
        vec_copy(m, plane).wait_send()
    for group in range(groups):
        for v in others(z, depth):
            far_copy(group, v, me).wait_send()
        for u in others(y, width):
            for v in range(depth):
                side_copy(group, u, v * width + y).wait_send()


def front(plan, slots, owned, points, cot, vectors, ids, send_pos, arrival):
    cols, rows = points.shape
    pts, mdl = plan.pts, plan.mdl
    share = C // pts
    total = len(ORDER)
    groups = total // PACK
    vmem = pltpu.VMEM
    scratch = dict(
        spread=vmem((total, share, cols), BF),
        vec_all=vmem((mdl,) + vectors.shape, F32),
        ext=vmem((cols, rows + 2 * HALO), BF),
        acc=vmem((C, rows), F32),
        parts=vmem((mdl, cols, rows), BF),
        normed=vmem((C, rows), BF),
        points_full=vmem((C, rows), BF),
        spread_send=dma(mdl),
        spread_recv=dma(mdl),
        vec_send=dma(mdl),
        vec_recv=dma(mdl),
        halo_send=dma(2),
        halo_recv=dma(2),
        far_send=dma(groups, plan.depth),
        far_recv=dma(groups, plan.depth),
        side_send=dma(groups, plan.width, plan.depth),
        side_recv=dma(groups, pts),
        **named("sum_", Sum.buffers(plan, (cols, rows))),
        **named("trade_", Trade.buffers(plan, cols, rows)),
    )
    for prefix in ("points_", "cot_", "pair_", "hidden_", "slot_"):
        scratch.update(named(prefix, Gather.semaphores(plan)))
    return call(
        functools.partial(front_kernel, plan),
        "front",
        5,
        dict(
            slots=slots, owned=owned, points=points, cot=cot, vectors=vectors, ids=ids,
            send_pos=send_pos, arrival=arrival,
        ),
        dict(
            blocks=((pts, total, share, cols), BF),
            taken=((TAPS, cols, rows), BF),
            cot_full=((C, rows), BF),
            pair=((mdl, 2, C, cols), BF),
            vec=((C, vectors.shape[0]), F32),
            hidden=((C, rows), BF),
            mixed_unit=((C, rows), F32),
            mixed_std=((1, rows), F32),
            stream=((C, rows), F32),
            one_unit=((C, rows), F32),
            one_std=((1, rows), F32),
            slot_in=((C, rows), BF),
        ),
        scratch,
        4 * TAPS * rows * (WINDOW + C) * cols,
        smem=("slots",),
    )


def back_kernel(
    plan, back_ref, x_ref, w_ref, ids_ref, early_ref, out_ref, turn_ref,
    own, side, acc, far, turn_acc, side_send, side_recv, far_send, far_recv,
):
    width, depth = plan.width, plan.depth
    cols, rows = turn_acc.shape
    share = C // plan.pts
    taps = x_ref.shape[0]
    extra = early_ref.shape[0]
    groups = own.shape[1]
    me = lax.axis_index("pts")
    y, z = lax.rem(me, width), me // width
    side_peers = [z * width + v for v in others(y, width)]
    far_peers = [v * width + y for v in others(z, depth)]
    greet([{"pts": v} for v in side_peers + far_peers])

    def store(block, group, place):
        grid = block.astype(BF).reshape(depth, width, share, cols)
        for v in range(width):
            own[v, group, :, pl.ds(place, 1)] = grid[:, v][:, None]

    def grads(group):
        low = max(group * PACK, extra)
        for b in range(group * PACK, min(extra, (group + 1) * PACK)):
            store(early_ref[b], group, b - group * PACK)

        def one(place, carry):
            tap = group * PACK + place - extra
            store(
                dot(back_ref[:, HALO : HALO + rows], x_ref[pl.ds(tap, 1)][0], NT), group, place
            )
            return carry

        if low < (group + 1) * PACK:
            lax.fori_loop(low - group * PACK, PACK, one, 0)

    def side_copy(group, v):
        return push(
            own.at[v, group], side.at[group, y], side_send.at[group, v], side_recv.at[group, y],
            pts=z * width + v,
        )

    def side_wait(group, v):
        return push(
            own.at[v, group], side.at[group, v], side_send.at[group, v], side_recv.at[group, v],
            pts=z * width + v,
        )

    def far_copy(group, v):
        return push(
            acc.at[group, v], far.at[group, z], far_send.at[group, v], far_recv.at[group, z],
            pts=v * width + y,
        )

    def far_wait(group, v):
        return push(
            acc.at[group, v], far.at[group, v], far_send.at[group, v], far_recv.at[group, v],
            pts=v * width + y,
        )

    def start_side(group):
        grads(group)
        for v in others(y, width):
            side_copy(group, v).start()

    def start_far(group):
        total = own[pl.ds(y, 1), group][0].astype(F32)
        for v in others(y, width):
            side_wait(group, v).wait_recv()
            total = total + side[group, pl.ds(v, 1)][0].astype(F32)
        acc[group] = total.astype(BF)
        for v in others(z, depth):
            far_copy(group, v).start()

    def finish(group):
        total = acc[group, pl.ds(z, 1)][0].astype(F32)
        for v in others(z, depth):
            far_wait(group, v).wait_recv()
            total = total + far[group, pl.ds(v, 1)][0].astype(F32)
        out_ref[group * PACK : (group + 1) * PACK] = total.astype(BF)

    def turn(tap, carry):
        weight = w_ref[:, pl.ds(taps + 1 - tap, 1)].reshape(C, cols)
        turned = dot(weight, back_ref[...], TN).astype(BF)
        for tile in range(rows // TILE):
            hot = one_hot_window(ids_ref, tap, tile)
            turn_acc[:, tile * TILE : (tile + 1) * TILE] += dot(
                turned[:, tile * TILE : tile * TILE + WINDOW], hot
            )
        return carry

    turn_acc[...] = jnp.zeros_like(turn_acc)
    lag = 2
    for group in range(groups):
        start_side(group)
        if group >= lag:
            start_far(group - lag)
    left = list(range(groups - lag, groups))
    cuts = [taps * i // (len(left) + 1) for i in range(len(left) + 2)]
    for i, group in enumerate(left):
        lax.fori_loop(cuts[i], cuts[i + 1], turn, 0)
        start_far(group)
    lax.fori_loop(cuts[-2], cuts[-1], turn, 0)
    turn_ref[...] = turn_acc[...].T
    for group in range(groups):
        finish(group)
    for group in range(groups):
        for v in others(y, width):
            side_copy(group, v).wait_send()
        for v in others(z, depth):
            far_copy(group, v).wait_send()


def back_pass(plan, back_ext, taken, blocks, ids, early):
    taps, cols, rows = taken.shape
    total = taps + early.shape[0]
    groups = total // PACK
    share = C // plan.pts
    width, depth = plan.width, plan.depth
    dma = pltpu.SemaphoreType.DMA
    vmem = pl.BlockSpec(memory_space=pltpu.VMEM)
    return pl.pallas_call(
        functools.partial(back_kernel, plan),
        in_specs=[vmem] * 5,
        out_specs=[vmem] * 2,
        out_shape=[
            jax.ShapeDtypeStruct((total, share, cols), BF),
            jax.ShapeDtypeStruct((rows, cols), F32),
        ],
        scratch_shapes=[
            pltpu.VMEM((width, groups, depth, PACK, share, cols), BF),
            pltpu.VMEM((groups, width, depth, PACK, share, cols), BF),
            pltpu.VMEM((groups, depth, PACK, share, cols), BF),
            pltpu.VMEM((groups, depth, PACK, share, cols), BF),
            pltpu.VMEM((cols, rows), F32),
            dma((groups, width)),
            dma((groups, width)),
            dma((groups, depth)),
            dma((groups, depth)),
        ],
        compiler_params=params(collective_id=1, has_side_effects=True),
        cost_estimate=pl.CostEstimate(
            flops=taps * rows * (WINDOW * 4 + 5 * C) * cols,
            bytes_accessed=30000000,
            transcendentals=0,
        ),
        name="back_pass",
    )(back_ext, taken, blocks, ids, early)


def head_lanes(ext, cols, head):
    lane = lax.broadcasted_iota(jnp.int32, ext.shape, 1)
    return jnp.where((lane >= cols) | (lane // HD == head), ext, jnp.zeros_like(ext))


def fetch_step(plan, srcs, dsts, sems):
    me = lax.axis_index("pts")

    @pl.when(pl.program_id(0) == 0)
    def _():
        greet([{"pts": v} for v in others(me, plan.pts)])
        for src, dst, group in zip(srcs, dsts, sems):
            fetch_copies(plan, src, dst, group, "start")


def fetch_end(plan, srcs, dsts, sems):
    @pl.when(pl.program_id(0) == pl.num_programs(0) - 1)
    def _():
        for src, dst, group in zip(srcs, dsts, sems):
            fetch_copies(plan, src, dst, group, "wait")


def attend_kernel(
    plan, q_ref, k_ref, v_ref, one, two, out_ref, lse_ref, one_to, two_to, *sems
):
    head = pl.program_id(0)
    moves = (plan, (one, two), (one_to, two_to), (sems[:3], sems[3:]))
    fetch_step(*moves)
    rows, width = q_ref.shape
    keys = k_ref[...]
    values = v_ref[0]
    for tile in range(rows // TILE):
        span = slice(tile * TILE, (tile + 1) * TILE)
        queries = head_lanes(q_ref[span, :], width // 2, head)
        scores = dot(keys, queries, NT)
        top = jnp.max(scores, 0, keepdims=True)
        soft = jnp.exp(scores - top).astype(BF)
        summed = dot(values, soft)
        total = summed[HD : HD + 1]
        out_ref[:, span] = (summed[:HD] / total).astype(BF)
        lse_ref[0, :, span] = top + jnp.log(total)
    fetch_end(*moves)


def attend(plan, q_ext, k_ext, v_aug, one, two):
    rows, width = q_ext.shape
    heads = v_aug.shape[0]
    return pl.pallas_call(
        functools.partial(attend_kernel, plan),
        grid=(heads,),
        in_specs=[
            pl.BlockSpec((rows, width), lambda h: (0, 0)),
            pl.BlockSpec((rows, width), lambda h: (0, 0)),
            pl.BlockSpec((1, 2 * HD, rows), lambda h: (h, 0, 0)),
            pl.BlockSpec(memory_space=pl.ANY),
            pl.BlockSpec(memory_space=pl.ANY),
        ],
        out_specs=[
            pl.BlockSpec((HD, rows), lambda h: (h, 0)),
            pl.BlockSpec((1, 1, rows), lambda h: (h, 0, 0)),
            pl.BlockSpec(memory_space=pl.ANY),
            pl.BlockSpec(memory_space=pl.ANY),
        ],
        out_shape=[
            jax.ShapeDtypeStruct((heads * HD, rows), BF),
            jax.ShapeDtypeStruct((heads, 1, rows), F32),
            fetch_shape(plan, one),
            fetch_shape(plan, two),
        ],
        scratch_shapes=fetch_sems(plan) + fetch_sems(plan),
        compiler_params=params(collective_id=2, has_side_effects=True),
        cost_estimate=pl.CostEstimate(
            flops=2 * heads * rows * rows * width, bytes_accessed=rows * width * 6, transcendentals=heads * rows * rows
        ),
        name="attend",
    )(q_ext, k_ext, v_aug, one, two)


def attend_back_kernel(
    plan, q_ref, k_ref, kt_ref, v_ref, do_ref, lse_ref, inner_ref, one, two,
    dq_ref, dk_ref, dv_ref, one_to, two_to, dk_acc, dv_acc, *sems,
):
    head = pl.program_id(0)
    moves = (plan, (one, two), (one_to, two_to), (sems[:3], sems[3:]))
    fetch_step(*moves)
    rows, width = q_ref.shape
    cols = width // 2

    @pl.when(head == 0)
    def _():
        dk_acc[...] = jnp.zeros_like(dk_acc)
        dv_acc[...] = jnp.zeros_like(dv_acc)

    queries = head_lanes(q_ref[...], cols, head)
    pure = queries[:, :cols]
    grad = head_lanes(do_ref[...], cols, head)
    lse = lse_ref[0]
    inner = inner_ref[0]
    dq = jnp.zeros((HD, rows), F32)
    for tile in range(rows // TILE):
        span = slice(tile * TILE, (tile + 1) * TILE)
        scores = dot(k_ref[span, :], queries, NT)
        soft = jnp.exp(scores - lse)
        grad_soft = dot(v_ref[span, :], grad, NT)
        grad_scores = (soft * (grad_soft - inner)).astype(BF)
        dv_acc[span, :] += dot(soft.astype(BF), grad)
        dk_acc[span, :] += dot(grad_scores, pure)
        dq = dq + dot(kt_ref[:, span], grad_scores)
    dq_ref[...] = (dq * HD ** (-0.5)).astype(BF)

    @pl.when(head == pl.num_programs(0) - 1)
    def _():
        dk_ref[...] = dk_acc[...].astype(BF)
        dv_ref[...] = dv_acc[...].astype(BF)

    fetch_end(*moves)


def attend_back(plan, q_ext, k_ext, keys_t, values, grad, lse, inner, one, two):
    rows, width = q_ext.shape
    cols = width // 2
    heads = cols // HD
    whole = lambda h: (0, 0)
    return pl.pallas_call(
        functools.partial(attend_back_kernel, plan),
        grid=(heads,),
        in_specs=[
            pl.BlockSpec((rows, width), whole),
            pl.BlockSpec((rows, width), whole),
            pl.BlockSpec((HD, rows), lambda h: (h, 0)),
            pl.BlockSpec((rows, cols), whole),
            pl.BlockSpec((rows, cols), whole),
            pl.BlockSpec((1, 1, rows), lambda h: (h, 0, 0)),
            pl.BlockSpec((1, 1, rows), lambda h: (h, 0, 0)),
            pl.BlockSpec(memory_space=pl.ANY),
            pl.BlockSpec(memory_space=pl.ANY),
        ],
        out_specs=[
            pl.BlockSpec((HD, rows), lambda h: (h, 0)),
            pl.BlockSpec((rows, cols), whole),
            pl.BlockSpec((rows, cols), whole),
            pl.BlockSpec(memory_space=pl.ANY),
            pl.BlockSpec(memory_space=pl.ANY),
        ],
        out_shape=[
            jax.ShapeDtypeStruct((cols, rows), BF),
            jax.ShapeDtypeStruct((rows, cols), BF),
            jax.ShapeDtypeStruct((rows, cols), BF),
            fetch_shape(plan, one),
            fetch_shape(plan, two),
        ],
        scratch_shapes=[pltpu.VMEM((rows, cols), F32), pltpu.VMEM((rows, cols), F32)]
        + fetch_sems(plan)
        + fetch_sems(plan),
        compiler_params=params(collective_id=3, has_side_effects=True),
        cost_estimate=pl.CostEstimate(
            flops=5 * heads * rows * rows * width, bytes_accessed=rows * width * 20, transcendentals=heads * rows * rows
        ),
        name="attend_back",
    )(q_ext, k_ext, keys_t, values, grad, lse, inner, one, two)


def adam(first, second, grad):
    new_first = BETA_ONE * first + (1.0 - BETA_ONE) * grad
    new_second = BETA_TWO * second + (1.0 - BETA_TWO) * grad * grad
    direction = (
        new_first
        / (1.0 - BETA_ONE**STEP)
        / (jnp.sqrt(new_second / (1.0 - BETA_TWO**STEP)) + ADAM_EPS)
    )
    return new_first, new_second, direction


def owner_kernel(
    plan, grad_ref, left_ref, right_ref, first_ref, second_ref, rows_ref, result_ref,
    whole, results, whole_send, whole_recv, whole_here,
    rows_send, rows_recv, rows_here, back_send, back_recv, back_here,
):
    pts, mdl, each = plan.pts, plan.mdl, plan.each
    slots = plan.slots
    share, cols = grad_ref.shape[1:]
    me, plane = lax.axis_index("pts"), lax.axis_index("mdl")
    is_active = (me >= plan.first) & (me < plan.first + plan.active)
    greet(
        [
            {"pts": p, "mdl": m}
            for i, p in enumerate([me] + others(me, pts))
            for j, m in enumerate([plane] + others(plane, mdl))
            if i + j > 0
        ]
    )

    def to_whole(act):
        for step in range(mdl):
            m = lax.rem(plane + step, mdl)
            for i in range(plan.active):
                target = plan.first + i
                piece = grad_ref.at[pl.ds(m * slots + i * each, each)]
                if step == 0:

                    @pl.when(me == target)
                    def _():
                        copy = pltpu.make_async_copy(piece, whole.at[me, plane], whole_here)
                        copy.start() if act == "start" else copy.wait()

                    remote = me != target
                else:
                    remote = me >= 0

                @pl.when(remote)
                def _():
                    copy = push(
                        piece, whole.at[me, plane], whole_send.at[step, i],
                        whole_recv.at[me, plane], pts=target, mdl=m,
                    )
                    copy.start() if act == "start" else copy.wait_send()

    def to_rows(act):
        for m in others(plane, mdl):
            copy = push(
                grad_ref.at[pl.ds(m * slots, slots)], rows_ref.at[plane], rows_send.at[m],
                rows_recv.at[plane], mdl=m,
            )
            if act == "start":
                copy.start()
            else:
                copy.wait_send()
                push(
                    grad_ref.at[pl.ds(m * slots, slots)], rows_ref.at[m], rows_send.at[m],
                    rows_recv.at[m], mdl=m,
                ).wait_recv()
        copy = pltpu.make_async_copy(
            grad_ref.at[pl.ds(plane * slots, slots)], rows_ref.at[plane], rows_here
        )
        copy.start() if act == "start" else copy.wait()

    to_whole("start")
    to_rows("start")

    base = (me - plan.first) * each

    def result_copy(k, p):
        return push(
            results.at[k, :, p], result_ref.at[base + k], back_send.at[k, p],
            back_recv.at[base + k], pts=p,
        )

    def result_here(k):
        return pltpu.make_async_copy(
            results.at[k, :, me], result_ref.at[base + k], back_here.at[k]
        )

    @pl.when(is_active)
    def _():
        pltpu.make_async_copy(
            grad_ref.at[pl.ds(plane * slots + base, each)], whole.at[me, plane], whole_here
        ).wait()
        for p_step in range(pts):
            for m_step in range(mdl):
                if p_step + m_step > 0:
                    p, m = lax.rem(me + p_step, pts), lax.rem(plane + m_step, mdl)
                    push(
                        grad_ref.at[pl.ds(0, each)], whole.at[p, m], whole_send.at[0, 0],
                        whole_recv.at[p, m], pts=p, mdl=m,
                    ).wait_recv()
        for k in range(each):
            left = left_ref[k].reshape(C, C)
            right = right_ref[k].reshape(C, C)
            turned = jnp.zeros((C, C), F32)
            for m in range(mdl):
                columns = whole[:, m, k].reshape(C, cols)
                half = dot(left, columns, TN).astype(BF)
                turned = turned + dot(half, right[m * cols : (m + 1) * cols])
            rotated = turned.astype(BF)
            _, _, direction = adam(
                first_ref[k].reshape(C, C).astype(F32),
                second_ref[k].reshape(C, C).astype(F32),
                rotated.astype(F32),
            )
            update = dot(left, dot(direction.astype(BF), right, NT).astype(BF))
            results[k, 0] = rotated.reshape(pts, share, C)
            results[k, 1] = update.astype(BF).reshape(pts, share, C)
            for p in others(me, pts):
                result_copy(k, p).start()
            result_here(k).start()

    to_rows("wait")
    for i in range(plan.active):
        source = plan.first + i
        for k in range(each):

            @pl.when(me != source)
            def _():
                push(
                    results.at[k, :, me], result_ref.at[i * each + k], back_send.at[k, source],
                    back_recv.at[i * each + k], pts=source,
                ).wait_recv()

    @pl.when(is_active)
    def _():
        for k in range(each):
            result_here(k).wait()
            for p in others(me, pts):
                result_copy(k, p).wait_send()

    for step in range(mdl):
        m = lax.rem(plane + step, mdl)
        for i in range(plan.active):
            target = plan.first + i

            @pl.when((me != target) if step == 0 else (me >= 0))
            def _():
                push(
                    grad_ref.at[pl.ds(m * slots + i * each, each)], whole.at[me, plane],
                    whole_send.at[step, i], whole_recv.at[me, plane], pts=target, mdl=m,
                ).wait_send()


def owner_update(plan, grads, left, right, first, second):
    share, cols = grads.shape[1:]
    pts, mdl, each = plan.pts, plan.mdl, plan.each
    dma = pltpu.SemaphoreType.DMA
    vmem = pl.BlockSpec(memory_space=pltpu.VMEM)
    return pl.pallas_call(
        functools.partial(owner_kernel, plan),
        in_specs=[vmem] * 5,
        out_specs=[vmem] * 2,
        out_shape=[
            jax.ShapeDtypeStruct((mdl, plan.slots, share, cols), BF),
            jax.ShapeDtypeStruct((plan.slots, 2, share, C), BF),
        ],
        scratch_shapes=[
            pltpu.VMEM((pts, mdl, each, share, cols), BF),
            pltpu.VMEM((each, 2, pts, share, C), BF),
            dma((mdl, plan.active)),
            dma((pts, mdl)),
            dma(()),
            dma((mdl,)),
            dma((mdl,)),
            dma(()),
            dma((each, pts)),
            dma((plan.slots,)),
            dma((each,)),
        ],
        compiler_params=params(collective_id=4, has_side_effects=True),
        cost_estimate=pl.CostEstimate(
            flops=8 * each * C * C * C, bytes_accessed=10000000, transcendentals=each * C * C
        ),
        name="owner_update",
    )(grads, left, right, first, second)


def widen(shard_rows):
    return lax.all_gather(shard_rows, "mdl", axis=1, tiled=True)


def add_parts(partial_value):
    return lax.psum_scatter(
        partial_value.astype(BF), "mdl", scatter_dimension=1, tiled=True
    ).astype(F32)


def trade(buffer):
    return lax.all_to_all(buffer, "pts", split_axis=0, concat_axis=0, tiled=True)


def scan_index(row_ids, scan_lengths):
    bounds = jnp.cumsum(scan_lengths)
    return jnp.sum((row_ids[..., None] >= bounds[:-1]).astype(jnp.int32), -1)


def count(mask):
    return jnp.sum(mask.astype(jnp.int32), 1)


def unit_rows(values):
    mean = jnp.mean(values, -1, keepdims=True)
    centred = values - mean
    inv_std = lax.rsqrt(jnp.mean(centred * centred, -1, keepdims=True) + NORM_EPS)
    return centred * inv_std, inv_std


def unit_back(grad_unit, unit, inv_std):
    mean = jnp.mean(grad_unit, -1, keepdims=True)
    cross = jnp.mean(grad_unit * unit, -1, keepdims=True)
    return inv_std * (grad_unit - mean - unit * cross)


def gelu_slope(pre_act):
    return (
        0.5 * (1.0 + lax.erf(pre_act * 0.7071067811865476))
        + pre_act * jnp.exp(-0.5 * pre_act * pre_act) * 0.3989422804014327
    )


def local(
    points,
    cotangent,
    neighbours,
    scan_lengths,
    to_patch,
    from_patch,
    owner_slot,
    weights,
    row_eigen_basis,
    right_basis,
    first_moment,
    second_moment,
    vectors,
    vector_first,
    vector_second,
):
    rows, cols = points.shape
    slot_count = from_patch.shape[0]
    pts = lax.axis_size("pts")
    mdl = lax.axis_size("mdl")
    pts_index = lax.axis_index("pts")
    mdl_index = lax.axis_index("mdl")
    heads = cols // HD
    ff_blocks = FF // C
    patch_count = slot_count // PATCH
    capacity = 2 * rows // pts
    matrix_rate = 1.6 * C ** (-0.5)
    plan = Layout(pts, mdl, owner_slot.shape[0])

    def own(full):
        return lax.dynamic_slice_in_dim(full, mdl_index * cols, cols, full.ndim - 1)

    row_ids = pts_index * rows + jnp.arange(rows, dtype=jnp.int32)
    own_scan = scan_index(row_ids, scan_lengths)
    near = neighbours.T
    usable = (near >= 0) & (scan_index(jnp.maximum(near, 0), scan_lengths) == own_scan[None, :])
    ids = jnp.where(usable, near - (pts_index * rows - HALO), -1)

    target = to_patch // slot_count
    place = jnp.arange(rows, dtype=jnp.int32)
    rank = count((target[None, :] == target[:, None]) & (place[None, :] < place[:, None]))
    send_pos = target * capacity + rank
    buffer_ids = jnp.arange(pts * capacity, dtype=jnp.int32)
    pack = (buffer_ids[:, None] == send_pos[None, :]).astype(BF)
    held = jnp.zeros((rows + PATCH,), jnp.int32)
    held_patch = jnp.zeros((rows + PATCH,), jnp.int32)
    offset = jnp.int32(0)
    for patch in range(patch_count):
        part = from_patch[patch * PATCH : (patch + 1) * PATCH]
        held = lax.dynamic_update_slice(held, part, (offset,))
        held_patch = lax.dynamic_update_slice(
            held_patch, jnp.full((PATCH,), patch, jnp.int32), (offset,)
        )
        offset = offset + jnp.sum((part >= 0).astype(jnp.int32))
    held = held[:rows]
    held_patch = held_patch[:rows]
    source = held // rows
    arrival = source * capacity + count(
        (source[None, :] == source[:, None]) & (held[None, :] < held[:, None])
    )
    order_key = held_patch * (pts * rows) + held
    order = count(order_key[None, :] < order_key[:, None])
    scan_count = scan_lengths.shape[0]
    held_group = held_patch * scan_count + scan_index(held, scan_lengths)
    sorting = order[None, :] == place[:, None]
    arrival = jnp.sum(jnp.where(sorting, arrival[None, :], 0), 1)
    group = jnp.sum(jnp.where(sorting, held_group[None, :], 0), 1)
    unpack = (buffer_ids[None, :] == arrival[:, None]).astype(BF)
    group_ids = jnp.arange(cols, dtype=jnp.int32)
    same = group[:, None] == group_ids[None, :]
    group_q = same.astype(BF)
    group_k = jnp.where(same | (group_ids[None, :] >= patch_count * scan_count), 0.0, -1e30).astype(BF)

    def to_slots(values):
        return dot(unpack, trade(dot(pack, values).astype(BF))).astype(BF)

    def from_slots(values):
        return dot(pack, trade(dot(unpack, values, TN).astype(BF)), TN).astype(BF)

    owned = weights.astype(BF).reshape(plan.slots, C // pts, mdl, cols).transpose(2, 0, 1, 3)
    first = front(
        plan,
        owner_slot[jnp.array(ORDER)],
        owned,
        points.T,
        cotangent.T,
        vectors,
        ids,
        send_pos[None],
        arrival[None],
    )
    blocks, taken, vec = first["blocks"], first["taken"], first["vec"].T
    cot_full = first["cot_full"].T
    linear_full = first["pair"][:, 0].transpose(1, 0, 2).reshape(C, C)
    projection_full = first["pair"][:, 1].transpose(1, 0, 2).reshape(C, C)
    hidden = first["hidden"].T
    mixed_unit, mixed_std = first["mixed_unit"].T, first["mixed_std"].T
    stream_one, one_unit, one_std = first["stream"].T, first["one_unit"].T, first["one_std"].T
    slot_in = first["slot_in"].T

    def block(b):
        return blocks[:, PLACE[b]].reshape(C, cols)

    query_map, key_map, value_map = block(TAPS + 1), block(TAPS + 2), block(TAPS + 3)
    projection = block(TAPS + 4)
    queries = (dot(slot_in, query_map) + vectors[6]).astype(BF)
    keys_all = dot(slot_in, key_map).astype(BF)
    values_all = (dot(slot_in, value_map) + vectors[7]).astype(BF)
    q_ext = jnp.concatenate([queries * BF(HD ** (-0.5)), group_q], 1)
    k_ext = jnp.concatenate([keys_all, group_k], 1)
    v_aug = jnp.concatenate(
        [values_all.T.reshape(heads, HD, rows), jnp.ones((heads, HD, rows), BF)], 1
    )
    attended_t, lse, left_whole, right_whole = attend(
        plan, q_ext, k_ext, v_aug, row_eigen_basis.astype(BF), right_basis.astype(BF)
    )
    attended = attended_t.T
    attended_rows = widen(from_slots(attended))
    branch = (dot(attended_rows, projection_full, NT) + vec[8]).astype(BF)

    stream_two = stream_one + branch.astype(F32)
    two_unit, two_std = unit_rows(stream_two)
    normed_two = (two_unit * vec[9] + vec[10]).astype(BF)
    first_mlp = jnp.concatenate([block(TAPS + 5 + k) for k in range(ff_blocks)], 1)
    second_mlp = jnp.concatenate([block(TAPS + 5 + ff_blocks + k) for k in range(ff_blocks)], 1)
    first_bias = vectors[11 : 11 + ff_blocks].reshape(ff_blocks * cols)
    pre_act = dot(normed_two, first_mlp) + first_bias
    activ = jax.nn.gelu(pre_act, approximate=False).astype(BF)
    out_part = dot(activ, second_mlp, NT)
    result = (own(stream_two) + add_parts(out_part) + vectors[11 + ff_blocks]).astype(BF)
    cot = cotangent.astype(F32)
    grad_pre = (dot(cot_full, second_mlp) * gelu_slope(pre_act)).astype(BF)
    grad_two_part = dot(grad_pre, first_mlp, NT)
    scaled_part = grad_two_part * vec[9]
    row_sums = lax.psum(
        jnp.stack([jnp.sum(scaled_part, 1), jnp.sum(scaled_part * two_unit, 1)]), "mdl"
    )
    grad_normed_two = add_parts(grad_two_part)
    own_two_unit = own(two_unit)
    grad_two = cot + two_std * (
        grad_normed_two * vectors[9]
        - row_sums[0][:, None] / C
        - own_two_unit * row_sums[1][:, None] / C
    )

    grad_branch = grad_two.astype(BF)
    grad_slot = widen(to_slots(grad_branch))
    grad_branch_full = widen(grad_branch)
    grad_attended = dot(grad_slot, projection).astype(BF)
    inner = jnp.sum(
        (grad_attended.astype(F32) * attended.astype(F32)).reshape(rows, heads, HD), -1
    ).T.reshape(heads, 1, rows)
    grad_queries_t, grad_keys, grad_values, first_whole, second_whole = attend_back(
        plan,
        q_ext,
        k_ext,
        keys_all.T,
        values_all,
        grad_attended,
        lse,
        inner,
        first_moment.astype(BF),
        second_moment.astype(BF),
    )
    grad_queries = grad_queries_t.T
    slot_back = (
        dot(grad_queries, query_map, NT)
        + dot(grad_keys, key_map, NT)
        + dot(grad_values, value_map, NT)
    )
    grad_normed = widen(from_slots(add_parts(slot_back).astype(BF))).astype(F32)
    grad_one = grad_branch_full.astype(F32) + unit_back(grad_normed * vec[4], one_unit, one_std)
    own_grad_one = grad_two + own(grad_one - grad_branch_full.astype(F32))
    grad_mixed = unit_back(grad_one * vec[2], mixed_unit, mixed_std).astype(BF)

    back = dot(linear_full, grad_mixed, NT).astype(BF)
    early = [
        dot(hidden, own(grad_mixed), TN),
        dot(slot_in, grad_queries, TN),
        dot(slot_in, grad_keys, TN),
        dot(slot_in, grad_values, TN),
        dot(grad_slot, attended, TN),
    ]
    early += [
        dot(normed_two, grad_pre[:, k * cols : (k + 1) * cols], TN) for k in range(ff_blocks)
    ]
    early += [dot(cot_full, activ[:, k * cols : (k + 1) * cols], TN) for k in range(ff_blocks)]
    early = jnp.stack([e.astype(BF) for e in early])
    up = [(i, i + 1) for i in range(pts - 1)]
    down = [(i + 1, i) for i in range(pts - 1)]
    low_back = lax.ppermute(back[:, rows - HALO :], "pts", up)
    high_back = lax.ppermute(back[:, :HALO], "pts", down)
    back_ext = jnp.concatenate([low_back, back, high_back], 1)
    summed, conv_grad = back_pass(plan, back_ext, taken, blocks, ids, early)
    point_grad = own_grad_one + conv_grad
    block_of_slot = jnp.zeros_like(owner_slot).at[owner_slot].set(
        jnp.arange(owner_slot.shape[0], dtype=jnp.int32)
    )
    summed = summed[(block_of_slot + early.shape[0]) % owner_slot.shape[0]]
    grad_rows, results = owner_update(
        plan, summed, left_whole, right_whole, first_whole, second_whole
    )
    reduced = grad_rows.transpose(1, 2, 0, 3).reshape(plan.slots, C // pts, C)

    def total(values):
        return jnp.sum(values.astype(F32), 0)

    vector_local = jnp.stack(
        [
            lax.dynamic_slice_in_dim(jnp.sum(back.astype(F32), 1), mdl_index * cols, cols, 0),
            total(own(grad_mixed)),
            total(own_grad_one * own(mixed_unit)),
            total(own_grad_one),
            total(own(grad_normed) * own(one_unit)),
            total(own(grad_normed)),
            total(grad_queries),
            total(grad_values),
            total(grad_branch),
            total(grad_normed_two * own_two_unit),
            total(grad_normed_two),
        ]
    )
    vector_local = jnp.concatenate(
        [vector_local, total(grad_pre).reshape(ff_blocks, cols), total(cot)[None]], 0
    )
    vector_grad = lax.psum(vector_local, "pts")

    rotated, update = results[:, 0].astype(F32), results[:, 1].astype(F32)
    new_first, new_second, _ = adam(first_moment, second_moment, rotated)
    new_weights = weights - matrix_rate * (update + MATRIX_DECAY * weights)
    new_vector_first, new_vector_second, vector_step = adam(
        vector_first, vector_second, vector_grad
    )
    new_vectors = vectors - VECTOR_RATE * vector_step
    return (
        result,
        point_grad,
        reduced.astype(F32),
        new_first,
        new_second,
        new_weights,
        new_weights.astype(BF),
        vector_grad,
        new_vector_first,
        new_vector_second,
        new_vectors,
    )


def solution(mesh):
    by_rows = P("pts", "mdl")
    owned = P("mdl", "pts", None)
    vector = P(None, "mdl")
    return jax.shard_map(
        local,
        mesh=mesh,
        in_specs=(
            by_rows,
            by_rows,
            P("pts", None),
            P(),
            P("pts"),
            P("pts"),
            P(),
            owned,
            owned,
            owned,
            owned,
            owned,
            vector,
            vector,
            vector,
        ),
        out_specs=(
            by_rows,
            by_rows,
            owned,
            owned,
            owned,
            owned,
            owned,
            vector,
            vector,
            vector,
            vector,
        ),
        check_vma=False,
    )
```

```python
import functools
import types

import jax
import jax.numpy as jnp
from jax import lax
from jax.experimental import pallas as pl
from jax.experimental.pallas import tpu as pltpu
from jax.sharding import PartitionSpec as P

C = 512
HD = 16
FF = 2048
TAPS = 27
HALO = 256
PATCH = 1024
STEP = 5

NORM_EPS = 1e-05
BETA_ONE = 0.9
BETA_TWO = 0.999
ADAM_EPS = 1e-08
VECTOR_RATE = 0.5
MATRIX_DECAY = 0.05
TILE = 256
WINDOW = TILE + 2 * HALO
BF = jnp.bfloat16
F32 = jnp.float32
VMEM_LIMIT = 56 * 1024 * 1024

NN = (((1,), (0,)), ((), ()))
NT = (((1,), (1,)), ((), ()))
TN = (((0,), (0,)), ((), ()))


def dot(a, b, dims=NN):
    return lax.dot_general(a, b, dims, preferred_element_type=F32)


def params(**kw):
    return pltpu.CompilerParams(vmem_limit_bytes=VMEM_LIMIT, **kw)


MESH = pl.DeviceIdType.MESH


def push(src, dst, send_sem, recv_sem, **target):
    return pltpu.make_async_remote_copy(
        src_ref=src,
        dst_ref=dst,
        send_sem=send_sem,
        recv_sem=recv_sem,
        device_id=target,
        device_id_type=MESH,
    )


def greet(peers):
    barrier = pltpu.get_barrier_semaphore()
    for peer in peers:
        pl.semaphore_signal(barrier, inc=1, device_id=peer, device_id_type=MESH)
    pl.semaphore_wait(barrier, len(peers))


def others(index, size):
    return [lax.rem(index + step, size) for step in range(1, size)]


class Layout:
    def __init__(self, pts, mdl, blocks):
        self.pts, self.mdl = pts, mdl
        self.slots = blocks // mdl
        self.each = min(k for k in range(1, self.slots + 1) if self.slots % k == 0 and self.slots // k <= pts)
        self.active = self.slots // self.each
        self.first = (pts - self.active) // 2
        self.width = mdl // 2 if pts % (mdl // 2) == 0 else 1
        self.depth = pts // self.width


def fetch_copies(plan, src, dst, sems, act):
    send, recv, here = sems
    me = lax.axis_index("pts")
    for i in range(plan.active):
        target = plan.first + i
        piece = src.at[pl.ds(i * plan.each, plan.each)]

        @pl.when(me != target)
        def _():
            copy = push(piece, dst.at[:, me], send.at[i], recv.at[me], pts=target)
            if act == "start":
                copy.start()
            else:
                copy.wait_send()

        @pl.when(me == target)
        def _():
            copy = pltpu.make_async_copy(piece, dst.at[:, me], here)
            if act == "start":
                copy.start()
            else:
                copy.wait()
                for source in others(me, plan.pts):
                    push(piece, dst.at[:, source], send.at[i], recv.at[source], pts=source).wait_recv()


def fetch_sems(plan):
    dma = pltpu.SemaphoreType.DMA
    return [dma((plan.active,)), dma((plan.pts,)), dma(())]


def fetch_shape(plan, src):
    return jax.ShapeDtypeStruct((plan.each, plan.pts) + src.shape[1:], src.dtype)


def call(kernel, name, collective, inputs, outputs, scratch, flops, smem=(), free=()):
    vmem = pltpu.VMEM
    names = list(inputs) + list(outputs) + list(scratch)

    def space(key):
        return pltpu.SMEM if key in smem else pl.ANY if key in free else vmem

    def body(*refs):
        kernel(types.SimpleNamespace(**dict(zip(names, refs))))

    results = pl.pallas_call(
        body,
        in_specs=[pl.BlockSpec(memory_space=space(key)) for key in inputs],
        out_specs=[pl.BlockSpec(memory_space=space(key)) for key in outputs],
        out_shape=[jax.ShapeDtypeStruct(*shape) for shape in outputs.values()],
        scratch_shapes=list(scratch.values()),
        compiler_params=params(collective_id=collective, has_side_effects=True),
        cost_estimate=pl.CostEstimate(
            flops=flops, bytes_accessed=20000000, transcendentals=1000000
        ),
        name=name,
    )(*inputs.values())
    return dict(zip(outputs, results))


def dma(*shape):
    return pltpu.SemaphoreType.DMA(shape)


class Gather:
    def __init__(self, plan, part, sems):
        self.part, self.sems = part, sems
        self.plane = lax.axis_index("mdl")
        self.size = plan.mdl // 2
        self.x, self.core = self.plane // 2, lax.rem(self.plane, 2)

    @staticmethod
    def semaphores(plan):
        return dict(x_send=dma(plan.mdl // 2), recv=dma(plan.mdl), core_send=dma(plan.mdl // 2))

    def along(self, m, target, send):
        return push(self.part(m), self.part(m), send, self.sems["recv"].at[m], mdl=target)

    def x_copy(self, x):
        return self.along(self.plane, x * 2 + self.core, self.sems["x_send"].at[x])

    def core_copy(self, x):
        return self.along(
            x * 2 + self.core, self.x * 2 + 1 - self.core, self.sems["core_send"].at[x]
        )

    def arrived(self, m):
        self.along(m, m, self.sems["x_send"].at[0]).wait_recv()

    def start(self):
        for x in others(self.x, self.size):
            self.x_copy(x).start()
        self.core_copy(self.x).start()

    def forward(self):
        for x in others(self.x, self.size):
            self.arrived(x * 2 + self.core)
            self.core_copy(x).start()

    def finish(self):
        for x in [self.x] + others(self.x, self.size):
            self.arrived(x * 2 + 1 - self.core)
        for x in others(self.x, self.size):
            self.x_copy(x).wait_send()
            self.core_copy(x).wait_send()
        self.core_copy(self.x).wait_send()

    def run(self):
        self.start()
        self.forward()
        self.finish()


class Sum:
    def __init__(self, plan, parts, bufs):
        self.parts, self.bufs = parts, bufs
        self.plane = lax.axis_index("mdl")
        self.size = plan.mdl // 2
        self.x, self.core = self.plane // 2, lax.rem(self.plane, 2)

    @staticmethod
    def buffers(plan, shape):
        x = plan.mdl // 2
        vmem = pltpu.VMEM((x,) + shape, BF)
        return dict(
            near=vmem, middle=vmem, far=vmem,
            near_send=dma(x), near_recv=dma(x), far_send=dma(x), far_recv=dma(x),
        )

    def near_copy(self, x):
        b = self.bufs
        return push(
            self.parts.at[x * 2 + 1 - self.core], b["near"].at[x], b["near_send"].at[x],
            b["near_recv"].at[x], mdl=self.x * 2 + 1 - self.core,
        )

    def far_copy(self, x, slot):
        b = self.bufs
        return push(
            b["middle"].at[x], b["far"].at[slot], b["far_send"].at[x], b["far_recv"].at[slot],
            mdl=x * 2 + self.core,
        )

    def both(self, x):
        self.near_copy(x).wait_recv()
        own = self.parts[pl.ds(x * 2 + self.core, 1)][0].astype(F32)
        return own + self.bufs["near"][pl.ds(x, 1)][0].astype(F32)

    def start(self):
        for x in others(self.x, self.size) + [self.x]:
            self.near_copy(x).start()

    def middle(self):
        for x in others(self.x, self.size):
            self.bufs["middle"][pl.ds(x, 1)] = self.both(x).astype(BF)[None]
            self.far_copy(x, self.x).start()

    def finish(self):
        total = self.both(self.x)
        for x in others(self.x, self.size):
            self.far_copy(x, x).wait_recv()
            total = total + self.bufs["far"][pl.ds(x, 1)][0].astype(F32)
        for x in others(self.x, self.size):
            self.near_copy(x).wait_send()
            self.far_copy(x, self.x).wait_send()
        self.near_copy(self.x).wait_send()
        return total

    def run(self):
        self.start()
        self.middle()
        return self.finish()


class Trade:
    def __init__(self, plan, out_index, in_index, bufs):
        self.out_index, self.in_index, self.bufs = out_index, in_index, bufs
        self.size = plan.pts
        self.me = lax.axis_index("pts")

    @staticmethod
    def buffers(plan, cols, rows):
        capacity = 2 * rows // plan.pts
        vmem = pltpu.VMEM((plan.pts, cols, capacity), BF)
        return dict(leave=vmem, land=vmem, send=dma(plan.pts), recv=dma(plan.pts))

    def hot(self, index, part):
        capacity = self.bufs["leave"].shape[2]
        row = index[...]
        places = lax.broadcasted_iota(jnp.int32, (capacity, row.shape[1]), 0) + part * capacity
        return jnp.where(places == row, 1.0, 0.0).astype(BF)

    def copy(self, part, slot):
        b = self.bufs
        return push(
            b["leave"].at[part], b["land"].at[slot], b["send"].at[part], b["recv"].at[slot],
            pts=part,
        )

    def start(self, values):
        b = self.bufs
        for part in others(self.me, self.size):
            b["leave"][pl.ds(part, 1)] = dot(values, self.hot(self.out_index, part), NT).astype(BF)[None]
            self.copy(part, self.me).start()
        b["land"][pl.ds(self.me, 1)] = dot(values, self.hot(self.out_index, self.me), NT).astype(BF)[None]

    def finish(self):
        b = self.bufs
        total = dot(b["land"][pl.ds(self.me, 1)][0], self.hot(self.in_index, self.me))
        for step in range(1, self.size):
            part = lax.rem(self.me + self.size - step, self.size)
            hot = self.hot(self.in_index, part)
            self.copy(part, part).wait_recv()
            total = total + dot(b["land"][pl.ds(part, 1)][0], hot)
        for part in others(self.me, self.size):
            self.copy(part, self.me).wait_send()
        return total.astype(BF)

    def run(self, values):
        self.start(values)
        return self.finish()


def named(prefix, buffers):
    return {prefix + key: value for key, value in buffers.items()}


def taken_from(refs, prefix, buffers):
    return {key: getattr(refs, prefix + key) for key in buffers}


def everyone(plan):
    me, plane = lax.axis_index("pts"), lax.axis_index("mdl")
    return [{"pts": p} for p in others(me, plan.pts)] + [{"mdl": m} for m in others(plane, plan.mdl)]


def unit_columns(values):
    mean = jnp.sum(values, 0, keepdims=True) / C
    centred = values - mean
    inv_std = lax.rsqrt(jnp.sum(centred * centred, 0, keepdims=True) / C + NORM_EPS)
    return centred * inv_std, inv_std


def one_hot_window(ids_ref, tap, tile):
    row = ids_ref[pl.ds(tap, 1), pl.ds(tile * TILE, TILE)]
    places = lax.broadcasted_iota(jnp.int32, (WINDOW, TILE), 0) + tile * TILE
    return jnp.where(places == row, 1.0, 0.0).astype(BF)


PACK = 5
ORDER = [TAPS, TAPS + 4] + list(range(TAPS)) + [TAPS + 1, TAPS + 2, TAPS + 3]
ORDER = ORDER + list(range(TAPS + 5, TAPS + 5 + 2 * FF // C))
PLACE = {block: place for place, block in enumerate(ORDER)}


def front_kernel(plan, r):
    pts, mdl, slots = plan.pts, plan.mdl, plan.slots
    width, depth = plan.width, plan.depth
    me, plane = lax.axis_index("pts"), lax.axis_index("mdl")
    y, z = lax.rem(me, width), me // width
    cols, rows = r.points.shape
    total = r.blocks.shape[1]
    groups = total // PACK
    conv_groups = -(-(2 + TAPS) // PACK)
    greet(everyone(plan))

    def spread_copy(m, slot):
        return push(
            r.owned.at[m], r.spread.at[pl.ds(slot * slots, slots)], r.spread_send.at[m],
            r.spread_recv.at[slot], mdl=m,
        )

    for m in others(plane, mdl):
        spread_copy(m, plane).start()

    def vec_copy(m, slot):
        return push(
            r.vectors, r.vec_all.at[slot], r.vec_send.at[m], r.vec_recv.at[slot], mdl=m
        )

    for m in others(plane, mdl):
        vec_copy(m, plane).start()

    def up_copy():
        return push(
            r.points.at[:, rows - HALO : rows], r.ext.at[:, 0:HALO], r.halo_send.at[0],
            r.halo_recv.at[0], pts=me + 1,
        )

    def down_copy():
        return push(
            r.points.at[:, 0:HALO], r.ext.at[:, HALO + rows : 2 * HALO + rows], r.halo_send.at[1],
            r.halo_recv.at[1], pts=me - 1,
        )

    @pl.when(me < pts - 1)
    def _():
        up_copy().start()

    @pl.when(me == pts - 1)
    def _():
        r.ext[:, HALO + rows :] = jnp.zeros((cols, HALO), BF)

    @pl.when(me > 0)
    def _():
        down_copy().start()

    @pl.when(me == 0)
    def _():
        r.ext[:, :HALO] = jnp.zeros((cols, HALO), BF)

    r.ext[:, HALO : HALO + rows] = r.points[...]
    r.spread[pl.ds(plane * slots, slots)] = r.owned[pl.ds(plane, 1)][0]
    r.vec_all[pl.ds(plane, 1)] = r.vectors[...][None]
    r.points_full[pl.ds(plane * cols, cols), :] = r.points[...]
    r.cot_full[pl.ds(plane * cols, cols), :] = r.cot[...]
    for m in others(plane, mdl):
        spread_copy(m, m).wait_recv()

    def order(place, carry):
        r.blocks[pl.ds(me, 1), pl.ds(place, 1)] = r.spread[pl.ds(r.slots[place], 1)][None]
        return carry

    lax.fori_loop(0, total, order, 0)

    def group_of(source, group):
        return r.blocks.at[source, group * PACK : (group + 1) * PACK]

    def far_copy(group, v, source):
        return push(
            group_of(source, group), group_of(source, group), r.far_send.at[group, v],
            r.far_recv.at[group, source // width], pts=v * width + y,
        )

    def side_copy(group, v, source):
        return push(
            group_of(source, group), group_of(source, group),
            r.side_send.at[group, v, source // width], r.side_recv.at[group, source],
            pts=z * width + v,
        )

    for group in range(groups):
        for v in others(z, depth):
            far_copy(group, v, me).start()
        for v in others(y, width):
            side_copy(group, v, me).start()

    points_gather = Gather(
        plan, lambda m: r.points_full.at[pl.ds(m * cols, cols)],
        taken_from(r, "points_", Gather.semaphores(plan)),
    )
    cot_gather = Gather(
        plan, lambda m: r.cot_full.at[pl.ds(m * cols, cols)],
        taken_from(r, "cot_", Gather.semaphores(plan)),
    )
    points_gather.start()
    cot_gather.start()

    @pl.when(me > 0)
    def _():
        push(
            r.points.at[:, 0:HALO], r.ext.at[:, 0:HALO], r.halo_send.at[0], r.halo_recv.at[0],
            pts=me - 1,
        ).wait_recv()

    @pl.when(me < pts - 1)
    def _():
        push(
            r.points.at[:, 0:HALO], r.ext.at[:, HALO + rows : 2 * HALO + rows], r.halo_send.at[1],
            r.halo_recv.at[1], pts=me + 1,
        ).wait_recv()

    def take(tap, carry):
        for tile in range(rows // TILE):
            hot = one_hot_window(r.ids, tap, tile)
            picked = dot(r.ext[:, tile * TILE : tile * TILE + WINDOW], hot).astype(BF)
            r.taken[pl.ds(tap, 1), :, tile * TILE : (tile + 1) * TILE] = picked[None]
        return carry

    cuts = [TAPS * i // groups for i in range(groups + 1)]
    for group in range(groups):
        lax.fori_loop(cuts[group], cuts[group + 1], take, 0)
        for v in others(z, depth):
            source = v * width + y
            far_copy(group, v, source).wait_recv()
            for u in others(y, width):
                side_copy(group, u, source).start()

    def complete(group):
        for u in others(y, width):
            for v in range(depth):
                side_copy(group, u, v * width + u).wait_recv()

    pair_gather = Gather(
        plan, lambda m: r.pair.at[m], taken_from(r, "pair_", Gather.semaphores(plan))
    )
    for group in range(conv_groups):
        complete(group)
        if group == 0:
            for i in range(2):
                r.pair[pl.ds(plane, 1), i] = r.blocks[:, i].reshape(1, C, cols)
            pair_gather.start()
        low = max(group * PACK - 2, 0)
        high = min(group * PACK - 2 + PACK, TAPS)
        if cols % 128 == 0:
            weight = jnp.concatenate(
                [r.blocks[:, t + 2].reshape(C, cols) for t in range(low, high)], 1
            )
            part = dot(weight, r.taken[low:high].reshape((high - low) * cols, rows))
        else:
            part = sum(dot(r.blocks[:, t + 2].reshape(C, cols), r.taken[t]) for t in range(low, high))
        if group == 0:
            r.acc[...] = part
            pair_gather.forward()
        else:
            r.acc[...] += part

    points_gather.forward()
    cot_gather.forward()
    r.parts[...] = r.acc[...].astype(BF).reshape(mdl, cols, rows)
    hidden_sum = Sum(plan, r.parts, taken_from(r, "sum_", Sum.buffers(plan, (cols, rows))))
    hidden_sum.start()
    for m in others(plane, mdl):
        vec_copy(m, m).wait_recv()
    for m in range(mdl):
        r.vec[m * cols : (m + 1) * cols, :] = r.vec_all[m].T
    pair_gather.finish()
    points_gather.finish()
    hidden_sum.middle()
    bias = r.vec[pl.ds(plane * cols, cols), 0:1]
    r.hidden[pl.ds(plane * cols, cols), :] = (hidden_sum.finish() + bias).astype(BF)
    Gather(
        plan, lambda m: r.hidden.at[pl.ds(m * cols, cols)],
        taken_from(r, "hidden_", Gather.semaphores(plan)),
    ).run()
    hidden = r.hidden[...]
    for m in range(mdl):
        r.acc[m * cols : (m + 1) * cols, :] = dot(r.pair[m, 0], hidden, TN)
    span_size = 128

    def norms(step, carry):
        span = pl.ds(pl.multiple_of(step * span_size, span_size), span_size)
        unit, inv_std = unit_columns(r.acc[:, span] + r.vec[:, 1:2])
        r.mixed_unit[:, span] = unit
        r.mixed_std[:, span] = inv_std
        stream = r.points_full[:, span].astype(F32) + unit * r.vec[:, 2:3] + r.vec[:, 3:4]
        r.stream[:, span] = stream
        unit, inv_std = unit_columns(stream)
        r.one_unit[:, span] = unit
        r.one_std[:, span] = inv_std
        r.normed[:, span] = (unit * r.vec[:, 4:5] + r.vec[:, 5:6]).astype(BF)
        return carry

    lax.fori_loop(0, rows // span_size, norms, 0)
    trade = Trade(
        plan, r.send_pos, r.arrival, taken_from(r, "trade_", Trade.buffers(plan, cols, rows))
    )
    r.slot_in[pl.ds(plane * cols, cols), :] = trade.run(r.normed[pl.ds(plane * cols, cols), :])
    Gather(
        plan, lambda m: r.slot_in.at[pl.ds(m * cols, cols)],
        taken_from(r, "slot_", Gather.semaphores(plan)),
    ).run()
    for group in range(conv_groups, groups):
        complete(group)
    for i in range(r.rest.shape[0]):
        r.rest[i] = r.blocks[:, TAPS + 2 + i].reshape(C, cols)
    cot_gather.finish()

    @pl.when(me < pts - 1)
    def _():
        up_copy().wait_send()

    @pl.when(me > 0)
    def _():
        down_copy().wait_send()

    for m in others(plane, mdl):
        spread_copy(m, plane).wait_send()
        vec_copy(m, plane).wait_send()
    for group in range(groups):
        for v in others(z, depth):
            far_copy(group, v, me).wait_send()
        for u in others(y, width):
            for v in range(depth):
                side_copy(group, u, v * width + y).wait_send()


def front(plan, slots, owned, points, cot, vectors, ids, send_pos, arrival):
    cols, rows = points.shape
    pts, mdl = plan.pts, plan.mdl
    share = C // pts
    total = len(ORDER)
    groups = total // PACK
    vmem = pltpu.VMEM
    scratch = dict(
        spread=vmem((total, share, cols), BF),
        vec_all=vmem((mdl,) + vectors.shape, F32),
        ext=vmem((cols, rows + 2 * HALO), BF),
        acc=vmem((C, rows), F32),
        parts=vmem((mdl, cols, rows), BF),
        normed=vmem((C, rows), BF),
        points_full=vmem((C, rows), BF),
        spread_send=dma(mdl),
        spread_recv=dma(mdl),
        vec_send=dma(mdl),
        vec_recv=dma(mdl),
        halo_send=dma(2),
        halo_recv=dma(2),
        far_send=dma(groups, plan.depth),
        far_recv=dma(groups, plan.depth),
        side_send=dma(groups, plan.width, plan.depth),
        side_recv=dma(groups, pts),
        **named("sum_", Sum.buffers(plan, (cols, rows))),
        **named("trade_", Trade.buffers(plan, cols, rows)),
    )
    for prefix in ("points_", "cot_", "pair_", "hidden_", "slot_"):
        scratch.update(named(prefix, Gather.semaphores(plan)))
    return call(
        functools.partial(front_kernel, plan),
        "front",
        5,
        dict(
            slots=slots, owned=owned, points=points, cot=cot, vectors=vectors, ids=ids,
            send_pos=send_pos, arrival=arrival,
        ),
        dict(
            blocks=((pts, total, share, cols), BF),
            taken=((TAPS, cols, rows), BF),
            cot_full=((C, rows), BF),
            pair=((mdl, 2, C, cols), BF),
            vec=((C, vectors.shape[0]), F32),
            hidden=((C, rows), BF),
            mixed_unit=((C, rows), F32),
            mixed_std=((1, rows), F32),
            stream=((C, rows), F32),
            one_unit=((C, rows), F32),
            one_std=((1, rows), F32),
            slot_in=((C, rows), BF),
            rest=((total - TAPS - 2, C, cols), BF),
        ),
        scratch,
        4 * TAPS * rows * (WINDOW + C) * cols,
        smem=("slots",),
    )


def fetches(plan, srcs, dsts, refs, act):
    for place, (src, dst) in enumerate(zip(srcs, dsts)):
        sems = [getattr(refs, f"fetch{place}_{key}") for key in ("send", "recv", "here")]
        fetch_copies(plan, src, dst, sems, act)


def fetch_scratch(plan):
    return {
        f"fetch{place}_{key}": sem
        for place in range(2)
        for key, sem in zip(("send", "recv", "here"), fetch_sems(plan))
    }


def head_lanes(ext, cols, head):
    lane = lax.broadcasted_iota(jnp.int32, ext.shape, 1)
    return jnp.where((lane >= cols) | (lane // HD == head), ext, jnp.zeros_like(ext))


def head_rows(head):
    return pl.ds(pl.multiple_of(head * HD, HD), HD)


def attend_kernel(plan, r):
    plane = lax.axis_index("mdl")
    rows, cols = r.values.shape
    heads = cols // HD
    greet(everyone(plan))
    moves = (plan, (r.left, r.right), (r.left_whole, r.right_whole), r)
    fetches(*moves, "start")
    slot_in = r.slot_in[...]
    queries = (dot(slot_in, r.rest[0], TN) + r.vectors[6:7, :]).astype(BF)
    r.q_ext[:, :cols] = queries * BF(HD ** (-0.5))
    r.q_ext[:, cols:] = r.group_q[...]
    r.k_ext[:, :cols] = dot(slot_in, r.rest[1], TN).astype(BF)
    r.k_ext[:, cols:] = r.group_k[...]
    values = dot(slot_in, r.rest[2], TN) + r.vectors[7:8, :]
    r.values[...] = values.astype(BF)
    r.v_aug[:, :HD] = values.T.astype(BF).reshape(heads, HD, rows)
    r.v_aug[:, HD:] = jnp.ones((heads, HD, rows), BF)

    def one(head, carry):
        keys = r.k_ext[...]
        values_t = r.v_aug[pl.ds(head, 1)][0]
        for tile in range(rows // TILE):
            span = slice(tile * TILE, (tile + 1) * TILE)
            scores = dot(keys, head_lanes(r.q_ext[span, :], cols, head), NT)
            top = jnp.max(scores, 0, keepdims=True)
            soft = jnp.exp(scores - top).astype(BF)
            summed = dot(values_t, soft)
            total = summed[HD : HD + 1]
            r.attended[head_rows(head), span] = (summed[:HD] / total).astype(BF)
            r.lse[pl.ds(head, 1), :, span] = (top + jnp.log(total))[None]
        return carry

    lax.fori_loop(0, heads, one, 0)
    trade = Trade(
        plan, r.arrival, r.send_pos, taken_from(r, "trade_", Trade.buffers(plan, cols, rows))
    )
    r.attended_rows[pl.ds(plane * cols, cols), :] = trade.run(r.attended[...])
    Gather(
        plan, lambda m: r.attended_rows.at[pl.ds(m * cols, cols)],
        taken_from(r, "rows_", Gather.semaphores(plan)),
    ).run()
    fetches(*moves, "wait")


def attend(plan, slot_in, rest, vectors, group_q, group_k, send_pos, arrival, left, right):
    rows, cols = group_q.shape
    heads = cols // HD
    fetched = fetch_shape(plan, left)
    return call(
        functools.partial(attend_kernel, plan),
        "attend",
        2,
        dict(
            slot_in=slot_in, rest=rest, vectors=vectors, group_q=group_q, group_k=group_k,
            send_pos=send_pos, arrival=arrival, left=left, right=right,
        ),
        dict(
            q_ext=((rows, 2 * cols), BF),
            k_ext=((rows, 2 * cols), BF),
            values=((rows, cols), BF),
            attended=((cols, rows), BF),
            lse=((heads, 1, rows), F32),
            attended_rows=((C, rows), BF),
            left_whole=(fetched.shape, fetched.dtype),
            right_whole=(fetched.shape, fetched.dtype),
        ),
        dict(
            v_aug=pltpu.VMEM((heads, 2 * HD, rows), BF),
            **fetch_scratch(plan),
            **named("trade_", Trade.buffers(plan, cols, rows)),
            **named("rows_", Gather.semaphores(plan)),
        ),
        4 * heads * rows * rows * cols,
        free=("left", "right", "left_whole", "right_whole"),
    )


def attend_back_kernel(plan, r):
    plane = lax.axis_index("mdl")
    rows, cols = r.values.shape
    heads = cols // HD
    greet(everyone(plan))
    moves = (plan, (r.first, r.second), (r.first_whole, r.second_whole), r)
    fetches(*moves, "start")
    grad_slot = r.grad_slot[...]
    grad_t = dot(r.pair[pl.ds(plane, 1), 1][0], grad_slot, TN).astype(BF).astype(F32)
    r.grad[...] = grad_t.T.astype(BF)
    weighed = grad_t * r.attended[...].astype(F32)
    r.inner[...] = jnp.sum(weighed.reshape(heads, HD, rows), 1, keepdims=True)
    r.keys_t[...] = r.k_ext[:, :cols].astype(F32).T.astype(BF)
    r.dk_acc[...] = jnp.zeros_like(r.dk_acc)
    r.dv_acc[...] = jnp.zeros_like(r.dv_acc)

    def one(head, carry):
        queries = head_lanes(r.q_ext[...], cols, head)
        pure = queries[:, :cols]
        grad = head_lanes(r.grad[...], cols, head)
        lse = r.lse[pl.ds(head, 1)][0]
        inner = r.inner[pl.ds(head, 1)][0]
        keys_t = r.keys_t[head_rows(head), :]
        dq = jnp.zeros((HD, rows), F32)
        for tile in range(rows // TILE):
            span = slice(tile * TILE, (tile + 1) * TILE)
            scores = dot(r.k_ext[span, :], queries, NT)
            soft = jnp.exp(scores - lse)
            grad_soft = dot(r.values[span, :], grad, NT)
            grad_scores = (soft * (grad_soft - inner)).astype(BF)
            r.dv_acc[span, :] += dot(soft.astype(BF), grad)
            r.dk_acc[span, :] += dot(grad_scores, pure)
            dq = dq + dot(keys_t[:, span], grad_scores)
        r.dq[head_rows(head), :] = (dq * HD ** (-0.5)).astype(BF)
        return carry

    lax.fori_loop(0, heads, one, 0)
    dk = r.dk_acc[...].astype(BF)
    dv = r.dv_acc[...].astype(BF)
    back = dot(r.rest[0], r.dq[...]) + dot(r.rest[1], dk, NT) + dot(r.rest[2], dv, NT)
    r.parts[...] = back.astype(BF).reshape(plan.mdl, cols, rows)
    back_sum = Sum(plan, r.parts, taken_from(r, "sum_", Sum.buffers(plan, (cols, rows))))
    back_sum.start()
    r.weight_grads[0] = dot(r.slot_in[...], r.dq[...], NT).astype(BF)
    r.weight_grads[1] = dot(r.slot_in[...], dk).astype(BF)
    back_sum.middle()
    r.weight_grads[2] = dot(r.slot_in[...], dv).astype(BF)
    r.weight_grads[3] = dot(r.grad_slot[...], r.attended[...], NT).astype(BF)
    trade = Trade(
        plan, r.arrival, r.send_pos, taken_from(r, "trade_", Trade.buffers(plan, cols, rows))
    )
    trade.start(back_sum.finish().astype(BF))
    r.sums[...] = jnp.zeros_like(r.sums)
    r.sums[:, 0:1] = jnp.sum(r.dq[...].astype(F32), 1, keepdims=True)
    r.sums[:, 1:2] = jnp.sum(dv.astype(F32), 0, keepdims=True).T
    r.grad_normed[pl.ds(plane * cols, cols), :] = trade.finish()
    Gather(
        plan, lambda m: r.grad_normed.at[pl.ds(m * cols, cols)],
        taken_from(r, "rows_", Gather.semaphores(plan)),
    ).run()
    fetches(*moves, "wait")


def attend_back(plan, kept, grad_slot, slot_in, rest, pair, send_pos, arrival, first, second):
    rows, cols = kept["values"].shape
    heads = cols // HD
    vmem = pltpu.VMEM
    fetched = fetch_shape(plan, first)
    names = ("q_ext", "k_ext", "values", "attended", "lse")
    return call(
        functools.partial(attend_back_kernel, plan),
        "attend_back",
        3,
        dict(
            **{key: kept[key] for key in names}, grad_slot=grad_slot, slot_in=slot_in, rest=rest,
            pair=pair, send_pos=send_pos, arrival=arrival, first=first, second=second,
        ),
        dict(
            grad_normed=((C, rows), BF),
            weight_grads=((4, C, cols), BF),
            sums=((cols, 8), F32),
            first_whole=(fetched.shape, fetched.dtype),
            second_whole=(fetched.shape, fetched.dtype),
        ),
        dict(
            grad=vmem((rows, cols), BF),
            inner=vmem((heads, 1, rows), F32),
            keys_t=vmem((cols, rows), BF),
            dk_acc=vmem((rows, cols), F32),
            dv_acc=vmem((rows, cols), F32),
            dq=vmem((cols, rows), BF),
            parts=vmem((plan.mdl, cols, rows), BF),
            **fetch_scratch(plan),
            **named("sum_", Sum.buffers(plan, (cols, rows))),
            **named("trade_", Trade.buffers(plan, cols, rows)),
            **named("rows_", Gather.semaphores(plan)),
        ),
        10 * heads * rows * rows * cols,
        free=("first", "second", "first_whole", "second_whole"),
    )


SPAN = 128


def over_spans(rows, body, size=SPAN):
    def step(index, carry):
        body(pl.ds(pl.multiple_of(index * size, size), size))
        return carry

    lax.fori_loop(0, rows // size, step, 0)


def beside(blocks):
    def times(right, cols):
        if cols % 128 == 0:
            return dot(jnp.concatenate(blocks, 1), right[...])
        return sum(
            dot(block, right[i * cols : (i + 1) * cols, :]) for i, block in enumerate(blocks)
        )

    return times


def mlp_kernel(plan, r):
    mdl = plan.mdl
    plane = lax.axis_index("mdl")
    cols, rows = r.cot.shape
    ff_blocks = FF // C
    own = pl.ds(plane * cols, cols)
    greet(everyone(plan))
    r.acc[...] = beside([r.pair[m, 1] for m in range(mdl)])(r.attended_rows, cols)

    def norms(span):
        branch = (r.acc[:, span] + r.vec[:, 8:9]).astype(BF).astype(F32)
        two = r.stream[:, span] + branch
        r.two[:, span] = two
        unit, inv_std = unit_columns(two)
        r.two_unit[:, span] = unit
        r.two_std[:, span] = inv_std
        r.normed[:, span] = (unit * r.vec[:, 9:10] + r.vec[:, 10:11]).astype(BF)

    over_spans(rows, norms)
    for k in range(ff_blocks):
        part = slice(k * cols, (k + 1) * cols)
        r.pre[...] = dot(r.rest[3 + k], r.normed[...], TN) + r.vec[own, 11 + k : 12 + k]
        r.grad_act[...] = dot(r.rest[3 + ff_blocks + k], r.cot_full[...], TN)

        def bend(span):
            pre = r.pre[:, span]
            half = 0.5 * (1.0 + lax.erf(pre * 0.7071067811865476))
            r.act[part, span] = (pre * half).astype(BF)
            slope = half + pre * jnp.exp(-0.5 * pre * pre) * 0.3989422804014327
            r.grad_pre[part, span] = (r.grad_act[:, span] * slope).astype(BF)

        over_spans(rows, bend, 256)
    r.acc[...] = beside([r.rest[3 + k] for k in range(ff_blocks)])(r.grad_pre, cols)

    def stats(span):
        scaled = r.acc[:, span] * r.vec[:, 9:10]
        r.stats[pl.ds(plane, 1), 0:1, span] = jnp.sum(scaled, 0, keepdims=True)[None]
        r.stats[pl.ds(plane, 1), 1:2, span] = jnp.sum(scaled * r.two_unit[:, span], 0, keepdims=True)[None]

    over_spans(rows, stats)

    def stats_copy(m, slot):
        return push(
            r.stats.at[slot], r.stats.at[slot], r.stats_send.at[m], r.stats_recv.at[slot], mdl=m
        )

    for m in others(plane, mdl):
        stats_copy(m, plane).start()
    r.parts[...] = r.acc[...].astype(BF).reshape(mdl, cols, rows)
    shape = Sum.buffers(plan, (cols, rows))
    grad_sum = Sum(plan, r.parts, taken_from(r, "grad_", shape))
    grad_sum.start()
    out = beside([r.rest[3 + ff_blocks + k] for k in range(ff_blocks)])(r.act, cols)
    r.out_parts[...] = out.astype(BF).reshape(mdl, cols, rows)
    grad_sum.middle()
    out_sum = Sum(plan, r.out_parts, taken_from(r, "out_", shape))
    out_sum.start()
    for m in others(plane, mdl):
        stats_copy(m, m).wait_recv()
    mean = sum(r.stats[m, 0:1] for m in range(mdl)) / C
    cross = sum(r.stats[m, 1:2] for m in range(mdl)) / C
    cot = r.cot[...].astype(F32)
    grad_normed = grad_sum.finish()
    unit = r.two_unit[own, :]
    grad_two = cot + r.two_std[...] * (grad_normed * r.vec[own, 9:10] - mean - unit * cross)
    r.grad_two[...] = grad_two
    branch = grad_two.astype(BF)
    r.branch_full[own, :] = branch
    trade = Trade(
        plan, r.send_pos, r.arrival, taken_from(r, "trade_", Trade.buffers(plan, cols, rows))
    )
    trade.start(branch)
    branch_gather = Gather(
        plan, lambda m: r.branch_full.at[pl.ds(m * cols, cols)],
        taken_from(r, "branch_", Gather.semaphores(plan)),
    )
    branch_gather.start()
    out_sum.middle()

    def along(values):
        return jnp.sum(values.astype(F32), 1, keepdims=True)

    r.sums[:, 0:1] = along(branch)
    r.sums[:, 1:2] = along(grad_normed * unit)
    r.sums[:, 2:3] = along(grad_normed)
    for k in range(ff_blocks):
        part = slice(k * cols, (k + 1) * cols)
        r.sums[:, 3 + k : 4 + k] = along(r.grad_pre[part, :])
        r.weight_grads[k] = dot(r.normed[...], r.grad_pre[part, :], NT).astype(BF)
        r.weight_grads[ff_blocks + k] = dot(r.cot_full[...], r.act[part, :], NT).astype(BF)
    r.sums[:, 3 + ff_blocks : 4 + ff_blocks] = along(cot)
    r.grad_slot[own, :] = trade.finish()
    slot_gather = Gather(
        plan, lambda m: r.grad_slot.at[pl.ds(m * cols, cols)],
        taken_from(r, "slot_", Gather.semaphores(plan)),
    )
    slot_gather.start()
    branch_gather.forward()
    bias = r.vec[own, 11 + ff_blocks : 12 + ff_blocks]
    r.out[...] = (r.two[own, :] + out_sum.finish() + bias).T.astype(BF)
    slot_gather.forward()
    branch_gather.finish()
    slot_gather.finish()
    for m in others(plane, mdl):
        stats_copy(m, plane).wait_send()


def mlp(plan, attended_rows, first, rest, cot, send_pos, arrival):
    cols, rows = cot.shape
    ff_blocks = FF // C
    vmem = pltpu.VMEM
    names = ("pair", "stream", "vec", "cot_full")
    scratch = dict(
        acc=vmem((C, rows), F32),
        two=vmem((C, rows), F32),
        two_unit=vmem((C, rows), F32),
        two_std=vmem((1, rows), F32),
        normed=vmem((C, rows), BF),
        pre=vmem((cols, rows), F32),
        grad_act=vmem((cols, rows), F32),
        act=vmem((ff_blocks * cols, rows), BF),
        grad_pre=vmem((ff_blocks * cols, rows), BF),
        stats=vmem((plan.mdl, 8, rows), F32),
        stats_send=dma(plan.mdl),
        stats_recv=dma(plan.mdl),
        parts=vmem((plan.mdl, cols, rows), BF),
        out_parts=vmem((plan.mdl, cols, rows), BF),
        **named("grad_", Sum.buffers(plan, (cols, rows))),
        **named("out_", Sum.buffers(plan, (cols, rows))),
        **named("trade_", Trade.buffers(plan, cols, rows)),
        **named("branch_", Gather.semaphores(plan)),
        **named("slot_", Gather.semaphores(plan)),
    )
    return call(
        functools.partial(mlp_kernel, plan),
        "mlp",
        6,
        dict(
            attended_rows=attended_rows, **{key: first[key] for key in names}, rest=rest, cot=cot,
            send_pos=send_pos, arrival=arrival,
        ),
        dict(
            grad_slot=((C, rows), BF),
            branch_full=((C, rows), BF),
            grad_two=((cols, rows), F32),
            out=((rows, cols), BF),
            weight_grads=((2 * ff_blocks, C, cols), BF),
            sums=((cols, 4 + ff_blocks), F32),
        ),
        scratch,
        16 * rows * C * cols * ff_blocks,
    )


BACK_ORDER = list(range(TAPS + 5, TAPS + 5 + 2 * FF // C)) + [TAPS + 1, TAPS + 2, TAPS + 3, TAPS + 4]
BACK_ORDER = BACK_ORDER + [TAPS] + list(range(TAPS))


def back_kernel(plan, r):
    pts, width, depth = plan.pts, plan.width, plan.depth
    cols, rows = r.turn_acc.shape
    share = C // pts
    taps = r.taken.shape[0]
    mlp_count, attend_count = r.mlp_grads.shape[0], r.attend_grads.shape[0]
    extra = mlp_count + attend_count + 1
    groups = r.own.shape[1]
    me, plane = lax.axis_index("pts"), lax.axis_index("mdl")
    y, z = lax.rem(me, width), me // width
    own_cols = pl.ds(plane * cols, cols)
    middle = slice(HALO, HALO + rows)
    greet([{"pts": v} for v in others(me, pts)])

    def store(block, group, place):
        grid = block.astype(BF).reshape(depth, width, share, cols)
        for v in range(width):
            r.own[v, group, :, pl.ds(place, 1)] = grid[:, v][:, None]

    def grads(group):
        for b in range(group * PACK, min(extra, (group + 1) * PACK)):
            if b < mlp_count:
                block = r.mlp_grads[b]
            elif b < extra - 1:
                block = r.attend_grads[b - mlp_count]
            else:
                block = dot(r.hidden[...], r.mixed[own_cols, :], NT)
            store(block, group, b - group * PACK)

        def one(place, carry):
            tap = group * PACK + place - extra
            store(dot(r.back[:, middle], r.taken[pl.ds(tap, 1)][0], NT), group, place)
            return carry

        low = max(group * PACK, extra)
        if low < (group + 1) * PACK:
            lax.fori_loop(low - group * PACK, PACK, one, 0)

    def side_copy(group, v, slot):
        return push(
            r.own.at[v, group], r.side.at[group, slot], r.side_send.at[group, v],
            r.side_recv.at[group, slot], pts=z * width + v,
        )

    def far_copy(group, v, slot):
        return push(
            r.acc.at[group, v], r.far.at[group, slot], r.far_send.at[group, v],
            r.far_recv.at[group, slot], pts=v * width + y,
        )

    def start_side(group):
        grads(group)
        for v in others(y, width):
            side_copy(group, v, y).start()

    def start_far(group):
        total = r.own[pl.ds(y, 1), group][0].astype(F32)
        for v in others(y, width):
            side_copy(group, v, v).wait_recv()
            total = total + r.side[group, pl.ds(v, 1)][0].astype(F32)
        r.acc[group] = total.astype(BF)
        for v in others(z, depth):
            far_copy(group, v, z).start()

    def finish(group):
        total = r.acc[group, pl.ds(z, 1)][0].astype(F32)
        for v in others(z, depth):
            far_copy(group, v, v).wait_recv()
            total = total + r.far[group, pl.ds(v, 1)][0].astype(F32)
        r.summed[group * PACK : (group + 1) * PACK] = total.astype(BF)

    ready = (mlp_count + attend_count) // PACK
    for group in range(ready):
        start_side(group)

    def norms(span):
        grad = r.grad_normed[:, span].astype(F32) * r.vec[:, 4:5]
        unit = r.one_unit[:, span]
        delta = r.one_std[:, span] * (
            grad
            - jnp.sum(grad, 0, keepdims=True) / C
            - unit * (jnp.sum(grad * unit, 0, keepdims=True) / C)
        )
        r.delta[:, span] = delta
        grad = (r.branch_full[:, span].astype(F32) + delta) * r.vec[:, 2:3]
        unit = r.mixed_unit[:, span]
        r.mixed[:, span] = (
            r.mixed_std[:, span]
            * (
                grad
                - jnp.sum(grad, 0, keepdims=True) / C
                - unit * (jnp.sum(grad * unit, 0, keepdims=True) / C)
            )
        ).astype(BF)

    over_spans(rows, norms)
    back = beside([r.pair[m, 0] for m in range(plan.mdl)])(r.mixed, cols)
    r.back[:, middle] = back.astype(BF)

    def up_copy(target):
        return push(
            r.back.at[:, rows : rows + HALO], r.back.at[:, 0:HALO], r.halo_send.at[0],
            r.halo_recv.at[0], pts=target,
        )

    def down_copy(target):
        return push(
            r.back.at[:, HALO : 2 * HALO], r.back.at[:, HALO + rows : 2 * HALO + rows],
            r.halo_send.at[1], r.halo_recv.at[1], pts=target,
        )

    @pl.when(me < pts - 1)
    def _():
        up_copy(me + 1).start()

    @pl.when(me == pts - 1)
    def _():
        r.back[:, HALO + rows :] = jnp.zeros((C, HALO), BF)

    @pl.when(me > 0)
    def _():
        down_copy(me - 1).start()

    @pl.when(me == 0)
    def _():
        r.back[:, :HALO] = jnp.zeros((C, HALO), BF)

    lag = 2
    for group in range(ready, groups):
        start_side(group)
        if group >= lag:
            start_far(group - lag)

    grad_one = r.grad_two[...] + r.delta[own_cols, :]
    r.grad_one[...] = grad_one

    def along(values):
        return jnp.sum(values.astype(F32), 1, keepdims=True)

    grad_normed = r.grad_normed[own_cols, :].astype(F32)
    columns = [
        along(r.back[own_cols, middle]),
        along(r.mixed[own_cols, :]),
        along(grad_one * r.mixed_unit[own_cols, :]),
        along(grad_one),
        along(grad_normed * r.one_unit[own_cols, :]),
        along(grad_normed),
        r.attend_sums[:, 0:2],
        r.mlp_sums[...],
    ]
    at = 0
    for column in columns:
        r.vectors[pl.ds(me, 1), :, at : at + column.shape[1]] = column[None]
        at += column.shape[1]

    def vector_copy(p, slot):
        return push(
            r.vectors.at[slot], r.vectors.at[slot], r.vector_send.at[p], r.vector_recv.at[slot],
            pts=p,
        )

    for p in others(me, pts):
        vector_copy(p, me).start()

    @pl.when(me > 0)
    def _():
        up_copy(me - 1).wait_recv()

    @pl.when(me < pts - 1)
    def _():
        down_copy(me + 1).wait_recv()

    def turn(tap, carry):
        weight = r.blocks[:, pl.ds(taps + 1 - tap, 1)].reshape(C, cols)
        turned = dot(weight, r.back[...], TN).astype(BF)
        for tile in range(rows // TILE):
            hot = one_hot_window(r.ids, tap, tile)
            r.turn_acc[:, tile * TILE : (tile + 1) * TILE] += dot(
                turned[:, tile * TILE : tile * TILE + WINDOW], hot
            )
        return carry

    r.turn_acc[...] = jnp.zeros_like(r.turn_acc)
    left = list(range(groups - lag, groups))
    cuts = [taps * i // (len(left) + 1) for i in range(len(left) + 2)]
    for i, group in enumerate(left):
        lax.fori_loop(cuts[i], cuts[i + 1], turn, 0)
        start_far(group)
    lax.fori_loop(cuts[-2], cuts[-1], turn, 0)
    r.point_grad[...] = (r.turn_acc[...] + r.grad_one[...]).T
    for group in range(groups):
        finish(group)
    total = r.vectors[pl.ds(me, 1)][0]
    for p in others(me, pts):
        vector_copy(p, p).wait_recv()
        total = total + r.vectors[pl.ds(p, 1)][0]
    r.vector_grad[...] = total.T
    for group in range(groups):
        for v in others(y, width):
            side_copy(group, v, y).wait_send()
        for v in others(z, depth):
            far_copy(group, v, z).wait_send()
    for p in others(me, pts):
        vector_copy(p, me).wait_send()

    @pl.when(me < pts - 1)
    def _():
        up_copy(me + 1).wait_send()

    @pl.when(me > 0)
    def _():
        down_copy(me - 1).wait_send()


def back_pass(plan, first, ids, grad_normed, branch_full, grad_two, mlp_grads, attend_grads, mlp_sums, attend_sums):
    taps, cols, rows = first["taken"].shape
    total = len(BACK_ORDER)
    groups = total // PACK
    share = C // plan.pts
    width, depth = plan.width, plan.depth
    vmem = pltpu.VMEM
    names = (
        "taken", "blocks", "pair", "vec", "hidden", "mixed_unit", "mixed_std", "one_unit", "one_std"
    )
    return call(
        functools.partial(back_kernel, plan),
        "back_pass",
        1,
        dict(
            **{key: first[key] for key in names}, ids=ids, grad_normed=grad_normed,
            branch_full=branch_full, grad_two=grad_two, mlp_grads=mlp_grads,
            attend_grads=attend_grads, mlp_sums=mlp_sums, attend_sums=attend_sums,
        ),
        dict(
            summed=((total, share, cols), BF),
            point_grad=((rows, cols), F32),
            vector_grad=((12 + FF // C, cols), F32),
        ),
        dict(
            own=vmem((width, groups, depth, PACK, share, cols), BF),
            side=vmem((groups, width, depth, PACK, share, cols), BF),
            acc=vmem((groups, depth, PACK, share, cols), BF),
            far=vmem((groups, depth, PACK, share, cols), BF),
            turn_acc=vmem((cols, rows), F32),
            grad_one=vmem((cols, rows), F32),
            delta=vmem((C, rows), F32),
            mixed=vmem((C, rows), BF),
            back=vmem((C, rows + 2 * HALO), BF),
            vectors=vmem((plan.pts, cols, 12 + FF // C), F32),
            side_send=dma(groups, width),
            side_recv=dma(groups, width),
            far_send=dma(groups, depth),
            far_recv=dma(groups, depth),
            halo_send=dma(2),
            halo_recv=dma(2),
            vector_send=dma(plan.pts),
            vector_recv=dma(plan.pts),
        ),
        taps * rows * (WINDOW * 4 + 5 * C) * cols,
    )


def adam(first, second, grad):
    new_first = BETA_ONE * first + (1.0 - BETA_ONE) * grad
    new_second = BETA_TWO * second + (1.0 - BETA_TWO) * grad * grad
    direction = (
        new_first
        / (1.0 - BETA_ONE**STEP)
        / (jnp.sqrt(new_second / (1.0 - BETA_TWO**STEP)) + ADAM_EPS)
    )
    return new_first, new_second, direction


def owner_kernel(
    plan, grad_ref, left_ref, right_ref, first_ref, second_ref, rows_ref, result_ref,
    whole, results, whole_send, whole_recv, whole_here,
    rows_send, rows_recv, rows_here, back_send, back_recv, back_here,
):
    pts, mdl, each = plan.pts, plan.mdl, plan.each
    slots = plan.slots
    share, cols = grad_ref.shape[1:]
    me, plane = lax.axis_index("pts"), lax.axis_index("mdl")
    is_active = (me >= plan.first) & (me < plan.first + plan.active)
    greet(
        [
            {"pts": p, "mdl": m}
            for i, p in enumerate([me] + others(me, pts))
            for j, m in enumerate([plane] + others(plane, mdl))
            if i + j > 0
        ]
    )

    def to_whole(act):
        for step in range(mdl):
            m = lax.rem(plane + step, mdl)
            for i in range(plan.active):
                target = plan.first + i
                piece = grad_ref.at[pl.ds(m * slots + i * each, each)]
                if step == 0:

                    @pl.when(me == target)
                    def _():
                        copy = pltpu.make_async_copy(piece, whole.at[me, plane], whole_here)
                        copy.start() if act == "start" else copy.wait()

                    remote = me != target
                else:
                    remote = me >= 0

                @pl.when(remote)
                def _():
                    copy = push(
                        piece, whole.at[me, plane], whole_send.at[step, i],
                        whole_recv.at[me, plane], pts=target, mdl=m,
                    )
                    copy.start() if act == "start" else copy.wait_send()

    def to_rows(act):
        for m in others(plane, mdl):
            copy = push(
                grad_ref.at[pl.ds(m * slots, slots)], rows_ref.at[plane], rows_send.at[m],
                rows_recv.at[plane], mdl=m,
            )
            if act == "start":
                copy.start()
            else:
                copy.wait_send()
                push(
                    grad_ref.at[pl.ds(m * slots, slots)], rows_ref.at[m], rows_send.at[m],
                    rows_recv.at[m], mdl=m,
                ).wait_recv()
        copy = pltpu.make_async_copy(
            grad_ref.at[pl.ds(plane * slots, slots)], rows_ref.at[plane], rows_here
        )
        copy.start() if act == "start" else copy.wait()

    to_whole("start")
    to_rows("start")

    base = (me - plan.first) * each

    def result_copy(k, p):
        return push(
            results.at[k, :, p], result_ref.at[base + k], back_send.at[k, p],
            back_recv.at[base + k], pts=p,
        )

    def result_here(k):
        return pltpu.make_async_copy(
            results.at[k, :, me], result_ref.at[base + k], back_here.at[k]
        )

    @pl.when(is_active)
    def _():
        pltpu.make_async_copy(
            grad_ref.at[pl.ds(plane * slots + base, each)], whole.at[me, plane], whole_here
        ).wait()
        for p_step in range(pts):
            for m_step in range(mdl):
                if p_step + m_step > 0:
                    p, m = lax.rem(me + p_step, pts), lax.rem(plane + m_step, mdl)
                    push(
                        grad_ref.at[pl.ds(0, each)], whole.at[p, m], whole_send.at[0, 0],
                        whole_recv.at[p, m], pts=p, mdl=m,
                    ).wait_recv()
        for k in range(each):
            left = left_ref[k].reshape(C, C)
            right = right_ref[k].reshape(C, C)
            turned = jnp.zeros((C, C), F32)
            for m in range(mdl):
                columns = whole[:, m, k].reshape(C, cols)
                half = dot(left, columns, TN).astype(BF)
                turned = turned + dot(half, right[m * cols : (m + 1) * cols])
            rotated = turned.astype(BF)
            _, _, direction = adam(
                first_ref[k].reshape(C, C).astype(F32),
                second_ref[k].reshape(C, C).astype(F32),
                rotated.astype(F32),
            )
            update = dot(left, dot(direction.astype(BF), right, NT).astype(BF))
            results[k, 0] = rotated.reshape(pts, share, C)
            results[k, 1] = update.astype(BF).reshape(pts, share, C)
            for p in others(me, pts):
                result_copy(k, p).start()
            result_here(k).start()

    to_rows("wait")
    for i in range(plan.active):
        source = plan.first + i
        for k in range(each):

            @pl.when(me != source)
            def _():
                push(
                    results.at[k, :, me], result_ref.at[i * each + k], back_send.at[k, source],
                    back_recv.at[i * each + k], pts=source,
                ).wait_recv()

    @pl.when(is_active)
    def _():
        for k in range(each):
            result_here(k).wait()
            for p in others(me, pts):
                result_copy(k, p).wait_send()

    for step in range(mdl):
        m = lax.rem(plane + step, mdl)
        for i in range(plan.active):
            target = plan.first + i

            @pl.when((me != target) if step == 0 else (me >= 0))
            def _():
                push(
                    grad_ref.at[pl.ds(m * slots + i * each, each)], whole.at[me, plane],
                    whole_send.at[step, i], whole_recv.at[me, plane], pts=target, mdl=m,
                ).wait_send()


def owner_update(plan, grads, left, right, first, second):
    share, cols = grads.shape[1:]
    pts, mdl, each = plan.pts, plan.mdl, plan.each
    dma = pltpu.SemaphoreType.DMA
    vmem = pl.BlockSpec(memory_space=pltpu.VMEM)
    return pl.pallas_call(
        functools.partial(owner_kernel, plan),
        in_specs=[vmem] * 5,
        out_specs=[vmem] * 2,
        out_shape=[
            jax.ShapeDtypeStruct((mdl, plan.slots, share, cols), BF),
            jax.ShapeDtypeStruct((plan.slots, 2, share, C), BF),
        ],
        scratch_shapes=[
            pltpu.VMEM((pts, mdl, each, share, cols), BF),
            pltpu.VMEM((each, 2, pts, share, C), BF),
            dma((mdl, plan.active)),
            dma((pts, mdl)),
            dma(()),
            dma((mdl,)),
            dma((mdl,)),
            dma(()),
            dma((each, pts)),
            dma((plan.slots,)),
            dma((each,)),
        ],
        compiler_params=params(collective_id=4, has_side_effects=True),
        cost_estimate=pl.CostEstimate(
            flops=8 * each * C * C * C, bytes_accessed=10000000, transcendentals=each * C * C
        ),
        name="owner_update",
    )(grads, left, right, first, second)


def scan_index(row_ids, scan_lengths):
    bounds = jnp.cumsum(scan_lengths)
    return jnp.sum((row_ids[..., None] >= bounds[:-1]).astype(jnp.int32), -1)


def count(mask):
    return jnp.sum(mask.astype(jnp.int32), 1)


def local(
    points,
    cotangent,
    neighbours,
    scan_lengths,
    to_patch,
    from_patch,
    owner_slot,
    weights,
    row_eigen_basis,
    right_basis,
    first_moment,
    second_moment,
    vectors,
    vector_first,
    vector_second,
):
    rows, cols = points.shape
    slot_count = from_patch.shape[0]
    pts = lax.axis_size("pts")
    mdl = lax.axis_size("mdl")
    pts_index = lax.axis_index("pts")
    mdl_index = lax.axis_index("mdl")
    patch_count = slot_count // PATCH
    capacity = 2 * rows // pts
    matrix_rate = 1.6 * C ** (-0.5)
    plan = Layout(pts, mdl, owner_slot.shape[0])

    row_ids = pts_index * rows + jnp.arange(rows, dtype=jnp.int32)
    own_scan = scan_index(row_ids, scan_lengths)
    near = neighbours.T
    usable = (near >= 0) & (scan_index(jnp.maximum(near, 0), scan_lengths) == own_scan[None, :])
    ids = jnp.where(usable, near - (pts_index * rows - HALO), -1)

    target = to_patch // slot_count
    place = jnp.arange(rows, dtype=jnp.int32)
    rank = count((target[None, :] == target[:, None]) & (place[None, :] < place[:, None]))
    send_pos = target * capacity + rank
    held = jnp.zeros((rows + PATCH,), jnp.int32)
    held_patch = jnp.zeros((rows + PATCH,), jnp.int32)
    offset = jnp.int32(0)
    for patch in range(patch_count):
        part = from_patch[patch * PATCH : (patch + 1) * PATCH]
        held = lax.dynamic_update_slice(held, part, (offset,))
        held_patch = lax.dynamic_update_slice(
            held_patch, jnp.full((PATCH,), patch, jnp.int32), (offset,)
        )
        offset = offset + jnp.sum((part >= 0).astype(jnp.int32))
    held = held[:rows]
    held_patch = held_patch[:rows]
    source = held // rows
    arrival = source * capacity + count(
        (source[None, :] == source[:, None]) & (held[None, :] < held[:, None])
    )
    order_key = held_patch * (pts * rows) + held
    order = count(order_key[None, :] < order_key[:, None])
    scan_count = scan_lengths.shape[0]
    held_group = held_patch * scan_count + scan_index(held, scan_lengths)
    sorting = order[None, :] == place[:, None]
    arrival = jnp.sum(jnp.where(sorting, arrival[None, :], 0), 1)
    group = jnp.sum(jnp.where(sorting, held_group[None, :], 0), 1)
    group_ids = jnp.arange(cols, dtype=jnp.int32)
    same = group[:, None] == group_ids[None, :]
    group_q = same.astype(BF)
    group_k = jnp.where(same | (group_ids[None, :] >= patch_count * scan_count), 0.0, -1e30).astype(BF)

    owned = weights.astype(BF).reshape(plan.slots, C // pts, mdl, cols).transpose(2, 0, 1, 3)
    cot = cotangent.T
    send_pos, arrival = send_pos[None], arrival[None]
    first = front(
        plan, owner_slot[jnp.array(ORDER)], owned, points.T, cot, vectors, ids, send_pos, arrival
    )
    rest = first["rest"]
    kept = attend(
        plan,
        first["slot_in"],
        rest,
        vectors,
        group_q,
        group_k,
        send_pos,
        arrival,
        row_eigen_basis.astype(BF),
        right_basis.astype(BF),
    )
    middle = mlp(plan, kept["attended_rows"], first, rest, cot, send_pos, arrival)
    back = attend_back(
        plan,
        kept,
        middle["grad_slot"],
        first["slot_in"],
        rest,
        first["pair"],
        send_pos,
        arrival,
        first_moment.astype(BF),
        second_moment.astype(BF),
    )
    last = back_pass(
        plan,
        first,
        ids,
        back["grad_normed"],
        middle["branch_full"],
        middle["grad_two"],
        middle["weight_grads"],
        back["weight_grads"],
        middle["sums"],
        back["sums"],
    )
    vector_grad = last["vector_grad"]
    places = jnp.array([BACK_ORDER.index(b) for b in range(len(BACK_ORDER))], jnp.int32)
    place_of_slot = jnp.zeros_like(owner_slot).at[owner_slot].set(places)
    grad_rows, results = owner_update(
        plan,
        last["summed"][place_of_slot],
        kept["left_whole"],
        kept["right_whole"],
        back["first_whole"],
        back["second_whole"],
    )
    reduced = grad_rows.transpose(1, 2, 0, 3).reshape(plan.slots, C // pts, C)
    rotated, update = results[:, 0].astype(F32), results[:, 1].astype(F32)
    new_first, new_second, _ = adam(first_moment, second_moment, rotated)
    new_weights = weights - matrix_rate * (update + MATRIX_DECAY * weights)
    new_vector_first, new_vector_second, vector_step = adam(
        vector_first, vector_second, vector_grad
    )
    new_vectors = vectors - VECTOR_RATE * vector_step
    return (
        middle["out"],
        last["point_grad"],
        reduced.astype(F32),
        new_first,
        new_second,
        new_weights,
        new_weights.astype(BF),
        vector_grad,
        new_vector_first,
        new_vector_second,
        new_vectors,
    )


def solution(mesh):
    by_rows = P("pts", "mdl")
    owned = P("mdl", "pts", None)
    vector = P(None, "mdl")
    return jax.shard_map(
        local,
        mesh=mesh,
        in_specs=(
            by_rows,
            by_rows,
            P("pts", None),
            P(),
            P("pts"),
            P("pts"),
            P(),
            owned,
            owned,
            owned,
            owned,
            owned,
            vector,
            vector,
            vector,
        ),
        out_specs=(
            by_rows,
            by_rows,
            owned,
            owned,
            owned,
            owned,
            owned,
            vector,
            vector,
            vector,
            vector,
        ),
        check_vma=False,
    )
```

```python
import functools
import types

import jax
import jax.numpy as jnp
from jax import lax
from jax.experimental import pallas as pl
from jax.experimental.pallas import tpu as pltpu
from jax.sharding import PartitionSpec as P

C = 512
HD = 16
FF = 2048
TAPS = 27
HALO = 256
PATCH = 1024
STEP = 5

NORM_EPS = 1e-05
BETA_ONE = 0.9
BETA_TWO = 0.999
ADAM_EPS = 1e-08
VECTOR_RATE = 0.5
MATRIX_DECAY = 0.05
TILE = 256
WINDOW = TILE + 2 * HALO
BF = jnp.bfloat16
F32 = jnp.float32
VMEM_LIMIT = 56 * 1024 * 1024

NN = (((1,), (0,)), ((), ()))
NT = (((1,), (1,)), ((), ()))
TN = (((0,), (0,)), ((), ()))


def dot(a, b, dims=NN):
    return lax.dot_general(a, b, dims, preferred_element_type=F32)


def params(**kw):
    return pltpu.CompilerParams(vmem_limit_bytes=VMEM_LIMIT, **kw)


MESH = pl.DeviceIdType.MESH
PTS, MDL = "pts", "mdl"
START, WAIT = range(2)


def push(src, dst, send_sem, recv_sem, **target):
    return pltpu.make_async_remote_copy(
        src_ref=src,
        dst_ref=dst,
        send_sem=send_sem,
        recv_sem=recv_sem,
        device_id=target,
        device_id_type=MESH,
    )


def greet(peers):
    barrier = pltpu.get_barrier_semaphore()
    for peer in peers:
        pl.semaphore_signal(barrier, inc=1, device_id=peer, device_id_type=MESH)
    pl.semaphore_wait(barrier, len(peers))


def others(index, size):
    return [lax.rem(index + step, size) for step in range(1, size)]


class Layout:
    def __init__(self, pts, mdl, blocks, groups):
        self.pts, self.mdl, self.groups = pts, mdl, groups
        self.slots = blocks // mdl
        self.each = -(-self.slots // pts)
        self.shift = max(pts - self.slots, 0) // 2 if self.slots < pts else (pts - self.slots % pts) // 2
        self.width = mdl // 2 if pts % (mdl // 2) == 0 else 1
        self.depth = pts // self.width

    def worker(self, j):
        return (j + self.shift) % self.pts

    def work(self, me, k):
        return lax.rem(me + self.pts - self.shift, self.pts) + k * self.pts


def fetch_copies(plan, src, dst, sems, act):
    send, recv, here = sems
    me = lax.axis_index(PTS)
    for j in range(plan.slots):
        target, k = plan.worker(j), j // plan.pts

        @pl.when(me != target)
        def _():
            copy = push(src.at[j], dst.at[k, me], send.at[j], recv.at[k, me], pts=target)
            copy.start() if act == START else copy.wait_send()

        @pl.when(me == target)
        def _():
            copy = pltpu.make_async_copy(src.at[j], dst.at[k, me], here.at[k])
            if act == START:
                copy.start()
            else:
                copy.wait()
                for source in others(me, plan.pts):
                    push(
                        src.at[j], dst.at[k, source], send.at[j], recv.at[k, source], pts=source
                    ).wait_recv()


def fetch_sems(plan):
    return [dma(plan.slots), dma(plan.each, plan.pts), dma(plan.each)]


def fetch_shape(plan, src):
    return jax.ShapeDtypeStruct((plan.each, plan.pts) + src.shape[1:], BF)


class Late:
    def __init__(self, *what):
        self.what = what


def call(kernel, name, collective, inputs, outputs, scratch, flops, smem=(), free=()):
    vmem = pltpu.VMEM
    leaves, tree = jax.tree.flatten(scratch, is_leaf=lambda x: not isinstance(x, (dict, list)))
    late_in = [key for key, value in inputs.items() if isinstance(value, Late)]
    late_out = [key for key, value in outputs.items() if isinstance(value, Late)]
    values = {key: v.what[0] if key in late_in else v for key, v in inputs.items()}
    shapes = {key: v.what if key in late_out else v for key, v in outputs.items()}
    near = [vmem(values[key].shape, values[key].dtype) for key in late_in]
    near += [vmem(*shapes[key]) for key in late_out]
    late = late_in + late_out

    def space(key, value):
        return pltpu.SMEM if key in smem else pl.ANY if key in free or key in late else vmem

    def grouped(x):
        if isinstance(x, dict):
            return types.SimpleNamespace(**{key: grouped(value) for key, value in x.items()})
        return [grouped(value) for value in x] if isinstance(x, list) else x

    def body(*refs):
        count = len(inputs) + len(outputs)
        given = dict(zip(inputs, refs))
        given.update(zip(outputs, refs[len(inputs) : count]))
        own, sems = refs[count : count + len(late)], refs[count + len(late) : count + 2 * len(late)]
        r = grouped(jax.tree.unflatten(tree, refs[count + 2 * len(late) :]))
        for key, ref in given.items():
            setattr(r, key, ref)
        for key, ref, sem in zip(late, own, sems):
            pair = (given[key], ref) if key in late_in else (ref, given[key])
            setattr(r, key, ref)
            setattr(r, key + "_move", functools.partial(pltpu.make_async_copy, *pair, sem))
        kernel(r)

    results = pl.pallas_call(
        body,
        in_specs=[pl.BlockSpec(memory_space=space(*item)) for item in inputs.items()],
        out_specs=[pl.BlockSpec(memory_space=space(*item)) for item in outputs.items()],
        out_shape=[jax.ShapeDtypeStruct(*shape) for shape in shapes.values()],
        scratch_shapes=near + [dma() for _ in late] + leaves,
        compiler_params=params(collective_id=collective, has_side_effects=True),
        cost_estimate=pl.CostEstimate(
            flops=flops, bytes_accessed=20000000, transcendentals=1000000
        ),
        name=name,
    )(*values.values())
    return types.SimpleNamespace(**dict(zip(outputs, results)))


def moves(act, *copies):
    for make in copies:
        copy = make()
        copy.start() if act == START else copy.wait()


def dma(*shape):
    return pltpu.SemaphoreType.DMA(shape)


class Gather:
    def __init__(self, plan, part, sems):
        self.part, self.sems = part, sems
        self.plane = lax.axis_index(MDL)
        self.size = plan.mdl // 2
        self.x, self.core = self.plane // 2, lax.rem(self.plane, 2)

    @staticmethod
    def semaphores(plan):
        return dict(x_send=dma(plan.mdl // 2), recv=dma(plan.mdl), core_send=dma(plan.mdl // 2))

    def along(self, m, target, send):
        return push(self.part(m), self.part(m), send, self.sems.recv.at[m], mdl=target)

    def x_copy(self, x):
        return self.along(self.plane, x * 2 + self.core, self.sems.x_send.at[x])

    def core_copy(self, x):
        return self.along(
            x * 2 + self.core, self.x * 2 + 1 - self.core, self.sems.core_send.at[x]
        )

    def arrived(self, m):
        self.along(m, m, self.sems.x_send.at[0]).wait_recv()

    def start(self):
        for x in others(self.x, self.size):
            self.x_copy(x).start()
        self.core_copy(self.x).start()

    def forward(self):
        for x in others(self.x, self.size):
            self.arrived(x * 2 + self.core)
            self.core_copy(x).start()

    def finish(self):
        for x in [self.x] + others(self.x, self.size):
            self.arrived(x * 2 + 1 - self.core)
        for x in others(self.x, self.size):
            self.x_copy(x).wait_send()
            self.core_copy(x).wait_send()
        self.core_copy(self.x).wait_send()

    def run(self):
        self.start()
        self.forward()
        self.finish()


class Sum:
    def __init__(self, plan, parts, bufs):
        self.parts, self.bufs = parts, bufs
        self.plane = lax.axis_index(MDL)
        self.size = plan.mdl // 2
        self.x, self.core = self.plane // 2, lax.rem(self.plane, 2)

    @staticmethod
    def buffers(plan, shape):
        x = plan.mdl // 2
        vmem = pltpu.VMEM((x,) + shape, BF)
        return dict(
            near=vmem, middle=vmem, far=vmem,
            near_send=dma(x), near_recv=dma(x), far_send=dma(x), far_recv=dma(x),
        )

    def near_copy(self, x):
        b = self.bufs
        return push(
            self.parts.at[x * 2 + 1 - self.core], b.near.at[x], b.near_send.at[x],
            b.near_recv.at[x], mdl=self.x * 2 + 1 - self.core,
        )

    def far_copy(self, x, slot):
        b = self.bufs
        return push(
            b.middle.at[x], b.far.at[slot], b.far_send.at[x], b.far_recv.at[slot],
            mdl=x * 2 + self.core,
        )

    def both(self, x):
        self.near_copy(x).wait_recv()
        own = self.parts[pl.ds(x * 2 + self.core, 1)][0].astype(F32)
        return own + self.bufs.near[pl.ds(x, 1)][0].astype(F32)

    def start(self):
        for x in others(self.x, self.size) + [self.x]:
            self.near_copy(x).start()

    def middle(self):
        for x in others(self.x, self.size):
            self.bufs.middle[pl.ds(x, 1)] = self.both(x).astype(BF)[None]
            self.far_copy(x, self.x).start()

    def finish(self):
        total = self.both(self.x)
        for x in others(self.x, self.size):
            self.far_copy(x, x).wait_recv()
            total = total + self.bufs.far[pl.ds(x, 1)][0].astype(F32)
        for x in others(self.x, self.size):
            self.near_copy(x).wait_send()
            self.far_copy(x, self.x).wait_send()
        self.near_copy(self.x).wait_send()
        return total

    def run(self):
        self.start()
        self.middle()
        return self.finish()


class Trade:
    def __init__(self, plan, out_index, in_index, bufs):
        self.out_index, self.in_index, self.bufs = out_index, in_index, bufs
        self.size = plan.pts
        self.me = lax.axis_index(PTS)

    @staticmethod
    def buffers(plan, cols, rows):
        capacity = 2 * rows // plan.pts
        vmem = pltpu.VMEM((plan.pts, cols, capacity), BF)
        return dict(leave=vmem, land=vmem, send=dma(plan.pts), recv=dma(plan.pts))

    def hot(self, index, part):
        capacity = self.bufs.leave.shape[2]
        row = index[...]
        places = lax.broadcasted_iota(jnp.int32, (capacity, row.shape[1]), 0) + part * capacity
        return jnp.where(places == row, 1.0, 0.0).astype(BF)

    def copy(self, part, slot):
        b = self.bufs
        return push(
            b.leave.at[part], b.land.at[slot], b.send.at[part], b.recv.at[slot],
            pts=part,
        )

    def start(self, values):
        b = self.bufs
        for part in others(self.me, self.size):
            b.leave[pl.ds(part, 1)] = dot(values, self.hot(self.out_index, part), NT).astype(BF)[None]
            self.copy(part, self.me).start()
        b.land[pl.ds(self.me, 1)] = dot(values, self.hot(self.out_index, self.me), NT).astype(BF)[None]

    def finish(self):
        b = self.bufs
        total = dot(b.land[pl.ds(self.me, 1)][0], self.hot(self.in_index, self.me))
        for step in range(1, self.size):
            part = lax.rem(self.me + self.size - step, self.size)
            hot = self.hot(self.in_index, part)
            self.copy(part, part).wait_recv()
            total = total + dot(b.land[pl.ds(part, 1)][0], hot)
        for part in others(self.me, self.size):
            self.copy(part, self.me).wait_send()
        return total.astype(BF)

    def run(self, values):
        self.start(values)
        return self.finish()


class Reduce:
    def __init__(self, plan, bufs):
        self.bufs = bufs
        self.width, self.depth = plan.width, plan.depth
        self.me = lax.axis_index(PTS)
        self.y, self.z = lax.rem(self.me, self.width), self.me // self.width
        self.groups, _, self.pack, self.share, self.cols = bufs.acc.shape
        self.steps = self.groups + self.depth - 1

    @staticmethod
    def buffers(plan, blocks, pack, cols):
        groups, share, vmem = blocks // pack, C // plan.pts, pltpu.VMEM
        line = (plan.depth, pack, share, cols)
        way = dict(
            land=vmem((groups,) + line, BF),
            send=dma(groups, plan.depth),
            recv=dma(groups, plan.depth),
        )
        return dict(
            own=vmem((plan.width, groups) + line, BF),
            side=vmem((plan.width, groups) + line, BF),
            acc=vmem((groups,) + line, BF),
            up=way,
            down=way,
            side_send=dma(plan.width, groups),
            side_recv=dma(plan.width, groups),
        )

    def store(self, block, group, place):
        grid = block.astype(BF).reshape(self.depth, self.width, self.share, self.cols)
        for v in range(self.width):
            self.bufs.own[v, group, :, pl.ds(place, 1)] = grid[:, v][:, None]

    def side_copy(self, group, v, slot):
        b = self.bufs
        return push(
            b.own.at[v, group], b.side.at[slot, group], b.side_send.at[v, group],
            b.side_recv.at[slot, group], pts=self.z * self.width + v,
        )

    def line_copy(self, way, group, to, step):
        b = self.bufs
        near = jnp.clip(self.z + step, 0, self.depth - 1)
        return push(
            b.acc.at[group, to], way.land.at[group, to], way.send.at[group, to],
            way.recv.at[group, to], pts=near * self.width + self.y,
        )

    def start(self, group):
        for v in others(self.y, self.width):
            self.side_copy(group, v, self.y).start()

    def sum_side(self, group):
        b = self.bufs
        total = b.own[pl.ds(self.y, 1), pl.ds(group, 1)][0].astype(F32)
        for v in others(self.y, self.width):
            self.side_copy(group, v, v).wait_recv()
            total = total + b.side[pl.ds(v, 1), pl.ds(group, 1)][0].astype(F32)
        b.acc[pl.ds(group, 1)] = total.astype(BF)

    def relay(self, way, group, step, first):
        b = self.bufs

        @pl.when((group >= 0) & (group < self.groups))
        def _():
            for to in range(self.depth):

                @pl.when((to - self.z) * step > 0)
                def _():
                    @pl.when(jnp.logical_not(first))
                    def _():
                        self.line_copy(way, group, to, -step).wait_recv()
                        spot = (pl.ds(group, 1), to)
                        b.acc[spot] = (
                            b.acc[spot].astype(F32) + way.land[spot].astype(F32)
                        ).astype(BF)

                    self.line_copy(way, group, to, step).start()

    def step(self, s):
        if isinstance(s, int):
            if s < self.groups:
                self.sum_side(s)
        else:

            @pl.when((s >= 0) & (s < self.groups))
            def _():
                self.sum_side(s)

        self.relay(self.bufs.up, s - self.z, 1, self.z == 0)
        self.relay(self.bufs.down, s - (self.depth - 1 - self.z), -1, self.z == self.depth - 1)

    def finish(self, out):
        b, z = self.bufs, self.z

        def total(way, group):
            b.acc[group, pl.ds(z, 1)] = (
                b.acc[group, pl.ds(z, 1)].astype(F32) + way.land[group, pl.ds(z, 1)].astype(F32)
            ).astype(BF)

        for group in range(self.groups):

            @pl.when(z > 0)
            def _():
                self.line_copy(self.bufs.up, group, z, -1).wait_recv()
                total(b.up, group)

            @pl.when(z < self.depth - 1)
            def _():
                self.line_copy(self.bufs.down, group, z, 1).wait_recv()
                total(b.down, group)

            out[group * self.pack : (group + 1) * self.pack] = b.acc[group, pl.ds(z, 1)][0]

    def end(self):
        for group in range(self.groups):
            for v in others(self.y, self.width):
                self.side_copy(group, v, self.y).wait_send()
            for to in range(self.depth):

                @pl.when(to > self.z)
                def _():
                    self.line_copy(self.bufs.up, group, to, 1).wait_send()

                @pl.when(to < self.z)
                def _():
                    self.line_copy(self.bufs.down, group, to, -1).wait_send()


def everyone(plan):
    me, plane = lax.axis_index(PTS), lax.axis_index(MDL)
    return [{PTS: p} for p in others(me, plan.pts)] + [{MDL: m} for m in others(plane, plan.mdl)]


def unit_columns(values):
    mean = jnp.sum(values, 0, keepdims=True) / C
    centred = values - mean
    inv_std = lax.rsqrt(jnp.sum(centred * centred, 0, keepdims=True) / C + NORM_EPS)
    return centred * inv_std, inv_std


def one_hot_window(ids_ref, tap, tile):
    row = ids_ref[pl.ds(tap, 1), pl.ds(tile * TILE, TILE)]
    places = lax.broadcasted_iota(jnp.int32, (WINDOW, TILE), 0) + tile * TILE
    return jnp.where(places == row, 1.0, 0.0).astype(BF)


PACK = 5
ORDER = [TAPS, TAPS + 4] + list(range(TAPS)) + [TAPS + 1, TAPS + 2, TAPS + 3]
ORDER = ORDER + list(range(TAPS + 5, TAPS + 5 + 2 * FF // C))
PLACE = {block: place for place, block in enumerate(ORDER)}


def column(row):
    wide = jnp.broadcast_to(row.astype(F32), (8, row.shape[1]))
    return wide.T[:, 0:1].astype(jnp.int32)


def steps_passed(values, bounds):
    return sum((values >= bound).astype(jnp.int32) for bound in bounds)


def routes(plan, r, rows):
    capacity = 2 * rows // plan.pts
    slot_count = r.from_patch.shape[1]
    patches = slot_count // PATCH
    scans = r.scan_lengths.shape[0]
    target = steps_passed(r.to_patch[...], [p * slot_count for p in range(1, plan.pts)])
    size = 256
    rank = jnp.zeros((1, rows), jnp.int32)
    target_column = column(target)
    ahead = lax.broadcasted_iota(jnp.int32, (size, rows), 1)
    for low in range(0, rows, size):
        earlier = lax.broadcasted_iota(jnp.int32, (size, rows), 0) + low < ahead
        same = target_column[low : low + size] == target
        rank = rank + jnp.sum((earlier & same).astype(jnp.int32), 0, keepdims=True)
    r.send_pos[...] = target * capacity + rank
    held = r.from_patch[...]
    used = held >= 0
    lanes = lax.broadcasted_iota(jnp.int32, (1, slot_count), 1)
    patch = steps_passed(lanes, [p * PATCH for p in range(1, patches)])
    source = steps_passed(held, [p * rows for p in range(1, plan.pts)])
    bounds, bound = [], 0
    for i in range(scans - 1):
        bound = bound + r.scan_lengths[i]
        bounds.append(bound)
    group = patch * scans + (steps_passed(held, bounds) if bounds else 0)
    top = patches * plan.pts * rows
    order_key = jnp.where(used, patch * (plan.pts * rows) + held, top)
    held_key = jnp.where(used, held, top)
    order_column, held_column = column(order_key), column(held_key)
    first_key = source * rows
    order = jnp.zeros((1, slot_count), jnp.int32)
    rank = jnp.zeros((1, slot_count), jnp.int32)
    for low in range(0, slot_count, size):
        part = slice(low, low + size)
        order = order + jnp.sum(
            (order_column[part] < order_key).astype(jnp.int32), 0, keepdims=True
        )
        among = (held_column[part] < held_key) & (held_column[part] >= first_key)
        rank = rank + jnp.sum(among.astype(jnp.int32), 0, keepdims=True)
    base = plan.pts * capacity
    both = column(group * base + source * capacity + rank)
    order = column(jnp.where(used, order, slot_count))
    places = lax.broadcasted_iota(jnp.int32, (size, rows), 1)
    found = jnp.zeros((1, rows), jnp.int32)
    for low in range(0, slot_count, size):
        part = slice(low, low + size)
        found = found + jnp.sum(
            jnp.where(order[part] == places, both[part], 0), 0, keepdims=True
        )
    group = steps_passed(found, [base * g for g in range(1, patches * scans)])
    r.group[...] = group
    r.arrival[...] = found - group * base


def front_kernel(plan, r):
    pts, mdl, slots = plan.pts, plan.mdl, plan.slots
    width, depth = plan.width, plan.depth
    me, plane = lax.axis_index(PTS), lax.axis_index(MDL)
    y, z = lax.rem(me, width), me // width
    rows, cols = r.points_rows.shape
    share = C // pts
    total = r.blocks.shape[1]
    groups = total // PACK
    conv_groups = -(-(2 + TAPS) // PACK)
    for m in range(mdl):
        r.owned[m] = r.weights[:, :, m * cols : (m + 1) * cols].astype(BF)
    greet(everyone(plan))

    def spread_copy(m, slot):
        return push(
            r.owned.at[m], r.spread.at[pl.ds(slot * slots, slots)], r.spread_send.at[m],
            r.spread_recv.at[slot], mdl=m,
        )

    for m in others(plane, mdl):
        spread_copy(m, plane).start()

    def vec_copy(m, slot):
        return push(
            r.vectors, r.vec_all.at[slot], r.vec_send.at[m], r.vec_recv.at[slot], mdl=m
        )

    for m in others(plane, mdl):
        vec_copy(m, plane).start()

    r.points[...] = r.points_rows[...].astype(F32).T.astype(BF)

    def up_copy():
        return push(
            r.points.at[:, rows - HALO : rows], r.ext.at[:, 0:HALO], r.halo_send.at[0],
            r.halo_recv.at[0], pts=me + 1,
        )

    def down_copy():
        return push(
            r.points.at[:, 0:HALO], r.ext.at[:, HALO + rows : 2 * HALO + rows], r.halo_send.at[1],
            r.halo_recv.at[1], pts=me - 1,
        )

    @pl.when(me < pts - 1)
    def _():
        up_copy().start()

    @pl.when(me == pts - 1)
    def _():
        r.ext[:, HALO + rows :] = jnp.zeros((cols, HALO), BF)

    @pl.when(me > 0)
    def _():
        down_copy().start()

    @pl.when(me == 0)
    def _():
        r.ext[:, :HALO] = jnp.zeros((cols, HALO), BF)

    r.ext[:, HALO : HALO + rows] = r.points[...]
    r.spread[pl.ds(plane * slots, slots)] = r.owned[pl.ds(plane, 1)][0]
    r.vec_all[pl.ds(plane, 1)] = r.vectors[...][None]
    r.points_full[pl.ds(plane * cols, cols), :] = r.points[...]
    for m in others(plane, mdl):
        spread_copy(m, m).wait_recv()
    for place, block in enumerate(ORDER):
        r.blocks[pl.ds(me, 1), place] = r.spread[pl.ds(r.slots[block], 1)]

    def group_of(source, group):
        return r.blocks.at[source, group * PACK : (group + 1) * PACK]

    def far_copy(group, source, step):
        return push(
            group_of(source, group), group_of(source, group),
            r.far_send.at[(step + 1) // 2, group, source // width],
            r.far_recv.at[group, source // width], pts=jnp.clip(z + step, 0, depth - 1) * width + y,
        )

    def side_copy(group, v, source):
        return push(
            group_of(source, group), group_of(source, group),
            r.side_send.at[group, v, source // width], r.side_recv.at[group, source],
            pts=z * width + v,
        )

    def pass_on(group, source, act):
        from_z = source // width

        @pl.when((z < depth - 1) & (from_z <= z))
        def _():
            copy = far_copy(group, source, 1)
            copy.start() if act == START else copy.wait_send()

        @pl.when((z > 0) & (from_z >= z))
        def _():
            copy = far_copy(group, source, -1)
            copy.start() if act == START else copy.wait_send()

        for v in others(y, width):
            copy = side_copy(group, v, source)
            copy.start() if act == START else copy.wait_send()

    def relay(group, away, act):
        for from_z in (z - away, z + away):

            @pl.when((from_z >= 0) & (from_z < depth))
            def _():
                source = from_z * width + y
                if act == START:
                    far_copy(group, source, 1).wait_recv()
                pass_on(group, source, act)

    ahead = 2
    for group in range(ahead):
        pass_on(group, me, START)

    points_gather = Gather(
        plan, lambda m: r.points_full.at[pl.ds(m * cols, cols)],
        r.points_net,
    )
    cot_gather = Gather(
        plan, lambda m: r.cot_full.at[pl.ds(m * cols, cols)],
        r.cot_net,
    )
    points_gather.start()
    r.cot_full[pl.ds(plane * cols, cols), :] = r.cot_rows[...].astype(F32).T.astype(BF)
    cot_gather.start()
    routes(plan, r, rows)

    @pl.when(me > 0)
    def _():
        push(
            r.points.at[:, 0:HALO], r.ext.at[:, 0:HALO], r.halo_send.at[0], r.halo_recv.at[0],
            pts=me - 1,
        ).wait_recv()

    @pl.when(me < pts - 1)
    def _():
        push(
            r.points.at[:, 0:HALO], r.ext.at[:, HALO + rows : 2 * HALO + rows], r.halo_send.at[1],
            r.halo_recv.at[1], pts=me + 1,
        ).wait_recv()

    def take(tap, carry):
        for tile in range(rows // TILE):
            hot = one_hot_window(r.ids, tap, tile)
            picked = dot(r.ext[:, tile * TILE : tile * TILE + WINDOW], hot).astype(BF)
            r.taken[pl.ds(tap, 1), :, tile * TILE : (tile + 1) * TILE] = picked[None]
        return carry

    steps = groups + depth - 2
    cuts = [min(TAPS, -(-TAPS * i // groups)) for i in range(steps + 1)]
    for step in range(steps):
        if step + ahead < groups:
            pass_on(step + ahead, me, START)
        if cuts[step] < cuts[step + 1]:
            lax.fori_loop(cuts[step], cuts[step + 1], take, 0)
        for away in range(1, depth):
            if 0 <= step + 1 - away < groups:
                relay(step + 1 - away, away, START)
    moves(START, r.taken_move)

    def complete(group):
        for u in others(y, width):
            for v in range(depth):
                side_copy(group, u, v * width + u).wait_recv()

    pair_gather = Gather(
        plan, lambda m: r.pair.at[m], r.pair_net
    )
    for group in range(conv_groups):
        complete(group)
        if group == 0:
            for i in range(2):
                r.pair[pl.ds(plane, 1), i] = r.blocks[:, i].reshape(1, C, cols)
            pair_gather.start()
        low = max(group * PACK - 2, 0)
        high = min(group * PACK - 2 + PACK, TAPS)
        if cols % 128 == 0:
            weight = jnp.concatenate(
                [r.blocks[:, t + 2].reshape(C, cols) for t in range(low, high)], 1
            )
            part = dot(weight, r.taken[low:high].reshape((high - low) * cols, rows))
        else:
            part = sum(dot(r.blocks[:, t + 2].reshape(C, cols), r.taken[t]) for t in range(low, high))
        if group == 0:
            r.acc[...] = part
            pair_gather.forward()
        else:
            r.acc[...] += part

    taps_copy = pltpu.make_async_copy(r.blocks.at[:, 2 : 2 + TAPS], r.taps_far, r.taps_sem)
    taps_copy.start()
    points_gather.forward()
    cot_gather.forward()
    r.parts[...] = r.acc[...].astype(BF).reshape(mdl, cols, rows)
    hidden_sum = Sum(plan, r.parts, r.sum_net)
    hidden_sum.start()
    for m in others(plane, mdl):
        vec_copy(m, m).wait_recv()
    for m in range(mdl):
        r.vec[m * cols : (m + 1) * cols, :] = r.vec_all[m].T
    pair_gather.finish()
    points_gather.finish()
    hidden_sum.middle()
    bias = r.vec[pl.ds(plane * cols, cols), 0:1]
    r.hidden[pl.ds(plane * cols, cols), :] = (hidden_sum.finish() + bias).astype(BF)
    Gather(
        plan, lambda m: r.hidden.at[pl.ds(m * cols, cols)],
        r.hidden_net,
    ).run()
    hidden = r.hidden[...]
    for m in range(mdl):
        r.acc[m * cols : (m + 1) * cols, :] = dot(r.pair[m, 0], hidden, TN)
    span_size = 128

    def norms(step, carry):
        span = pl.ds(pl.multiple_of(step * span_size, span_size), span_size)
        unit, inv_std = unit_columns(r.acc[:, span] + r.vec[:, 1:2])
        r.mixed_unit[:, span] = unit.astype(BF)
        r.mixed_std[:, span] = inv_std
        stream = r.points_full[:, span].astype(F32) + unit * r.vec[:, 2:3] + r.vec[:, 3:4]
        r.stream[:, span] = stream
        unit, inv_std = unit_columns(stream)
        r.one_unit[:, span] = unit.astype(BF)
        r.one_std[:, span] = inv_std
        r.normed[:, span] = (unit * r.vec[:, 4:5] + r.vec[:, 5:6]).astype(BF)
        return carry

    lax.fori_loop(0, rows // span_size, norms, 0)
    trade = Trade(
        plan, r.send_pos, r.arrival, r.trade_net
    )
    trade.start(r.normed[pl.ds(plane * cols, cols), :])
    moves(START, r.hidden_move, r.mixed_unit_move, r.one_unit_move, r.stream_move, r.pair_move)
    for group in range(conv_groups, groups):
        complete(group)
    for i in range(r.rest.shape[0]):
        r.rest[i] = r.blocks[:, TAPS + 2 + i].reshape(C, cols)
    cot_gather.finish()
    moves(START, r.rest_move, r.cot_full_move)
    r.slot_in[pl.ds(plane * cols, cols), :] = trade.finish()
    Gather(
        plan, lambda m: r.slot_in.at[pl.ds(m * cols, cols)],
        r.slot_net,
    ).run()
    moves(START, r.slot_in_move)

    @pl.when(me < pts - 1)
    def _():
        up_copy().wait_send()

    @pl.when(me > 0)
    def _():
        down_copy().wait_send()

    for m in others(plane, mdl):
        spread_copy(m, plane).wait_send()
        vec_copy(m, plane).wait_send()
    for group in range(groups):
        pass_on(group, me, WAIT)
        for away in range(1, depth):
            relay(group, away, WAIT)
    moves(WAIT, r.taken_move, r.cot_full_move, r.pair_move, r.hidden_move, r.mixed_unit_move, r.one_unit_move, r.stream_move, r.slot_in_move, r.rest_move)
    taps_copy.wait()


def front(plan, slots, weights, points, cot, vectors, ids, to_patch, from_patch, scan_lengths):
    rows, cols = points.shape
    pts, mdl = plan.pts, plan.mdl
    share = C // pts
    total = len(ORDER)
    groups = total // PACK
    vmem = pltpu.VMEM
    ring = Gather.semaphores(plan)
    scratch = dict(
        points_net=ring,
        cot_net=ring,
        pair_net=ring,
        hidden_net=ring,
        slot_net=ring,
        owned=vmem((mdl, plan.slots, share, cols), BF),
        points=vmem((cols, rows), BF),
        spread=vmem((total, share, cols), BF),
        vec_all=vmem((mdl,) + vectors.shape, F32),
        ext=vmem((cols, rows + 2 * HALO), BF),
        acc=vmem((C, rows), F32),
        parts=vmem((mdl, cols, rows), BF),
        normed=vmem((C, rows), BF),
        points_full=vmem((C, rows), BF),
        spread_send=dma(mdl),
        spread_recv=dma(mdl),
        vec_send=dma(mdl),
        vec_recv=dma(mdl),
        halo_send=dma(2),
        halo_recv=dma(2),
        blocks=vmem((pts, total, share, cols), BF),
        taps_sem=dma(),
        far_send=dma(2, groups, plan.depth),
        far_recv=dma(groups, plan.depth),
        side_send=dma(groups, plan.width, plan.depth),
        side_recv=dma(groups, pts),
        sum_net=(Sum.buffers(plan, (cols, rows))),
        trade_net=(Trade.buffers(plan, cols, rows)),
    )
    return call(
        functools.partial(front_kernel, plan),
        "front",
        5,
        dict(
            slots=slots, weights=weights, points_rows=points, cot_rows=cot, vectors=vectors,
            ids=ids, to_patch=to_patch, from_patch=from_patch, scan_lengths=scan_lengths,
        ),
        dict(
            taps_far=((pts, TAPS, share, cols), BF),
            taken=Late((TAPS, cols, rows), BF),
            cot_full=Late((C, rows), BF),
            pair=Late((mdl, 2, C, cols), BF),
            vec=((C, vectors.shape[0]), F32),
            hidden=Late((C, rows), BF),
            mixed_unit=Late((C, rows), BF),
            mixed_std=((1, rows), F32),
            stream=Late((C, rows), F32),
            one_unit=Late((C, rows), BF),
            one_std=((1, rows), F32),
            send_pos=((1, rows), jnp.int32),
            arrival=((1, rows), jnp.int32),
            group=((1, rows), jnp.int32),
            slot_in=Late((C, rows), BF),
            rest=Late((total - TAPS - 2, C, cols), BF),
        ),
        scratch,
        4 * TAPS * rows * (WINDOW + C) * cols,
        smem=("slots", "scan_lengths"),
        free=("taps_far",),
    )


def fetches(plan, srcs, dsts, refs, act):
    for src, dst, sems in zip(srcs, dsts, refs.fetch_net):
        fetch_copies(plan, src, dst, sems, act)


def head_lanes(ext, cols, head):
    lane = lax.broadcasted_iota(jnp.int32, ext.shape, 1)
    return jnp.where((lane >= cols) | (lane // HD == head), ext, jnp.zeros_like(ext))


def head_rows(head):
    return pl.ds(pl.multiple_of(head * HD, HD), HD)


def attend_kernel(plan, r):
    plane = lax.axis_index(MDL)
    rows, cols = r.values.shape
    heads = cols // HD
    moves(START, r.left32_move, r.right32_move)
    greet(everyone(plan))
    moves(WAIT, r.left32_move, r.right32_move)
    r.left[...] = r.left32[...].astype(BF)
    r.right[...] = r.right32[...].astype(BF)
    fetched = (plan, (r.left, r.right), (r.left_whole, r.right_whole), r)
    fetches(*fetched, START)
    group = column(r.group[...])
    lane = lax.broadcasted_iota(jnp.int32, (rows, cols), 1)
    same = lane == group
    slot_in = r.slot_in[...]
    queries = (dot(slot_in, r.rest[0], TN) + r.vectors[6:7, :]).astype(BF)
    r.q_ext[:, :cols] = queries * BF(HD ** (-0.5))
    r.q_ext[:, cols:] = jnp.where(same, 1.0, 0.0).astype(BF)
    r.k_ext[:, :cols] = dot(slot_in, r.rest[1], TN).astype(BF)
    r.k_ext[:, cols:] = jnp.where(same | (lane >= plan.groups), 0.0, -1e30).astype(BF)
    values = dot(slot_in, r.rest[2], TN) + r.vectors[7:8, :]
    r.values[...] = values.astype(BF)
    r.v_aug[:, :HD] = values.T.astype(BF).reshape(heads, HD, rows)
    r.v_aug[:, HD:] = jnp.ones((heads, HD, rows), BF)
    moves(START, r.q_ext_move, r.k_ext_move, r.values_move)

    def one(head, carry):
        keys = r.k_ext[...]
        values_t = r.v_aug[pl.ds(head, 1)][0]
        for tile in range(rows // TILE):
            span = slice(tile * TILE, (tile + 1) * TILE)
            scores = dot(keys, head_lanes(r.q_ext[span, :], cols, head), NT)
            top = jnp.max(scores, 0, keepdims=True)
            soft = jnp.exp(scores - top).astype(BF)
            summed = dot(values_t, soft)
            total = summed[HD : HD + 1]
            r.attended[head_rows(head), span] = (summed[:HD] / total).astype(BF)
            r.lse[pl.ds(head, 1), :, span] = (top + jnp.log(total))[None]
        return carry

    lax.fori_loop(0, heads, one, 0)
    moves(START, r.attended_move, r.lse_move)
    trade = Trade(
        plan, r.arrival, r.send_pos, r.trade_net
    )
    r.attended_rows[pl.ds(plane * cols, cols), :] = trade.run(r.attended[...])
    Gather(
        plan, lambda m: r.attended_rows.at[pl.ds(m * cols, cols)],
        r.rows_net,
    ).run()
    fetches(*fetched, WAIT)
    moves(WAIT, r.q_ext_move, r.k_ext_move, r.values_move, r.attended_move, r.lse_move)


def attend(plan, slot_in, rest, vectors, group, send_pos, arrival, left, right):
    rows, cols = group.shape[1], vectors.shape[1]
    heads = cols // HD
    fetched = fetch_shape(plan, left)
    vmem = pltpu.VMEM
    return call(
        functools.partial(attend_kernel, plan),
        "attend",
        2,
        dict(
            slot_in=slot_in, rest=rest, vectors=vectors, group=group,
            send_pos=send_pos, arrival=arrival, left32=Late(left), right32=Late(right),
        ),
        dict(
            q_ext=Late((rows, 2 * cols), BF),
            k_ext=Late((rows, 2 * cols), BF),
            values=Late((rows, cols), BF),
            attended=Late((cols, rows), BF),
            lse=Late((heads, 1, rows), F32),
            attended_rows=((C, rows), BF),
            left_whole=(fetched.shape, fetched.dtype),
            right_whole=(fetched.shape, fetched.dtype),
        ),
        dict(
            left=vmem(left.shape, BF),
            right=vmem(right.shape, BF),
            v_aug=vmem((heads, 2 * HD, rows), BF),
            fetch_net=[fetch_sems(plan), fetch_sems(plan)],
            trade_net=(Trade.buffers(plan, cols, rows)),
            rows_net=(Gather.semaphores(plan)),
        ),
        4 * heads * rows * rows * cols,
        free=("left_whole", "right_whole"),
    )


def attend_back_kernel(plan, r):
    plane = lax.axis_index(MDL)
    rows, cols = r.values.shape
    heads = cols // HD
    greet(everyone(plan))
    moves(START, r.second32_move, r.slot_in_move, r.rest_move)
    fetched = (plan, (r.second,), (r.second_whole,), r)
    mlp_count = r.mlp_grads.shape[0]
    reduce = Reduce(
        plan, r.reduce_net
    )
    for group in range(reduce.groups):
        for place in range(MLP_PACK):
            reduce.store(r.mlp_grads[group * MLP_PACK + place], group, place)
        reduce.start(group)
    moves(WAIT, r.second32_move)
    r.second[...] = r.second32[...].astype(BF)
    fetches(*fetched, START)
    grad_slot = r.grad_slot[...]
    grad_t = dot(r.pair[pl.ds(plane, 1), 1][0], grad_slot, TN).astype(BF).astype(F32)
    r.grad[...] = grad_t.T.astype(BF)
    weighed = grad_t * r.attended[...].astype(F32)
    r.inner[...] = jnp.sum(weighed.reshape(heads, HD, rows), 1, keepdims=True)
    r.keys_t[...] = r.k_ext[:, :cols].astype(F32).T.astype(BF)
    r.dk_acc[...] = jnp.zeros_like(r.dk_acc)
    r.dv_acc[...] = jnp.zeros_like(r.dv_acc)

    def one(head, carry):
        queries = head_lanes(r.q_ext[...], cols, head)
        pure = queries[:, :cols]
        grad = head_lanes(r.grad[...], cols, head)
        lse = r.lse[pl.ds(head, 1)][0]
        inner = r.inner[pl.ds(head, 1)][0]
        keys_t = r.keys_t[head_rows(head), :]
        dq = jnp.zeros((HD, rows), F32)
        for tile in range(rows // TILE):
            span = slice(tile * TILE, (tile + 1) * TILE)
            scores = dot(r.k_ext[span, :], queries, NT)
            soft = jnp.exp(scores - lse)
            grad_soft = dot(r.values[span, :], grad, NT)
            grad_scores = (soft * (grad_soft - inner)).astype(BF)
            r.dv_acc[span, :] += dot(soft.astype(BF), grad)
            r.dk_acc[span, :] += dot(grad_scores, pure)
            dq = dq + dot(keys_t[:, span], grad_scores)
        r.dq[head_rows(head), :] = (dq * HD ** (-0.5)).astype(BF)
        reduce.step(head - delay)
        return carry

    delay = max(heads - reduce.steps, 0)
    lax.fori_loop(0, heads, one, 0)
    for s in range(heads - delay, reduce.steps):
        reduce.step(s)
    moves(WAIT, r.slot_in_move, r.rest_move)
    dk = r.dk_acc[...].astype(BF)
    dv = r.dv_acc[...].astype(BF)
    back = dot(r.rest[0], r.dq[...]) + dot(r.rest[1], dk, NT) + dot(r.rest[2], dv, NT)
    r.parts[...] = back.astype(BF).reshape(plan.mdl, cols, rows)
    back_sum = Sum(plan, r.parts, r.sum_net)
    back_sum.start()
    r.weight_grads[0] = dot(r.slot_in[...], r.dq[...], NT).astype(BF)
    r.weight_grads[1] = dot(r.slot_in[...], dk).astype(BF)
    back_sum.middle()
    r.weight_grads[2] = dot(r.slot_in[...], dv).astype(BF)
    r.weight_grads[3] = dot(r.grad_slot[...], r.attended[...], NT).astype(BF)
    trade = Trade(
        plan, r.arrival, r.send_pos, r.trade_net
    )
    trade.start(back_sum.finish().astype(BF))
    moves(START, r.weight_grads_move)
    r.sums[...] = jnp.zeros_like(r.sums)
    r.sums[:, 0:1] = jnp.sum(r.dq[...].astype(F32), 1, keepdims=True)
    r.sums[:, 1:2] = jnp.sum(dv.astype(F32), 0, keepdims=True).T
    r.grad_normed[pl.ds(plane * cols, cols), :] = trade.finish()
    Gather(
        plan, lambda m: r.grad_normed.at[pl.ds(m * cols, cols)],
        r.rows_net,
    ).run()
    reduce.finish(r.mlp_summed)
    reduce.end()
    fetches(*fetched, WAIT)
    moves(WAIT, r.weight_grads_move)


MLP_PACK = 4


def attend_back(
    plan, kept, grad_slot, slot_in, rest, pair, send_pos, arrival, mlp_grads, second
):
    rows, cols = kept.values.shape
    heads = cols // HD
    vmem = pltpu.VMEM
    fetched = fetch_shape(plan, second)
    return call(
        functools.partial(attend_back_kernel, plan),
        "attend_back",
        3,
        dict(
            q_ext=kept.q_ext, k_ext=kept.k_ext, values=kept.values, attended=kept.attended, lse=kept.lse, grad_slot=grad_slot, slot_in=Late(slot_in), rest=Late(rest),
            pair=pair, send_pos=send_pos, arrival=arrival, mlp_grads=mlp_grads, second32=Late(second),
        ),
        dict(
            grad_normed=((C, rows), BF),
            weight_grads=Late((4, C, cols), BF),
            sums=((cols, 8), F32),
            mlp_summed=((mlp_grads.shape[0], C // plan.pts, cols), BF),
            second_whole=(fetched.shape, fetched.dtype),
        ),
        dict(
            second=vmem(second.shape, BF),
            grad=vmem((rows, cols), BF),
            inner=vmem((heads, 1, rows), F32),
            keys_t=vmem((cols, rows), BF),
            dk_acc=vmem((rows, cols), F32),
            dv_acc=vmem((rows, cols), F32),
            dq=vmem((cols, rows), BF),
            parts=vmem((plan.mdl, cols, rows), BF),
            reduce_net=(Reduce.buffers(plan, mlp_grads.shape[0], MLP_PACK, cols)),
            fetch_net=[fetch_sems(plan)],
            sum_net=(Sum.buffers(plan, (cols, rows))),
            trade_net=(Trade.buffers(plan, cols, rows)),
            rows_net=(Gather.semaphores(plan)),
        ),
        10 * heads * rows * rows * cols,
        free=("second_whole",),
    )


SPAN = 128


def over_spans(rows, body, size=SPAN):
    def step(index, carry):
        body(pl.ds(pl.multiple_of(index * size, size), size))
        return carry

    lax.fori_loop(0, rows // size, step, 0)


def beside(blocks):
    def times(right, cols):
        if cols % 128 == 0:
            return dot(jnp.concatenate(blocks, 1), right[...])
        return sum(
            dot(block, right[i * cols : (i + 1) * cols, :]) for i, block in enumerate(blocks)
        )

    return times


def mlp_kernel(plan, r):
    mdl = plan.mdl
    plane = lax.axis_index(MDL)
    cols, rows = r.cot.shape
    ff_blocks = FF // C
    own = pl.ds(plane * cols, cols)
    moves(START, r.first32_move, r.stream_move, r.rest_move, r.cot_full_move)
    r.cot[...] = r.cot_rows[...].astype(F32).T.astype(BF)
    greet(everyone(plan))
    moves(WAIT, r.first32_move)
    r.first[...] = r.first32[...].astype(BF)
    fetched = (plan, (r.first,), (r.first_whole,), r)
    fetches(*fetched, START)
    r.acc[...] = beside([r.pair[m, 1] for m in range(mdl)])(r.attended_rows, cols)
    moves(WAIT, r.stream_move, r.rest_move, r.cot_full_move)

    def norms(span):
        branch = (r.acc[:, span] + r.vec[:, 8:9]).astype(BF).astype(F32)
        two = r.stream[:, span] + branch
        r.two[:, span] = two
        unit, inv_std = unit_columns(two)
        r.two_unit[:, span] = unit
        r.two_std[:, span] = inv_std
        r.normed[:, span] = (unit * r.vec[:, 9:10] + r.vec[:, 10:11]).astype(BF)

    over_spans(rows, norms)
    for k in range(ff_blocks):
        part = slice(k * cols, (k + 1) * cols)
        r.pre[...] = dot(r.rest[3 + k], r.normed[...], TN) + r.vec[own, 11 + k : 12 + k]
        r.grad_act[...] = dot(r.rest[3 + ff_blocks + k], r.cot_full[...], TN)

        def bend(span):
            pre = r.pre[:, span]
            half = 0.5 * (1.0 + lax.erf(pre * 0.7071067811865476))
            r.act[part, span] = (pre * half).astype(BF)
            slope = half + pre * jnp.exp(-0.5 * pre * pre) * 0.3989422804014327
            r.grad_pre[part, span] = (r.grad_act[:, span] * slope).astype(BF)

        over_spans(rows, bend, 256)
    r.acc[...] = beside([r.rest[3 + k] for k in range(ff_blocks)])(r.grad_pre, cols)

    def stats(span):
        scaled = r.acc[:, span] * r.vec[:, 9:10]
        r.stats[pl.ds(plane, 1), 0:1, span] = jnp.sum(scaled, 0, keepdims=True)[None]
        r.stats[pl.ds(plane, 1), 1:2, span] = jnp.sum(scaled * r.two_unit[:, span], 0, keepdims=True)[None]

    over_spans(rows, stats)

    def stats_copy(m, slot):
        return push(
            r.stats.at[slot], r.stats.at[slot], r.stats_send.at[m], r.stats_recv.at[slot], mdl=m
        )

    for m in others(plane, mdl):
        stats_copy(m, plane).start()
    r.parts[...] = r.acc[...].astype(BF).reshape(mdl, cols, rows)
    shape = Sum.buffers(plan, (cols, rows))
    grad_sum = Sum(plan, r.parts, r.grad_net)
    grad_sum.start()
    out = beside([r.rest[3 + ff_blocks + k] for k in range(ff_blocks)])(r.act, cols)
    r.out_parts[...] = out.astype(BF).reshape(mdl, cols, rows)
    grad_sum.middle()
    out_sum = Sum(plan, r.out_parts, r.out_net)
    out_sum.start()
    for m in others(plane, mdl):
        stats_copy(m, m).wait_recv()
    mean = sum(r.stats[m, 0:1] for m in range(mdl)) / C
    cross = sum(r.stats[m, 1:2] for m in range(mdl)) / C
    cot = r.cot[...].astype(F32)
    grad_normed = grad_sum.finish()
    unit = r.two_unit[own, :]
    grad_two = cot + r.two_std[...] * (grad_normed * r.vec[own, 9:10] - mean - unit * cross)
    r.grad_two[...] = grad_two
    branch = grad_two.astype(BF)
    r.branch_full[own, :] = branch
    trade = Trade(
        plan, r.send_pos, r.arrival, r.trade_net
    )
    trade.start(branch)
    branch_gather = Gather(
        plan, lambda m: r.branch_full.at[pl.ds(m * cols, cols)],
        r.branch_net,
    )
    branch_gather.start()
    out_sum.middle()

    def along(values):
        return jnp.sum(values.astype(F32), 1, keepdims=True)

    r.sums[:, 0:1] = along(branch)
    r.sums[:, 1:2] = along(grad_normed * unit)
    r.sums[:, 2:3] = along(grad_normed)
    for k in range(ff_blocks):
        part = slice(k * cols, (k + 1) * cols)
        r.sums[:, 3 + k : 4 + k] = along(r.grad_pre[part, :])
        r.weight_grads[k] = dot(r.normed[...], r.grad_pre[part, :], NT).astype(BF)
        r.weight_grads[ff_blocks + k] = dot(r.cot_full[...], r.act[part, :], NT).astype(BF)
    r.sums[:, 3 + ff_blocks : 4 + ff_blocks] = along(cot)
    r.grad_slot[own, :] = trade.finish()
    slot_gather = Gather(
        plan, lambda m: r.grad_slot.at[pl.ds(m * cols, cols)],
        r.slot_net,
    )
    slot_gather.start()
    moves(START, r.weight_grads_move, r.grad_two_move)
    branch_gather.forward()
    bias = r.vec[own, 11 + ff_blocks : 12 + ff_blocks]
    r.out[...] = (r.two[own, :] + out_sum.finish() + bias).T.astype(BF)
    slot_gather.forward()
    branch_gather.finish()
    moves(START, r.branch_full_move)
    slot_gather.finish()
    fetches(*fetched, WAIT)
    moves(WAIT, r.weight_grads_move, r.grad_two_move, r.branch_full_move)
    for m in others(plane, mdl):
        stats_copy(m, plane).wait_send()


def mlp(plan, attended_rows, first, rest, cot, send_pos, arrival, moment):
    rows, cols = cot.shape
    ff_blocks = FF // C
    vmem = pltpu.VMEM
    scratch = dict(
        cot=vmem((cols, rows), BF),
        first=vmem(moment.shape, BF),
        acc=vmem((C, rows), F32),
        two=vmem((C, rows), F32),
        two_unit=vmem((C, rows), F32),
        two_std=vmem((1, rows), F32),
        normed=vmem((C, rows), BF),
        pre=vmem((cols, rows), F32),
        grad_act=vmem((cols, rows), F32),
        act=vmem((ff_blocks * cols, rows), BF),
        grad_pre=vmem((ff_blocks * cols, rows), BF),
        stats=vmem((plan.mdl, 8, rows), F32),
        stats_send=dma(plan.mdl),
        stats_recv=dma(plan.mdl),
        parts=vmem((plan.mdl, cols, rows), BF),
        out_parts=vmem((plan.mdl, cols, rows), BF),
        grad_net=(Sum.buffers(plan, (cols, rows))),
        out_net=(Sum.buffers(plan, (cols, rows))),
        trade_net=(Trade.buffers(plan, cols, rows)),
        branch_net=(Gather.semaphores(plan)),
        slot_net=(Gather.semaphores(plan)),
        fetch_net=[fetch_sems(plan)],
    )
    return call(
        functools.partial(mlp_kernel, plan),
        "mlp",
        6,
        dict(
            attended_rows=attended_rows, pair=first.pair, stream=Late(first.stream), vec=first.vec, cot_full=Late(first.cot_full), rest=Late(rest), cot_rows=cot,
            send_pos=send_pos, arrival=arrival, first32=Late(moment),
        ),
        dict(
            first_whole=(fetch_shape(plan, moment).shape, BF),
            grad_slot=((C, rows), BF),
            branch_full=Late((C, rows), BF),
            grad_two=Late((cols, rows), F32),
            out=((rows, cols), BF),
            weight_grads=Late((2 * ff_blocks, C, cols), BF),
            sums=((cols, 4 + ff_blocks), F32),
        ),
        scratch,
        16 * rows * C * cols * ff_blocks,
        free=("first_whole",),
    )


BACK_ORDER = [TAPS + 1, TAPS + 2, TAPS + 3, TAPS + 4, TAPS] + list(range(TAPS))
MLP_ORDER = list(range(TAPS + 5, TAPS + 5 + 2 * FF // C))
BACK_PACK = 4


def back_kernel(plan, r):
    pts = plan.pts
    cols, rows = r.turn_acc.shape
    taps = r.taken.shape[0]
    ready = r.attend_grads.shape[0]
    extra = ready + 1
    me, plane = lax.axis_index(PTS), lax.axis_index(MDL)
    own_cols = pl.ds(plane * cols, cols)
    middle = slice(HALO, HALO + rows)
    moves(START, r.grad_normed_move, r.branch_full_move, r.one_unit_move, r.mixed_unit_move, r.pair_move, r.hidden_move, r.taken_move, r.taps_move, r.grad_two_move)
    greet([{PTS: v} for v in others(me, pts)] + [{MDL: plane + 1 - 2 * lax.rem(plane, 2)}])
    reduce = Reduce(
        plan, r.reduce_net
    )
    groups = reduce.groups
    for b in range(ready):
        reduce.store(r.attend_grads[b], b // BACK_PACK, b % BACK_PACK)
    reduce.start(0)
    moves(WAIT, r.grad_normed_move, r.branch_full_move, r.one_unit_move, r.mixed_unit_move, r.pair_move, r.hidden_move, r.taken_move, r.taps_move, r.grad_two_move)

    def grads(group):
        if group == ready // BACK_PACK:
            reduce.store(dot(r.hidden[...], r.mixed[own_cols, :], NT), group, ready % BACK_PACK)

        def one(place, carry):
            tap = group * BACK_PACK + place - extra
            reduce.store(
                dot(r.back[:, middle], r.taken[pl.ds(tap, 1)][0], NT), group, place
            )
            return carry

        low = max(group * BACK_PACK, extra)
        lax.fori_loop(low - group * BACK_PACK, BACK_PACK, one, 0)

    def norms(span):
        grad = r.grad_normed[:, span].astype(F32) * r.vec[:, 4:5]
        unit = r.one_unit[:, span].astype(F32)
        delta = r.one_std[:, span] * (
            grad
            - jnp.sum(grad, 0, keepdims=True) / C
            - unit * (jnp.sum(grad * unit, 0, keepdims=True) / C)
        )
        r.delta[:, span] = delta
        grad = (r.branch_full[:, span].astype(F32) + delta) * r.vec[:, 2:3]
        unit = r.mixed_unit[:, span].astype(F32)
        r.mixed[:, span] = (
            r.mixed_std[:, span]
            * (
                grad
                - jnp.sum(grad, 0, keepdims=True) / C
                - unit * (jnp.sum(grad * unit, 0, keepdims=True) / C)
            )
        ).astype(BF)

    over_spans(rows, norms)
    back = beside([r.pair[m, 0] for m in range(plan.mdl)])(r.mixed, cols)
    r.back[:, middle] = back.astype(BF)

    core = lax.rem(plane, 2)
    mine = pl.ds(core * (C // 2), C // 2)
    low_end, high_end = slice(0, HALO), slice(HALO + rows, 2 * HALO + rows)

    def up_copy(target):
        return push(
            r.back.at[mine, rows : rows + HALO], r.back.at[mine, low_end], r.halo_send.at[0],
            r.halo_recv.at[0], pts=target,
        )

    def down_copy(target):
        return push(
            r.back.at[mine, HALO : 2 * HALO], r.back.at[mine, high_end],
            r.halo_send.at[1], r.halo_recv.at[1], pts=target,
        )

    def core_copy(end, which, part):
        half = pl.ds(part * (C // 2), C // 2)
        return push(
            r.back.at[half, end], r.back.at[half, end], r.core_send.at[which],
            r.core_recv.at[which], mdl=plane + 1 - 2 * core,
        )

    @pl.when(me < pts - 1)
    def _():
        up_copy(me + 1).start()

    @pl.when(me == pts - 1)
    def _():
        r.back[:, HALO + rows :] = jnp.zeros((C, HALO), BF)

    @pl.when(me > 0)
    def _():
        down_copy(me - 1).start()

    @pl.when(me == 0)
    def _():
        r.back[:, :HALO] = jnp.zeros((C, HALO), BF)

    for group in range(1, groups):
        grads(group)
        reduce.start(group)
        if group >= LAG:
            reduce.step(group - LAG)

    grad_one = r.grad_two[...] + r.delta[own_cols, :]
    r.grad_one[...] = grad_one

    def along(values):
        return jnp.sum(values.astype(F32), 1, keepdims=True)

    grad_normed = r.grad_normed[own_cols, :].astype(F32)
    columns = [
        along(r.back[own_cols, middle]),
        along(r.mixed[own_cols, :]),
        along(grad_one * r.mixed_unit[own_cols, :]),
        along(grad_one),
        along(grad_normed * r.one_unit[own_cols, :]),
        along(grad_normed),
        r.attend_sums[:, 0:2],
        r.mlp_sums[...],
    ]
    at = 0
    for column in columns:
        r.vectors[pl.ds(me, 1), :, at : at + column.shape[1]] = column[None]
        at += column.shape[1]

    def vector_copy(p, slot):
        return push(
            r.vectors.at[slot], r.vectors.at[slot], r.vector_send.at[p], r.vector_recv.at[slot],
            pts=p,
        )

    for p in others(me, pts):
        vector_copy(p, me).start()

    @pl.when(me > 0)
    def _():
        up_copy(me - 1).wait_recv()
        core_copy(low_end, 0, core).start()

    @pl.when(me < pts - 1)
    def _():
        down_copy(me + 1).wait_recv()
        core_copy(high_end, 1, core).start()

    @pl.when(me > 0)
    def _():
        core_copy(low_end, 0, 1 - core).wait_recv()

    @pl.when(me < pts - 1)
    def _():
        core_copy(high_end, 1, 1 - core).wait_recv()

    def turn(tap, carry):
        weight = r.taps[:, pl.ds(taps - 1 - tap, 1)].reshape(C, cols)
        turned = dot(weight, r.back[...], TN).astype(BF)
        for tile in range(rows // TILE):
            hot = one_hot_window(r.ids, tap, tile)
            r.turn_acc[:, tile * TILE : (tile + 1) * TILE] += dot(
                turned[:, tile * TILE : tile * TILE + WINDOW], hot
            )
        return carry

    r.turn_acc[...] = jnp.zeros_like(r.turn_acc)
    left = list(range(groups - LAG, reduce.steps))
    cuts = [taps * i // len(left) for i in range(len(left) + 1)]
    for i, s in enumerate(left):
        lax.fori_loop(cuts[i], cuts[i + 1], turn, 0)
        reduce.step(s)
    r.point_grad[...] = (r.turn_acc[...] + r.grad_one[...]).T
    reduce.finish(r.summed)
    total = r.vectors[pl.ds(me, 1)][0]
    for p in others(me, pts):
        vector_copy(p, p).wait_recv()
        total = total + r.vectors[pl.ds(p, 1)][0]
    r.vector_grad[...] = total.T
    reduce.end()
    for p in others(me, pts):
        vector_copy(p, me).wait_send()

    @pl.when(me < pts - 1)
    def _():
        up_copy(me + 1).wait_send()
        core_copy(high_end, 1, core).wait_send()

    @pl.when(me > 0)
    def _():
        down_copy(me - 1).wait_send()
        core_copy(low_end, 0, core).wait_send()


LAG = 2


def back_pass(
    plan, first, ids, grad_normed, branch_full, grad_two, attend_grads, mlp_sums, attend_sums
):
    taps, cols, rows = first.taken.shape
    total = len(BACK_ORDER)
    share = C // plan.pts
    vmem = pltpu.VMEM
    return call(
        functools.partial(back_kernel, plan),
        "back_pass",
        1,
        dict(
            taken=Late(first.taken), pair=Late(first.pair), vec=first.vec, hidden=Late(first.hidden), mixed_unit=Late(first.mixed_unit), mixed_std=first.mixed_std, one_unit=Late(first.one_unit), one_std=first.one_std, taps=Late(first.taps_far), ids=ids,
            grad_normed=Late(grad_normed),
            branch_full=Late(branch_full), grad_two=Late(grad_two), attend_grads=attend_grads, mlp_sums=mlp_sums, attend_sums=attend_sums,
        ),
        dict(
            summed=((total, share, cols), BF),
            point_grad=((rows, cols), F32),
            vector_grad=((12 + FF // C, cols), F32),
        ),
        dict(
            reduce_net=(Reduce.buffers(plan, total, BACK_PACK, cols)),
            turn_acc=vmem((cols, rows), F32),
            grad_one=vmem((cols, rows), F32),
            delta=vmem((C, rows), F32),
            mixed=vmem((C, rows), BF),
            back=vmem((C, rows + 2 * HALO), BF),
            vectors=vmem((plan.pts, cols, 12 + FF // C), F32),
            halo_send=dma(2),
            halo_recv=dma(2),
            core_send=dma(2),
            core_recv=dma(2),
            vector_send=dma(plan.pts),
            vector_recv=dma(plan.pts),
        ),
        taps * rows * (WINDOW * 4 + 5 * C) * cols,
    )


def adam(first, second, grad):
    new_first = BETA_ONE * first + (1.0 - BETA_ONE) * grad
    new_second = BETA_TWO * second + (1.0 - BETA_TWO) * grad * grad
    direction = (
        new_first
        / (1.0 - BETA_ONE**STEP)
        / (jnp.sqrt(new_second / (1.0 - BETA_TWO**STEP)) + ADAM_EPS)
    )
    return new_first, new_second, direction


def owner_kernel(plan, r):
    pts, mdl, slots = plan.pts, plan.mdl, plan.slots
    share, cols = r.summed.shape[1:]
    me, plane = lax.axis_index(PTS), lax.axis_index(MDL)
    moves(START, r.left_move, r.right_move, r.first_move, r.second_move)
    greet(
        [
            {PTS: p, MDL: m}
            for i, p in enumerate([me] + others(me, pts))
            for j, m in enumerate([plane] + others(plane, mdl))
            if i + j > 0
        ]
    )

    count = r.summed.shape[0]
    r.listed[:count] = r.summed[...]
    r.listed[count:] = r.mlp_summed[...]

    def order(slot, carry):
        r.grads[pl.ds(slot, 1)] = r.listed[pl.ds(r.places[slot], 1)]
        return carry

    def whole_copy(j, step):
        m = lax.rem(plane + step, mdl)
        target, k = plan.worker(j), j // pts
        piece, spot = r.grads.at[m * slots + j], r.whole.at[k, me, plane]

        def near():
            return pltpu.make_async_copy(piece, spot, r.whole_here.at[k])

        def far():
            return push(
                piece, spot, r.whole_send.at[step, j], r.whole_recv.at[k, me, plane], pts=target,
                mdl=m,
            )

        return (me == target) & (step == 0), near, far

    def rows_copy(m, slot):
        return push(
            r.grads.at[pl.ds(m * slots, slots)], r.rows.at[slot], r.rows_send.at[m],
            r.rows_recv.at[slot], mdl=m,
        )

    def rows_here():
        return pltpu.make_async_copy(
            r.grads.at[pl.ds(plane * slots, slots)], r.rows.at[plane], r.rows_home
        )

    for step in range(mdl):
        m = lax.rem(plane + step, mdl)
        lax.fori_loop(m * slots, (m + 1) * slots, order, 0)
        for j in range(slots):
            home, near, far = whole_copy(j, step)

            @pl.when(home)
            def _():
                near().start()

            @pl.when(jnp.logical_not(home))
            def _():
                far().start()

    for m in others(plane, mdl):
        rows_copy(m, plane).start()
    rows_here().start()
    moves(WAIT, r.left_move, r.right_move, r.first_move, r.second_move)

    def result_copy(k, kind, p):
        return push(
            r.turned.at[k, kind, p], r.results.at[plan.work(me, k), kind], r.back_send.at[k, kind, p],
            r.back_recv.at[plan.work(me, k), kind], pts=p,
        )

    def result_here(k, kind):
        return pltpu.make_async_copy(
            r.turned.at[k, kind, me], r.results.at[plan.work(me, k), kind], r.back_home.at[k, kind]
        )

    def send_result(k, kind, value):
        r.turned[k, kind] = value.astype(BF).reshape(pts, share, C)
        for p in others(me, pts):
            result_copy(k, kind, p).start()
        result_here(k, kind).start()

    for k in range(plan.each):

        @pl.when(plan.work(me, k) < slots)
        def _():
            pltpu.make_async_copy(
                r.grads.at[0], r.whole.at[k, me, plane], r.whole_here.at[k]
            ).wait()
            for p_step in range(pts):
                for m_step in range(mdl):
                    if p_step + m_step > 0:
                        p, m = lax.rem(me + p_step, pts), lax.rem(plane + m_step, mdl)
                        push(
                            r.grads.at[0], r.whole.at[k, p, m], r.whole_send.at[0, 0],
                            r.whole_recv.at[k, p, m], pts=p, mdl=m,
                        ).wait_recv()
            left = r.left[k].reshape(C, C)
            right = r.right[k].reshape(C, C)
            halves = [
                dot(left, r.whole[k, :, m].reshape(C, cols), TN).astype(BF) for m in range(mdl)
            ]
            if cols % 128 == 0:
                rotated = dot(jnp.concatenate(halves, 1), right)
            else:
                rotated = sum(
                    dot(half, right[m * cols : (m + 1) * cols]) for m, half in enumerate(halves)
                )
            send_result(k, 0, rotated)
            _, _, direction = adam(
                r.first[k].reshape(C, C).astype(F32),
                r.second[k].reshape(C, C).astype(F32),
                rotated.astype(BF).astype(F32),
            )
            send_result(k, 1, dot(left, dot(direction.astype(BF), right, NT).astype(BF)))

    for m in others(plane, mdl):
        rows_copy(m, plane).wait_send()
        rows_copy(m, m).wait_recv()
    rows_here().wait()
    for j in range(slots):
        source, k = plan.worker(j), j // pts
        for kind in range(2):

            @pl.when(me != source)
            def _():
                push(
                    r.turned.at[k, kind, me], r.results.at[j, kind], r.back_send.at[k, kind, source],
                    r.back_recv.at[j, kind], pts=source,
                ).wait_recv()

    for k in range(plan.each):

        @pl.when(plan.work(me, k) < slots)
        def _():
            for kind in range(2):
                result_here(k, kind).wait()
                for p in others(me, pts):
                    result_copy(k, kind, p).wait_send()

    for step in range(mdl):
        for j in range(slots):
            home, near, far = whole_copy(j, step)

            @pl.when(jnp.logical_not(home))
            def _():
                far().wait_send()


def owner_update(plan, places, summed, mlp_summed, left, right, first, second):
    _, share, cols = summed.shape
    blocks = len(BACK_ORDER) + len(MLP_ORDER)
    pts, mdl, each, slots = plan.pts, plan.mdl, plan.each, plan.slots
    vmem = pltpu.VMEM
    return call(
        functools.partial(owner_kernel, plan),
        "owner_update",
        4,
        dict(places=places, summed=summed, mlp_summed=mlp_summed, left=Late(left), right=Late(right), first=Late(first), second=Late(second)),
        dict(
            rows=((mdl, slots, share, cols), BF),
            results=((slots, 2, share, C), BF),
        ),
        dict(
            grads=vmem((blocks, share, cols), BF),
            listed=vmem((blocks, share, cols), BF),
            whole=vmem((each, pts, mdl, share, cols), BF),
            turned=vmem((each, 2, pts, share, C), BF),
            whole_send=dma(mdl, slots),
            whole_recv=dma(each, pts, mdl),
            whole_here=dma(each),
            rows_send=dma(mdl),
            rows_recv=dma(mdl),
            rows_home=dma(),
            back_send=dma(each, 2, pts),
            back_recv=dma(slots, 2),
            back_home=dma(each, 2),
        ),
        8 * each * C * C * C,
        smem=("places",),
    )


def scan_index(row_ids, scan_lengths):
    bounds = jnp.cumsum(scan_lengths)
    return jnp.sum((row_ids[..., None] >= bounds[:-1]).astype(jnp.int32), -1)


def local(
    points,
    cotangent,
    neighbours,
    scan_lengths,
    to_patch,
    from_patch,
    owner_slot,
    weights,
    row_eigen_basis,
    right_basis,
    first_moment,
    second_moment,
    vectors,
    vector_first,
    vector_second,
):
    rows, cols = points.shape
    slot_count = from_patch.shape[0]
    pts = lax.axis_size(PTS)
    mdl = lax.axis_size(MDL)
    pts_index = lax.axis_index(PTS)
    patch_count = slot_count // PATCH
    matrix_rate = 1.6 * C ** (-0.5)
    plan = Layout(pts, mdl, owner_slot.shape[0], patch_count * scan_lengths.shape[0])

    row_ids = pts_index * rows + jnp.arange(rows, dtype=jnp.int32)
    own_scan = scan_index(row_ids, scan_lengths)
    near = neighbours.T
    usable = (near >= 0) & (scan_index(jnp.maximum(near, 0), scan_lengths) == own_scan[None, :])
    ids = jnp.where(usable, near - (pts_index * rows - HALO), -1)

    first = front(
        plan,
        owner_slot,
        weights,
        points,
        cotangent,
        vectors,
        ids,
        to_patch[None],
        from_patch[None],
        scan_lengths,
    )
    rest, send_pos, arrival = first.rest, first.send_pos, first.arrival
    kept = attend(
        plan,
        first.slot_in,
        rest,
        vectors,
        first.group,
        send_pos,
        arrival,
        row_eigen_basis,
        right_basis,
    )
    middle = mlp(
        plan, kept.attended_rows, first, rest, cotangent, send_pos, arrival, first_moment
    )
    back = attend_back(
        plan,
        kept,
        middle.grad_slot,
        first.slot_in,
        rest,
        first.pair,
        send_pos,
        arrival,
        middle.weight_grads,
        second_moment,
    )
    last = back_pass(
        plan,
        first,
        ids,
        back.grad_normed,
        middle.branch_full,
        middle.grad_two,
        back.weight_grads,
        middle.sums,
        back.sums,
    )
    vector_grad = last.vector_grad
    listed = BACK_ORDER + MLP_ORDER
    places = jnp.array([listed.index(b) for b in range(len(listed))], jnp.int32)
    slot_ids = jnp.arange(len(listed), dtype=jnp.int32)
    place_of_slot = jnp.sum(
        jnp.where(owner_slot[None, :] == slot_ids[:, None], places[None, :], 0), 1
    )
    ended = owner_update(
        plan,
        place_of_slot,
        last.summed,
        back.mlp_summed,
        kept.left_whole,
        kept.right_whole,
        middle.first_whole,
        back.second_whole,
    )
    reduced = ended.rows.transpose(1, 2, 0, 3).reshape(plan.slots, C // pts, C)
    results = ended.results
    rotated, update = results[:, 0].astype(F32), results[:, 1].astype(F32)
    new_first, new_second, _ = adam(first_moment, second_moment, rotated)
    new_weights = weights - matrix_rate * (update + MATRIX_DECAY * weights)
    new_vector_first, new_vector_second, vector_step = adam(
        vector_first, vector_second, vector_grad
    )
    new_vectors = vectors - VECTOR_RATE * vector_step
    return (
        middle.out,
        last.point_grad,
        reduced.astype(F32),
        new_first,
        new_second,
        new_weights,
        new_weights.astype(BF),
        vector_grad,
        new_vector_first,
        new_vector_second,
        new_vectors,
    )


def solution(mesh):
    by_rows = P(PTS, MDL)
    owned = P(MDL, PTS, None)
    vector = P(None, MDL)
    return jax.shard_map(
        local,
        mesh=mesh,
        in_specs=(
            by_rows,
            by_rows,
            P(PTS, None),
            P(),
            P(PTS),
            P(PTS),
            P(),
            owned,
            owned,
            owned,
            owned,
            owned,
            vector,
            vector,
            vector,
        ),
        out_specs=(
            by_rows,
            by_rows,
            owned,
            owned,
            owned,
            owned,
            owned,
            vector,
            vector,
            vector,
            vector,
        ),
        check_vma=False,
    )
```

```python
import functools
import types

import jax
import jax.numpy as jnp
from jax import lax
from jax.experimental import pallas as pl
from jax.experimental.pallas import tpu as pltpu
from jax.sharding import PartitionSpec as P

C = 512
HD = 16
FF = 2048
TAPS = 27
HALO = 256
PATCH = 1024
STEP = 5

NORM_EPS = 1e-05
BETA_ONE = 0.9
BETA_TWO = 0.999
ADAM_EPS = 1e-08
VECTOR_RATE = 0.5
MATRIX_DECAY = 0.05
TILE = 256
WINDOW = TILE + 2 * HALO
BF = jnp.bfloat16
F32 = jnp.float32
VMEM_LIMIT = 56 * 1024 * 1024

NN = (((1,), (0,)), ((), ()))
NT = (((1,), (1,)), ((), ()))
TN = (((0,), (0,)), ((), ()))


def dot(a, b, dims=NN):
    return lax.dot_general(a, b, dims, preferred_element_type=F32)


def params(**kw):
    return pltpu.CompilerParams(vmem_limit_bytes=VMEM_LIMIT, **kw)


MESH = pl.DeviceIdType.MESH
PTS, MDL = "pts", "mdl"
START, WAIT = range(2)


def push(src, dst, send_sem, recv_sem, **target):
    return pltpu.make_async_remote_copy(
        src_ref=src,
        dst_ref=dst,
        send_sem=send_sem,
        recv_sem=recv_sem,
        device_id=target,
        device_id_type=MESH,
    )


def greet(peers):
    barrier = pltpu.get_barrier_semaphore()
    for peer in peers:
        pl.semaphore_signal(barrier, inc=1, device_id=peer, device_id_type=MESH)
    pl.semaphore_wait(barrier, len(peers))


def others(index, size):
    return [lax.rem(index + step, size) for step in range(1, size)]


class Layout:
    def __init__(self, pts, mdl, blocks, groups):
        self.pts, self.mdl, self.groups = pts, mdl, groups
        self.slots = blocks // mdl
        self.each = -(-self.slots // pts)
        self.shift = max(pts - self.slots, 0) // 2 if self.slots < pts else (pts - self.slots % pts) // 2
        self.width = mdl // 2 if pts % (mdl // 2) == 0 else 1
        self.depth = pts // self.width

    def worker(self, j):
        return (j + self.shift) % self.pts

    def work(self, me, k):
        return lax.rem(me + self.pts - self.shift, self.pts) + k * self.pts


def fetch_copies(plan, src, dst, sems, act):
    send, recv, here = sems
    me = lax.axis_index(PTS)
    for j in range(plan.slots):
        target, k = plan.worker(j), j // plan.pts

        @pl.when(me != target)
        def _():
            copy = push(src.at[j], dst.at[k, me], send.at[j], recv.at[k, me], pts=target)
            copy.start() if act == START else copy.wait_send()

        @pl.when(me == target)
        def _():
            copy = pltpu.make_async_copy(src.at[j], dst.at[k, me], here.at[k])
            if act == START:
                copy.start()
            else:
                copy.wait()
                for source in others(me, plan.pts):
                    push(
                        src.at[j], dst.at[k, source], send.at[j], recv.at[k, source], pts=source
                    ).wait_recv()


def fetch_sems(plan):
    return [dma(plan.slots), dma(plan.each, plan.pts), dma(plan.each)]


def fetch_shape(plan, src):
    return jax.ShapeDtypeStruct((plan.each, plan.pts) + src.shape[1:], BF)


class Late:
    def __init__(self, *what):
        self.what = what


def call(kernel, name, collective, inputs, outputs, scratch, flops, smem=(), free=()):
    vmem = pltpu.VMEM
    leaves, tree = jax.tree.flatten(scratch, is_leaf=lambda x: not isinstance(x, (dict, list)))
    late_in = [key for key, value in inputs.items() if isinstance(value, Late)]
    late_out = [key for key, value in outputs.items() if isinstance(value, Late)]
    values = {key: v.what[0] if key in late_in else v for key, v in inputs.items()}
    shapes = {key: v.what if key in late_out else v for key, v in outputs.items()}
    near = [vmem(values[key].shape, values[key].dtype) for key in late_in]
    near += [vmem(*shapes[key]) for key in late_out]
    late = late_in + late_out

    def space(key, value):
        return pltpu.SMEM if key in smem else pl.ANY if key in free or key in late else vmem

    def grouped(x):
        if isinstance(x, dict):
            return types.SimpleNamespace(**{key: grouped(value) for key, value in x.items()})
        return [grouped(value) for value in x] if isinstance(x, list) else x

    def body(*refs):
        count = len(inputs) + len(outputs)
        given = dict(zip(inputs, refs))
        given.update(zip(outputs, refs[len(inputs) : count]))
        own, sems = refs[count : count + len(late)], refs[count + len(late) : count + 2 * len(late)]
        r = grouped(jax.tree.unflatten(tree, refs[count + 2 * len(late) :]))
        for key, ref in given.items():
            setattr(r, key, ref)
        for key, ref, sem in zip(late, own, sems):
            pair = (given[key], ref) if key in late_in else (ref, given[key])
            setattr(r, key, ref)
            setattr(r, key + "_move", functools.partial(pltpu.make_async_copy, *pair, sem))
        kernel(r)

    results = pl.pallas_call(
        body,
        in_specs=[pl.BlockSpec(memory_space=space(*item)) for item in inputs.items()],
        out_specs=[pl.BlockSpec(memory_space=space(*item)) for item in outputs.items()],
        out_shape=[jax.ShapeDtypeStruct(*shape) for shape in shapes.values()],
        scratch_shapes=near + [dma() for _ in late] + leaves,
        compiler_params=params(collective_id=collective, has_side_effects=True),
        cost_estimate=pl.CostEstimate(
            flops=flops, bytes_accessed=20000000, transcendentals=1000000
        ),
        name=name,
    )(*values.values())
    return types.SimpleNamespace(**dict(zip(outputs, results)))


def moves(act, *copies):
    for make in copies:
        copy = make()
        copy.start() if act == START else copy.wait()


def dma(*shape):
    return pltpu.SemaphoreType.DMA(shape)


class Gather:
    def __init__(self, plan, part, sems):
        self.part, self.sems = part, sems
        self.plane = lax.axis_index(MDL)
        self.size = plan.mdl // 2
        self.x, self.core = self.plane // 2, lax.rem(self.plane, 2)

    @staticmethod
    def semaphores(plan):
        return dict(x_send=dma(plan.mdl // 2), recv=dma(plan.mdl), core_send=dma(plan.mdl // 2))

    def along(self, m, target, send):
        return push(self.part(m), self.part(m), send, self.sems.recv.at[m], mdl=target)

    def x_copy(self, x):
        return self.along(self.plane, x * 2 + self.core, self.sems.x_send.at[x])

    def core_copy(self, x):
        return self.along(
            x * 2 + self.core, self.x * 2 + 1 - self.core, self.sems.core_send.at[x]
        )

    def arrived(self, m):
        self.along(m, m, self.sems.x_send.at[0]).wait_recv()

    def start(self):
        for x in others(self.x, self.size):
            self.x_copy(x).start()
        self.core_copy(self.x).start()

    def forward(self):
        for x in others(self.x, self.size):
            self.arrived(x * 2 + self.core)
            self.core_copy(x).start()

    def finish(self):
        for x in [self.x] + others(self.x, self.size):
            self.arrived(x * 2 + 1 - self.core)
        for x in others(self.x, self.size):
            self.x_copy(x).wait_send()
            self.core_copy(x).wait_send()
        self.core_copy(self.x).wait_send()

    def run(self):
        self.start()
        self.forward()
        self.finish()


class Sum:
    def __init__(self, plan, parts, bufs):
        self.parts, self.bufs = parts, bufs
        self.plane = lax.axis_index(MDL)
        self.size = plan.mdl // 2
        self.x, self.core = self.plane // 2, lax.rem(self.plane, 2)

    @staticmethod
    def buffers(plan, shape):
        x = plan.mdl // 2
        vmem = pltpu.VMEM((x,) + shape, BF)
        return dict(
            near=vmem, middle=vmem, far=vmem,
            near_send=dma(x), near_recv=dma(x), far_send=dma(x), far_recv=dma(x),
        )

    def near_copy(self, x):
        b = self.bufs
        return push(
            self.parts.at[x * 2 + 1 - self.core], b.near.at[x], b.near_send.at[x],
            b.near_recv.at[x], mdl=self.x * 2 + 1 - self.core,
        )

    def far_copy(self, x, slot):
        b = self.bufs
        return push(
            b.middle.at[x], b.far.at[slot], b.far_send.at[x], b.far_recv.at[slot],
            mdl=x * 2 + self.core,
        )

    def both(self, x):
        self.near_copy(x).wait_recv()
        own = self.parts[pl.ds(x * 2 + self.core, 1)][0].astype(F32)
        return own + self.bufs.near[pl.ds(x, 1)][0].astype(F32)

    def start(self):
        for x in others(self.x, self.size) + [self.x]:
            self.near_copy(x).start()

    def middle(self):
        for x in others(self.x, self.size):
            self.bufs.middle[pl.ds(x, 1)] = self.both(x).astype(BF)[None]
            self.far_copy(x, self.x).start()

    def finish(self):
        total = self.both(self.x)
        for x in others(self.x, self.size):
            self.far_copy(x, x).wait_recv()
            total = total + self.bufs.far[pl.ds(x, 1)][0].astype(F32)
        for x in others(self.x, self.size):
            self.near_copy(x).wait_send()
            self.far_copy(x, self.x).wait_send()
        self.near_copy(self.x).wait_send()
        return total

    def run(self):
        self.start()
        self.middle()
        return self.finish()


class Trade:
    def __init__(self, plan, out_index, in_index, bufs):
        self.out_index, self.in_index, self.bufs = out_index, in_index, bufs
        self.size = plan.pts
        self.me = lax.axis_index(PTS)

    @staticmethod
    def buffers(plan, cols, rows):
        capacity = 2 * rows // plan.pts
        vmem = pltpu.VMEM((plan.pts, cols, capacity), BF)
        return dict(leave=vmem, land=vmem, send=dma(plan.pts), recv=dma(plan.pts))

    def hot(self, index, part):
        capacity = self.bufs.leave.shape[2]
        row = index[...]
        places = lax.broadcasted_iota(jnp.int32, (capacity, row.shape[1]), 0) + part * capacity
        return jnp.where(places == row, 1.0, 0.0).astype(BF)

    def copy(self, part, slot):
        b = self.bufs
        return push(
            b.leave.at[part], b.land.at[slot], b.send.at[part], b.recv.at[slot],
            pts=part,
        )

    def start(self, values):
        b = self.bufs
        for part in others(self.me, self.size):
            b.leave[pl.ds(part, 1)] = dot(values, self.hot(self.out_index, part), NT).astype(BF)[None]
            self.copy(part, self.me).start()
        b.land[pl.ds(self.me, 1)] = dot(values, self.hot(self.out_index, self.me), NT).astype(BF)[None]

    def finish(self):
        b = self.bufs
        total = dot(b.land[pl.ds(self.me, 1)][0], self.hot(self.in_index, self.me))
        for step in range(1, self.size):
            part = lax.rem(self.me + self.size - step, self.size)
            hot = self.hot(self.in_index, part)
            self.copy(part, part).wait_recv()
            total = total + dot(b.land[pl.ds(part, 1)][0], hot)
        for part in others(self.me, self.size):
            self.copy(part, self.me).wait_send()
        return total.astype(BF)

    def run(self, values):
        self.start(values)
        return self.finish()


class Route:
    PIECES = 2

    def __init__(self, plan, out_index, in_index, full, nets):
        cols = full.shape[0] // plan.mdl
        self.size = cols // self.PIECES
        self.full, self.base = full, lax.axis_index(MDL) * cols
        self.trades = [Trade(plan, out_index, in_index, net.trade) for net in nets]
        self.gathers = [
            Gather(
                plan, lambda m, i=i: full.at[pl.ds(m * cols + i * self.size, self.size)], net.ring
            )
            for i, net in enumerate(nets)
        ]

    @classmethod
    def buffers(cls, plan, cols, rows):
        net = dict(
            trade=Trade.buffers(plan, cols // cls.PIECES, rows), ring=Gather.semaphores(plan)
        )
        return [net] * cls.PIECES

    def start(self, values):
        for i, trade in enumerate(self.trades):
            trade.start(values[i * self.size : (i + 1) * self.size])

    def land(self):
        for i, (trade, gather) in enumerate(zip(self.trades, self.gathers)):
            self.full[pl.ds(self.base + i * self.size, self.size), :] = trade.finish()
            gather.start()
            if i > 0:
                self.gathers[i - 1].forward()
        self.gathers[-1].forward()

    def finish(self):
        for gather in self.gathers:
            gather.finish()


class Reduce:
    def __init__(self, plan, bufs):
        self.bufs = bufs
        self.width, self.depth = plan.width, plan.depth
        self.me = lax.axis_index(PTS)
        self.y, self.z = lax.rem(self.me, self.width), self.me // self.width
        self.groups, _, self.pack, self.share, self.cols = bufs.acc.shape
        self.steps = self.groups + self.depth - 1

    @staticmethod
    def buffers(plan, blocks, pack, cols):
        groups, share, vmem = blocks // pack, C // plan.pts, pltpu.VMEM
        line = (plan.depth, pack, share, cols)
        way = dict(
            land=vmem((groups,) + line, BF),
            send=dma(groups, plan.depth),
            recv=dma(groups, plan.depth),
        )
        return dict(
            own=vmem((plan.width, groups) + line, BF),
            side=vmem((plan.width, groups) + line, BF),
            acc=vmem((groups,) + line, BF),
            up=way,
            down=way,
            side_send=dma(plan.width, groups),
            side_recv=dma(plan.width, groups),
        )

    def store(self, block, group, place):
        grid = block.astype(BF).reshape(self.depth, self.width, self.share, self.cols)
        for v in range(self.width):
            self.bufs.own[v, group, :, pl.ds(place, 1)] = grid[:, v][:, None]

    def side_copy(self, group, v, slot):
        b = self.bufs
        return push(
            b.own.at[v, group], b.side.at[slot, group], b.side_send.at[v, group],
            b.side_recv.at[slot, group], pts=self.z * self.width + v,
        )

    def line_copy(self, way, group, to, step):
        b = self.bufs
        near = jnp.clip(self.z + step, 0, self.depth - 1)
        return push(
            b.acc.at[group, to], way.land.at[group, to], way.send.at[group, to],
            way.recv.at[group, to], pts=near * self.width + self.y,
        )

    def start(self, group):
        for v in others(self.y, self.width):
            self.side_copy(group, v, self.y).start()

    def sum_side(self, group):
        b = self.bufs
        total = b.own[pl.ds(self.y, 1), pl.ds(group, 1)][0].astype(F32)
        for v in others(self.y, self.width):
            self.side_copy(group, v, v).wait_recv()
            total = total + b.side[pl.ds(v, 1), pl.ds(group, 1)][0].astype(F32)
        b.acc[pl.ds(group, 1)] = total.astype(BF)

    def relay(self, way, group, step, first):
        b = self.bufs

        @pl.when((group >= 0) & (group < self.groups))
        def _():
            for to in range(self.depth):

                @pl.when((to - self.z) * step > 0)
                def _():
                    @pl.when(jnp.logical_not(first))
                    def _():
                        self.line_copy(way, group, to, -step).wait_recv()
                        spot = (pl.ds(group, 1), to)
                        b.acc[spot] = (
                            b.acc[spot].astype(F32) + way.land[spot].astype(F32)
                        ).astype(BF)

                    self.line_copy(way, group, to, step).start()

    def step(self, s):
        if isinstance(s, int):
            if s < self.groups:
                self.sum_side(s)
        else:

            @pl.when((s >= 0) & (s < self.groups))
            def _():
                self.sum_side(s)

        self.relay(self.bufs.up, s - self.z, 1, self.z == 0)
        self.relay(self.bufs.down, s - (self.depth - 1 - self.z), -1, self.z == self.depth - 1)

    def finish(self, out):
        b, z = self.bufs, self.z

        def total(way, group):
            b.acc[group, pl.ds(z, 1)] = (
                b.acc[group, pl.ds(z, 1)].astype(F32) + way.land[group, pl.ds(z, 1)].astype(F32)
            ).astype(BF)

        for group in range(self.groups):

            @pl.when(z > 0)
            def _():
                self.line_copy(self.bufs.up, group, z, -1).wait_recv()
                total(b.up, group)

            @pl.when(z < self.depth - 1)
            def _():
                self.line_copy(self.bufs.down, group, z, 1).wait_recv()
                total(b.down, group)

            out[group * self.pack : (group + 1) * self.pack] = b.acc[group, pl.ds(z, 1)][0]

    def end(self):
        for group in range(self.groups):
            for v in others(self.y, self.width):
                self.side_copy(group, v, self.y).wait_send()
            for to in range(self.depth):

                @pl.when(to > self.z)
                def _():
                    self.line_copy(self.bufs.up, group, to, 1).wait_send()

                @pl.when(to < self.z)
                def _():
                    self.line_copy(self.bufs.down, group, to, -1).wait_send()


def everyone(plan):
    me, plane = lax.axis_index(PTS), lax.axis_index(MDL)
    return [{PTS: p} for p in others(me, plan.pts)] + [{MDL: m} for m in others(plane, plan.mdl)]


def unit_columns(values):
    mean = jnp.sum(values, 0, keepdims=True) / C
    centred = values - mean
    inv_std = lax.rsqrt(jnp.sum(centred * centred, 0, keepdims=True) / C + NORM_EPS)
    return centred * inv_std, inv_std


def one_hot_window(ids_ref, tap, tile):
    row = ids_ref[pl.ds(tap, 1), pl.ds(tile * TILE, TILE)]
    places = lax.broadcasted_iota(jnp.int32, (WINDOW, TILE), 0) + tile * TILE
    return jnp.where(places == row, 1.0, 0.0).astype(BF)


PACK = 5
ORDER = [TAPS, TAPS + 4] + list(range(TAPS)) + [TAPS + 1, TAPS + 2, TAPS + 3]
ORDER = ORDER + list(range(TAPS + 5, TAPS + 5 + 2 * FF // C))
PLACE = {block: place for place, block in enumerate(ORDER)}


def column(row):
    wide = jnp.broadcast_to(row.astype(F32), (8, row.shape[1]))
    return wide.T[:, 0:1].astype(jnp.int32)


def steps_passed(values, bounds):
    return sum((values >= bound).astype(jnp.int32) for bound in bounds)


def routes(plan, r, rows):
    capacity = 2 * rows // plan.pts
    slot_count = r.from_patch.shape[1]
    patches = slot_count // PATCH
    scans = r.scan_lengths.shape[0]
    target = steps_passed(r.to_patch[...], [p * slot_count for p in range(1, plan.pts)])
    size = 256
    rank = jnp.zeros((1, rows), jnp.int32)
    target_column = column(target)
    ahead = lax.broadcasted_iota(jnp.int32, (size, rows), 1)
    for low in range(0, rows, size):
        earlier = lax.broadcasted_iota(jnp.int32, (size, rows), 0) + low < ahead
        same = target_column[low : low + size] == target
        rank = rank + jnp.sum((earlier & same).astype(jnp.int32), 0, keepdims=True)
    r.send_pos[...] = target * capacity + rank
    held = r.from_patch[...]
    used = held >= 0
    lanes = lax.broadcasted_iota(jnp.int32, (1, slot_count), 1)
    patch = steps_passed(lanes, [p * PATCH for p in range(1, patches)])
    source = steps_passed(held, [p * rows for p in range(1, plan.pts)])
    bounds, bound = [], 0
    for i in range(scans - 1):
        bound = bound + r.scan_lengths[i]
        bounds.append(bound)
    group = patch * scans + (steps_passed(held, bounds) if bounds else 0)
    top = patches * plan.pts * rows
    order_key = jnp.where(used, patch * (plan.pts * rows) + held, top)
    held_key = jnp.where(used, held, top)
    order_column, held_column = column(order_key), column(held_key)
    first_key = source * rows
    order = jnp.zeros((1, slot_count), jnp.int32)
    rank = jnp.zeros((1, slot_count), jnp.int32)
    for low in range(0, slot_count, size):
        part = slice(low, low + size)
        order = order + jnp.sum(
            (order_column[part] < order_key).astype(jnp.int32), 0, keepdims=True
        )
        among = (held_column[part] < held_key) & (held_column[part] >= first_key)
        rank = rank + jnp.sum(among.astype(jnp.int32), 0, keepdims=True)
    base = plan.pts * capacity
    both = column(group * base + source * capacity + rank)
    order = column(jnp.where(used, order, slot_count))
    places = lax.broadcasted_iota(jnp.int32, (size, rows), 1)
    found = jnp.zeros((1, rows), jnp.int32)
    for low in range(0, slot_count, size):
        part = slice(low, low + size)
        found = found + jnp.sum(
            jnp.where(order[part] == places, both[part], 0), 0, keepdims=True
        )
    group = steps_passed(found, [base * g for g in range(1, patches * scans)])
    r.group[...] = group
    r.arrival[...] = found - group * base


def front_kernel(plan, r):
    pts, mdl, slots = plan.pts, plan.mdl, plan.slots
    width, depth = plan.width, plan.depth
    me, plane = lax.axis_index(PTS), lax.axis_index(MDL)
    y, z = lax.rem(me, width), me // width
    rows, cols = r.points_rows.shape
    share = C // pts
    total = r.blocks.shape[1]
    groups = total // PACK
    conv_groups = -(-(2 + TAPS) // PACK)
    for m in range(mdl):
        r.owned[m] = r.weights[:, :, m * cols : (m + 1) * cols].astype(BF)
    greet(everyone(plan))

    def spread_copy(m, slot):
        return push(
            r.owned.at[m], r.spread.at[pl.ds(slot * slots, slots)], r.spread_send.at[m],
            r.spread_recv.at[slot], mdl=m,
        )

    for m in others(plane, mdl):
        spread_copy(m, plane).start()

    def vec_copy(m, slot):
        return push(
            r.vectors, r.vec_all.at[slot], r.vec_send.at[m], r.vec_recv.at[slot], mdl=m
        )

    for m in others(plane, mdl):
        vec_copy(m, plane).start()

    r.points[...] = r.points_rows[...].astype(F32).T.astype(BF)

    def up_copy():
        return push(
            r.points.at[:, rows - HALO : rows], r.ext.at[:, 0:HALO], r.halo_send.at[0],
            r.halo_recv.at[0], pts=me + 1,
        )

    def down_copy():
        return push(
            r.points.at[:, 0:HALO], r.ext.at[:, HALO + rows : 2 * HALO + rows], r.halo_send.at[1],
            r.halo_recv.at[1], pts=me - 1,
        )

    @pl.when(me < pts - 1)
    def _():
        up_copy().start()

    @pl.when(me == pts - 1)
    def _():
        r.ext[:, HALO + rows :] = jnp.zeros((cols, HALO), BF)

    @pl.when(me > 0)
    def _():
        down_copy().start()

    @pl.when(me == 0)
    def _():
        r.ext[:, :HALO] = jnp.zeros((cols, HALO), BF)

    r.ext[:, HALO : HALO + rows] = r.points[...]
    r.spread[pl.ds(plane * slots, slots)] = r.owned[pl.ds(plane, 1)][0]
    r.vec_all[pl.ds(plane, 1)] = r.vectors[...][None]
    r.points_full[pl.ds(plane * cols, cols), :] = r.points[...]
    for m in others(plane, mdl):
        spread_copy(m, m).wait_recv()
    for place, block in enumerate(ORDER):
        r.blocks[pl.ds(me, 1), place] = r.spread[pl.ds(r.slots[block], 1)]

    def group_of(source, group):
        return r.blocks.at[source, group * PACK : (group + 1) * PACK]

    def far_copy(group, source, step):
        return push(
            group_of(source, group), group_of(source, group),
            r.far_send.at[(step + 1) // 2, group, source // width],
            r.far_recv.at[group, source // width], pts=jnp.clip(z + step, 0, depth - 1) * width + y,
        )

    def side_copy(group, v, source):
        return push(
            group_of(source, group), group_of(source, group),
            r.side_send.at[group, v, source // width], r.side_recv.at[group, source],
            pts=z * width + v,
        )

    def pass_on(group, source, act):
        from_z = source // width

        @pl.when((z < depth - 1) & (from_z <= z))
        def _():
            copy = far_copy(group, source, 1)
            copy.start() if act == START else copy.wait_send()

        @pl.when((z > 0) & (from_z >= z))
        def _():
            copy = far_copy(group, source, -1)
            copy.start() if act == START else copy.wait_send()

        for v in others(y, width):
            copy = side_copy(group, v, source)
            copy.start() if act == START else copy.wait_send()

    def relay(group, away, act):
        for from_z in (z - away, z + away):

            @pl.when((from_z >= 0) & (from_z < depth))
            def _():
                source = from_z * width + y
                if act == START:
                    far_copy(group, source, 1).wait_recv()
                pass_on(group, source, act)

    ahead = 2
    for group in range(ahead):
        pass_on(group, me, START)

    points_gather = Gather(
        plan, lambda m: r.points_full.at[pl.ds(m * cols, cols)],
        r.points_net,
    )
    cot_gather = Gather(
        plan, lambda m: r.cot_full.at[pl.ds(m * cols, cols)],
        r.cot_net,
    )
    points_gather.start()
    r.cot_full[pl.ds(plane * cols, cols), :] = r.cot_rows[...].astype(F32).T.astype(BF)
    cot_gather.start()
    routes(plan, r, rows)

    @pl.when(me > 0)
    def _():
        push(
            r.points.at[:, 0:HALO], r.ext.at[:, 0:HALO], r.halo_send.at[0], r.halo_recv.at[0],
            pts=me - 1,
        ).wait_recv()

    @pl.when(me < pts - 1)
    def _():
        push(
            r.points.at[:, 0:HALO], r.ext.at[:, HALO + rows : 2 * HALO + rows], r.halo_send.at[1],
            r.halo_recv.at[1], pts=me + 1,
        ).wait_recv()

    def take(tap, carry):
        for tile in range(rows // TILE):
            hot = one_hot_window(r.ids, tap, tile)
            picked = dot(r.ext[:, tile * TILE : tile * TILE + WINDOW], hot).astype(BF)
            r.taken[pl.ds(tap, 1), :, tile * TILE : (tile + 1) * TILE] = picked[None]
        return carry

    steps = groups + depth - 2
    cuts = [min(TAPS, -(-TAPS * i // groups)) for i in range(steps + 1)]
    for step in range(steps):
        if step + ahead < groups:
            pass_on(step + ahead, me, START)
        if cuts[step] < cuts[step + 1]:
            lax.fori_loop(cuts[step], cuts[step + 1], take, 0)
        for away in range(1, depth):
            if 0 <= step + 1 - away < groups:
                relay(step + 1 - away, away, START)
    moves(START, r.taken_move)

    def complete(group):
        for u in others(y, width):
            for v in range(depth):
                side_copy(group, u, v * width + u).wait_recv()

    pair_gather = Gather(
        plan, lambda m: r.pair.at[m], r.pair_net
    )
    for group in range(conv_groups):
        complete(group)
        if group == 0:
            for i in range(2):
                r.pair[pl.ds(plane, 1), i] = r.blocks[:, i].reshape(1, C, cols)
            pair_gather.start()
        low = max(group * PACK - 2, 0)
        high = min(group * PACK - 2 + PACK, TAPS)
        if cols % 128 == 0:
            weight = jnp.concatenate(
                [r.blocks[:, t + 2].reshape(C, cols) for t in range(low, high)], 1
            )
            part = dot(weight, r.taken[low:high].reshape((high - low) * cols, rows))
        else:
            part = sum(dot(r.blocks[:, t + 2].reshape(C, cols), r.taken[t]) for t in range(low, high))
        if group == 0:
            r.acc[...] = part
            pair_gather.forward()
        else:
            r.acc[...] += part

    taps_copy = pltpu.make_async_copy(r.blocks.at[:, 2 : 2 + TAPS], r.taps_far, r.taps_sem)
    taps_copy.start()
    points_gather.forward()
    cot_gather.forward()
    r.parts[...] = r.acc[...].astype(BF).reshape(mdl, cols, rows)
    hidden_sum = Sum(plan, r.parts, r.sum_net)
    hidden_sum.start()
    for m in others(plane, mdl):
        vec_copy(m, m).wait_recv()
    for m in range(mdl):
        r.vec[m * cols : (m + 1) * cols, :] = r.vec_all[m].T
    pair_gather.finish()
    points_gather.finish()
    hidden_sum.middle()
    bias = r.vec[pl.ds(plane * cols, cols), 0:1]
    r.hidden[pl.ds(plane * cols, cols), :] = (hidden_sum.finish() + bias).astype(BF)
    Gather(
        plan, lambda m: r.hidden.at[pl.ds(m * cols, cols)],
        r.hidden_net,
    ).run()
    hidden = r.hidden[...]
    for m in range(mdl):
        r.acc[m * cols : (m + 1) * cols, :] = dot(r.pair[m, 0], hidden, TN)
    span_size = 128

    def norms(step, carry):
        span = pl.ds(pl.multiple_of(step * span_size, span_size), span_size)
        unit, inv_std = unit_columns(r.acc[:, span] + r.vec[:, 1:2])
        r.mixed_unit[:, span] = unit.astype(BF)
        r.mixed_std[:, span] = inv_std
        stream = r.points_full[:, span].astype(F32) + unit * r.vec[:, 2:3] + r.vec[:, 3:4]
        r.stream[:, span] = stream
        unit, inv_std = unit_columns(stream)
        r.one_unit[:, span] = unit.astype(BF)
        r.one_std[:, span] = inv_std
        r.normed[:, span] = (unit * r.vec[:, 4:5] + r.vec[:, 5:6]).astype(BF)
        return carry

    lax.fori_loop(0, rows // span_size, norms, 0)
    route = Route(plan, r.send_pos, r.arrival, r.slot_in, r.route_net)
    route.start(r.normed[pl.ds(plane * cols, cols), :])
    moves(START, r.hidden_move, r.mixed_unit_move, r.one_unit_move, r.stream_move, r.pair_move)
    for group in range(conv_groups, groups):
        complete(group)
    for i in range(r.rest.shape[0]):
        r.rest[i] = r.blocks[:, TAPS + 2 + i].reshape(C, cols)
    cot_gather.finish()
    moves(START, r.rest_move, r.cot_full_move)
    route.land()
    route.finish()
    moves(START, r.slot_in_move)

    @pl.when(me < pts - 1)
    def _():
        up_copy().wait_send()

    @pl.when(me > 0)
    def _():
        down_copy().wait_send()

    for m in others(plane, mdl):
        spread_copy(m, plane).wait_send()
        vec_copy(m, plane).wait_send()
    for group in range(groups):
        pass_on(group, me, WAIT)
        for away in range(1, depth):
            relay(group, away, WAIT)
    moves(WAIT, r.taken_move, r.cot_full_move, r.pair_move, r.hidden_move, r.mixed_unit_move, r.one_unit_move, r.stream_move, r.slot_in_move, r.rest_move)
    taps_copy.wait()


def front(plan, slots, weights, points, cot, vectors, ids, to_patch, from_patch, scan_lengths):
    rows, cols = points.shape
    pts, mdl = plan.pts, plan.mdl
    share = C // pts
    total = len(ORDER)
    groups = total // PACK
    vmem = pltpu.VMEM
    ring = Gather.semaphores(plan)
    scratch = dict(
        points_net=ring,
        cot_net=ring,
        pair_net=ring,
        hidden_net=ring,
        owned=vmem((mdl, plan.slots, share, cols), BF),
        points=vmem((cols, rows), BF),
        spread=vmem((total, share, cols), BF),
        vec_all=vmem((mdl,) + vectors.shape, F32),
        ext=vmem((cols, rows + 2 * HALO), BF),
        acc=vmem((C, rows), F32),
        parts=vmem((mdl, cols, rows), BF),
        normed=vmem((C, rows), BF),
        points_full=vmem((C, rows), BF),
        spread_send=dma(mdl),
        spread_recv=dma(mdl),
        vec_send=dma(mdl),
        vec_recv=dma(mdl),
        halo_send=dma(2),
        halo_recv=dma(2),
        blocks=vmem((pts, total, share, cols), BF),
        taps_sem=dma(),
        far_send=dma(2, groups, plan.depth),
        far_recv=dma(groups, plan.depth),
        side_send=dma(groups, plan.width, plan.depth),
        side_recv=dma(groups, pts),
        sum_net=(Sum.buffers(plan, (cols, rows))),
        route_net=Route.buffers(plan, cols, rows),
    )
    return call(
        functools.partial(front_kernel, plan),
        "front",
        5,
        dict(
            slots=slots, weights=weights, points_rows=points, cot_rows=cot, vectors=vectors,
            ids=ids, to_patch=to_patch, from_patch=from_patch, scan_lengths=scan_lengths,
        ),
        dict(
            taps_far=((pts, TAPS, share, cols), BF),
            taken=Late((TAPS, cols, rows), BF),
            cot_full=Late((C, rows), BF),
            pair=Late((mdl, 2, C, cols), BF),
            vec=((C, vectors.shape[0]), F32),
            hidden=Late((C, rows), BF),
            mixed_unit=Late((C, rows), BF),
            mixed_std=((1, rows), F32),
            stream=Late((C, rows), F32),
            one_unit=Late((C, rows), BF),
            one_std=((1, rows), F32),
            send_pos=((1, rows), jnp.int32),
            arrival=((1, rows), jnp.int32),
            group=((1, rows), jnp.int32),
            slot_in=Late((C, rows), BF),
            rest=Late((total - TAPS - 2, C, cols), BF),
        ),
        scratch,
        4 * TAPS * rows * (WINDOW + C) * cols,
        smem=("slots", "scan_lengths"),
        free=("taps_far",),
    )


def head_lanes(ext, cols, head):
    lane = lax.broadcasted_iota(jnp.int32, ext.shape, 1)
    return jnp.where((lane >= cols) | (lane // HD == head), ext, jnp.zeros_like(ext))


def head_rows(head):
    return pl.ds(pl.multiple_of(head * HD, HD), HD)


SPAN = 128


def over_spans(rows, body, size=SPAN):
    def step(index, carry):
        body(pl.ds(pl.multiple_of(index * size, size), size))
        return carry

    lax.fori_loop(0, rows // size, step, 0)


def beside(blocks):
    def times(right, cols):
        if cols % 128 == 0:
            return dot(jnp.concatenate(blocks, 1), right[...])
        return sum(
            dot(block, right[i * cols : (i + 1) * cols, :]) for i, block in enumerate(blocks)
        )

    return times


def mlp_part(plan, r):
    mdl = plan.mdl
    plane = lax.axis_index(MDL)
    cols, rows = r.cot.shape
    ff_blocks = FF // C
    own = pl.ds(plane * cols, cols)
    moves(WAIT, r.pair_move)
    r.acc[...] = beside([r.pair[m, 1] for m in range(mdl)])(r.attended_rows, cols)
    moves(WAIT, r.stream_move, r.cot_full_move)

    def norms(span):
        branch = (r.acc[:, span] + r.vec[:, 8:9]).astype(BF).astype(F32)
        two = r.stream[:, span] + branch
        r.two[:, span] = two
        unit, inv_std = unit_columns(two)
        r.two_unit[:, span] = unit
        r.two_std[:, span] = inv_std
        r.normed[:, span] = (unit * r.vec[:, 9:10] + r.vec[:, 10:11]).astype(BF)

    over_spans(rows, norms)
    for k in range(ff_blocks):
        part = slice(k * cols, (k + 1) * cols)
        r.pre[...] = dot(r.rest[3 + k], r.normed[...], TN) + r.vec[own, 11 + k : 12 + k]
        r.grad_act[...] = dot(r.rest[3 + ff_blocks + k], r.cot_full[...], TN)

        def bend(span):
            pre = r.pre[:, span]
            half = 0.5 * (1.0 + lax.erf(pre * 0.7071067811865476))
            r.act[part, span] = (pre * half).astype(BF)
            slope = half + pre * jnp.exp(-0.5 * pre * pre) * 0.3989422804014327
            r.grad_pre[part, span] = (r.grad_act[:, span] * slope).astype(BF)

        over_spans(rows, bend, 256)
    r.acc[...] = beside([r.rest[3 + k] for k in range(ff_blocks)])(r.grad_pre, cols)

    def stats(span):
        scaled = r.acc[:, span] * r.vec[:, 9:10]
        r.stats[pl.ds(plane, 1), 0:1, span] = jnp.sum(scaled, 0, keepdims=True)[None]
        r.stats[pl.ds(plane, 1), 1:2, span] = jnp.sum(scaled * r.two_unit[:, span], 0, keepdims=True)[None]

    over_spans(rows, stats)

    def stats_copy(m, slot):
        return push(
            r.stats.at[slot], r.stats.at[slot], r.stats_send.at[m], r.stats_recv.at[slot], mdl=m
        )

    for m in others(plane, mdl):
        stats_copy(m, plane).start()
    r.parts[...] = r.acc[...].astype(BF).reshape(mdl, cols, rows)
    shape = Sum.buffers(plan, (cols, rows))
    grad_sum = Sum(plan, r.parts, r.grad_net)
    grad_sum.start()
    out = beside([r.rest[3 + ff_blocks + k] for k in range(ff_blocks)])(r.act, cols)
    r.out_parts[...] = out.astype(BF).reshape(mdl, cols, rows)
    grad_sum.middle()
    out_sum = Sum(plan, r.out_parts, r.out_net)
    out_sum.start()
    for m in others(plane, mdl):
        stats_copy(m, m).wait_recv()
    mean = sum(r.stats[m, 0:1] for m in range(mdl)) / C
    cross = sum(r.stats[m, 1:2] for m in range(mdl)) / C
    cot = r.cot[...].astype(F32)
    grad_normed = grad_sum.finish()
    unit = r.two_unit[own, :]
    grad_two = cot + r.two_std[...] * (grad_normed * r.vec[own, 9:10] - mean - unit * cross)
    r.grad_two[...] = grad_two
    branch = grad_two.astype(BF)
    r.branch_full[own, :] = branch
    route = Route(plan, r.send_pos, r.arrival, r.grad_slot, r.in_route)
    route.start(branch)
    fetch(plan, r, 2, START)
    out_sum.middle()

    def along(values):
        return jnp.sum(values.astype(F32), 1, keepdims=True)

    r.mlp_sums[:, 0:1] = along(branch)
    r.mlp_sums[:, 1:2] = along(grad_normed * unit)
    r.mlp_sums[:, 2:3] = along(grad_normed)
    for k in range(ff_blocks):
        part = slice(k * cols, (k + 1) * cols)
        r.mlp_sums[:, 3 + k : 4 + k] = along(r.grad_pre[part, :])
        r.mlp_grads[k] = dot(r.normed[...], r.grad_pre[part, :], NT).astype(BF)
        r.mlp_grads[ff_blocks + k] = dot(r.cot_full[...], r.act[part, :], NT).astype(BF)
    r.mlp_sums[:, 3 + ff_blocks : 4 + ff_blocks] = along(cot)
    moves(START, r.grad_two_move)
    route.land()
    bias = r.vec[own, 11 + ff_blocks : 12 + ff_blocks]
    r.out[...] = (r.two[own, :] + out_sum.finish() + bias).T.astype(BF)
    route.finish()
    for m in others(plane, mdl):
        stats_copy(m, plane).wait_send()


def attend_part(plan, r):
    plane = lax.axis_index(MDL)
    rows, cols = r.values.shape
    heads = cols // HD
    group = column(r.group[...])
    lane = lax.broadcasted_iota(jnp.int32, (rows, cols), 1)
    same = lane == group
    slot_in = r.slot_in[...]
    queries = (dot(slot_in, r.rest[0], TN) + r.vectors[6:7, :]).astype(BF)
    r.q_ext[:, :cols] = queries * BF(HD ** (-0.5))
    r.q_ext[:, cols:] = jnp.where(same, 1.0, 0.0).astype(BF)
    r.k_ext[:, :cols] = dot(slot_in, r.rest[1], TN).astype(BF)
    r.k_ext[:, cols:] = jnp.where(same | (lane >= plan.groups), 0.0, -1e30).astype(BF)
    values = dot(slot_in, r.rest[2], TN) + r.vectors[7:8, :]
    r.values[...] = values.astype(BF)
    r.v_aug[:, :HD] = values.T.astype(BF).reshape(heads, HD, rows)
    r.v_aug[:, HD:] = jnp.ones((heads, HD, rows), BF)

    def one(head, carry):
        keys = r.k_ext[...]
        values_t = r.v_aug[pl.ds(head, 1)][0]
        for tile in range(rows // TILE):
            span = slice(tile * TILE, (tile + 1) * TILE)
            scores = dot(keys, head_lanes(r.q_ext[span, :], cols, head), NT)
            top = jnp.max(scores, 0, keepdims=True)
            soft = jnp.exp(scores - top).astype(BF)
            summed = dot(values_t, soft)
            total = summed[HD : HD + 1]
            r.attended[head_rows(head), span] = (summed[:HD] / total).astype(BF)
            r.lse[pl.ds(head, 1), :, span] = (top + jnp.log(total))[None]
        return carry

    route = Route(plan, r.arrival, r.send_pos, r.attended_rows, r.out_route)
    for i, trade in enumerate(route.trades):
        share = heads // route.PIECES
        lax.fori_loop(i * share, (i + 1) * share, one, 0)
        trade.start(r.attended[i * route.size : (i + 1) * route.size, :])
    fetch(plan, r, 1, START)
    route.land()
    route.finish()


def attend_back_part(plan, r):
    plane = lax.axis_index(MDL)
    rows, cols = r.values.shape
    heads = cols // HD
    greet(everyone(plan))
    mlp_count = r.mlp_grads.shape[0]
    reduce = Reduce(
        plan, r.reduce_net
    )
    for group in range(reduce.groups):
        for place in range(MLP_PACK):
            reduce.store(r.mlp_grads[group * MLP_PACK + place], group, place)
        reduce.start(group)
    branch_gather = Gather(
        plan, lambda m: r.branch_full.at[pl.ds(m * cols, cols)],
        r.branch_net,
    )
    branch_gather.start()
    fetch(plan, r, 3, START)
    grad_slot = r.grad_slot[...]
    grad_t = dot(r.pair[pl.ds(plane, 1), 1][0], grad_slot, TN).astype(BF).astype(F32)
    r.grad[...] = grad_t.T.astype(BF)
    weighed = grad_t * r.attended[...].astype(F32)
    r.inner[...] = jnp.sum(weighed.reshape(heads, HD, rows), 1, keepdims=True)
    r.keys_t[...] = r.k_ext[:, :cols].astype(F32).T.astype(BF)
    r.dk_acc[...] = jnp.zeros_like(r.dk_acc)
    r.dv_acc[...] = jnp.zeros_like(r.dv_acc)

    def one(head, carry):
        queries = head_lanes(r.q_ext[...], cols, head)
        pure = queries[:, :cols]
        grad = head_lanes(r.grad[...], cols, head)
        lse = r.lse[pl.ds(head, 1)][0]
        inner = r.inner[pl.ds(head, 1)][0]
        keys_t = r.keys_t[head_rows(head), :]
        dq = jnp.zeros((HD, rows), F32)
        for tile in range(rows // TILE):
            span = slice(tile * TILE, (tile + 1) * TILE)
            scores = dot(r.k_ext[span, :], queries, NT)
            soft = jnp.exp(scores - lse)
            grad_soft = dot(r.values[span, :], grad, NT)
            grad_scores = (soft * (grad_soft - inner)).astype(BF)
            r.dv_acc[span, :] += dot(soft.astype(BF), grad)
            r.dk_acc[span, :] += dot(grad_scores, pure)
            dq = dq + dot(keys_t[:, span], grad_scores)
        r.dq[head_rows(head), :] = (dq * HD ** (-0.5)).astype(BF)
        reduce.step(head - delay)
        return carry

    delay = max(heads - reduce.steps, 0)
    lax.fori_loop(0, heads, one, 0)
    for s in range(heads - delay, reduce.steps):
        reduce.step(s)
    branch_gather.forward()
    dk = r.dk_acc[...].astype(BF)
    dv = r.dv_acc[...].astype(BF)
    back = dot(r.rest[0], r.dq[...]) + dot(r.rest[1], dk, NT) + dot(r.rest[2], dv, NT)
    r.back_parts[...] = back.astype(BF).reshape(plan.mdl, cols, rows)
    back_sum = Sum(plan, r.back_parts, r.sum_net)
    back_sum.start()
    r.attend_grads[0] = dot(r.slot_in[...], r.dq[...], NT).astype(BF)
    r.attend_grads[1] = dot(r.slot_in[...], dk).astype(BF)
    back_sum.middle()
    r.attend_grads[2] = dot(r.slot_in[...], dv).astype(BF)
    r.attend_grads[3] = dot(r.grad_slot[...], r.attended[...], NT).astype(BF)
    route = Route(plan, r.arrival, r.send_pos, r.grad_normed, r.back_route)
    route.start(back_sum.finish().astype(BF))
    moves(START, r.attend_grads_move)
    r.attend_sums[...] = jnp.zeros_like(r.attend_sums)
    r.attend_sums[:, 0:1] = jnp.sum(r.dq[...].astype(F32), 1, keepdims=True)
    r.attend_sums[:, 1:2] = jnp.sum(dv.astype(F32), 0, keepdims=True).T
    route.land()
    branch_gather.finish()
    moves(START, r.branch_full_move)
    route.finish()
    reduce.finish(r.mlp_summed)
    reduce.end()


MLP_PACK = 4


MLP_PACK = 4


def fetch(plan, r, place, act):
    source = (r.left32, r.right32, r.first32, r.second32)[place]
    whole = (r.left_whole, r.right_whole, r.first_whole, r.second_whole)[place]
    if act == START:
        moves(WAIT, (r.left32_move, r.right32_move, r.first32_move, r.second32_move)[place])
        r.low[place] = source[...].astype(BF)
    fetch_copies(plan, r.low.at[place], whole, r.fetch_net[place], act)


def middle_kernel(plan, r):
    moves(START, r.left32_move, r.pair_move, r.stream_move, r.cot_full_move)
    moves(START, r.right32_move, r.first32_move, r.second32_move)
    greet(everyone(plan))
    fetch(plan, r, 0, START)
    r.cot[...] = r.cot_rows[...].astype(F32).T.astype(BF)
    attend_part(plan, r)
    mlp_part(plan, r)
    attend_back_part(plan, r)
    for place in range(4):
        fetch(plan, r, place, WAIT)
    moves(WAIT, r.grad_two_move, r.attend_grads_move, r.branch_full_move)


def middle(plan, first, vectors, cot, left, right, moment, second):
    rows, cols = cot.shape
    ff_blocks = FF // C
    heads = cols // HD
    vmem = pltpu.VMEM
    whole = (fetch_shape(plan, left).shape, BF)
    route = Route.buffers(plan, cols, rows)
    total = Sum.buffers(plan, (cols, rows))
    return call(
        functools.partial(middle_kernel, plan),
        "middle",
        2,
        dict(
            slot_in=first.slot_in, rest=first.rest, vectors=vectors, group=first.group,
            send_pos=first.send_pos, arrival=first.arrival, vec=first.vec, cot_rows=cot,
            pair=Late(first.pair), stream=Late(first.stream), cot_full=Late(first.cot_full),
            left32=Late(left), right32=Late(right), first32=Late(moment), second32=Late(second),
        ),
        dict(
            left_whole=whole,
            right_whole=whole,
            first_whole=whole,
            second_whole=whole,
            grad_two=Late((cols, rows), F32),
            out=((rows, cols), BF),
            mlp_sums=((cols, 4 + ff_blocks), F32),
            grad_normed=((C, rows), BF),
            attend_grads=Late((4, C, cols), BF),
            attend_sums=((cols, 8), F32),
            branch_full=Late((C, rows), BF),
            mlp_summed=((2 * ff_blocks, C // plan.pts, cols), BF),
        ),
        dict(
            low=vmem((4,) + left.shape, BF),
            q_ext=vmem((rows, 2 * cols), BF),
            k_ext=vmem((rows, 2 * cols), BF),
            values=vmem((rows, cols), BF),
            attended=vmem((cols, rows), BF),
            lse=vmem((heads, 1, rows), F32),
            attended_rows=vmem((C, rows), BF),
            v_aug=vmem((heads, 2 * HD, rows), BF),
            cot=vmem((cols, rows), BF),
            acc=vmem((C, rows), F32),
            two=vmem((C, rows), F32),
            two_unit=vmem((C, rows), F32),
            two_std=vmem((1, rows), F32),
            normed=vmem((C, rows), BF),
            pre=vmem((cols, rows), F32),
            grad_act=vmem((cols, rows), F32),
            act=vmem((ff_blocks * cols, rows), BF),
            grad_pre=vmem((ff_blocks * cols, rows), BF),
            stats=vmem((plan.mdl, 8, rows), F32),
            stats_send=dma(plan.mdl),
            stats_recv=dma(plan.mdl),
            parts=vmem((plan.mdl, cols, rows), BF),
            out_parts=vmem((plan.mdl, cols, rows), BF),
            grad_slot=vmem((C, rows), BF),
            mlp_grads=vmem((2 * ff_blocks, C, cols), BF),
            grad=vmem((rows, cols), BF),
            inner=vmem((heads, 1, rows), F32),
            keys_t=vmem((cols, rows), BF),
            dk_acc=vmem((rows, cols), F32),
            dv_acc=vmem((rows, cols), F32),
            dq=vmem((cols, rows), BF),
            back_parts=vmem((plan.mdl, cols, rows), BF),
            grad_net=total,
            out_net=total,
            sum_net=total,
            out_route=route,
            in_route=route,
            back_route=route,
            branch_net=Gather.semaphores(plan),
            reduce_net=Reduce.buffers(plan, 2 * ff_blocks, MLP_PACK, cols),
            fetch_net=[fetch_sems(plan)] * 4,
        ),
        14 * heads * rows * rows * cols + 16 * rows * C * cols * ff_blocks,
        free=("left_whole", "right_whole", "first_whole", "second_whole"),
    )


BACK_ORDER = [TAPS + 1, TAPS + 2, TAPS + 3, TAPS + 4, TAPS] + list(range(TAPS))
MLP_ORDER = list(range(TAPS + 5, TAPS + 5 + 2 * FF // C))
BACK_PACK = 4


def back_kernel(plan, r):
    pts = plan.pts
    cols, rows = r.turn_acc.shape
    taps = r.taken.shape[0]
    ready = r.attend_grads.shape[0]
    extra = ready + 1
    me, plane = lax.axis_index(PTS), lax.axis_index(MDL)
    own_cols = pl.ds(plane * cols, cols)
    middle = slice(HALO, HALO + rows)
    first = (r.grad_normed_move, r.one_unit_move, r.branch_full_move, r.mixed_unit_move, r.pair_move)
    second = (r.hidden_move, r.taken_move, r.grad_two_move, r.taps_move)
    moves(START, *first, *second)
    greet([{PTS: v} for v in others(me, pts)] + [{MDL: plane + 1 - 2 * lax.rem(plane, 2)}])
    reduce = Reduce(
        plan, r.reduce_net
    )
    groups = reduce.groups
    for b in range(ready):
        reduce.store(r.attend_grads[b], b // BACK_PACK, b % BACK_PACK)
    reduce.start(0)
    moves(WAIT, *first)

    def grads(group):
        if group == ready // BACK_PACK:
            reduce.store(dot(r.hidden[...], r.mixed[own_cols, :], NT), group, ready % BACK_PACK)

        def one(place, carry):
            tap = group * BACK_PACK + place - extra
            reduce.store(
                dot(r.back[:, middle], r.taken[pl.ds(tap, 1)][0], NT), group, place
            )
            return carry

        low = max(group * BACK_PACK, extra)
        lax.fori_loop(low - group * BACK_PACK, BACK_PACK, one, 0)

    def norms(span):
        grad = r.grad_normed[:, span].astype(F32) * r.vec[:, 4:5]
        unit = r.one_unit[:, span].astype(F32)
        delta = r.one_std[:, span] * (
            grad
            - jnp.sum(grad, 0, keepdims=True) / C
            - unit * (jnp.sum(grad * unit, 0, keepdims=True) / C)
        )
        r.delta[:, span] = delta
        grad = (r.branch_full[:, span].astype(F32) + delta) * r.vec[:, 2:3]
        unit = r.mixed_unit[:, span].astype(F32)
        r.mixed[:, span] = (
            r.mixed_std[:, span]
            * (
                grad
                - jnp.sum(grad, 0, keepdims=True) / C
                - unit * (jnp.sum(grad * unit, 0, keepdims=True) / C)
            )
        ).astype(BF)

    over_spans(rows, norms)
    back = beside([r.pair[m, 0] for m in range(plan.mdl)])(r.mixed, cols)
    r.back[:, middle] = back.astype(BF)

    core = lax.rem(plane, 2)
    mine = pl.ds(core * (C // 2), C // 2)
    low_end, high_end = slice(0, HALO), slice(HALO + rows, 2 * HALO + rows)

    def up_copy(target):
        return push(
            r.back.at[mine, rows : rows + HALO], r.back.at[mine, low_end], r.halo_send.at[0],
            r.halo_recv.at[0], pts=target,
        )

    def down_copy(target):
        return push(
            r.back.at[mine, HALO : 2 * HALO], r.back.at[mine, high_end],
            r.halo_send.at[1], r.halo_recv.at[1], pts=target,
        )

    def core_copy(end, which, part):
        half = pl.ds(part * (C // 2), C // 2)
        return push(
            r.back.at[half, end], r.back.at[half, end], r.core_send.at[which],
            r.core_recv.at[which], mdl=plane + 1 - 2 * core,
        )

    @pl.when(me < pts - 1)
    def _():
        up_copy(me + 1).start()

    @pl.when(me == pts - 1)
    def _():
        r.back[:, HALO + rows :] = jnp.zeros((C, HALO), BF)

    @pl.when(me > 0)
    def _():
        down_copy(me - 1).start()

    @pl.when(me == 0)
    def _():
        r.back[:, :HALO] = jnp.zeros((C, HALO), BF)

    moves(WAIT, *second)
    for group in range(1, groups):
        grads(group)
        reduce.start(group)
        if group >= LAG:
            reduce.step(group - LAG)

    grad_one = r.grad_two[...] + r.delta[own_cols, :]
    r.grad_one[...] = grad_one

    def along(values):
        return jnp.sum(values.astype(F32), 1, keepdims=True)

    grad_normed = r.grad_normed[own_cols, :].astype(F32)
    columns = [
        along(r.back[own_cols, middle]),
        along(r.mixed[own_cols, :]),
        along(grad_one * r.mixed_unit[own_cols, :]),
        along(grad_one),
        along(grad_normed * r.one_unit[own_cols, :]),
        along(grad_normed),
        r.attend_sums[:, 0:2],
        r.mlp_sums[...],
    ]
    r.vectors[pl.ds(me, 1)] = jnp.concatenate(columns, 1).T[None]

    def vector_copy(p, slot):
        return push(
            r.vectors.at[slot], r.vectors.at[slot], r.vector_send.at[p], r.vector_recv.at[slot],
            pts=p,
        )

    for p in others(me, pts):
        vector_copy(p, me).start()

    @pl.when(me > 0)
    def _():
        up_copy(me - 1).wait_recv()
        core_copy(low_end, 0, core).start()

    @pl.when(me < pts - 1)
    def _():
        down_copy(me + 1).wait_recv()
        core_copy(high_end, 1, core).start()

    @pl.when(me > 0)
    def _():
        core_copy(low_end, 0, 1 - core).wait_recv()

    @pl.when(me < pts - 1)
    def _():
        core_copy(high_end, 1, 1 - core).wait_recv()

    def turn(tap, carry):
        weight = r.taps[:, pl.ds(taps - 1 - tap, 1)].reshape(C, cols)
        turned = dot(weight, r.back[...], TN).astype(BF)
        for tile in range(rows // TILE):
            hot = one_hot_window(r.ids, tap, tile)
            r.turn_acc[:, tile * TILE : (tile + 1) * TILE] += dot(
                turned[:, tile * TILE : tile * TILE + WINDOW], hot
            )
        return carry

    r.turn_acc[...] = jnp.zeros_like(r.turn_acc)
    left = list(range(groups - LAG, reduce.steps))
    cuts = [taps * i // len(left) for i in range(len(left) + 1)]
    for i, s in enumerate(left):
        lax.fori_loop(cuts[i], cuts[i + 1], turn, 0)
        reduce.step(s)
    r.point_grad[...] = (r.turn_acc[...] + r.grad_one[...]).T
    reduce.finish(r.summed)
    total = r.vectors[pl.ds(me, 1)][0]
    for p in others(me, pts):
        vector_copy(p, p).wait_recv()
        total = total + r.vectors[pl.ds(p, 1)][0]
    r.vector_grad[...] = total
    reduce.end()
    for p in others(me, pts):
        vector_copy(p, me).wait_send()

    @pl.when(me < pts - 1)
    def _():
        up_copy(me + 1).wait_send()
        core_copy(high_end, 1, core).wait_send()

    @pl.when(me > 0)
    def _():
        down_copy(me - 1).wait_send()
        core_copy(low_end, 0, core).wait_send()


LAG = 2


def back_pass(
    plan, first, ids, grad_normed, branch_full, grad_two, attend_grads, mlp_sums, attend_sums
):
    taps, cols, rows = first.taken.shape
    total = len(BACK_ORDER)
    share = C // plan.pts
    vmem = pltpu.VMEM
    return call(
        functools.partial(back_kernel, plan),
        "back_pass",
        1,
        dict(
            taken=Late(first.taken), pair=Late(first.pair), vec=first.vec, hidden=Late(first.hidden), mixed_unit=Late(first.mixed_unit), mixed_std=first.mixed_std, one_unit=Late(first.one_unit), one_std=first.one_std, taps=Late(first.taps_far), ids=ids,
            grad_normed=Late(grad_normed),
            branch_full=Late(branch_full), grad_two=Late(grad_two), attend_grads=attend_grads, mlp_sums=mlp_sums, attend_sums=attend_sums,
        ),
        dict(
            summed=((total, share, cols), BF),
            point_grad=((rows, cols), F32),
            vector_grad=((12 + FF // C, cols), F32),
        ),
        dict(
            reduce_net=(Reduce.buffers(plan, total, BACK_PACK, cols)),
            turn_acc=vmem((cols, rows), F32),
            grad_one=vmem((cols, rows), F32),
            delta=vmem((C, rows), F32),
            mixed=vmem((C, rows), BF),
            back=vmem((C, rows + 2 * HALO), BF),
            vectors=vmem((plan.pts, 12 + FF // C, cols), F32),
            halo_send=dma(2),
            halo_recv=dma(2),
            core_send=dma(2),
            core_recv=dma(2),
            vector_send=dma(plan.pts),
            vector_recv=dma(plan.pts),
        ),
        taps * rows * (WINDOW * 4 + 5 * C) * cols,
    )


def adam(first, second, grad):
    new_first = BETA_ONE * first + (1.0 - BETA_ONE) * grad
    new_second = BETA_TWO * second + (1.0 - BETA_TWO) * grad * grad
    direction = (
        new_first
        / (1.0 - BETA_ONE**STEP)
        / (jnp.sqrt(new_second / (1.0 - BETA_TWO**STEP)) + ADAM_EPS)
    )
    return new_first, new_second, direction


def owner_kernel(plan, r):
    pts, mdl, slots = plan.pts, plan.mdl, plan.slots
    share, cols = r.summed.shape[1:]
    me, plane = lax.axis_index(PTS), lax.axis_index(MDL)
    moves(START, r.left_move, r.right_move, r.first_move, r.second_move)
    greet(
        [
            {PTS: p, MDL: m}
            for i, p in enumerate([me] + others(me, pts))
            for j, m in enumerate([plane] + others(plane, mdl))
            if i + j > 0
        ]
    )

    count = r.summed.shape[0]
    r.listed[:count] = r.summed[...]
    r.listed[count:] = r.mlp_summed[...]

    def order(slot, carry):
        r.grads[pl.ds(slot, 1)] = r.listed[pl.ds(r.places[slot], 1)]
        return carry

    def whole_copy(j, step):
        m = lax.rem(plane + step, mdl)
        target, k = plan.worker(j), j // pts
        piece, spot = r.grads.at[m * slots + j], r.whole.at[k, me, plane]

        def near():
            return pltpu.make_async_copy(piece, spot, r.whole_here.at[k])

        def far():
            return push(
                piece, spot, r.whole_send.at[step, j], r.whole_recv.at[k, me, plane], pts=target,
                mdl=m,
            )

        return (me == target) & (step == 0), near, far

    def rows_copy(m, slot):
        return push(
            r.grads.at[pl.ds(m * slots, slots)], r.rows.at[slot], r.rows_send.at[m],
            r.rows_recv.at[slot], mdl=m,
        )

    def rows_here():
        return pltpu.make_async_copy(
            r.grads.at[pl.ds(plane * slots, slots)], r.rows.at[plane], r.rows_home
        )

    for step in range(mdl):
        m = lax.rem(plane + step, mdl)
        lax.fori_loop(m * slots, (m + 1) * slots, order, 0)
        for j in range(slots):
            home, near, far = whole_copy(j, step)

            @pl.when(home)
            def _():
                near().start()

            @pl.when(jnp.logical_not(home))
            def _():
                far().start()

    for m in others(plane, mdl):
        rows_copy(m, plane).start()
    rows_here().start()
    moves(WAIT, r.left_move, r.right_move, r.first_move, r.second_move)

    def result_copy(k, kind, p):
        return push(
            r.turned.at[k, kind, p], r.results.at[plan.work(me, k), kind], r.back_send.at[k, kind, p],
            r.back_recv.at[plan.work(me, k), kind], pts=p,
        )

    def result_here(k, kind):
        return pltpu.make_async_copy(
            r.turned.at[k, kind, me], r.results.at[plan.work(me, k), kind], r.back_home.at[k, kind]
        )

    def send_result(k, kind, value):
        r.turned[k, kind] = value.astype(BF).reshape(pts, share, C)
        for p in others(me, pts):
            result_copy(k, kind, p).start()
        result_here(k, kind).start()

    for k in range(plan.each):

        @pl.when(plan.work(me, k) < slots)
        def _():
            pltpu.make_async_copy(
                r.grads.at[0], r.whole.at[k, me, plane], r.whole_here.at[k]
            ).wait()
            for p_step in range(pts):
                for m_step in range(mdl):
                    if p_step + m_step > 0:
                        p, m = lax.rem(me + p_step, pts), lax.rem(plane + m_step, mdl)
                        push(
                            r.grads.at[0], r.whole.at[k, p, m], r.whole_send.at[0, 0],
                            r.whole_recv.at[k, p, m], pts=p, mdl=m,
                        ).wait_recv()
            left = r.left[k].reshape(C, C)
            right = r.right[k].reshape(C, C)
            halves = [
                dot(left, r.whole[k, :, m].reshape(C, cols), TN).astype(BF) for m in range(mdl)
            ]
            if cols % 128 == 0:
                rotated = dot(jnp.concatenate(halves, 1), right)
            else:
                rotated = sum(
                    dot(half, right[m * cols : (m + 1) * cols]) for m, half in enumerate(halves)
                )
            send_result(k, 0, rotated)
            _, _, direction = adam(
                r.first[k].reshape(C, C).astype(F32),
                r.second[k].reshape(C, C).astype(F32),
                rotated.astype(BF).astype(F32),
            )
            send_result(k, 1, dot(left, dot(direction.astype(BF), right, NT).astype(BF)))

    for m in others(plane, mdl):
        rows_copy(m, plane).wait_send()
        rows_copy(m, m).wait_recv()
    rows_here().wait()
    for j in range(slots):
        source, k = plan.worker(j), j // pts
        for kind in range(2):

            @pl.when(me != source)
            def _():
                push(
                    r.turned.at[k, kind, me], r.results.at[j, kind], r.back_send.at[k, kind, source],
                    r.back_recv.at[j, kind], pts=source,
                ).wait_recv()

    for k in range(plan.each):

        @pl.when(plan.work(me, k) < slots)
        def _():
            for kind in range(2):
                result_here(k, kind).wait()
                for p in others(me, pts):
                    result_copy(k, kind, p).wait_send()

    for step in range(mdl):
        for j in range(slots):
            home, near, far = whole_copy(j, step)

            @pl.when(jnp.logical_not(home))
            def _():
                far().wait_send()


def owner_update(plan, places, summed, mlp_summed, left, right, first, second):
    _, share, cols = summed.shape
    blocks = len(BACK_ORDER) + len(MLP_ORDER)
    pts, mdl, each, slots = plan.pts, plan.mdl, plan.each, plan.slots
    vmem = pltpu.VMEM
    return call(
        functools.partial(owner_kernel, plan),
        "owner_update",
        4,
        dict(places=places, summed=summed, mlp_summed=mlp_summed, left=Late(left), right=Late(right), first=Late(first), second=Late(second)),
        dict(
            rows=((mdl, slots, share, cols), BF),
            results=((slots, 2, share, C), BF),
        ),
        dict(
            grads=vmem((blocks, share, cols), BF),
            listed=vmem((blocks, share, cols), BF),
            whole=vmem((each, pts, mdl, share, cols), BF),
            turned=vmem((each, 2, pts, share, C), BF),
            whole_send=dma(mdl, slots),
            whole_recv=dma(each, pts, mdl),
            whole_here=dma(each),
            rows_send=dma(mdl),
            rows_recv=dma(mdl),
            rows_home=dma(),
            back_send=dma(each, 2, pts),
            back_recv=dma(slots, 2),
            back_home=dma(each, 2),
        ),
        8 * each * C * C * C,
        smem=("places",),
    )


def scan_index(row_ids, scan_lengths):
    bounds = jnp.cumsum(scan_lengths)
    return jnp.sum((row_ids[..., None] >= bounds[:-1]).astype(jnp.int32), -1)


def local(
    points,
    cotangent,
    neighbours,
    scan_lengths,
    to_patch,
    from_patch,
    owner_slot,
    weights,
    row_eigen_basis,
    right_basis,
    first_moment,
    second_moment,
    vectors,
    vector_first,
    vector_second,
):
    rows, cols = points.shape
    slot_count = from_patch.shape[0]
    pts = lax.axis_size(PTS)
    mdl = lax.axis_size(MDL)
    pts_index = lax.axis_index(PTS)
    patch_count = slot_count // PATCH
    matrix_rate = 1.6 * C ** (-0.5)
    plan = Layout(pts, mdl, owner_slot.shape[0], patch_count * scan_lengths.shape[0])

    row_ids = pts_index * rows + jnp.arange(rows, dtype=jnp.int32)
    own_scan = scan_index(row_ids, scan_lengths)
    near = neighbours.T
    usable = (near >= 0) & (scan_index(jnp.maximum(near, 0), scan_lengths) == own_scan[None, :])
    ids = jnp.where(usable, near - (pts_index * rows - HALO), -1)

    first = front(
        plan,
        owner_slot,
        weights,
        points,
        cotangent,
        vectors,
        ids,
        to_patch[None],
        from_patch[None],
        scan_lengths,
    )
    between = middle(
        plan, first, vectors, cotangent, row_eigen_basis, right_basis, first_moment, second_moment
    )
    last = back_pass(
        plan,
        first,
        ids,
        between.grad_normed,
        between.branch_full,
        between.grad_two,
        between.attend_grads,
        between.mlp_sums,
        between.attend_sums,
    )
    vector_grad = last.vector_grad
    listed = BACK_ORDER + MLP_ORDER
    places = jnp.array([listed.index(b) for b in range(len(listed))], jnp.int32)
    slot_ids = jnp.arange(len(listed), dtype=jnp.int32)
    place_of_slot = jnp.sum(
        jnp.where(owner_slot[None, :] == slot_ids[:, None], places[None, :], 0), 1
    )
    ended = owner_update(
        plan,
        place_of_slot,
        last.summed,
        between.mlp_summed,
        between.left_whole,
        between.right_whole,
        between.first_whole,
        between.second_whole,
    )
    reduced = ended.rows.transpose(1, 2, 0, 3).reshape(plan.slots, C // pts, C)
    results = ended.results
    rotated, update = results[:, 0].astype(F32), results[:, 1].astype(F32)
    new_first, new_second, _ = adam(first_moment, second_moment, rotated)
    new_weights = weights - matrix_rate * (update + MATRIX_DECAY * weights)
    new_vector_first, new_vector_second, vector_step = adam(
        vector_first, vector_second, vector_grad
    )
    new_vectors = vectors - VECTOR_RATE * vector_step
    return (
        between.out,
        last.point_grad,
        reduced.astype(F32),
        new_first,
        new_second,
        new_weights,
        new_weights.astype(BF),
        vector_grad,
        new_vector_first,
        new_vector_second,
        new_vectors,
    )


def solution(mesh):
    by_rows = P(PTS, MDL)
    owned = P(MDL, PTS, None)
    vector = P(None, MDL)
    return jax.shard_map(
        local,
        mesh=mesh,
        in_specs=(
            by_rows,
            by_rows,
            P(PTS, None),
            P(),
            P(PTS),
            P(PTS),
            P(),
            owned,
            owned,
            owned,
            owned,
            owned,
            vector,
            vector,
            vector,
        ),
        out_specs=(
            by_rows,
            by_rows,
            owned,
            owned,
            owned,
            owned,
            owned,
            vector,
            vector,
            vector,
            vector,
        ),
        check_vma=False,
    )
```

```python
import functools
import types

import jax
import jax.numpy as jnp
from jax import lax
from jax.experimental import pallas as pl
from jax.experimental.pallas import tpu as pltpu
from jax.sharding import PartitionSpec as P

C = 512
HD = 16
FF = 2048
TAPS = 27
HALO = 256
PATCH = 1024
STEP = 5

NORM_EPS = 1e-05
BETA_ONE = 0.9
BETA_TWO = 0.999
ADAM_EPS = 1e-08
VECTOR_RATE = 0.5
MATRIX_DECAY = 0.05
TILE = 256
WINDOW = TILE + 2 * HALO
BF = jnp.bfloat16
F32 = jnp.float32
VMEM_LIMIT = 58 * 1024 * 1024

NN = (((1,), (0,)), ((), ()))
NT = (((1,), (1,)), ((), ()))
TN = (((0,), (0,)), ((), ()))


def dot(a, b, dims=NN):
    return lax.dot_general(a, b, dims, preferred_element_type=F32)


def params(**kw):
    return pltpu.CompilerParams(vmem_limit_bytes=VMEM_LIMIT, **kw)


MESH = pl.DeviceIdType.MESH
PTS, MDL = "pts", "mdl"
START, WAIT = range(2)


def push(src, dst, send_sem, recv_sem, **target):
    return pltpu.make_async_remote_copy(
        src_ref=src,
        dst_ref=dst,
        send_sem=send_sem,
        recv_sem=recv_sem,
        device_id=target,
        device_id_type=MESH,
    )


def greet(peers):
    barrier = pltpu.get_barrier_semaphore()
    for peer in peers:
        pl.semaphore_signal(barrier, inc=1, device_id=peer, device_id_type=MESH)
    pl.semaphore_wait(barrier, len(peers))


def others(index, size):
    return [lax.rem(index + step, size) for step in range(1, size)]


class Layout:
    def __init__(self, pts, mdl, blocks, groups):
        self.pts, self.mdl, self.groups = pts, mdl, groups
        self.slots = blocks // mdl
        self.each = -(-self.slots // pts)
        self.shift = max(pts - self.slots, 0) // 2 if self.slots < pts else (pts - self.slots % pts) // 2
        self.width = mdl // 2 if pts % (mdl // 2) == 0 else 1
        self.depth = pts // self.width

    def worker(self, j):
        return (j + self.shift) % self.pts

    def work(self, me, k):
        return lax.rem(me + self.pts - self.shift, self.pts) + k * self.pts


def fetch_copies(plan, src, dst, sems, act):
    send, recv, here = sems
    me = lax.axis_index(PTS)
    for j in range(plan.slots):
        target, k = plan.worker(j), j // plan.pts

        @pl.when(me != target)
        def _():
            copy = push(src.at[j], dst.at[k, me], send.at[j], recv.at[k, me], pts=target)
            copy.start() if act == START else copy.wait_send()

        @pl.when(me == target)
        def _():
            copy = pltpu.make_async_copy(src.at[j], dst.at[k, me], here.at[k])
            if act == START:
                copy.start()
            else:
                copy.wait()
                for source in others(me, plan.pts):
                    push(
                        src.at[j], dst.at[k, source], send.at[j], recv.at[k, source], pts=source
                    ).wait_recv()


def fetch_sems(plan):
    return [dma(plan.slots), dma(plan.each, plan.pts), dma(plan.each)]


def fetch_shape(plan, src):
    return jax.ShapeDtypeStruct((plan.each, plan.pts) + src.shape[1:], BF)


class Late:
    def __init__(self, *what):
        self.what = what


def call(kernel, name, collective, inputs, outputs, scratch, flops, smem=(), free=()):
    vmem = pltpu.VMEM
    leaves, tree = jax.tree.flatten(scratch, is_leaf=lambda x: not isinstance(x, (dict, list)))
    late_in = [key for key, value in inputs.items() if isinstance(value, Late)]
    late_out = [key for key, value in outputs.items() if isinstance(value, Late)]
    values = {key: v.what[0] if key in late_in else v for key, v in inputs.items()}
    shapes = {key: v.what if key in late_out else v for key, v in outputs.items()}
    near = [vmem(values[key].shape, values[key].dtype) for key in late_in]
    near += [vmem(*shapes[key]) for key in late_out]
    late = late_in + late_out

    def space(key, value):
        return pltpu.SMEM if key in smem else pl.ANY if key in free or key in late else vmem

    def grouped(x):
        if isinstance(x, dict):
            return types.SimpleNamespace(**{key: grouped(value) for key, value in x.items()})
        return [grouped(value) for value in x] if isinstance(x, list) else x

    def body(*refs):
        count = len(inputs) + len(outputs)
        given = dict(zip(inputs, refs))
        given.update(zip(outputs, refs[len(inputs) : count]))
        own, sems = refs[count : count + len(late)], refs[count + len(late) : count + 2 * len(late)]
        r = grouped(jax.tree.unflatten(tree, refs[count + 2 * len(late) :]))
        for key, ref in given.items():
            setattr(r, key, ref)
        for key, ref, sem in zip(late, own, sems):
            pair = (given[key], ref) if key in late_in else (ref, given[key])
            setattr(r, key, ref)
            setattr(r, key + "_move", functools.partial(pltpu.make_async_copy, *pair, sem))
        kernel(r)

    results = pl.pallas_call(
        body,
        in_specs=[pl.BlockSpec(memory_space=space(*item)) for item in inputs.items()],
        out_specs=[pl.BlockSpec(memory_space=space(*item)) for item in outputs.items()],
        out_shape=[jax.ShapeDtypeStruct(*shape) for shape in shapes.values()],
        scratch_shapes=near + [dma() for _ in late] + leaves,
        compiler_params=params(collective_id=collective, has_side_effects=True),
        cost_estimate=pl.CostEstimate(
            flops=flops, bytes_accessed=20000000, transcendentals=1000000
        ),
        name=name,
    )(*values.values())
    return types.SimpleNamespace(**dict(zip(outputs, results)))


def moves(act, *copies):
    for make in copies:
        copy = make()
        copy.start() if act == START else copy.wait()


def dma(*shape):
    return pltpu.SemaphoreType.DMA(shape)


class Gather:
    def __init__(self, plan, part, sems):
        self.part, self.sems = part, sems
        self.plane = lax.axis_index(MDL)
        self.size = plan.mdl // 2
        self.x, self.core = self.plane // 2, lax.rem(self.plane, 2)

    @staticmethod
    def semaphores(plan):
        return dict(x_send=dma(plan.mdl // 2), recv=dma(plan.mdl), core_send=dma(plan.mdl // 2))

    def along(self, m, target, send):
        return push(self.part(m), self.part(m), send, self.sems.recv.at[m], mdl=target)

    def x_copy(self, x):
        return self.along(self.plane, x * 2 + self.core, self.sems.x_send.at[x])

    def core_copy(self, x):
        return self.along(
            x * 2 + self.core, self.x * 2 + 1 - self.core, self.sems.core_send.at[x]
        )

    def arrived(self, m):
        self.along(m, m, self.sems.x_send.at[0]).wait_recv()

    def start(self):
        for x in others(self.x, self.size):
            self.x_copy(x).start()
        self.core_copy(self.x).start()

    def forward(self):
        for x in others(self.x, self.size):
            self.arrived(x * 2 + self.core)
            self.core_copy(x).start()

    def finish(self):
        for x in [self.x] + others(self.x, self.size):
            self.arrived(x * 2 + 1 - self.core)
        for x in others(self.x, self.size):
            self.x_copy(x).wait_send()
            self.core_copy(x).wait_send()
        self.core_copy(self.x).wait_send()

    def run(self):
        self.start()
        self.forward()
        self.finish()


class Sum:
    def __init__(self, plan, parts, bufs):
        self.parts, self.bufs = parts, bufs
        self.plane = lax.axis_index(MDL)
        self.size = plan.mdl // 2
        self.x, self.core = self.plane // 2, lax.rem(self.plane, 2)

    @staticmethod
    def buffers(plan, shape):
        x = plan.mdl // 2
        vmem = pltpu.VMEM((x,) + shape, BF)
        return dict(
            near=vmem, middle=vmem, far=vmem,
            near_send=dma(x), near_recv=dma(x), far_send=dma(x), far_recv=dma(x),
        )

    def near_copy(self, x):
        b = self.bufs
        return push(
            self.parts.at[x * 2 + 1 - self.core], b.near.at[x], b.near_send.at[x],
            b.near_recv.at[x], mdl=self.x * 2 + 1 - self.core,
        )

    def far_copy(self, x, slot):
        b = self.bufs
        return push(
            b.middle.at[x], b.far.at[slot], b.far_send.at[x], b.far_recv.at[slot],
            mdl=x * 2 + self.core,
        )

    def both(self, x):
        self.near_copy(x).wait_recv()
        own = self.parts[pl.ds(x * 2 + self.core, 1)][0].astype(F32)
        return own + self.bufs.near[pl.ds(x, 1)][0].astype(F32)

    def start(self):
        for x in others(self.x, self.size) + [self.x]:
            self.near_copy(x).start()

    def middle(self):
        for x in others(self.x, self.size):
            self.bufs.middle[pl.ds(x, 1)] = self.both(x).astype(BF)[None]
            self.far_copy(x, self.x).start()

    def finish(self):
        total = self.both(self.x)
        for x in others(self.x, self.size):
            self.far_copy(x, x).wait_recv()
            total = total + self.bufs.far[pl.ds(x, 1)][0].astype(F32)
        for x in others(self.x, self.size):
            self.near_copy(x).wait_send()
            self.far_copy(x, self.x).wait_send()
        self.near_copy(self.x).wait_send()
        return total

    def run(self):
        self.start()
        self.middle()
        return self.finish()


class Trade:
    def __init__(self, plan, out_index, in_index, bufs):
        self.out_index, self.in_index, self.bufs = out_index, in_index, bufs
        self.size = plan.pts
        self.me = lax.axis_index(PTS)

    @staticmethod
    def buffers(plan, cols, rows):
        capacity = 2 * rows // plan.pts
        vmem = pltpu.VMEM((plan.pts, cols, capacity), BF)
        return dict(leave=vmem, land=vmem, send=dma(plan.pts), recv=dma(plan.pts))

    def leaving(self, values, part):
        capacity = self.bufs.leave.shape[2]
        row = self.out_index[...]
        places = lax.broadcasted_iota(jnp.int32, (capacity, row.shape[1]), 0) + part * capacity
        hot = jnp.where(places == row, 1.0, 0.0).astype(BF)
        return dot(hot, values, NT).T.astype(BF)

    def landing(self, part):
        capacity = self.bufs.land.shape[2]
        shape = (self.in_index.shape[1], capacity)
        places = lax.broadcasted_iota(jnp.int32, shape, 1) + part * capacity
        return jnp.where(places == self.in_column, 1.0, 0.0).astype(BF)

    def copy(self, part, slot):
        b = self.bufs
        return push(
            b.leave.at[part], b.land.at[slot], b.send.at[part], b.recv.at[slot],
            pts=part,
        )

    def start(self, values):
        b = self.bufs
        for part in others(self.me, self.size):
            b.leave[pl.ds(part, 1)] = self.leaving(values, part)[None]
            self.copy(part, self.me).start()
        b.land[pl.ds(self.me, 1)] = self.leaving(values, self.me)[None]

    def finish(self):
        b = self.bufs
        self.in_column = column(self.in_index[...])
        total = dot(self.landing(self.me), b.land[pl.ds(self.me, 1)][0], NT)
        for step in range(1, self.size):
            part = lax.rem(self.me + self.size - step, self.size)
            hot = self.landing(part)
            self.copy(part, part).wait_recv()
            total = total + dot(hot, b.land[pl.ds(part, 1)][0], NT)
        for part in others(self.me, self.size):
            self.copy(part, self.me).wait_send()
        return total.T.astype(BF)


class Route:
    PIECES = 2

    def __init__(self, plan, out_index, in_index, full, nets):
        cols = full.shape[0] // plan.mdl
        self.size = cols // self.PIECES
        self.full, self.base = full, lax.axis_index(MDL) * cols
        self.trades = [Trade(plan, out_index, in_index, net.trade) for net in nets]
        self.gathers = [
            Gather(
                plan, lambda m, i=i: full.at[pl.ds(m * cols + i * self.size, self.size)], net.ring
            )
            for i, net in enumerate(nets)
        ]

    @classmethod
    def buffers(cls, plan, cols, rows):
        net = dict(
            trade=Trade.buffers(plan, cols // cls.PIECES, rows), ring=Gather.semaphores(plan)
        )
        return [net] * cls.PIECES

    def start(self, values):
        for i, trade in enumerate(self.trades):
            trade.start(values[i * self.size : (i + 1) * self.size])

    def land(self):
        for i, (trade, gather) in enumerate(zip(self.trades, self.gathers)):
            self.full[pl.ds(self.base + i * self.size, self.size), :] = trade.finish()
            gather.start()
            if i > 0:
                self.gathers[i - 1].forward()
        self.gathers[-1].forward()

    def finish(self):
        for gather in self.gathers:
            gather.finish()


class Reduce:
    def __init__(self, plan, bufs):
        self.bufs = bufs
        self.width, self.depth = plan.width, plan.depth
        self.me = lax.axis_index(PTS)
        self.y, self.z = lax.rem(self.me, self.width), self.me // self.width
        self.groups, _, self.pack, self.share, self.cols = bufs.acc.shape
        self.steps = self.groups + self.depth - 1

    @staticmethod
    def buffers(plan, blocks, pack, cols):
        groups, share, vmem = blocks // pack, C // plan.pts, pltpu.VMEM
        line = (plan.depth, pack, share, cols)
        way = dict(
            land=vmem((groups,) + line, BF),
            send=dma(groups, plan.depth),
            recv=dma(groups, plan.depth),
        )
        return dict(
            own=vmem((plan.width, groups) + line, BF),
            side=vmem((plan.width, groups) + line, BF),
            acc=vmem((groups,) + line, BF),
            up=way,
            down=way,
            side_send=dma(plan.width, groups),
            side_recv=dma(plan.width, groups),
        )

    def store(self, block, group, place):
        grid = block.astype(BF).reshape(self.depth, self.width, self.share, self.cols)
        for v in range(self.width):
            self.bufs.own[v, group, :, pl.ds(place, 1)] = grid[:, v][:, None]

    def side_copy(self, group, v, slot):
        b = self.bufs
        return push(
            b.own.at[v, group], b.side.at[slot, group], b.side_send.at[v, group],
            b.side_recv.at[slot, group], pts=self.z * self.width + v,
        )

    def line_copy(self, way, group, to, step):
        b = self.bufs
        near = jnp.clip(self.z + step, 0, self.depth - 1)
        return push(
            b.acc.at[group, to], way.land.at[group, to], way.send.at[group, to],
            way.recv.at[group, to], pts=near * self.width + self.y,
        )

    def start(self, group):
        for v in others(self.y, self.width):
            self.side_copy(group, v, self.y).start()

    def sum_side(self, group):
        b = self.bufs
        total = b.own[pl.ds(self.y, 1), pl.ds(group, 1)][0].astype(F32)
        for v in others(self.y, self.width):
            self.side_copy(group, v, v).wait_recv()
            total = total + b.side[pl.ds(v, 1), pl.ds(group, 1)][0].astype(F32)
        b.acc[pl.ds(group, 1)] = total.astype(BF)

    def relay(self, way, group, step, first):
        b = self.bufs

        @pl.when((group >= 0) & (group < self.groups))
        def _():
            for to in range(self.depth):

                @pl.when((to - self.z) * step > 0)
                def _():
                    @pl.when(jnp.logical_not(first))
                    def _():
                        self.line_copy(way, group, to, -step).wait_recv()
                        spot = (pl.ds(group, 1), to)
                        b.acc[spot] = (
                            b.acc[spot].astype(F32) + way.land[spot].astype(F32)
                        ).astype(BF)

                    self.line_copy(way, group, to, step).start()

    def step(self, s):
        if isinstance(s, int):
            if s < self.groups:
                self.sum_side(s)
        else:

            @pl.when((s >= 0) & (s < self.groups))
            def _():
                self.sum_side(s)

        self.relay(self.bufs.up, s - self.z, 1, self.z == 0)
        self.relay(self.bufs.down, s - (self.depth - 1 - self.z), -1, self.z == self.depth - 1)

    def finish(self, out):
        b, z = self.bufs, self.z

        def total(way, group):
            b.acc[group, pl.ds(z, 1)] = (
                b.acc[group, pl.ds(z, 1)].astype(F32) + way.land[group, pl.ds(z, 1)].astype(F32)
            ).astype(BF)

        for group in range(self.groups):

            @pl.when(z > 0)
            def _():
                self.line_copy(self.bufs.up, group, z, -1).wait_recv()
                total(b.up, group)

            @pl.when(z < self.depth - 1)
            def _():
                self.line_copy(self.bufs.down, group, z, 1).wait_recv()
                total(b.down, group)

            out[group * self.pack : (group + 1) * self.pack] = b.acc[group, pl.ds(z, 1)][0]

    def end(self):
        for group in range(self.groups):
            for v in others(self.y, self.width):
                self.side_copy(group, v, self.y).wait_send()
            for to in range(self.depth):

                @pl.when(to > self.z)
                def _():
                    self.line_copy(self.bufs.up, group, to, 1).wait_send()

                @pl.when(to < self.z)
                def _():
                    self.line_copy(self.bufs.down, group, to, -1).wait_send()


def everyone(plan):
    me, plane = lax.axis_index(PTS), lax.axis_index(MDL)
    return [{PTS: p} for p in others(me, plan.pts)] + [{MDL: m} for m in others(plane, plan.mdl)]


def unit_columns(values):
    mean = jnp.sum(values, 0, keepdims=True) / C
    centred = values - mean
    inv_std = lax.rsqrt(jnp.sum(centred * centred, 0, keepdims=True) / C + NORM_EPS)
    return centred * inv_std, inv_std


def one_hot_window(ids_ref, tap, tile):
    row = ids_ref[pl.ds(tap, 1), pl.ds(tile * TILE, TILE)]
    places = lax.broadcasted_iota(jnp.int32, (WINDOW, TILE), 0) + tile * TILE
    return jnp.where(places == row, 1.0, 0.0).astype(BF)


PACK = 5
ORDER = [TAPS, TAPS + 4] + list(range(TAPS)) + [TAPS + 1, TAPS + 2, TAPS + 3]
ORDER = ORDER + list(range(TAPS + 5, TAPS + 5 + 2 * FF // C))
PLACE = {block: place for place, block in enumerate(ORDER)}


def column(row):
    wide = jnp.broadcast_to(row.astype(F32), (8, row.shape[1]))
    return wide.T[:, 0:1].astype(jnp.int32)


def steps_passed(values, bounds):
    return sum((values >= bound).astype(jnp.int32) for bound in bounds)


def routes(plan, r, rows):
    capacity = 2 * rows // plan.pts
    slot_count = r.from_patch.shape[1]
    patches = slot_count // PATCH
    scans = r.scan_lengths.shape[0]
    target = steps_passed(r.to_patch[...], [p * slot_count for p in range(1, plan.pts)])
    size = 256
    rank = jnp.zeros((1, rows), jnp.int32)
    target_column = column(target)
    ahead = lax.broadcasted_iota(jnp.int32, (size, rows), 1)
    for low in range(0, rows, size):
        earlier = lax.broadcasted_iota(jnp.int32, (size, rows), 0) + low < ahead
        same = target_column[low : low + size] == target
        rank = rank + jnp.sum((earlier & same).astype(jnp.int32), 0, keepdims=True)
    r.send_pos[...] = target * capacity + rank
    held = r.from_patch[...]
    used = held >= 0
    lanes = lax.broadcasted_iota(jnp.int32, (1, slot_count), 1)
    patch = steps_passed(lanes, [p * PATCH for p in range(1, patches)])
    source = steps_passed(held, [p * rows for p in range(1, plan.pts)])
    bounds, bound = [], 0
    for i in range(scans - 1):
        bound = bound + r.scan_lengths[i]
        bounds.append(bound)
    group = patch * scans + (steps_passed(held, bounds) if bounds else 0)
    top = patches * plan.pts * rows
    order_key = jnp.where(used, patch * (plan.pts * rows) + held, top)
    held_key = jnp.where(used, held, top)
    order_column, held_column = column(order_key), column(held_key)
    first_key = source * rows
    order = jnp.zeros((1, slot_count), jnp.int32)
    rank = jnp.zeros((1, slot_count), jnp.int32)
    for low in range(0, slot_count, size):
        part = slice(low, low + size)
        order = order + jnp.sum(
            (order_column[part] < order_key).astype(jnp.int32), 0, keepdims=True
        )
        among = (held_column[part] < held_key) & (held_column[part] >= first_key)
        rank = rank + jnp.sum(among.astype(jnp.int32), 0, keepdims=True)
    base = plan.pts * capacity
    both = column(group * base + source * capacity + rank)
    order = column(jnp.where(used, order, slot_count))
    places = lax.broadcasted_iota(jnp.int32, (size, rows), 1)
    found = jnp.zeros((1, rows), jnp.int32)
    for low in range(0, slot_count, size):
        part = slice(low, low + size)
        found = found + jnp.sum(
            jnp.where(order[part] == places, both[part], 0), 0, keepdims=True
        )
    group = steps_passed(found, [base * g for g in range(1, patches * scans)])
    r.group[...] = group
    r.arrival[...] = found - group * base


def front_kernel(plan, r):
    pts, mdl, slots = plan.pts, plan.mdl, plan.slots
    width, depth = plan.width, plan.depth
    me, plane = lax.axis_index(PTS), lax.axis_index(MDL)
    y, z = lax.rem(me, width), me // width
    rows, cols = r.points_rows.shape
    share = C // pts
    total = r.blocks.shape[1]
    groups = total // PACK
    conv_groups = -(-(2 + TAPS) // PACK)
    for m in range(mdl):
        r.owned[m] = r.weights[:, :, m * cols : (m + 1) * cols].astype(BF)
    greet(everyone(plan))

    def spread_copy(m, slot):
        return push(
            r.owned.at[m], r.spread.at[pl.ds(slot * slots, slots)], r.spread_send.at[m],
            r.spread_recv.at[slot], mdl=m,
        )

    for m in others(plane, mdl):
        spread_copy(m, plane).start()

    def vec_copy(m, slot):
        return push(
            r.vectors, r.vec_all.at[slot], r.vec_send.at[m], r.vec_recv.at[slot], mdl=m
        )

    for m in others(plane, mdl):
        vec_copy(m, plane).start()

    r.points[...] = r.points_rows[...].astype(F32).T.astype(BF)

    def up_copy():
        return push(
            r.points.at[:, rows - HALO : rows], r.ext.at[:, 0:HALO], r.halo_send.at[0],
            r.halo_recv.at[0], pts=me + 1,
        )

    def down_copy():
        return push(
            r.points.at[:, 0:HALO], r.ext.at[:, HALO + rows : 2 * HALO + rows], r.halo_send.at[1],
            r.halo_recv.at[1], pts=me - 1,
        )

    @pl.when(me < pts - 1)
    def _():
        up_copy().start()

    @pl.when(me == pts - 1)
    def _():
        r.ext[:, HALO + rows :] = jnp.zeros((cols, HALO), BF)

    @pl.when(me > 0)
    def _():
        down_copy().start()

    @pl.when(me == 0)
    def _():
        r.ext[:, :HALO] = jnp.zeros((cols, HALO), BF)

    r.ext[:, HALO : HALO + rows] = r.points[...]
    r.spread[pl.ds(plane * slots, slots)] = r.owned[pl.ds(plane, 1)][0]
    r.vec_all[pl.ds(plane, 1)] = r.vectors[...][None]
    r.points_full[pl.ds(plane * cols, cols), :] = r.points[...]
    for m in others(plane, mdl):
        spread_copy(m, m).wait_recv()
    for place, block in enumerate(ORDER):
        r.blocks[pl.ds(me, 1), place] = r.spread[pl.ds(r.slots[block], 1)]

    def group_of(source, group):
        return r.blocks.at[source, group * PACK : (group + 1) * PACK]

    def far_copy(group, source, step):
        return push(
            group_of(source, group), group_of(source, group),
            r.far_send.at[(step + 1) // 2, group, source // width],
            r.far_recv.at[group, source // width], pts=jnp.clip(z + step, 0, depth - 1) * width + y,
        )

    def side_copy(group, v, source):
        return push(
            group_of(source, group), group_of(source, group),
            r.side_send.at[group, v, source // width], r.side_recv.at[group, source],
            pts=z * width + v,
        )

    def pass_on(group, source, act):
        from_z = source // width

        @pl.when((z < depth - 1) & (from_z <= z))
        def _():
            copy = far_copy(group, source, 1)
            copy.start() if act == START else copy.wait_send()

        @pl.when((z > 0) & (from_z >= z))
        def _():
            copy = far_copy(group, source, -1)
            copy.start() if act == START else copy.wait_send()

        for v in others(y, width):
            copy = side_copy(group, v, source)
            copy.start() if act == START else copy.wait_send()

    def relay(group, away, act):
        for from_z in (z - away, z + away):

            @pl.when((from_z >= 0) & (from_z < depth))
            def _():
                source = from_z * width + y
                if act == START:
                    far_copy(group, source, 1).wait_recv()
                pass_on(group, source, act)

    ahead = groups
    for group in range(ahead):
        pass_on(group, me, START)

    points_gather = Gather(
        plan, lambda m: r.points_full.at[pl.ds(m * cols, cols)],
        r.points_net,
    )
    cot_gather = Gather(
        plan, lambda m: r.cot_full.at[pl.ds(m * cols, cols)],
        r.cot_net,
    )
    points_gather.start()
    r.cot_full[pl.ds(plane * cols, cols), :] = r.cot_rows[...].astype(F32).T.astype(BF)
    cot_gather.start()
    routes(plan, r, rows)

    @pl.when(me > 0)
    def _():
        push(
            r.points.at[:, 0:HALO], r.ext.at[:, 0:HALO], r.halo_send.at[0], r.halo_recv.at[0],
            pts=me - 1,
        ).wait_recv()

    @pl.when(me < pts - 1)
    def _():
        push(
            r.points.at[:, 0:HALO], r.ext.at[:, HALO + rows : 2 * HALO + rows], r.halo_send.at[1],
            r.halo_recv.at[1], pts=me + 1,
        ).wait_recv()

    def take(tap, carry):
        for tile in range(rows // TILE):
            hot = one_hot_window(r.ids, tap, tile)
            picked = dot(r.ext[:, tile * TILE : tile * TILE + WINDOW], hot).astype(BF)
            r.taken[pl.ds(tap, 1), :, tile * TILE : (tile + 1) * TILE] = picked[None]
        return carry

    steps = groups + depth - 2
    cuts = [min(TAPS, -(-TAPS * i // groups)) for i in range(steps + 1)]
    for step in range(steps):
        if step + ahead < groups:
            pass_on(step + ahead, me, START)
        if cuts[step] < cuts[step + 1]:
            lax.fori_loop(cuts[step], cuts[step + 1], take, 0)
        for away in range(1, depth):
            if 0 <= step + 1 - away < groups:
                relay(step + 1 - away, away, START)
    moves(START, r.taken_move)

    def complete(group):
        for u in others(y, width):
            for v in range(depth):
                side_copy(group, u, v * width + u).wait_recv()

    pair_gather = Gather(
        plan, lambda m: r.pair.at[m], r.pair_net
    )
    for group in range(conv_groups):
        complete(group)
        if group == 0:
            for i in range(2):
                r.pair[pl.ds(plane, 1), i] = r.blocks[:, i].reshape(1, C, cols)
            pair_gather.start()
        low = max(group * PACK - 2, 0)
        high = min(group * PACK - 2 + PACK, TAPS)
        if cols % 128 == 0:
            weight = jnp.concatenate(
                [r.blocks[:, t + 2].reshape(C, cols) for t in range(low, high)], 1
            )
            part = dot(weight, r.taken[low:high].reshape((high - low) * cols, rows))
        else:
            part = sum(dot(r.blocks[:, t + 2].reshape(C, cols), r.taken[t]) for t in range(low, high))
        if group == 0:
            r.acc[...] = part
            pair_gather.forward()
        else:
            r.acc[...] += part

    taps_copy = pltpu.make_async_copy(r.blocks.at[:, 2 : 2 + TAPS], r.taps_far, r.taps_sem)
    taps_copy.start()
    points_gather.forward()
    cot_gather.forward()
    r.parts[...] = r.acc[...].astype(BF).reshape(mdl, cols, rows)
    hidden_sum = Sum(plan, r.parts, r.sum_net)
    hidden_sum.start()
    for m in others(plane, mdl):
        vec_copy(m, m).wait_recv()
    for m in range(mdl):
        r.vec[m * cols : (m + 1) * cols, :] = r.vec_all[m].T
    pair_gather.finish()
    points_gather.finish()
    hidden_sum.middle()
    bias = r.vec[pl.ds(plane * cols, cols), 0:1]
    r.hidden[pl.ds(plane * cols, cols), :] = (hidden_sum.finish() + bias).astype(BF)
    Gather(
        plan, lambda m: r.hidden.at[pl.ds(m * cols, cols)],
        r.hidden_net,
    ).run()
    hidden = r.hidden[...]
    for m in range(mdl):
        r.acc[m * cols : (m + 1) * cols, :] = dot(r.pair[m, 0], hidden, TN)
    span_size = 128

    def norms(step, carry):
        span = pl.ds(pl.multiple_of(step * span_size, span_size), span_size)
        unit, inv_std = unit_columns(r.acc[:, span] + r.vec[:, 1:2])
        r.mixed_unit[:, span] = unit.astype(BF)
        r.mixed_std[:, span] = inv_std
        stream = r.points_full[:, span].astype(F32) + unit * r.vec[:, 2:3] + r.vec[:, 3:4]
        r.stream[:, span] = stream
        unit, inv_std = unit_columns(stream)
        r.one_unit[:, span] = unit.astype(BF)
        r.one_std[:, span] = inv_std
        r.normed[:, span] = (unit * r.vec[:, 4:5] + r.vec[:, 5:6]).astype(BF)
        return carry

    lax.fori_loop(0, rows // span_size, norms, 0)
    route = Route(plan, r.send_pos, r.arrival, r.slot_in, r.route_net)
    route.start(r.normed[pl.ds(plane * cols, cols), :])
    moves(START, r.hidden_move, r.mixed_unit_move, r.one_unit_move, r.stream_move, r.pair_move)
    for group in range(conv_groups, groups):
        complete(group)
    for i in range(r.rest.shape[0]):
        r.rest[i] = r.blocks[:, TAPS + 2 + i].reshape(C, cols)
    cot_gather.finish()
    moves(START, r.rest_move, r.cot_full_move)
    route.land()
    route.finish()
    moves(START, r.slot_in_move)

    @pl.when(me < pts - 1)
    def _():
        up_copy().wait_send()

    @pl.when(me > 0)
    def _():
        down_copy().wait_send()

    for m in others(plane, mdl):
        spread_copy(m, plane).wait_send()
        vec_copy(m, plane).wait_send()
    for group in range(groups):
        pass_on(group, me, WAIT)
        for away in range(1, depth):
            relay(group, away, WAIT)
    moves(WAIT, r.taken_move, r.cot_full_move, r.pair_move, r.hidden_move, r.mixed_unit_move, r.one_unit_move, r.stream_move, r.slot_in_move, r.rest_move)
    taps_copy.wait()


def front(plan, slots, weights, points, cot, vectors, ids, to_patch, from_patch, scan_lengths):
    rows, cols = points.shape
    pts, mdl = plan.pts, plan.mdl
    share = C // pts
    total = len(ORDER)
    groups = total // PACK
    vmem = pltpu.VMEM
    ring = Gather.semaphores(plan)
    scratch = dict(
        points_net=ring,
        cot_net=ring,
        pair_net=ring,
        hidden_net=ring,
        owned=vmem((mdl, plan.slots, share, cols), BF),
        points=vmem((cols, rows), BF),
        spread=vmem((total, share, cols), BF),
        vec_all=vmem((mdl,) + vectors.shape, F32),
        ext=vmem((cols, rows + 2 * HALO), BF),
        acc=vmem((C, rows), F32),
        parts=vmem((mdl, cols, rows), BF),
        normed=vmem((C, rows), BF),
        points_full=vmem((C, rows), BF),
        spread_send=dma(mdl),
        spread_recv=dma(mdl),
        vec_send=dma(mdl),
        vec_recv=dma(mdl),
        halo_send=dma(2),
        halo_recv=dma(2),
        blocks=vmem((pts, total, share, cols), BF),
        taps_sem=dma(),
        far_send=dma(2, groups, plan.depth),
        far_recv=dma(groups, plan.depth),
        side_send=dma(groups, plan.width, plan.depth),
        side_recv=dma(groups, pts),
        sum_net=(Sum.buffers(plan, (cols, rows))),
        route_net=Route.buffers(plan, cols, rows),
    )
    return call(
        functools.partial(front_kernel, plan),
        "front",
        5,
        dict(
            slots=slots, weights=weights, points_rows=points, cot_rows=cot, vectors=vectors,
            ids=ids, to_patch=to_patch, from_patch=from_patch, scan_lengths=scan_lengths,
        ),
        dict(
            taps_far=((pts, TAPS, share, cols), BF),
            taken=Late((TAPS, cols, rows), BF),
            cot_full=Late((C, rows), BF),
            pair=Late((mdl, 2, C, cols), BF),
            vec=((C, vectors.shape[0]), F32),
            hidden=Late((C, rows), BF),
            mixed_unit=Late((C, rows), BF),
            mixed_std=((1, rows), F32),
            stream=Late((C, rows), F32),
            one_unit=Late((C, rows), BF),
            one_std=((1, rows), F32),
            send_pos=((1, rows), jnp.int32),
            arrival=((1, rows), jnp.int32),
            group=((1, rows), jnp.int32),
            slot_in=Late((C, rows), BF),
            rest=Late((total - TAPS - 2, C, cols), BF),
        ),
        scratch,
        4 * TAPS * rows * (WINDOW + C) * cols,
        smem=("slots", "scan_lengths"),
        free=("taps_far",),
    )


def head_lanes(ext, cols, head):
    lane = lax.broadcasted_iota(jnp.int32, ext.shape, 1)
    return jnp.where((lane >= cols) | (lane // HD == head), ext, jnp.zeros_like(ext))


def head_rows(head):
    return pl.ds(pl.multiple_of(head * HD, HD), HD)


SPAN = 128


def over_spans(rows, body, size=SPAN):
    def step(index, carry):
        body(pl.ds(pl.multiple_of(index * size, size), size))
        return carry

    lax.fori_loop(0, rows // size, step, 0)


def beside(blocks):
    def times(right, cols):
        if cols % 128 == 0:
            return dot(jnp.concatenate(blocks, 1), right[...])
        return sum(
            dot(block, right[i * cols : (i + 1) * cols, :]) for i, block in enumerate(blocks)
        )

    return times


def mlp_part(plan, r):
    mdl = plan.mdl
    plane = lax.axis_index(MDL)
    cols, rows = r.cot.shape
    ff_blocks = FF // C
    own = pl.ds(plane * cols, cols)
    moves(WAIT, r.pair_move)
    r.acc[...] = beside([r.pair[m, 1] for m in range(mdl)])(r.attended_rows, cols)
    moves(WAIT, r.stream_move, r.cot_full_move)

    def norms(span):
        branch = (r.acc[:, span] + r.vec[:, 8:9]).astype(BF).astype(F32)
        two = r.stream[:, span] + branch
        r.stream[:, span] = two
        unit, inv_std = unit_columns(two)
        r.two_unit[:, span] = unit
        r.two_std[:, span] = inv_std
        r.normed[:, span] = (unit * r.vec[:, 9:10] + r.vec[:, 10:11]).astype(BF)

    over_spans(rows, norms)
    if cols % 128 == 0:
        first, second = (
            jnp.concatenate([r.rest[low + k] for k in range(ff_blocks)], 1)
            for low in (3, 3 + ff_blocks)
        )
        r.acc[...] = dot(first, r.normed[...], TN)
        r.grad_act[...] = dot(second, r.cot_full[...], TN)
    for k in range(ff_blocks):
        part = slice(k * cols, (k + 1) * cols)
        if cols % 128 != 0:
            r.acc[part, :] = dot(r.rest[3 + k], r.normed[...], TN)
            r.grad_act[part, :] = dot(r.rest[3 + ff_blocks + k], r.cot_full[...], TN)

        def bend(span):
            pre = r.acc[part, span] + r.vec[own, 11 + k : 12 + k]
            half = 0.5 * (1.0 + lax.erf(pre * 0.7071067811865476))
            r.act[part, span] = (pre * half).astype(BF)
            slope = half + pre * jnp.exp(-0.5 * pre * pre) * 0.3989422804014327
            r.grad_pre[part, span] = (r.grad_act[part, span] * slope).astype(BF)

        over_spans(rows, bend, 256)
    r.acc[...] = beside([r.rest[3 + k] for k in range(ff_blocks)])(r.grad_pre, cols)

    def stats(span):
        scaled = r.acc[:, span] * r.vec[:, 9:10]
        r.stats[pl.ds(plane, 1), 0:1, span] = jnp.sum(scaled, 0, keepdims=True)[None]
        r.stats[pl.ds(plane, 1), 1:2, span] = jnp.sum(scaled * r.two_unit[:, span], 0, keepdims=True)[None]

    over_spans(rows, stats)

    def stats_copy(m, slot):
        return push(
            r.stats.at[slot], r.stats.at[slot], r.stats_send.at[m], r.stats_recv.at[slot], mdl=m
        )

    for m in others(plane, mdl):
        stats_copy(m, plane).start()
    r.parts[...] = r.acc[...].astype(BF).reshape(mdl, cols, rows)
    shape = Sum.buffers(plan, (cols, rows))
    grad_sum = Sum(plan, r.parts, r.grad_net)
    grad_sum.start()
    out = beside([r.rest[3 + ff_blocks + k] for k in range(ff_blocks)])(r.act, cols)
    r.out_parts[...] = out.astype(BF).reshape(mdl, cols, rows)
    grad_sum.middle()
    out_sum = Sum(plan, r.out_parts, r.out_net)
    out_sum.start()
    for m in others(plane, mdl):
        stats_copy(m, m).wait_recv()
    mean = sum(r.stats[m, 0:1] for m in range(mdl)) / C
    cross = sum(r.stats[m, 1:2] for m in range(mdl)) / C
    cot = r.cot[...].astype(F32)
    grad_normed = grad_sum.finish()
    unit = r.two_unit[own, :]
    grad_two = cot + r.two_std[...] * (grad_normed * r.vec[own, 9:10] - mean - unit * cross)
    r.grad_two[...] = grad_two
    branch = grad_two.astype(BF)
    r.branch_full[own, :] = branch
    route = Route(plan, r.send_pos, r.arrival, r.grad_slot, r.in_route)
    route.start(branch)
    fetch(plan, r, 2, START)
    out_sum.middle()

    def along(values):
        return jnp.sum(values.astype(F32), 1, keepdims=True)

    r.mlp_sums[:, 0:1] = along(branch)
    r.mlp_sums[:, 1:2] = along(grad_normed * unit)
    r.mlp_sums[:, 2:3] = along(grad_normed)
    for k in range(ff_blocks):
        part = slice(k * cols, (k + 1) * cols)
        r.mlp_sums[:, 3 + k : 4 + k] = along(r.grad_pre[part, :])
        r.mlp_grads[k] = dot(r.normed[...], r.grad_pre[part, :], NT).astype(BF)
        r.mlp_grads[ff_blocks + k] = dot(r.cot_full[...], r.act[part, :], NT).astype(BF)
    r.mlp_sums[:, 3 + ff_blocks : 4 + ff_blocks] = along(cot)
    moves(START, r.grad_two_move)
    route.land()
    bias = r.vec[own, 11 + ff_blocks : 12 + ff_blocks]
    r.out[...] = (r.stream[own, :] + out_sum.finish() + bias).T.astype(BF)
    route.finish()
    for m in others(plane, mdl):
        stats_copy(m, plane).wait_send()


def attend_part(plan, r):
    plane = lax.axis_index(MDL)
    rows, cols = r.values.shape
    heads = cols // HD
    group = column(r.group[...])
    lane = lax.broadcasted_iota(jnp.int32, (rows, cols), 1)
    same = lane == group
    slot_in = r.slot_in[...]
    queries = (dot(slot_in, r.rest[0], TN) + r.vectors[6:7, :]).astype(BF)
    r.q_ext[:, :cols] = queries * BF(HD ** (-0.5))
    r.q_ext[:, cols:] = jnp.where(same, 1.0, 0.0).astype(BF)
    r.k_ext[:, :cols] = dot(slot_in, r.rest[1], TN).astype(BF)
    r.k_ext[:, cols:] = jnp.where(same | (lane >= plan.groups), 0.0, -1e30).astype(BF)
    values = dot(slot_in, r.rest[2], TN) + r.vectors[7:8, :]
    r.values[...] = values.astype(BF)
    r.v_ext[:, :cols] = values.astype(BF)
    r.v_ext[:, cols:] = jnp.ones((rows, cols), BF)
    r.heads_out[...] = jnp.zeros_like(r.heads_out)
    r.heads_lse[...] = jnp.zeros_like(r.heads_lse)

    def one(head, carry):
        keys, weights = r.k_ext[...], r.v_ext[...]
        lane = lax.broadcasted_iota(jnp.int32, (TILE, cols), 1)
        for tile in range(rows // TILE):
            span = slice(tile * TILE, (tile + 1) * TILE)
            scores = dot(head_lanes(r.q_ext[span, :], cols, head), keys, NT)
            top = jnp.max(scores, 1, keepdims=True)
            summed = dot(jnp.exp(scores - top).astype(BF), weights)
            total = summed[:, cols : cols + 1]
            r.heads_out[span, :] = jnp.where(
                lane // HD == head, summed[:, :cols] / total, r.heads_out[span, :]
            )
            r.heads_lse[span, :] = jnp.where(
                lane == head, top + jnp.log(total), r.heads_lse[span, :]
            )
        return carry

    route = Route(plan, r.arrival, r.send_pos, r.attended_rows, r.out_route)
    for i, trade in enumerate(route.trades):
        share = heads // route.PIECES
        lax.fori_loop(i * share, (i + 1) * share, one, 0, unroll=2)
        part = slice(i * route.size, (i + 1) * route.size)
        r.attended[part, :] = r.heads_out[...].T[part].astype(BF)
        trade.start(r.attended[part, :])
    r.lse[...] = r.heads_lse[...].T[:heads][:, None]
    fetch(plan, r, 0, START)
    fetch(plan, r, 1, START)
    route.land()
    route.finish()


def attend_back_part(plan, r):
    plane = lax.axis_index(MDL)
    rows, cols = r.values.shape
    heads = cols // HD
    greet(everyone(plan))
    mlp_count = r.mlp_grads.shape[0]
    reduce = Reduce(
        plan, r.reduce_net
    )
    for group in range(reduce.groups):
        for place in range(MLP_PACK):
            reduce.store(r.mlp_grads[group * MLP_PACK + place], group, place)
        reduce.start(group)
    branch_gather = Gather(
        plan, lambda m: r.branch_full.at[pl.ds(m * cols, cols)],
        r.branch_net,
    )
    branch_gather.start()
    fetch(plan, r, 3, START)
    grad_slot = r.grad_slot[...]
    grad_t = dot(r.pair[pl.ds(plane, 1), 1][0], grad_slot, TN).astype(BF).astype(F32)
    r.grad[...] = grad_t.T.astype(BF)
    weighed = grad_t * r.attended[...].astype(F32)
    r.inner[...] = jnp.sum(weighed.reshape(heads, HD, rows), 1, keepdims=True)
    r.keys_t[...] = r.k_ext[:, :cols].astype(F32).T.astype(BF)
    r.dk_acc[...] = jnp.zeros_like(r.dk_acc)
    r.dv_acc[...] = jnp.zeros_like(r.dv_acc)

    def one(head, carry):
        queries = head_lanes(r.q_ext[...], cols, head)
        pure = queries[:, :cols]
        grad = head_lanes(r.grad[...], cols, head)
        lse = r.lse[pl.ds(head, 1)][0]
        inner = r.inner[pl.ds(head, 1)][0]
        keys_t = r.keys_t[head_rows(head), :]
        dq = jnp.zeros((HD, rows), F32)
        for tile in range(rows // TILE):
            span = slice(tile * TILE, (tile + 1) * TILE)
            scores = dot(r.k_ext[span, :], queries, NT)
            soft = jnp.exp(scores - lse)
            grad_soft = dot(r.values[span, :], grad, NT)
            grad_scores = (soft * (grad_soft - inner)).astype(BF)
            r.dv_acc[span, :] += dot(soft.astype(BF), grad)
            r.dk_acc[span, :] += dot(grad_scores, pure)
            dq = dq + dot(keys_t[:, span], grad_scores)
        r.dq[head_rows(head), :] = (dq * HD ** (-0.5)).astype(BF)
        reduce.step(head - delay)
        return carry

    delay = max(heads - reduce.steps, 0)
    lax.fori_loop(0, heads, one, 0)
    for s in range(heads - delay, reduce.steps):
        reduce.step(s)
    branch_gather.forward()
    dk = r.dk_acc[...].astype(BF)
    dv = r.dv_acc[...].astype(BF)
    back = dot(r.rest[0], r.dq[...]) + dot(r.rest[1], dk, NT) + dot(r.rest[2], dv, NT)
    r.parts[...] = back.astype(BF).reshape(plan.mdl, cols, rows)
    back_sum = Sum(plan, r.parts, r.sum_net)
    back_sum.start()
    r.attend_grads[0] = dot(r.slot_in[...], r.dq[...], NT).astype(BF)
    r.attend_grads[1] = dot(r.slot_in[...], dk).astype(BF)
    back_sum.middle()
    r.attend_grads[2] = dot(r.slot_in[...], dv).astype(BF)
    r.attend_grads[3] = dot(r.grad_slot[...], r.attended[...], NT).astype(BF)
    route = Route(plan, r.arrival, r.send_pos, r.grad_normed, r.back_route)
    route.start(back_sum.finish().astype(BF))
    moves(START, r.attend_grads_move)
    r.attend_sums[...] = jnp.zeros_like(r.attend_sums)
    r.attend_sums[:, 0:1] = jnp.sum(r.dq[...].astype(F32), 1, keepdims=True)
    r.attend_sums[:, 1:2] = jnp.sum(dv.astype(F32), 0, keepdims=True).T
    route.land()
    branch_gather.finish()
    moves(START, r.branch_full_move)
    route.finish()
    reduce.finish(r.mlp_summed)
    reduce.end()


MLP_PACK = 4


MLP_PACK = 4


def fetch(plan, r, place, act):
    source = (r.left32, r.right32, r.first32, r.second32)[place]
    whole = (r.left_whole, r.right_whole, r.first_whole, r.second_whole)[place]
    if act == START:
        moves(WAIT, (r.left32_move, r.right32_move, r.first32_move, r.second32_move)[place])
        r.low[place] = source[...].astype(BF)
    fetch_copies(plan, r.low.at[place], whole, r.fetch_net[place], act)


def middle_kernel(plan, r):
    moves(START, r.left32_move, r.pair_move, r.stream_move, r.cot_full_move)
    moves(START, r.right32_move, r.first32_move, r.second32_move)
    greet(everyone(plan))
    r.cot[...] = r.cot_rows[...].astype(F32).T.astype(BF)
    attend_part(plan, r)
    mlp_part(plan, r)
    attend_back_part(plan, r)
    for place in range(4):
        fetch(plan, r, place, WAIT)
    moves(WAIT, r.grad_two_move, r.attend_grads_move, r.branch_full_move)


def middle(plan, first, vectors, cot, left, right, moment, second):
    rows, cols = cot.shape
    ff_blocks = FF // C
    heads = cols // HD
    vmem = pltpu.VMEM
    whole = (fetch_shape(plan, left).shape, BF)
    route = Route.buffers(plan, cols, rows)
    total = Sum.buffers(plan, (cols, rows))
    return call(
        functools.partial(middle_kernel, plan),
        "middle",
        2,
        dict(
            slot_in=first.slot_in, rest=first.rest, vectors=vectors, group=first.group,
            send_pos=first.send_pos, arrival=first.arrival, vec=first.vec, cot_rows=cot,
            pair=Late(first.pair), stream=Late(first.stream), cot_full=Late(first.cot_full),
            left32=Late(left), right32=Late(right), first32=Late(moment), second32=Late(second),
        ),
        dict(
            left_whole=whole,
            right_whole=whole,
            first_whole=whole,
            second_whole=whole,
            grad_two=Late((cols, rows), F32),
            out=((rows, cols), BF),
            mlp_sums=((cols, 4 + ff_blocks), F32),
            grad_normed=((C, rows), BF),
            attend_grads=Late((4, C, cols), BF),
            attend_sums=((cols, 8), F32),
            branch_full=Late((C, rows), BF),
            mlp_summed=((2 * ff_blocks, C // plan.pts, cols), BF),
        ),
        dict(
            low=vmem((4,) + left.shape, BF),
            q_ext=vmem((rows, 2 * cols), BF),
            k_ext=vmem((rows, 2 * cols), BF),
            values=vmem((rows, cols), BF),
            attended=vmem((cols, rows), BF),
            lse=vmem((heads, 1, rows), F32),
            attended_rows=vmem((C, rows), BF),
            v_ext=vmem((rows, 2 * cols), BF),
            heads_out=vmem((rows, cols), F32),
            heads_lse=vmem((rows, cols), F32),
            cot=vmem((cols, rows), BF),
            acc=vmem((C, rows), F32),
            two_unit=vmem((C, rows), F32),
            two_std=vmem((1, rows), F32),
            normed=vmem((C, rows), BF),
            grad_act=vmem((ff_blocks * cols, rows), F32),
            act=vmem((ff_blocks * cols, rows), BF),
            grad_pre=vmem((ff_blocks * cols, rows), BF),
            stats=vmem((plan.mdl, 8, rows), F32),
            stats_send=dma(plan.mdl),
            stats_recv=dma(plan.mdl),
            parts=vmem((plan.mdl, cols, rows), BF),
            out_parts=vmem((plan.mdl, cols, rows), BF),
            grad_slot=vmem((C, rows), BF),
            mlp_grads=vmem((2 * ff_blocks, C, cols), BF),
            grad=vmem((rows, cols), BF),
            inner=vmem((heads, 1, rows), F32),
            keys_t=vmem((cols, rows), BF),
            dk_acc=vmem((rows, cols), F32),
            dv_acc=vmem((rows, cols), F32),
            dq=vmem((cols, rows), BF),
            grad_net=total,
            out_net=total,
            sum_net=total,
            out_route=route,
            in_route=route,
            back_route=route,
            branch_net=Gather.semaphores(plan),
            reduce_net=Reduce.buffers(plan, 2 * ff_blocks, MLP_PACK, cols),
            fetch_net=[fetch_sems(plan)] * 4,
        ),
        14 * heads * rows * rows * cols + 16 * rows * C * cols * ff_blocks,
        free=("left_whole", "right_whole", "first_whole", "second_whole"),
    )


BACK_ORDER = [TAPS + 1, TAPS + 2, TAPS + 3, TAPS + 4, TAPS] + list(range(TAPS))
MLP_ORDER = list(range(TAPS + 5, TAPS + 5 + 2 * FF // C))
BACK_PACK = 4


def back_kernel(plan, r):
    pts = plan.pts
    cols, rows = r.turn_acc.shape
    taps = r.taken.shape[0]
    ready = r.attend_grads.shape[0]
    extra = ready + 1
    me, plane = lax.axis_index(PTS), lax.axis_index(MDL)
    own_cols = pl.ds(plane * cols, cols)
    middle = slice(HALO, HALO + rows)
    first = (r.grad_normed_move, r.one_unit_move, r.branch_full_move, r.mixed_unit_move, r.pair_move)
    second = (r.hidden_move, r.taken_move, r.grad_two_move, r.taps_move)
    moves(START, *first, *second)
    greet([{PTS: v} for v in others(me, pts)] + [{MDL: plane + 1 - 2 * lax.rem(plane, 2)}])
    reduce = Reduce(
        plan, r.reduce_net
    )
    groups = reduce.groups
    for b in range(ready):
        reduce.store(r.attend_grads[b], b // BACK_PACK, b % BACK_PACK)
    reduce.start(0)
    moves(WAIT, *first)

    def grads(group):
        if group == ready // BACK_PACK:
            reduce.store(dot(r.hidden[...], r.mixed[own_cols, :], NT), group, ready % BACK_PACK)

        def one(place, carry):
            tap = group * BACK_PACK + place - extra
            reduce.store(
                dot(r.back[:, middle], r.taken[pl.ds(tap, 1)][0], NT), group, place
            )
            return carry

        low = max(group * BACK_PACK, extra)
        lax.fori_loop(low - group * BACK_PACK, BACK_PACK, one, 0)

    def norms(span):
        grad = r.grad_normed[:, span].astype(F32) * r.vec[:, 4:5]
        unit = r.one_unit[:, span].astype(F32)
        delta = r.one_std[:, span] * (
            grad
            - jnp.sum(grad, 0, keepdims=True) / C
            - unit * (jnp.sum(grad * unit, 0, keepdims=True) / C)
        )
        r.delta[:, span] = delta
        grad = (r.branch_full[:, span].astype(F32) + delta) * r.vec[:, 2:3]
        unit = r.mixed_unit[:, span].astype(F32)
        r.mixed[:, span] = (
            r.mixed_std[:, span]
            * (
                grad
                - jnp.sum(grad, 0, keepdims=True) / C
                - unit * (jnp.sum(grad * unit, 0, keepdims=True) / C)
            )
        ).astype(BF)

    over_spans(rows, norms)
    back = beside([r.pair[m, 0] for m in range(plan.mdl)])(r.mixed, cols)
    r.back[:, middle] = back.astype(BF)

    core = lax.rem(plane, 2)
    mine = pl.ds(core * (C // 2), C // 2)
    low_end, high_end = slice(0, HALO), slice(HALO + rows, 2 * HALO + rows)

    def up_copy(target):
        return push(
            r.back.at[mine, rows : rows + HALO], r.back.at[mine, low_end], r.halo_send.at[0],
            r.halo_recv.at[0], pts=target,
        )

    def down_copy(target):
        return push(
            r.back.at[mine, HALO : 2 * HALO], r.back.at[mine, high_end],
            r.halo_send.at[1], r.halo_recv.at[1], pts=target,
        )

    def core_copy(end, which, part):
        half = pl.ds(part * (C // 2), C // 2)
        return push(
            r.back.at[half, end], r.back.at[half, end], r.core_send.at[which],
            r.core_recv.at[which], mdl=plane + 1 - 2 * core,
        )

    @pl.when(me < pts - 1)
    def _():
        up_copy(me + 1).start()

    @pl.when(me == pts - 1)
    def _():
        r.back[:, HALO + rows :] = jnp.zeros((C, HALO), BF)

    @pl.when(me > 0)
    def _():
        down_copy(me - 1).start()

    @pl.when(me == 0)
    def _():
        r.back[:, :HALO] = jnp.zeros((C, HALO), BF)

    moves(WAIT, *second)
    for group in range(1, groups):
        grads(group)
        reduce.start(group)
        if group >= LAG:
            reduce.step(group - LAG)

    grad_one = r.grad_two[...] + r.delta[own_cols, :]
    r.grad_one[...] = grad_one

    def along(values):
        return jnp.sum(values.astype(F32), 1, keepdims=True)

    grad_normed = r.grad_normed[own_cols, :].astype(F32)
    columns = [
        along(r.back[own_cols, middle]),
        along(r.mixed[own_cols, :]),
        along(grad_one * r.mixed_unit[own_cols, :]),
        along(grad_one),
        along(grad_normed * r.one_unit[own_cols, :]),
        along(grad_normed),
        r.attend_sums[:, 0:2],
        r.mlp_sums[...],
    ]
    r.vectors[pl.ds(me, 1)] = jnp.concatenate(columns, 1).T[None]

    def vector_copy(p, slot):
        return push(
            r.vectors.at[slot], r.vectors.at[slot], r.vector_send.at[p], r.vector_recv.at[slot],
            pts=p,
        )

    for p in others(me, pts):
        vector_copy(p, me).start()

    @pl.when(me > 0)
    def _():
        up_copy(me - 1).wait_recv()
        core_copy(low_end, 0, core).start()

    @pl.when(me < pts - 1)
    def _():
        down_copy(me + 1).wait_recv()
        core_copy(high_end, 1, core).start()

    @pl.when(me > 0)
    def _():
        core_copy(low_end, 0, 1 - core).wait_recv()

    @pl.when(me < pts - 1)
    def _():
        core_copy(high_end, 1, 1 - core).wait_recv()

    def turn(tap, carry):
        weight = r.taps[:, pl.ds(taps - 1 - tap, 1)].reshape(C, cols)
        turned = dot(weight, r.back[...], TN).astype(BF)
        for tile in range(rows // TILE):
            hot = one_hot_window(r.ids, tap, tile)
            r.turn_acc[:, tile * TILE : (tile + 1) * TILE] += dot(
                turned[:, tile * TILE : tile * TILE + WINDOW], hot
            )
        return carry

    r.turn_acc[...] = jnp.zeros_like(r.turn_acc)
    left = list(range(groups - LAG, reduce.steps))
    cuts = [taps * i // len(left) for i in range(len(left) + 1)]
    for i, s in enumerate(left):
        lax.fori_loop(cuts[i], cuts[i + 1], turn, 0)
        reduce.step(s)
    r.point_grad[...] = (r.turn_acc[...] + r.grad_one[...]).T
    reduce.finish(r.summed)
    total = r.vectors[pl.ds(me, 1)][0]
    for p in others(me, pts):
        vector_copy(p, p).wait_recv()
        total = total + r.vectors[pl.ds(p, 1)][0]
    r.vector_grad[...] = total
    reduce.end()
    for p in others(me, pts):
        vector_copy(p, me).wait_send()

    @pl.when(me < pts - 1)
    def _():
        up_copy(me + 1).wait_send()
        core_copy(high_end, 1, core).wait_send()

    @pl.when(me > 0)
    def _():
        down_copy(me - 1).wait_send()
        core_copy(low_end, 0, core).wait_send()


LAG = 4


def back_pass(
    plan, first, ids, grad_normed, branch_full, grad_two, attend_grads, mlp_sums, attend_sums
):
    taps, cols, rows = first.taken.shape
    total = len(BACK_ORDER)
    share = C // plan.pts
    vmem = pltpu.VMEM
    return call(
        functools.partial(back_kernel, plan),
        "back_pass",
        1,
        dict(
            taken=Late(first.taken), pair=Late(first.pair), vec=first.vec, hidden=Late(first.hidden), mixed_unit=Late(first.mixed_unit), mixed_std=first.mixed_std, one_unit=Late(first.one_unit), one_std=first.one_std, taps=Late(first.taps_far), ids=ids,
            grad_normed=Late(grad_normed),
            branch_full=Late(branch_full), grad_two=Late(grad_two), attend_grads=attend_grads, mlp_sums=mlp_sums, attend_sums=attend_sums,
        ),
        dict(
            summed=((total, share, cols), BF),
            point_grad=((rows, cols), F32),
            vector_grad=((12 + FF // C, cols), F32),
        ),
        dict(
            reduce_net=(Reduce.buffers(plan, total, BACK_PACK, cols)),
            turn_acc=vmem((cols, rows), F32),
            grad_one=vmem((cols, rows), F32),
            delta=vmem((C, rows), F32),
            mixed=vmem((C, rows), BF),
            back=vmem((C, rows + 2 * HALO), BF),
            vectors=vmem((plan.pts, 12 + FF // C, cols), F32),
            halo_send=dma(2),
            halo_recv=dma(2),
            core_send=dma(2),
            core_recv=dma(2),
            vector_send=dma(plan.pts),
            vector_recv=dma(plan.pts),
        ),
        taps * rows * (WINDOW * 4 + 5 * C) * cols,
    )


def adam(first, second, grad):
    new_first = BETA_ONE * first + (1.0 - BETA_ONE) * grad
    new_second = BETA_TWO * second + (1.0 - BETA_TWO) * grad * grad
    direction = (
        new_first
        / (1.0 - BETA_ONE**STEP)
        / (jnp.sqrt(new_second / (1.0 - BETA_TWO**STEP)) + ADAM_EPS)
    )
    return new_first, new_second, direction


def owner_kernel(plan, r):
    pts, mdl, slots = plan.pts, plan.mdl, plan.slots
    share, cols = r.summed.shape[1:]
    me, plane = lax.axis_index(PTS), lax.axis_index(MDL)
    moves(START, r.left_move, r.right_move, r.first_move, r.second_move)
    greet(
        [
            {PTS: p, MDL: m}
            for i, p in enumerate([me] + others(me, pts))
            for j, m in enumerate([plane] + others(plane, mdl))
            if i + j > 0
        ]
    )

    count = r.summed.shape[0]
    r.listed[:count] = r.summed[...]
    r.listed[count:] = r.mlp_summed[...]

    def order(slot, carry):
        r.grads[pl.ds(slot, 1)] = r.listed[pl.ds(r.places[slot], 1)]
        return carry

    def whole_copy(j, step):
        m = lax.rem(plane + step, mdl)
        target, k = plan.worker(j), j // pts
        piece, spot = r.grads.at[m * slots + j], r.whole.at[k, me, plane]

        def near():
            return pltpu.make_async_copy(piece, spot, r.whole_here.at[k])

        def far():
            return push(
                piece, spot, r.whole_send.at[step, j], r.whole_recv.at[k, me, plane], pts=target,
                mdl=m,
            )

        return (me == target) & (step == 0), near, far

    def rows_copy(m, slot):
        return push(
            r.grads.at[pl.ds(m * slots, slots)], r.rows.at[slot], r.rows_send.at[m],
            r.rows_recv.at[slot], mdl=m,
        )

    def rows_here():
        return pltpu.make_async_copy(
            r.grads.at[pl.ds(plane * slots, slots)], r.rows.at[plane], r.rows_home
        )

    for step in range(mdl):
        m = lax.rem(plane + step, mdl)
        lax.fori_loop(m * slots, (m + 1) * slots, order, 0)
        for j in range(slots):
            home, near, far = whole_copy(j, step)

            @pl.when(home)
            def _():
                near().start()

            @pl.when(jnp.logical_not(home))
            def _():
                far().start()

    for m in others(plane, mdl):
        rows_copy(m, plane).start()
    rows_here().start()
    moves(WAIT, r.left_move, r.right_move, r.first_move, r.second_move)

    def result_copy(k, kind, p):
        return push(
            r.turned.at[k, kind, p], r.results.at[plan.work(me, k), kind], r.back_send.at[k, kind, p],
            r.back_recv.at[plan.work(me, k), kind], pts=p,
        )

    def result_here(k, kind):
        return pltpu.make_async_copy(
            r.turned.at[k, kind, me], r.results.at[plan.work(me, k), kind], r.back_home.at[k, kind]
        )

    def send_result(k, kind, value):
        r.turned[k, kind] = value.astype(BF).reshape(pts, share, C)
        for p in others(me, pts):
            result_copy(k, kind, p).start()
        result_here(k, kind).start()

    for k in range(plan.each):

        @pl.when(plan.work(me, k) < slots)
        def _():
            pltpu.make_async_copy(
                r.grads.at[0], r.whole.at[k, me, plane], r.whole_here.at[k]
            ).wait()
            for p_step in range(pts):
                for m_step in range(mdl):
                    if p_step + m_step > 0:
                        p, m = lax.rem(me + p_step, pts), lax.rem(plane + m_step, mdl)
                        push(
                            r.grads.at[0], r.whole.at[k, p, m], r.whole_send.at[0, 0],
                            r.whole_recv.at[k, p, m], pts=p, mdl=m,
                        ).wait_recv()
            left = r.left[k].reshape(C, C)
            right = r.right[k].reshape(C, C)
            halves = [
                dot(left, r.whole[k, :, m].reshape(C, cols), TN).astype(BF) for m in range(mdl)
            ]
            if cols % 128 == 0:
                rotated = dot(jnp.concatenate(halves, 1), right)
            else:
                rotated = sum(
                    dot(half, right[m * cols : (m + 1) * cols]) for m, half in enumerate(halves)
                )
            send_result(k, 0, rotated)
            _, _, direction = adam(
                r.first[k].reshape(C, C).astype(F32),
                r.second[k].reshape(C, C).astype(F32),
                rotated.astype(BF).astype(F32),
            )
            send_result(k, 1, dot(left, dot(direction.astype(BF), right, NT).astype(BF)))

    for m in others(plane, mdl):
        rows_copy(m, plane).wait_send()
        rows_copy(m, m).wait_recv()
    rows_here().wait()
    for j in range(slots):
        source, k = plan.worker(j), j // pts
        for kind in range(2):

            @pl.when(me != source)
            def _():
                push(
                    r.turned.at[k, kind, me], r.results.at[j, kind], r.back_send.at[k, kind, source],
                    r.back_recv.at[j, kind], pts=source,
                ).wait_recv()

    for k in range(plan.each):

        @pl.when(plan.work(me, k) < slots)
        def _():
            for kind in range(2):
                result_here(k, kind).wait()
                for p in others(me, pts):
                    result_copy(k, kind, p).wait_send()

    for step in range(mdl):
        for j in range(slots):
            home, near, far = whole_copy(j, step)

            @pl.when(jnp.logical_not(home))
            def _():
                far().wait_send()


def owner_update(plan, places, summed, mlp_summed, left, right, first, second):
    _, share, cols = summed.shape
    blocks = len(BACK_ORDER) + len(MLP_ORDER)
    pts, mdl, each, slots = plan.pts, plan.mdl, plan.each, plan.slots
    vmem = pltpu.VMEM
    return call(
        functools.partial(owner_kernel, plan),
        "owner_update",
        4,
        dict(places=places, summed=summed, mlp_summed=mlp_summed, left=Late(left), right=Late(right), first=Late(first), second=Late(second)),
        dict(
            rows=((mdl, slots, share, cols), BF),
            results=((slots, 2, share, C), BF),
        ),
        dict(
            grads=vmem((blocks, share, cols), BF),
            listed=vmem((blocks, share, cols), BF),
            whole=vmem((each, pts, mdl, share, cols), BF),
            turned=vmem((each, 2, pts, share, C), BF),
            whole_send=dma(mdl, slots),
            whole_recv=dma(each, pts, mdl),
            whole_here=dma(each),
            rows_send=dma(mdl),
            rows_recv=dma(mdl),
            rows_home=dma(),
            back_send=dma(each, 2, pts),
            back_recv=dma(slots, 2),
            back_home=dma(each, 2),
        ),
        8 * each * C * C * C,
        smem=("places",),
    )


def scan_index(row_ids, scan_lengths):
    bounds = jnp.cumsum(scan_lengths)
    return jnp.sum((row_ids[..., None] >= bounds[:-1]).astype(jnp.int32), -1)


def local(
    points,
    cotangent,
    neighbours,
    scan_lengths,
    to_patch,
    from_patch,
    owner_slot,
    weights,
    row_eigen_basis,
    right_basis,
    first_moment,
    second_moment,
    vectors,
    vector_first,
    vector_second,
):
    rows, cols = points.shape
    slot_count = from_patch.shape[0]
    pts = lax.axis_size(PTS)
    mdl = lax.axis_size(MDL)
    pts_index = lax.axis_index(PTS)
    patch_count = slot_count // PATCH
    matrix_rate = 1.6 * C ** (-0.5)
    plan = Layout(pts, mdl, owner_slot.shape[0], patch_count * scan_lengths.shape[0])

    row_ids = pts_index * rows + jnp.arange(rows, dtype=jnp.int32)
    own_scan = scan_index(row_ids, scan_lengths)
    near = neighbours.T
    usable = (near >= 0) & (scan_index(jnp.maximum(near, 0), scan_lengths) == own_scan[None, :])
    ids = jnp.where(usable, near - (pts_index * rows - HALO), -1)

    first = front(
        plan,
        owner_slot,
        weights,
        points,
        cotangent,
        vectors,
        ids,
        to_patch[None],
        from_patch[None],
        scan_lengths,
    )
    between = middle(
        plan, first, vectors, cotangent, row_eigen_basis, right_basis, first_moment, second_moment
    )
    last = back_pass(
        plan,
        first,
        ids,
        between.grad_normed,
        between.branch_full,
        between.grad_two,
        between.attend_grads,
        between.mlp_sums,
        between.attend_sums,
    )
    vector_grad = last.vector_grad
    listed = BACK_ORDER + MLP_ORDER
    places = jnp.array([listed.index(b) for b in range(len(listed))], jnp.int32)
    slot_ids = jnp.arange(len(listed), dtype=jnp.int32)
    place_of_slot = jnp.sum(
        jnp.where(owner_slot[None, :] == slot_ids[:, None], places[None, :], 0), 1
    )
    ended = owner_update(
        plan,
        place_of_slot,
        last.summed,
        between.mlp_summed,
        between.left_whole,
        between.right_whole,
        between.first_whole,
        between.second_whole,
    )
    reduced = ended.rows.transpose(1, 2, 0, 3).reshape(plan.slots, C // pts, C)
    results = ended.results
    rotated, update = results[:, 0].astype(F32), results[:, 1].astype(F32)
    new_first, new_second, _ = adam(first_moment, second_moment, rotated)
    new_weights = weights - matrix_rate * (update + MATRIX_DECAY * weights)
    new_vector_first, new_vector_second, vector_step = adam(
        vector_first, vector_second, vector_grad
    )
    new_vectors = vectors - VECTOR_RATE * vector_step
    return (
        between.out,
        last.point_grad,
        reduced.astype(F32),
        new_first,
        new_second,
        new_weights,
        new_weights.astype(BF),
        vector_grad,
        new_vector_first,
        new_vector_second,
        new_vectors,
    )


def solution(mesh):
    by_rows = P(PTS, MDL)
    owned = P(MDL, PTS, None)
    vector = P(None, MDL)
    return jax.shard_map(
        local,
        mesh=mesh,
        in_specs=(
            by_rows,
            by_rows,
            P(PTS, None),
            P(),
            P(PTS),
            P(PTS),
            P(),
            owned,
            owned,
            owned,
            owned,
            owned,
            vector,
            vector,
            vector,
        ),
        out_specs=(
            by_rows,
            by_rows,
            owned,
            owned,
            owned,
            owned,
            owned,
            vector,
            vector,
            vector,
            vector,
        ),
        check_vma=False,
    )
```

```python
import functools
import types

import jax
import jax.numpy as jnp
from jax import lax
from jax.experimental import pallas as pl
from jax.experimental.pallas import tpu as pltpu
from jax.sharding import PartitionSpec as P

C = 512
HD = 16
FF = 2048
TAPS = 27
HALO = 256
PATCH = 1024
STEP = 5

NORM_EPS = 1e-05
BETA_ONE = 0.9
BETA_TWO = 0.999
ADAM_EPS = 1e-08
VECTOR_RATE = 0.5
MATRIX_DECAY = 0.05
TILE = 256
WINDOW = TILE + 2 * HALO
BF = jnp.bfloat16
F32 = jnp.float32
VMEM_LIMIT = 58 * 1024 * 1024

NN = (((1,), (0,)), ((), ()))
NT = (((1,), (1,)), ((), ()))
TN = (((0,), (0,)), ((), ()))


def dot(a, b, dims=NN):
    return lax.dot_general(a, b, dims, preferred_element_type=F32)


def params(**kw):
    return pltpu.CompilerParams(vmem_limit_bytes=VMEM_LIMIT, **kw)


MESH = pl.DeviceIdType.MESH
PTS, MDL = "pts", "mdl"
START, WAIT = range(2)


def push(src, dst, send_sem, recv_sem, **target):
    return pltpu.make_async_remote_copy(
        src_ref=src,
        dst_ref=dst,
        send_sem=send_sem,
        recv_sem=recv_sem,
        device_id=target,
        device_id_type=MESH,
    )


def greet(peers):
    barrier = pltpu.get_barrier_semaphore()
    for peer in peers:
        pl.semaphore_signal(barrier, inc=1, device_id=peer, device_id_type=MESH)
    pl.semaphore_wait(barrier, len(peers))


def others(index, size):
    return [lax.rem(index + step, size) for step in range(1, size)]


class Layout:
    def __init__(self, pts, mdl, blocks, groups):
        self.pts, self.mdl, self.groups = pts, mdl, groups
        self.slots = blocks // mdl
        self.each = -(-self.slots // pts)
        self.shift = max(pts - self.slots, 0) // 2 if self.slots < pts else (pts - self.slots % pts) // 2
        self.width = mdl // 2 if pts % (mdl // 2) == 0 else 1
        self.depth = pts // self.width

    def worker(self, j):
        return (j + self.shift) % self.pts

    def work(self, me, k):
        return lax.rem(me + self.pts - self.shift, self.pts) + k * self.pts


def fetch_copies(plan, src, dst, sems, act):
    send, recv, here = sems
    me = lax.axis_index(PTS)
    for j in range(plan.slots):
        target, k = plan.worker(j), j // plan.pts

        @pl.when(me != target)
        def _():
            copy = push(src.at[j], dst.at[k, me], send.at[j], recv.at[k, me], pts=target)
            copy.start() if act == START else copy.wait_send()

        @pl.when(me == target)
        def _():
            copy = pltpu.make_async_copy(src.at[j], dst.at[k, me], here.at[k])
            if act == START:
                copy.start()
            else:
                copy.wait()
                for source in others(me, plan.pts):
                    push(
                        src.at[j], dst.at[k, source], send.at[j], recv.at[k, source], pts=source
                    ).wait_recv()


def fetch_sems(plan):
    return [dma(plan.slots), dma(plan.each, plan.pts), dma(plan.each)]


def fetch_shape(plan, src):
    return jax.ShapeDtypeStruct((plan.each, plan.pts) + src.shape[1:], BF)


class Late:
    def __init__(self, *what):
        self.what = what


def call(kernel, name, collective, inputs, outputs, scratch, flops, smem=(), free=()):
    vmem = pltpu.VMEM
    leaves, tree = jax.tree.flatten(scratch, is_leaf=lambda x: not isinstance(x, (dict, list)))
    late_in = [key for key, value in inputs.items() if isinstance(value, Late)]
    late_out = [key for key, value in outputs.items() if isinstance(value, Late)]
    values = {key: v.what[0] if key in late_in else v for key, v in inputs.items()}
    shapes = {key: v.what if key in late_out else v for key, v in outputs.items()}
    near = [vmem(values[key].shape, values[key].dtype) for key in late_in]
    near += [vmem(*shapes[key]) for key in late_out]
    late = late_in + late_out

    def space(key, value):
        return pltpu.SMEM if key in smem else pl.ANY if key in free or key in late else vmem

    def grouped(x):
        if isinstance(x, dict):
            return types.SimpleNamespace(**{key: grouped(value) for key, value in x.items()})
        return [grouped(value) for value in x] if isinstance(x, list) else x

    def body(*refs):
        count = len(inputs) + len(outputs)
        given = dict(zip(inputs, refs))
        given.update(zip(outputs, refs[len(inputs) : count]))
        own, sems = refs[count : count + len(late)], refs[count + len(late) : count + 2 * len(late)]
        r = grouped(jax.tree.unflatten(tree, refs[count + 2 * len(late) :]))
        for key, ref in given.items():
            setattr(r, key, ref)
        for key, ref, sem in zip(late, own, sems):
            pair = (given[key], ref) if key in late_in else (ref, given[key])
            setattr(r, key, ref)
            setattr(r, key + "_move", functools.partial(pltpu.make_async_copy, *pair, sem))
        kernel(r)

    results = pl.pallas_call(
        body,
        in_specs=[pl.BlockSpec(memory_space=space(*item)) for item in inputs.items()],
        out_specs=[pl.BlockSpec(memory_space=space(*item)) for item in outputs.items()],
        out_shape=[jax.ShapeDtypeStruct(*shape) for shape in shapes.values()],
        scratch_shapes=near + [dma() for _ in late] + leaves,
        compiler_params=params(collective_id=collective, has_side_effects=True),
        cost_estimate=pl.CostEstimate(
            flops=flops, bytes_accessed=20000000, transcendentals=1000000
        ),
        name=name,
    )(*values.values())
    return types.SimpleNamespace(**dict(zip(outputs, results)))


def moves(act, *copies):
    for make in copies:
        copy = make()
        copy.start() if act == START else copy.wait()


def dma(*shape):
    return pltpu.SemaphoreType.DMA(shape)


class Gather:
    def __init__(self, plan, part, sems):
        self.part, self.sems = part, sems
        self.plane = lax.axis_index(MDL)
        self.size = plan.mdl // 2
        self.x, self.core = self.plane // 2, lax.rem(self.plane, 2)

    @staticmethod
    def semaphores(plan):
        return dict(x_send=dma(plan.mdl // 2), recv=dma(plan.mdl), core_send=dma(plan.mdl // 2))

    def along(self, m, target, send):
        return push(self.part(m), self.part(m), send, self.sems.recv.at[m], mdl=target)

    def x_copy(self, x):
        return self.along(self.plane, x * 2 + self.core, self.sems.x_send.at[x])

    def core_copy(self, x):
        return self.along(
            x * 2 + self.core, self.x * 2 + 1 - self.core, self.sems.core_send.at[x]
        )

    def arrived(self, m):
        self.along(m, m, self.sems.x_send.at[0]).wait_recv()

    def start(self):
        for x in others(self.x, self.size):
            self.x_copy(x).start()
        self.core_copy(self.x).start()

    def forward(self):
        for x in others(self.x, self.size):
            self.arrived(x * 2 + self.core)
            self.core_copy(x).start()

    def finish(self):
        for x in [self.x] + others(self.x, self.size):
            self.arrived(x * 2 + 1 - self.core)
        for x in others(self.x, self.size):
            self.x_copy(x).wait_send()
            self.core_copy(x).wait_send()
        self.core_copy(self.x).wait_send()

    def run(self):
        self.start()
        self.forward()
        self.finish()


class Sum:
    def __init__(self, plan, parts, bufs):
        self.parts, self.bufs = parts, bufs
        self.plane = lax.axis_index(MDL)
        self.size = plan.mdl // 2
        self.x, self.core = self.plane // 2, lax.rem(self.plane, 2)

    @staticmethod
    def buffers(plan, shape):
        x = plan.mdl // 2
        vmem = pltpu.VMEM((x,) + shape, BF)
        return dict(
            near=vmem, middle=vmem, far=vmem,
            near_send=dma(x), near_recv=dma(x), far_send=dma(x), far_recv=dma(x),
        )

    def near_copy(self, x):
        b = self.bufs
        return push(
            self.parts.at[x * 2 + 1 - self.core], b.near.at[x], b.near_send.at[x],
            b.near_recv.at[x], mdl=self.x * 2 + 1 - self.core,
        )

    def far_copy(self, x, slot):
        b = self.bufs
        return push(
            b.middle.at[x], b.far.at[slot], b.far_send.at[x], b.far_recv.at[slot],
            mdl=x * 2 + self.core,
        )

    def both(self, x):
        self.near_copy(x).wait_recv()
        own = self.parts[pl.ds(x * 2 + self.core, 1)][0].astype(F32)
        return own + self.bufs.near[pl.ds(x, 1)][0].astype(F32)

    def start(self):
        for x in others(self.x, self.size) + [self.x]:
            self.near_copy(x).start()

    def middle(self):
        for x in others(self.x, self.size):
            self.bufs.middle[pl.ds(x, 1)] = self.both(x).astype(BF)[None]
            self.far_copy(x, self.x).start()

    def finish(self):
        total = self.both(self.x)
        for x in others(self.x, self.size):
            self.far_copy(x, x).wait_recv()
            total = total + self.bufs.far[pl.ds(x, 1)][0].astype(F32)
        for x in others(self.x, self.size):
            self.near_copy(x).wait_send()
            self.far_copy(x, self.x).wait_send()
        self.near_copy(self.x).wait_send()
        return total

    def run(self):
        self.start()
        self.middle()
        return self.finish()


class Trade:
    def __init__(self, plan, out_index, in_index, bufs):
        self.out_index, self.in_index, self.bufs = out_index, in_index, bufs
        self.size = plan.pts
        self.me = lax.axis_index(PTS)

    @staticmethod
    def buffers(plan, cols, rows):
        capacity = 2 * rows // plan.pts
        vmem = pltpu.VMEM((plan.pts, cols, capacity), BF)
        return dict(leave=vmem, land=vmem, send=dma(plan.pts), recv=dma(plan.pts))

    def leaving(self, values, part):
        capacity = self.bufs.leave.shape[2]
        row = self.out_index[...]
        places = lax.broadcasted_iota(jnp.int32, (capacity, row.shape[1]), 0) + part * capacity
        hot = jnp.where(places == row, 1.0, 0.0).astype(BF)
        return dot(hot, values, NT).T.astype(BF)

    def landing(self, part):
        capacity = self.bufs.land.shape[2]
        shape = (self.in_index.shape[1], capacity)
        places = lax.broadcasted_iota(jnp.int32, shape, 1) + part * capacity
        return jnp.where(places == self.in_column, 1.0, 0.0).astype(BF)

    def copy(self, part, slot):
        b = self.bufs
        return push(
            b.leave.at[part], b.land.at[slot], b.send.at[part], b.recv.at[slot],
            pts=part,
        )

    def start(self, values):
        b = self.bufs
        for part in others(self.me, self.size):
            b.leave[pl.ds(part, 1)] = self.leaving(values, part)[None]
            self.copy(part, self.me).start()
        b.land[pl.ds(self.me, 1)] = self.leaving(values, self.me)[None]

    def finish(self):
        b = self.bufs
        self.in_column = column(self.in_index[...])
        total = dot(self.landing(self.me), b.land[pl.ds(self.me, 1)][0], NT)
        for step in range(1, self.size):
            part = lax.rem(self.me + self.size - step, self.size)
            hot = self.landing(part)
            self.copy(part, part).wait_recv()
            total = total + dot(hot, b.land[pl.ds(part, 1)][0], NT)
        for part in others(self.me, self.size):
            self.copy(part, self.me).wait_send()
        return total.T.astype(BF)


class Route:
    PIECES = 2

    def __init__(self, plan, out_index, in_index, full, nets):
        cols = full.shape[0] // plan.mdl
        self.size = cols // self.PIECES
        self.full, self.base = full, lax.axis_index(MDL) * cols
        self.trades = [Trade(plan, out_index, in_index, net.trade) for net in nets]
        self.gathers = [
            Gather(
                plan, lambda m, i=i: full.at[pl.ds(m * cols + i * self.size, self.size)], net.ring
            )
            for i, net in enumerate(nets)
        ]

    @classmethod
    def buffers(cls, plan, cols, rows):
        net = dict(
            trade=Trade.buffers(plan, cols // cls.PIECES, rows), ring=Gather.semaphores(plan)
        )
        return [net] * cls.PIECES

    def start(self, values):
        for i, trade in enumerate(self.trades):
            trade.start(values[i * self.size : (i + 1) * self.size])

    def land(self):
        for i, (trade, gather) in enumerate(zip(self.trades, self.gathers)):
            self.full[pl.ds(self.base + i * self.size, self.size), :] = trade.finish()
            gather.start()
            if i > 0:
                self.gathers[i - 1].forward()
        self.gathers[-1].forward()

    def finish(self):
        for gather in self.gathers:
            gather.finish()


class Reduce:
    def __init__(self, plan, bufs):
        self.bufs = bufs
        self.width, self.depth = plan.width, plan.depth
        self.me = lax.axis_index(PTS)
        self.y, self.z = lax.rem(self.me, self.width), self.me // self.width
        self.groups, _, self.pack, self.share, self.cols = bufs.acc.shape
        self.steps = self.groups + self.depth - 1

    @staticmethod
    def buffers(plan, blocks, pack, cols):
        groups, share, vmem = blocks // pack, C // plan.pts, pltpu.VMEM
        line = (plan.depth, pack, share, cols)
        way = dict(
            land=vmem((groups,) + line, BF),
            send=dma(groups, plan.depth),
            recv=dma(groups, plan.depth),
        )
        return dict(
            own=vmem((plan.width, groups) + line, BF),
            side=vmem((plan.width, groups) + line, BF),
            acc=vmem((groups,) + line, BF),
            up=way,
            down=way,
            side_send=dma(plan.width, groups),
            side_recv=dma(plan.width, groups),
        )

    def store(self, block, group, place):
        grid = block.astype(BF).reshape(self.depth, self.width, self.share, self.cols)
        for v in range(self.width):
            self.bufs.own[v, group, :, pl.ds(place, 1)] = grid[:, v][:, None]

    def side_copy(self, group, v, slot):
        b = self.bufs
        return push(
            b.own.at[v, group], b.side.at[slot, group], b.side_send.at[v, group],
            b.side_recv.at[slot, group], pts=self.z * self.width + v,
        )

    def line_copy(self, way, group, to, step):
        b = self.bufs
        near = jnp.clip(self.z + step, 0, self.depth - 1)
        return push(
            b.acc.at[group, to], way.land.at[group, to], way.send.at[group, to],
            way.recv.at[group, to], pts=near * self.width + self.y,
        )

    def start(self, group):
        for v in others(self.y, self.width):
            self.side_copy(group, v, self.y).start()

    def sum_side(self, group):
        b = self.bufs
        total = b.own[pl.ds(self.y, 1), pl.ds(group, 1)][0].astype(F32)
        for v in others(self.y, self.width):
            self.side_copy(group, v, v).wait_recv()
            total = total + b.side[pl.ds(v, 1), pl.ds(group, 1)][0].astype(F32)
        b.acc[pl.ds(group, 1)] = total.astype(BF)

    def relay(self, way, group, step, first):
        b = self.bufs

        @pl.when((group >= 0) & (group < self.groups))
        def _():
            for to in range(self.depth):

                @pl.when((to - self.z) * step > 0)
                def _():
                    @pl.when(jnp.logical_not(first))
                    def _():
                        self.line_copy(way, group, to, -step).wait_recv()
                        spot = (pl.ds(group, 1), to)
                        b.acc[spot] = (
                            b.acc[spot].astype(F32) + way.land[spot].astype(F32)
                        ).astype(BF)

                    self.line_copy(way, group, to, step).start()

    def step(self, s):
        if isinstance(s, int):
            if s < self.groups:
                self.sum_side(s)
        else:

            @pl.when((s >= 0) & (s < self.groups))
            def _():
                self.sum_side(s)

        self.relay(self.bufs.up, s - self.z, 1, self.z == 0)
        self.relay(self.bufs.down, s - (self.depth - 1 - self.z), -1, self.z == self.depth - 1)

    def finish(self, out):
        b, z = self.bufs, self.z

        def total(way, group):
            b.acc[group, pl.ds(z, 1)] = (
                b.acc[group, pl.ds(z, 1)].astype(F32) + way.land[group, pl.ds(z, 1)].astype(F32)
            ).astype(BF)

        for group in range(self.groups):

            @pl.when(z > 0)
            def _():
                self.line_copy(self.bufs.up, group, z, -1).wait_recv()
                total(b.up, group)

            @pl.when(z < self.depth - 1)
            def _():
                self.line_copy(self.bufs.down, group, z, 1).wait_recv()
                total(b.down, group)

            out[group * self.pack : (group + 1) * self.pack] = b.acc[group, pl.ds(z, 1)][0]

    def end(self):
        for group in range(self.groups):
            for v in others(self.y, self.width):
                self.side_copy(group, v, self.y).wait_send()
            for to in range(self.depth):

                @pl.when(to > self.z)
                def _():
                    self.line_copy(self.bufs.up, group, to, 1).wait_send()

                @pl.when(to < self.z)
                def _():
                    self.line_copy(self.bufs.down, group, to, -1).wait_send()


def everyone(plan):
    me, plane = lax.axis_index(PTS), lax.axis_index(MDL)
    return [{PTS: p} for p in others(me, plan.pts)] + [{MDL: m} for m in others(plane, plan.mdl)]


def unit_columns(values):
    mean = jnp.sum(values, 0, keepdims=True) / C
    centred = values - mean
    inv_std = lax.rsqrt(jnp.sum(centred * centred, 0, keepdims=True) / C + NORM_EPS)
    return centred * inv_std, inv_std


def one_hot_window(ids_ref, tap, tile):
    row = ids_ref[pl.ds(tap, 1), pl.ds(tile * TILE, TILE)]
    places = lax.broadcasted_iota(jnp.int32, (WINDOW, TILE), 0) + tile * TILE
    return jnp.where(places == row, 1.0, 0.0).astype(BF)


PACK = 5
ORDER = [TAPS, TAPS + 4] + list(range(TAPS)) + [TAPS + 1, TAPS + 2, TAPS + 3]
ORDER = ORDER + list(range(TAPS + 5, TAPS + 5 + 2 * FF // C))
PLACE = {block: place for place, block in enumerate(ORDER)}


def column(row):
    wide = jnp.broadcast_to(row.astype(F32), (8, row.shape[1]))
    return wide.T[:, 0:1].astype(jnp.int32)


def steps_passed(values, bounds):
    return sum((values >= bound).astype(jnp.int32) for bound in bounds)


def routes(plan, r, rows):
    capacity = 2 * rows // plan.pts
    slot_count = r.from_patch.shape[1]
    patches = slot_count // PATCH
    scans = r.scan_lengths.shape[0]
    target = steps_passed(r.to_patch[...], [p * slot_count for p in range(1, plan.pts)])
    size = 256
    rank = jnp.zeros((1, rows), jnp.int32)
    target_column = column(target)
    ahead = lax.broadcasted_iota(jnp.int32, (size, rows), 1)
    for low in range(0, rows, size):
        earlier = lax.broadcasted_iota(jnp.int32, (size, rows), 0) + low < ahead
        same = target_column[low : low + size] == target
        rank = rank + jnp.sum((earlier & same).astype(jnp.int32), 0, keepdims=True)
    r.send_pos[...] = target * capacity + rank
    held = r.from_patch[...]
    used = held >= 0
    lanes = lax.broadcasted_iota(jnp.int32, (1, slot_count), 1)
    patch = steps_passed(lanes, [p * PATCH for p in range(1, patches)])
    source = steps_passed(held, [p * rows for p in range(1, plan.pts)])
    bounds, bound = [], 0
    for i in range(scans - 1):
        bound = bound + r.scan_lengths[i]
        bounds.append(bound)
    group = patch * scans + (steps_passed(held, bounds) if bounds else 0)
    top = patches * plan.pts * rows
    order_key = jnp.where(used, patch * (plan.pts * rows) + held, top)
    held_key = jnp.where(used, held, top)
    order_column, held_column = column(order_key), column(held_key)
    first_key = source * rows
    order = jnp.zeros((1, slot_count), jnp.int32)
    rank = jnp.zeros((1, slot_count), jnp.int32)
    for low in range(0, slot_count, size):
        part = slice(low, low + size)
        order = order + jnp.sum(
            (order_column[part] < order_key).astype(jnp.int32), 0, keepdims=True
        )
        among = (held_column[part] < held_key) & (held_column[part] >= first_key)
        rank = rank + jnp.sum(among.astype(jnp.int32), 0, keepdims=True)
    base = plan.pts * capacity
    both = column(group * base + source * capacity + rank)
    order = column(jnp.where(used, order, slot_count))
    places = lax.broadcasted_iota(jnp.int32, (size, rows), 1)
    found = jnp.zeros((1, rows), jnp.int32)
    for low in range(0, slot_count, size):
        part = slice(low, low + size)
        found = found + jnp.sum(
            jnp.where(order[part] == places, both[part], 0), 0, keepdims=True
        )
    group = steps_passed(found, [base * g for g in range(1, patches * scans)])
    r.group[...] = group
    r.arrival[...] = found - group * base


def front_kernel(plan, r):
    pts, mdl, slots = plan.pts, plan.mdl, plan.slots
    width, depth = plan.width, plan.depth
    me, plane = lax.axis_index(PTS), lax.axis_index(MDL)
    y, z = lax.rem(me, width), me // width
    rows, cols = r.points_rows.shape
    share = C // pts
    total = r.blocks.shape[1]
    groups = total // PACK
    conv_groups = -(-(2 + TAPS) // PACK)
    for m in range(mdl):
        r.owned[m] = r.weights[:, :, m * cols : (m + 1) * cols].astype(BF)
    greet(everyone(plan))

    def spread_copy(m, slot):
        return push(
            r.owned.at[m], r.spread.at[pl.ds(slot * slots, slots)], r.spread_send.at[m],
            r.spread_recv.at[slot], mdl=m,
        )

    for m in others(plane, mdl):
        spread_copy(m, plane).start()

    def vec_copy(m, slot):
        return push(
            r.vectors, r.vec_all.at[slot], r.vec_send.at[m], r.vec_recv.at[slot], mdl=m
        )

    for m in others(plane, mdl):
        vec_copy(m, plane).start()

    r.points[...] = r.points_rows[...].astype(F32).T.astype(BF)

    def up_copy():
        return push(
            r.points.at[:, rows - HALO : rows], r.ext.at[:, 0:HALO], r.halo_send.at[0],
            r.halo_recv.at[0], pts=me + 1,
        )

    def down_copy():
        return push(
            r.points.at[:, 0:HALO], r.ext.at[:, HALO + rows : 2 * HALO + rows], r.halo_send.at[1],
            r.halo_recv.at[1], pts=me - 1,
        )

    @pl.when(me < pts - 1)
    def _():
        up_copy().start()

    @pl.when(me == pts - 1)
    def _():
        r.ext[:, HALO + rows :] = jnp.zeros((cols, HALO), BF)

    @pl.when(me > 0)
    def _():
        down_copy().start()

    @pl.when(me == 0)
    def _():
        r.ext[:, :HALO] = jnp.zeros((cols, HALO), BF)

    r.ext[:, HALO : HALO + rows] = r.points[...]
    r.spread[pl.ds(plane * slots, slots)] = r.owned[pl.ds(plane, 1)][0]
    r.vec_all[pl.ds(plane, 1)] = r.vectors[...][None]
    r.points_full[pl.ds(plane * cols, cols), :] = r.points[...]
    for m in others(plane, mdl):
        spread_copy(m, m).wait_recv()
    for place, block in enumerate(ORDER):
        r.blocks[pl.ds(me, 1), place] = r.spread[pl.ds(r.slots[block], 1)]

    def group_of(source, group):
        return r.blocks.at[source, group * PACK : (group + 1) * PACK]

    def far_copy(group, source, step):
        return push(
            group_of(source, group), group_of(source, group),
            r.far_send.at[(step + 1) // 2, group, source // width],
            r.far_recv.at[group, source // width], pts=jnp.clip(z + step, 0, depth - 1) * width + y,
        )

    def side_copy(group, v, source):
        return push(
            group_of(source, group), group_of(source, group),
            r.side_send.at[group, v, source // width], r.side_recv.at[group, source],
            pts=z * width + v,
        )

    def pass_on(group, source, act):
        from_z = source // width

        @pl.when((z < depth - 1) & (from_z <= z))
        def _():
            copy = far_copy(group, source, 1)
            copy.start() if act == START else copy.wait_send()

        @pl.when((z > 0) & (from_z >= z))
        def _():
            copy = far_copy(group, source, -1)
            copy.start() if act == START else copy.wait_send()

        for v in others(y, width):
            copy = side_copy(group, v, source)
            copy.start() if act == START else copy.wait_send()

    def relay(group, away, act):
        for from_z in (z - away, z + away):

            @pl.when((from_z >= 0) & (from_z < depth))
            def _():
                source = from_z * width + y
                if act == START:
                    far_copy(group, source, 1).wait_recv()
                pass_on(group, source, act)

    ahead = groups
    for group in range(ahead):
        pass_on(group, me, START)

    points_gather = Gather(
        plan, lambda m: r.points_full.at[pl.ds(m * cols, cols)],
        r.points_net,
    )
    cot_gather = Gather(
        plan, lambda m: r.cot_full.at[pl.ds(m * cols, cols)],
        r.cot_net,
    )
    points_gather.start()
    r.cot_full[pl.ds(plane * cols, cols), :] = r.cot_rows[...].astype(F32).T.astype(BF)
    cot_gather.start()
    routes(plan, r, rows)

    @pl.when(me > 0)
    def _():
        push(
            r.points.at[:, 0:HALO], r.ext.at[:, 0:HALO], r.halo_send.at[0], r.halo_recv.at[0],
            pts=me - 1,
        ).wait_recv()

    @pl.when(me < pts - 1)
    def _():
        push(
            r.points.at[:, 0:HALO], r.ext.at[:, HALO + rows : 2 * HALO + rows], r.halo_send.at[1],
            r.halo_recv.at[1], pts=me + 1,
        ).wait_recv()

    def take(tap, carry):
        for tile in range(rows // TILE):
            hot = one_hot_window(r.ids, tap, tile)
            picked = dot(r.ext[:, tile * TILE : tile * TILE + WINDOW], hot).astype(BF)
            r.taken[pl.ds(tap, 1), :, tile * TILE : (tile + 1) * TILE] = picked[None]
        return carry

    steps = groups + depth - 2
    cuts = [min(TAPS, -(-TAPS * i // groups)) for i in range(steps + 1)]
    for step in range(steps):
        if step + ahead < groups:
            pass_on(step + ahead, me, START)
        if cuts[step] < cuts[step + 1]:
            lax.fori_loop(cuts[step], cuts[step + 1], take, 0)
        for away in range(1, depth):
            if 0 <= step + 1 - away < groups:
                relay(step + 1 - away, away, START)
    moves(START, r.taken_move)

    def complete(group):
        for u in others(y, width):
            for v in range(depth):
                side_copy(group, u, v * width + u).wait_recv()

    pair_gather = Gather(
        plan, lambda m: r.pair.at[m], r.pair_net
    )
    for group in range(conv_groups):
        complete(group)
        if group == 0:
            for i in range(2):
                r.pair[pl.ds(plane, 1), i] = r.blocks[:, i].reshape(1, C, cols)
            pair_gather.start()
        low = max(group * PACK - 2, 0)
        high = min(group * PACK - 2 + PACK, TAPS)
        if cols % 128 == 0:
            weight = jnp.concatenate(
                [r.blocks[:, t + 2].reshape(C, cols) for t in range(low, high)], 1
            )
            part = dot(weight, r.taken[low:high].reshape((high - low) * cols, rows))
        else:
            part = sum(dot(r.blocks[:, t + 2].reshape(C, cols), r.taken[t]) for t in range(low, high))
        if group == 0:
            r.acc[...] = part
            pair_gather.forward()
        else:
            r.acc[...] += part

    taps_copy = pltpu.make_async_copy(r.blocks.at[:, 2 : 2 + TAPS], r.taps_far, r.taps_sem)
    taps_copy.start()
    points_gather.forward()
    cot_gather.forward()
    r.parts[...] = r.acc[...].astype(BF).reshape(mdl, cols, rows)
    hidden_sum = Sum(plan, r.parts, r.sum_net)
    hidden_sum.start()
    for m in others(plane, mdl):
        vec_copy(m, m).wait_recv()
    for m in range(mdl):
        r.vec[m * cols : (m + 1) * cols, :] = r.vec_all[m].T
    pair_gather.finish()
    points_gather.finish()
    hidden_sum.middle()
    bias = r.vec[pl.ds(plane * cols, cols), 0:1]
    r.hidden[pl.ds(plane * cols, cols), :] = (hidden_sum.finish() + bias).astype(BF)
    Gather(
        plan, lambda m: r.hidden.at[pl.ds(m * cols, cols)],
        r.hidden_net,
    ).run()
    hidden = r.hidden[...]
    for m in range(mdl):
        r.acc[m * cols : (m + 1) * cols, :] = dot(r.pair[m, 0], hidden, TN)
    span_size = 128

    def norms(step, carry):
        span = pl.ds(pl.multiple_of(step * span_size, span_size), span_size)
        unit, inv_std = unit_columns(r.acc[:, span] + r.vec[:, 1:2])
        r.mixed_unit[:, span] = unit.astype(BF)
        r.mixed_std[:, span] = inv_std
        stream = r.points_full[:, span].astype(F32) + unit * r.vec[:, 2:3] + r.vec[:, 3:4]
        r.stream[:, span] = stream
        unit, inv_std = unit_columns(stream)
        r.one_unit[:, span] = unit.astype(BF)
        r.one_std[:, span] = inv_std
        r.normed[:, span] = (unit * r.vec[:, 4:5] + r.vec[:, 5:6]).astype(BF)
        return carry

    lax.fori_loop(0, rows // span_size, norms, 0)
    route = Route(plan, r.send_pos, r.arrival, r.slot_in, r.route_net)
    route.start(r.normed[pl.ds(plane * cols, cols), :])
    moves(START, r.hidden_move, r.mixed_unit_move, r.one_unit_move, r.stream_move, r.pair_move)
    for group in range(conv_groups, groups):
        complete(group)
    for i in range(r.rest.shape[0]):
        r.rest[i] = r.blocks[:, TAPS + 2 + i].reshape(C, cols)
    cot_gather.finish()
    moves(START, r.rest_move, r.cot_full_move)
    route.land()
    route.finish()
    moves(START, r.slot_in_move)

    @pl.when(me < pts - 1)
    def _():
        up_copy().wait_send()

    @pl.when(me > 0)
    def _():
        down_copy().wait_send()

    for m in others(plane, mdl):
        spread_copy(m, plane).wait_send()
        vec_copy(m, plane).wait_send()
    for group in range(groups):
        pass_on(group, me, WAIT)
        for away in range(1, depth):
            relay(group, away, WAIT)
    moves(WAIT, r.taken_move, r.cot_full_move, r.pair_move, r.hidden_move, r.mixed_unit_move, r.one_unit_move, r.stream_move, r.slot_in_move, r.rest_move)
    taps_copy.wait()


def front(plan, slots, weights, points, cot, vectors, ids, to_patch, from_patch, scan_lengths):
    rows, cols = points.shape
    pts, mdl = plan.pts, plan.mdl
    share = C // pts
    total = len(ORDER)
    groups = total // PACK
    vmem = pltpu.VMEM
    ring = Gather.semaphores(plan)
    scratch = dict(
        points_net=ring,
        cot_net=ring,
        pair_net=ring,
        hidden_net=ring,
        owned=vmem((mdl, plan.slots, share, cols), BF),
        points=vmem((cols, rows), BF),
        spread=vmem((total, share, cols), BF),
        vec_all=vmem((mdl,) + vectors.shape, F32),
        ext=vmem((cols, rows + 2 * HALO), BF),
        acc=vmem((C, rows), F32),
        parts=vmem((mdl, cols, rows), BF),
        normed=vmem((C, rows), BF),
        points_full=vmem((C, rows), BF),
        spread_send=dma(mdl),
        spread_recv=dma(mdl),
        vec_send=dma(mdl),
        vec_recv=dma(mdl),
        halo_send=dma(2),
        halo_recv=dma(2),
        blocks=vmem((pts, total, share, cols), BF),
        taps_sem=dma(),
        far_send=dma(2, groups, plan.depth),
        far_recv=dma(groups, plan.depth),
        side_send=dma(groups, plan.width, plan.depth),
        side_recv=dma(groups, pts),
        sum_net=(Sum.buffers(plan, (cols, rows))),
        route_net=Route.buffers(plan, cols, rows),
    )
    return call(
        functools.partial(front_kernel, plan),
        "front",
        5,
        dict(
            slots=slots, weights=weights, points_rows=points, cot_rows=cot, vectors=vectors,
            ids=ids, to_patch=to_patch, from_patch=from_patch, scan_lengths=scan_lengths,
        ),
        dict(
            taps_far=((pts, TAPS, share, cols), BF),
            taken=Late((TAPS, cols, rows), BF),
            cot_full=Late((C, rows), BF),
            pair=Late((mdl, 2, C, cols), BF),
            vec=((C, vectors.shape[0]), F32),
            hidden=Late((C, rows), BF),
            mixed_unit=Late((C, rows), BF),
            mixed_std=((1, rows), F32),
            stream=Late((C, rows), F32),
            one_unit=Late((C, rows), BF),
            one_std=((1, rows), F32),
            send_pos=((1, rows), jnp.int32),
            arrival=((1, rows), jnp.int32),
            group=((1, rows), jnp.int32),
            slot_in=Late((C, rows), BF),
            rest=Late((total - TAPS - 2, C, cols), BF),
        ),
        scratch,
        4 * TAPS * rows * (WINDOW + C) * cols,
        smem=("slots", "scan_lengths"),
        free=("taps_far",),
    )


def head_lanes(ext, cols, head):
    lane = lax.broadcasted_iota(jnp.int32, ext.shape, 1)
    return jnp.where((lane >= cols) | (lane // HD == head), ext, jnp.zeros_like(ext))


def head_rows(head):
    return pl.ds(pl.multiple_of(head * HD, HD), HD)


SPAN = 128


def over_spans(rows, body, size=SPAN):
    def step(index, carry):
        body(pl.ds(pl.multiple_of(index * size, size), size))
        return carry

    lax.fori_loop(0, rows // size, step, 0)


def beside(blocks):
    def times(right, cols):
        if cols % 128 == 0:
            return dot(jnp.concatenate(blocks, 1), right[...])
        return sum(
            dot(block, right[i * cols : (i + 1) * cols, :]) for i, block in enumerate(blocks)
        )

    return times


def mlp_part(plan, r):
    mdl = plan.mdl
    plane = lax.axis_index(MDL)
    cols, rows = r.cot.shape
    ff_blocks = FF // C
    own = pl.ds(plane * cols, cols)
    moves(WAIT, r.pair_move)
    r.acc[...] = beside([r.pair[m, 1] for m in range(mdl)])(r.attended_rows, cols)
    moves(WAIT, r.stream_move, r.cot_full_move)

    def norms(span):
        branch = (r.acc[:, span] + r.vec[:, 8:9]).astype(BF).astype(F32)
        two = r.stream[:, span] + branch
        r.stream[:, span] = two
        unit, inv_std = unit_columns(two)
        r.two_unit[:, span] = unit
        r.two_std[:, span] = inv_std
        r.normed[:, span] = (unit * r.vec[:, 9:10] + r.vec[:, 10:11]).astype(BF)

    over_spans(rows, norms)
    if cols % 128 == 0:
        first, second = (
            jnp.concatenate([r.rest[low + k] for k in range(ff_blocks)], 1)
            for low in (3, 3 + ff_blocks)
        )
        r.acc[...] = dot(first, r.normed[...], TN)
        r.grad_act[...] = dot(second, r.cot_full[...], TN)
    for k in range(ff_blocks):
        part = slice(k * cols, (k + 1) * cols)
        if cols % 128 != 0:
            r.acc[part, :] = dot(r.rest[3 + k], r.normed[...], TN)
            r.grad_act[part, :] = dot(r.rest[3 + ff_blocks + k], r.cot_full[...], TN)

        def bend(span):
            pre = r.acc[part, span] + r.vec[own, 11 + k : 12 + k]
            half = 0.5 * (1.0 + lax.erf(pre * 0.7071067811865476))
            r.act[part, span] = (pre * half).astype(BF)
            slope = half + pre * jnp.exp(-0.5 * pre * pre) * 0.3989422804014327
            r.grad_pre[part, span] = (r.grad_act[part, span] * slope).astype(BF)

        over_spans(rows, bend, 256)
    r.acc[...] = beside([r.rest[3 + k] for k in range(ff_blocks)])(r.grad_pre, cols)

    def stats(span):
        scaled = r.acc[:, span] * r.vec[:, 9:10]
        r.stats[pl.ds(plane, 1), 0:1, span] = jnp.sum(scaled, 0, keepdims=True)[None]
        r.stats[pl.ds(plane, 1), 1:2, span] = jnp.sum(scaled * r.two_unit[:, span], 0, keepdims=True)[None]

    over_spans(rows, stats)

    def stats_copy(m, slot):
        return push(
            r.stats.at[slot], r.stats.at[slot], r.stats_send.at[m], r.stats_recv.at[slot], mdl=m
        )

    for m in others(plane, mdl):
        stats_copy(m, plane).start()
    r.parts[...] = r.acc[...].astype(BF).reshape(mdl, cols, rows)
    shape = Sum.buffers(plan, (cols, rows))
    grad_sum = Sum(plan, r.parts, r.grad_net)
    grad_sum.start()
    out = beside([r.rest[3 + ff_blocks + k] for k in range(ff_blocks)])(r.act, cols)
    r.out_parts[...] = out.astype(BF).reshape(mdl, cols, rows)
    grad_sum.middle()
    out_sum = Sum(plan, r.out_parts, r.out_net)
    out_sum.start()
    for m in others(plane, mdl):
        stats_copy(m, m).wait_recv()
    mean = sum(r.stats[m, 0:1] for m in range(mdl)) / C
    cross = sum(r.stats[m, 1:2] for m in range(mdl)) / C
    cot = r.cot[...].astype(F32)
    grad_normed = grad_sum.finish()
    unit = r.two_unit[own, :]
    grad_two = cot + r.two_std[...] * (grad_normed * r.vec[own, 9:10] - mean - unit * cross)
    r.grad_two[...] = grad_two
    branch = grad_two.astype(BF)
    r.branch_full[own, :] = branch
    route = Route(plan, r.send_pos, r.arrival, r.grad_slot, r.in_route)
    route.start(branch)
    fetch(plan, r, 2, START)
    out_sum.middle()

    def along(values):
        return jnp.sum(values.astype(F32), 1, keepdims=True)

    r.mlp_sums[:, 0:1] = along(branch)
    r.mlp_sums[:, 1:2] = along(grad_normed * unit)
    r.mlp_sums[:, 2:3] = along(grad_normed)
    for k in range(ff_blocks):
        part = slice(k * cols, (k + 1) * cols)
        r.mlp_sums[:, 3 + k : 4 + k] = along(r.grad_pre[part, :])
        r.mlp_grads[k] = dot(r.normed[...], r.grad_pre[part, :], NT).astype(BF)
        r.mlp_grads[ff_blocks + k] = dot(r.cot_full[...], r.act[part, :], NT).astype(BF)
    r.mlp_sums[:, 3 + ff_blocks : 4 + ff_blocks] = along(cot)
    moves(START, r.grad_two_move)
    route.land()
    bias = r.vec[own, 11 + ff_blocks : 12 + ff_blocks]
    r.out[...] = (r.stream[own, :] + out_sum.finish() + bias).T.astype(BF)
    route.finish()
    for m in others(plane, mdl):
        stats_copy(m, plane).wait_send()


def attend_part(plan, r):
    plane = lax.axis_index(MDL)
    rows, cols = r.values.shape
    heads = cols // HD
    group = column(r.group[...])
    lane = lax.broadcasted_iota(jnp.int32, (rows, cols), 1)
    same = lane == group
    slot_in = r.slot_in[...]
    queries = (dot(slot_in, r.rest[0], TN) + r.vectors[6:7, :]).astype(BF)
    r.q_ext[:, :cols] = queries * BF(HD ** (-0.5))
    r.q_ext[:, cols:] = jnp.where(same, 1.0, 0.0).astype(BF)
    r.k_ext[:, :cols] = dot(slot_in, r.rest[1], TN).astype(BF)
    r.k_ext[:, cols:] = jnp.where(same | (lane >= plan.groups), 0.0, -1e30).astype(BF)
    values = dot(slot_in, r.rest[2], TN) + r.vectors[7:8, :]
    r.values[...] = values.astype(BF)
    r.v_ext[:, :cols] = values.astype(BF)
    r.v_ext[:, cols:] = jnp.ones((rows, cols), BF)
    r.heads_out[...] = jnp.zeros_like(r.heads_out)
    r.heads_lse[...] = jnp.zeros_like(r.heads_lse)

    def one(head, carry):
        keys, weights = r.k_ext[...], r.v_ext[...]
        lane = lax.broadcasted_iota(jnp.int32, (TILE, cols), 1)
        for tile in range(rows // TILE):
            span = slice(tile * TILE, (tile + 1) * TILE)
            scores = dot(head_lanes(r.q_ext[span, :], cols, head), keys, NT)
            top = jnp.max(scores, 1, keepdims=True)
            summed = dot(jnp.exp(scores - top).astype(BF), weights)
            total = summed[:, cols : cols + 1]
            r.heads_out[span, :] = jnp.where(
                lane // HD == head, summed[:, :cols] / total, r.heads_out[span, :]
            )
            r.heads_lse[span, :] = jnp.where(
                lane == head, top + jnp.log(total), r.heads_lse[span, :]
            )
        return carry

    route = Route(plan, r.arrival, r.send_pos, r.attended_rows, r.out_route)
    for i, trade in enumerate(route.trades):
        share = heads // route.PIECES
        lax.fori_loop(i * share, (i + 1) * share, one, 0, unroll=2)
        part = slice(i * route.size, (i + 1) * route.size)
        r.attended[part, :] = r.heads_out[...].T[part].astype(BF)
        trade.start(r.attended[part, :])
    r.lse[...] = r.heads_lse[...].T[:heads][:, None]
    fetch(plan, r, 0, START)
    fetch(plan, r, 1, START)
    route.land()
    route.finish()


def attend_back_part(plan, r):
    plane = lax.axis_index(MDL)
    rows, cols = r.values.shape
    heads = cols // HD
    greet(everyone(plan))
    mlp_count = r.mlp_grads.shape[0]
    reduce = Reduce(
        plan, r.reduce_net
    )
    for group in range(reduce.groups):
        for place in range(MLP_PACK):
            reduce.store(r.mlp_grads[group * MLP_PACK + place], group, place)
        reduce.start(group)
    branch_gather = Gather(
        plan, lambda m: r.branch_full.at[pl.ds(m * cols, cols)],
        r.branch_net,
    )
    branch_gather.start()
    fetch(plan, r, 3, START)
    grad_slot = r.grad_slot[...]
    grad_t = dot(r.pair[pl.ds(plane, 1), 1][0], grad_slot, TN).astype(BF).astype(F32)
    r.grad[...] = grad_t.T.astype(BF)
    weighed = grad_t * r.attended[...].astype(F32)
    r.inner[...] = jnp.sum(weighed.reshape(heads, HD, rows), 1, keepdims=True)
    r.keys_t[...] = r.k_ext[:, :cols].astype(F32).T.astype(BF)
    r.dk_acc[...] = jnp.zeros_like(r.dk_acc)
    r.dv_acc[...] = jnp.zeros_like(r.dv_acc)

    def one(head, carry):
        queries = head_lanes(r.q_ext[...], cols, head)
        pure = queries[:, :cols]
        grad = head_lanes(r.grad[...], cols, head)
        lse = r.lse[pl.ds(head, 1)][0]
        inner = r.inner[pl.ds(head, 1)][0]
        keys_t = r.keys_t[head_rows(head), :]
        dq = jnp.zeros((HD, rows), F32)
        for tile in range(rows // TILE):
            span = slice(tile * TILE, (tile + 1) * TILE)
            scores = dot(r.k_ext[span, :], queries, NT)
            soft = jnp.exp(scores - lse)
            grad_soft = dot(r.values[span, :], grad, NT)
            grad_scores = (soft * (grad_soft - inner)).astype(BF)
            r.dv_acc[span, :] += dot(soft.astype(BF), grad)
            r.dk_acc[span, :] += dot(grad_scores, pure)
            dq = dq + dot(keys_t[:, span], grad_scores)
        r.dq[head_rows(head), :] = (dq * HD ** (-0.5)).astype(BF)
        reduce.step(head - delay)
        return carry

    delay = max(heads - reduce.steps, 0)
    lax.fori_loop(0, heads, one, 0, unroll=2)
    for s in range(heads - delay, reduce.steps):
        reduce.step(s)
    branch_gather.forward()
    dk = r.dk_acc[...].astype(BF)
    dv = r.dv_acc[...].astype(BF)
    back = dot(r.rest[0], r.dq[...]) + dot(r.rest[1], dk, NT) + dot(r.rest[2], dv, NT)
    r.parts[...] = back.astype(BF).reshape(plan.mdl, cols, rows)
    back_sum = Sum(plan, r.parts, r.sum_net)
    back_sum.start()
    r.attend_grads[0] = dot(r.slot_in[...], r.dq[...], NT).astype(BF)
    r.attend_grads[1] = dot(r.slot_in[...], dk).astype(BF)
    back_sum.middle()
    r.attend_grads[2] = dot(r.slot_in[...], dv).astype(BF)
    r.attend_grads[3] = dot(r.grad_slot[...], r.attended[...], NT).astype(BF)
    route = Route(plan, r.arrival, r.send_pos, r.grad_normed, r.back_route)
    route.start(back_sum.finish().astype(BF))
    moves(START, r.attend_grads_move)
    r.attend_sums[...] = jnp.zeros_like(r.attend_sums)
    r.attend_sums[:, 0:1] = jnp.sum(r.dq[...].astype(F32), 1, keepdims=True)
    r.attend_sums[:, 1:2] = jnp.sum(dv.astype(F32), 0, keepdims=True).T
    route.land()
    branch_gather.finish()
    moves(START, r.branch_full_move)
    route.finish()
    reduce.finish(r.mlp_summed)
    reduce.end()


MLP_PACK = 4


MLP_PACK = 4


def fetch(plan, r, place, act):
    source = (r.left32, r.right32, r.first32, r.second32)[place]
    whole = (r.left_whole, r.right_whole, r.first_whole, r.second_whole)[place]
    if act == START:
        moves(WAIT, (r.left32_move, r.right32_move, r.first32_move, r.second32_move)[place])
        r.low[place] = source[...].astype(BF)
    fetch_copies(plan, r.low.at[place], whole, r.fetch_net[place], act)


def middle_kernel(plan, r):
    moves(START, r.left32_move, r.pair_move, r.stream_move, r.cot_full_move)
    moves(START, r.right32_move, r.first32_move, r.second32_move)
    greet(everyone(plan))
    r.cot[...] = r.cot_rows[...].astype(F32).T.astype(BF)
    attend_part(plan, r)
    mlp_part(plan, r)
    attend_back_part(plan, r)
    for place in range(4):
        fetch(plan, r, place, WAIT)
    moves(WAIT, r.grad_two_move, r.attend_grads_move, r.branch_full_move)


def middle(plan, first, vectors, cot, left, right, moment, second):
    rows, cols = cot.shape
    ff_blocks = FF // C
    heads = cols // HD
    vmem = pltpu.VMEM
    whole = (fetch_shape(plan, left).shape, BF)
    route = Route.buffers(plan, cols, rows)
    total = Sum.buffers(plan, (cols, rows))
    return call(
        functools.partial(middle_kernel, plan),
        "middle",
        2,
        dict(
            slot_in=first.slot_in, rest=first.rest, vectors=vectors, group=first.group,
            send_pos=first.send_pos, arrival=first.arrival, vec=first.vec, cot_rows=cot,
            pair=Late(first.pair), stream=Late(first.stream), cot_full=Late(first.cot_full),
            left32=Late(left), right32=Late(right), first32=Late(moment), second32=Late(second),
        ),
        dict(
            left_whole=whole,
            right_whole=whole,
            first_whole=whole,
            second_whole=whole,
            grad_two=Late((cols, rows), F32),
            out=((rows, cols), BF),
            mlp_sums=((cols, 4 + ff_blocks), F32),
            grad_normed=((C, rows), BF),
            attend_grads=Late((4, C, cols), BF),
            attend_sums=((cols, 8), F32),
            branch_full=Late((C, rows), BF),
            mlp_summed=((2 * ff_blocks, C // plan.pts, cols), BF),
        ),
        dict(
            low=vmem((4,) + left.shape, BF),
            q_ext=vmem((rows, 2 * cols), BF),
            k_ext=vmem((rows, 2 * cols), BF),
            values=vmem((rows, cols), BF),
            attended=vmem((cols, rows), BF),
            lse=vmem((heads, 1, rows), F32),
            attended_rows=vmem((C, rows), BF),
            v_ext=vmem((rows, 2 * cols), BF),
            heads_out=vmem((rows, cols), F32),
            heads_lse=vmem((rows, cols), F32),
            cot=vmem((cols, rows), BF),
            acc=vmem((C, rows), F32),
            two_unit=vmem((C, rows), F32),
            two_std=vmem((1, rows), F32),
            normed=vmem((C, rows), BF),
            grad_act=vmem((ff_blocks * cols, rows), F32),
            act=vmem((ff_blocks * cols, rows), BF),
            grad_pre=vmem((ff_blocks * cols, rows), BF),
            stats=vmem((plan.mdl, 8, rows), F32),
            stats_send=dma(plan.mdl),
            stats_recv=dma(plan.mdl),
            parts=vmem((plan.mdl, cols, rows), BF),
            out_parts=vmem((plan.mdl, cols, rows), BF),
            grad_slot=vmem((C, rows), BF),
            mlp_grads=vmem((2 * ff_blocks, C, cols), BF),
            grad=vmem((rows, cols), BF),
            inner=vmem((heads, 1, rows), F32),
            keys_t=vmem((cols, rows), BF),
            dk_acc=vmem((rows, cols), F32),
            dv_acc=vmem((rows, cols), F32),
            dq=vmem((cols, rows), BF),
            grad_net=total,
            out_net=total,
            sum_net=total,
            out_route=route,
            in_route=route,
            back_route=route,
            branch_net=Gather.semaphores(plan),
            reduce_net=Reduce.buffers(plan, 2 * ff_blocks, MLP_PACK, cols),
            fetch_net=[fetch_sems(plan)] * 4,
        ),
        14 * heads * rows * rows * cols + 16 * rows * C * cols * ff_blocks,
        free=("left_whole", "right_whole", "first_whole", "second_whole"),
    )


BACK_ORDER = [TAPS + 1, TAPS + 2, TAPS + 3, TAPS + 4, TAPS] + list(range(TAPS))
MLP_ORDER = list(range(TAPS + 5, TAPS + 5 + 2 * FF // C))
BACK_PACK = 4


def back_kernel(plan, r):
    pts = plan.pts
    cols, rows = r.turn_acc.shape
    taps = r.taken.shape[0]
    ready = r.attend_grads.shape[0]
    extra = ready + 1
    me, plane = lax.axis_index(PTS), lax.axis_index(MDL)
    own_cols = pl.ds(plane * cols, cols)
    middle = slice(HALO, HALO + rows)
    first = (r.grad_normed_move, r.one_unit_move, r.branch_full_move, r.mixed_unit_move, r.pair_move)
    second = (r.hidden_move, r.taken_move, r.grad_two_move, r.taps_move)
    moves(START, *first, *second)
    greet([{PTS: v} for v in others(me, pts)] + [{MDL: plane + 1 - 2 * lax.rem(plane, 2)}])
    reduce = Reduce(
        plan, r.reduce_net
    )
    groups = reduce.groups
    for b in range(ready):
        reduce.store(r.attend_grads[b], b // BACK_PACK, b % BACK_PACK)
    reduce.start(0)
    moves(WAIT, *first)

    def grads(group):
        if group == ready // BACK_PACK:
            reduce.store(dot(r.hidden[...], r.mixed[own_cols, :], NT), group, ready % BACK_PACK)

        def one(place, carry):
            tap = group * BACK_PACK + place - extra
            reduce.store(
                dot(r.back[:, middle], r.taken[pl.ds(tap, 1)][0], NT), group, place
            )
            return carry

        low = max(group * BACK_PACK, extra)
        lax.fori_loop(low - group * BACK_PACK, BACK_PACK, one, 0)

    def norms(span):
        grad = r.grad_normed[:, span].astype(F32) * r.vec[:, 4:5]
        unit = r.one_unit[:, span].astype(F32)
        delta = r.one_std[:, span] * (
            grad
            - jnp.sum(grad, 0, keepdims=True) / C
            - unit * (jnp.sum(grad * unit, 0, keepdims=True) / C)
        )
        r.delta[:, span] = delta
        grad = (r.branch_full[:, span].astype(F32) + delta) * r.vec[:, 2:3]
        unit = r.mixed_unit[:, span].astype(F32)
        r.mixed[:, span] = (
            r.mixed_std[:, span]
            * (
                grad
                - jnp.sum(grad, 0, keepdims=True) / C
                - unit * (jnp.sum(grad * unit, 0, keepdims=True) / C)
            )
        ).astype(BF)

    over_spans(rows, norms)
    back = beside([r.pair[m, 0] for m in range(plan.mdl)])(r.mixed, cols)
    r.back[:, middle] = back.astype(BF)

    core = lax.rem(plane, 2)
    mine = pl.ds(core * (C // 2), C // 2)
    low_end, high_end = slice(0, HALO), slice(HALO + rows, 2 * HALO + rows)

    def up_copy(target):
        return push(
            r.back.at[mine, rows : rows + HALO], r.back.at[mine, low_end], r.halo_send.at[0],
            r.halo_recv.at[0], pts=target,
        )

    def down_copy(target):
        return push(
            r.back.at[mine, HALO : 2 * HALO], r.back.at[mine, high_end],
            r.halo_send.at[1], r.halo_recv.at[1], pts=target,
        )

    def core_copy(end, which, part):
        half = pl.ds(part * (C // 2), C // 2)
        return push(
            r.back.at[half, end], r.back.at[half, end], r.core_send.at[which],
            r.core_recv.at[which], mdl=plane + 1 - 2 * core,
        )

    @pl.when(me < pts - 1)
    def _():
        up_copy(me + 1).start()

    @pl.when(me == pts - 1)
    def _():
        r.back[:, HALO + rows :] = jnp.zeros((C, HALO), BF)

    @pl.when(me > 0)
    def _():
        down_copy(me - 1).start()

    @pl.when(me == 0)
    def _():
        r.back[:, :HALO] = jnp.zeros((C, HALO), BF)

    moves(WAIT, *second)
    for group in range(1, groups):
        grads(group)
        reduce.start(group)
        if group >= LAG:
            reduce.step(group - LAG)

    grad_one = r.grad_two[...] + r.delta[own_cols, :]
    r.grad_one[...] = grad_one

    def along(values):
        return jnp.sum(values.astype(F32), 1, keepdims=True)

    grad_normed = r.grad_normed[own_cols, :].astype(F32)
    columns = [
        along(r.back[own_cols, middle]),
        along(r.mixed[own_cols, :]),
        along(grad_one * r.mixed_unit[own_cols, :]),
        along(grad_one),
        along(grad_normed * r.one_unit[own_cols, :]),
        along(grad_normed),
        r.attend_sums[:, 0:2],
        r.mlp_sums[...],
    ]
    r.vectors[pl.ds(me, 1)] = jnp.concatenate(columns, 1).T[None]

    def vector_copy(p, slot):
        return push(
            r.vectors.at[slot], r.vectors.at[slot], r.vector_send.at[p], r.vector_recv.at[slot],
            pts=p,
        )

    for p in others(me, pts):
        vector_copy(p, me).start()

    @pl.when(me > 0)
    def _():
        up_copy(me - 1).wait_recv()
        core_copy(low_end, 0, core).start()

    @pl.when(me < pts - 1)
    def _():
        down_copy(me + 1).wait_recv()
        core_copy(high_end, 1, core).start()

    @pl.when(me > 0)
    def _():
        core_copy(low_end, 0, 1 - core).wait_recv()

    @pl.when(me < pts - 1)
    def _():
        core_copy(high_end, 1, 1 - core).wait_recv()

    def turn(tap, carry):
        weight = r.taps[:, pl.ds(taps - 1 - tap, 1)].reshape(C, cols)
        turned = dot(weight, r.back[...], TN).astype(BF)
        for tile in range(rows // TILE):
            hot = one_hot_window(r.ids, tap, tile)
            r.turn_acc[:, tile * TILE : (tile + 1) * TILE] += dot(
                turned[:, tile * TILE : tile * TILE + WINDOW], hot
            )
        return carry

    r.turn_acc[...] = jnp.zeros_like(r.turn_acc)
    left = list(range(groups - LAG, reduce.steps))
    cuts = [taps * i // len(left) for i in range(len(left) + 1)]
    for i, s in enumerate(left):
        lax.fori_loop(cuts[i], cuts[i + 1], turn, 0)
        reduce.step(s)
    r.point_grad[...] = (r.turn_acc[...] + r.grad_one[...]).T
    reduce.finish(r.summed)
    total = r.vectors[pl.ds(me, 1)][0]
    for p in others(me, pts):
        vector_copy(p, p).wait_recv()
        total = total + r.vectors[pl.ds(p, 1)][0]
    r.vector_grad[...] = total
    reduce.end()
    for p in others(me, pts):
        vector_copy(p, me).wait_send()

    @pl.when(me < pts - 1)
    def _():
        up_copy(me + 1).wait_send()
        core_copy(high_end, 1, core).wait_send()

    @pl.when(me > 0)
    def _():
        down_copy(me - 1).wait_send()
        core_copy(low_end, 0, core).wait_send()


LAG = 5


def back_pass(
    plan, first, ids, grad_normed, branch_full, grad_two, attend_grads, mlp_sums, attend_sums
):
    taps, cols, rows = first.taken.shape
    total = len(BACK_ORDER)
    share = C // plan.pts
    vmem = pltpu.VMEM
    return call(
        functools.partial(back_kernel, plan),
        "back_pass",
        1,
        dict(
            taken=Late(first.taken), pair=Late(first.pair), vec=first.vec, hidden=Late(first.hidden), mixed_unit=Late(first.mixed_unit), mixed_std=first.mixed_std, one_unit=Late(first.one_unit), one_std=first.one_std, taps=Late(first.taps_far), ids=ids,
            grad_normed=Late(grad_normed),
            branch_full=Late(branch_full), grad_two=Late(grad_two), attend_grads=attend_grads, mlp_sums=mlp_sums, attend_sums=attend_sums,
        ),
        dict(
            summed=((total, share, cols), BF),
            point_grad=((rows, cols), F32),
            vector_grad=((12 + FF // C, cols), F32),
        ),
        dict(
            reduce_net=(Reduce.buffers(plan, total, BACK_PACK, cols)),
            turn_acc=vmem((cols, rows), F32),
            grad_one=vmem((cols, rows), F32),
            delta=vmem((C, rows), F32),
            mixed=vmem((C, rows), BF),
            back=vmem((C, rows + 2 * HALO), BF),
            vectors=vmem((plan.pts, 12 + FF // C, cols), F32),
            halo_send=dma(2),
            halo_recv=dma(2),
            core_send=dma(2),
            core_recv=dma(2),
            vector_send=dma(plan.pts),
            vector_recv=dma(plan.pts),
        ),
        taps * rows * (WINDOW * 4 + 5 * C) * cols,
    )


def adam(first, second, grad):
    new_first = BETA_ONE * first + (1.0 - BETA_ONE) * grad
    new_second = BETA_TWO * second + (1.0 - BETA_TWO) * grad * grad
    direction = (
        new_first
        / (1.0 - BETA_ONE**STEP)
        / (jnp.sqrt(new_second / (1.0 - BETA_TWO**STEP)) + ADAM_EPS)
    )
    return new_first, new_second, direction


def owner_kernel(plan, r):
    pts, mdl, slots = plan.pts, plan.mdl, plan.slots
    share, cols = r.summed.shape[1:]
    me, plane = lax.axis_index(PTS), lax.axis_index(MDL)
    moves(START, r.left_move, r.right_move, r.first_move, r.second_move)
    greet(
        [
            {PTS: p, MDL: m}
            for i, p in enumerate([me] + others(me, pts))
            for j, m in enumerate([plane] + others(plane, mdl))
            if i + j > 0
        ]
    )

    count = r.summed.shape[0]
    r.listed[:count] = r.summed[...]
    r.listed[count:] = r.mlp_summed[...]

    def order(slot, carry):
        r.grads[pl.ds(slot, 1)] = r.listed[pl.ds(r.places[slot], 1)]
        return carry

    def whole_copy(j, step):
        m = lax.rem(plane + step, mdl)
        target, k = plan.worker(j), j // pts
        piece, spot = r.grads.at[m * slots + j], r.whole.at[k, me, plane]

        def near():
            return pltpu.make_async_copy(piece, spot, r.whole_here.at[k])

        def far():
            return push(
                piece, spot, r.whole_send.at[step, j], r.whole_recv.at[k, me, plane], pts=target,
                mdl=m,
            )

        return (me == target) & (step == 0), near, far

    def rows_copy(m, slot):
        return push(
            r.grads.at[pl.ds(m * slots, slots)], r.rows.at[slot], r.rows_send.at[m],
            r.rows_recv.at[slot], mdl=m,
        )

    def rows_here():
        return pltpu.make_async_copy(
            r.grads.at[pl.ds(plane * slots, slots)], r.rows.at[plane], r.rows_home
        )

    for step in range(mdl):
        m = lax.rem(plane + step, mdl)
        lax.fori_loop(m * slots, (m + 1) * slots, order, 0)
        for j in range(slots):
            home, near, far = whole_copy(j, step)

            @pl.when(home)
            def _():
                near().start()

            @pl.when(jnp.logical_not(home))
            def _():
                far().start()

    for m in others(plane, mdl):
        rows_copy(m, plane).start()
    rows_here().start()
    moves(WAIT, r.left_move, r.right_move, r.first_move, r.second_move)

    def result_copy(k, kind, p):
        return push(
            r.turned.at[k, kind, p], r.results.at[plan.work(me, k), kind], r.back_send.at[k, kind, p],
            r.back_recv.at[plan.work(me, k), kind], pts=p,
        )

    def result_here(k, kind):
        return pltpu.make_async_copy(
            r.turned.at[k, kind, me], r.results.at[plan.work(me, k), kind], r.back_home.at[k, kind]
        )

    def send_result(k, kind, value):
        r.turned[k, kind] = value.astype(BF).reshape(pts, share, C)
        for p in others(me, pts):
            result_copy(k, kind, p).start()
        result_here(k, kind).start()

    for k in range(plan.each):

        @pl.when(plan.work(me, k) < slots)
        def _():
            pltpu.make_async_copy(
                r.grads.at[0], r.whole.at[k, me, plane], r.whole_here.at[k]
            ).wait()
            for p_step in range(pts):
                for m_step in range(mdl):
                    if p_step + m_step > 0:
                        p, m = lax.rem(me + p_step, pts), lax.rem(plane + m_step, mdl)
                        push(
                            r.grads.at[0], r.whole.at[k, p, m], r.whole_send.at[0, 0],
                            r.whole_recv.at[k, p, m], pts=p, mdl=m,
                        ).wait_recv()
            left = r.left[k].reshape(C, C)
            right = r.right[k].reshape(C, C)
            halves = [
                dot(left, r.whole[k, :, m].reshape(C, cols), TN).astype(BF) for m in range(mdl)
            ]
            if cols % 128 == 0:
                rotated = dot(jnp.concatenate(halves, 1), right)
            else:
                rotated = sum(
                    dot(half, right[m * cols : (m + 1) * cols]) for m, half in enumerate(halves)
                )
            send_result(k, 0, rotated)
            _, _, direction = adam(
                r.first[k].reshape(C, C).astype(F32),
                r.second[k].reshape(C, C).astype(F32),
                rotated.astype(BF).astype(F32),
            )
            send_result(k, 1, dot(left, dot(direction.astype(BF), right, NT).astype(BF)))

    for m in others(plane, mdl):
        rows_copy(m, plane).wait_send()
        rows_copy(m, m).wait_recv()
    rows_here().wait()
    for j in range(slots):
        source, k = plan.worker(j), j // pts
        for kind in range(2):

            @pl.when(me != source)
            def _():
                push(
                    r.turned.at[k, kind, me], r.results.at[j, kind], r.back_send.at[k, kind, source],
                    r.back_recv.at[j, kind], pts=source,
                ).wait_recv()

    for k in range(plan.each):

        @pl.when(plan.work(me, k) < slots)
        def _():
            for kind in range(2):
                result_here(k, kind).wait()
                for p in others(me, pts):
                    result_copy(k, kind, p).wait_send()

    for step in range(mdl):
        for j in range(slots):
            home, near, far = whole_copy(j, step)

            @pl.when(jnp.logical_not(home))
            def _():
                far().wait_send()


def owner_update(plan, places, summed, mlp_summed, left, right, first, second):
    _, share, cols = summed.shape
    blocks = len(BACK_ORDER) + len(MLP_ORDER)
    pts, mdl, each, slots = plan.pts, plan.mdl, plan.each, plan.slots
    vmem = pltpu.VMEM
    return call(
        functools.partial(owner_kernel, plan),
        "owner_update",
        4,
        dict(places=places, summed=summed, mlp_summed=mlp_summed, left=Late(left), right=Late(right), first=Late(first), second=Late(second)),
        dict(
            rows=((mdl, slots, share, cols), BF),
            results=((slots, 2, share, C), BF),
        ),
        dict(
            grads=vmem((blocks, share, cols), BF),
            listed=vmem((blocks, share, cols), BF),
            whole=vmem((each, pts, mdl, share, cols), BF),
            turned=vmem((each, 2, pts, share, C), BF),
            whole_send=dma(mdl, slots),
            whole_recv=dma(each, pts, mdl),
            whole_here=dma(each),
            rows_send=dma(mdl),
            rows_recv=dma(mdl),
            rows_home=dma(),
            back_send=dma(each, 2, pts),
            back_recv=dma(slots, 2),
            back_home=dma(each, 2),
        ),
        8 * each * C * C * C,
        smem=("places",),
    )


def scan_index(row_ids, scan_lengths):
    bounds = jnp.cumsum(scan_lengths)
    return jnp.sum((row_ids[..., None] >= bounds[:-1]).astype(jnp.int32), -1)


def local(
    points,
    cotangent,
    neighbours,
    scan_lengths,
    to_patch,
    from_patch,
    owner_slot,
    weights,
    row_eigen_basis,
    right_basis,
    first_moment,
    second_moment,
    vectors,
    vector_first,
    vector_second,
):
    rows, cols = points.shape
    slot_count = from_patch.shape[0]
    pts = lax.axis_size(PTS)
    mdl = lax.axis_size(MDL)
    pts_index = lax.axis_index(PTS)
    patch_count = slot_count // PATCH
    matrix_rate = 1.6 * C ** (-0.5)
    plan = Layout(pts, mdl, owner_slot.shape[0], patch_count * scan_lengths.shape[0])

    row_ids = pts_index * rows + jnp.arange(rows, dtype=jnp.int32)
    own_scan = scan_index(row_ids, scan_lengths)
    near = neighbours.T
    usable = (near >= 0) & (scan_index(jnp.maximum(near, 0), scan_lengths) == own_scan[None, :])
    ids = jnp.where(usable, near - (pts_index * rows - HALO), -1)

    first = front(
        plan,
        owner_slot,
        weights,
        points,
        cotangent,
        vectors,
        ids,
        to_patch[None],
        from_patch[None],
        scan_lengths,
    )
    between = middle(
        plan, first, vectors, cotangent, row_eigen_basis, right_basis, first_moment, second_moment
    )
    last = back_pass(
        plan,
        first,
        ids,
        between.grad_normed,
        between.branch_full,
        between.grad_two,
        between.attend_grads,
        between.mlp_sums,
        between.attend_sums,
    )
    vector_grad = last.vector_grad
    listed = BACK_ORDER + MLP_ORDER
    places = jnp.array([listed.index(b) for b in range(len(listed))], jnp.int32)
    slot_ids = jnp.arange(len(listed), dtype=jnp.int32)
    place_of_slot = jnp.sum(
        jnp.where(owner_slot[None, :] == slot_ids[:, None], places[None, :], 0), 1
    )
    ended = owner_update(
        plan,
        place_of_slot,
        last.summed,
        between.mlp_summed,
        between.left_whole,
        between.right_whole,
        between.first_whole,
        between.second_whole,
    )
    reduced = ended.rows.transpose(1, 2, 0, 3).reshape(plan.slots, C // pts, C)
    results = ended.results
    rotated, update = results[:, 0].astype(F32), results[:, 1].astype(F32)
    new_first, new_second, _ = adam(first_moment, second_moment, rotated)
    new_weights = weights - matrix_rate * (update + MATRIX_DECAY * weights)
    new_vector_first, new_vector_second, vector_step = adam(
        vector_first, vector_second, vector_grad
    )
    new_vectors = vectors - VECTOR_RATE * vector_step
    return (
        between.out,
        last.point_grad,
        reduced.astype(F32),
        new_first,
        new_second,
        new_weights,
        new_weights.astype(BF),
        vector_grad,
        new_vector_first,
        new_vector_second,
        new_vectors,
    )


def solution(mesh):
    by_rows = P(PTS, MDL)
    owned = P(MDL, PTS, None)
    vector = P(None, MDL)
    return jax.shard_map(
        local,
        mesh=mesh,
        in_specs=(
            by_rows,
            by_rows,
            P(PTS, None),
            P(),
            P(PTS),
            P(PTS),
            P(),
            owned,
            owned,
            owned,
            owned,
            owned,
            vector,
            vector,
            vector,
        ),
        out_specs=(
            by_rows,
            by_rows,
            owned,
            owned,
            owned,
            owned,
            owned,
            vector,
            vector,
            vector,
            vector,
        ),
        check_vma=False,
    )
```
